32 devices in a mesh: dp: 16 (over z, x, core), mp: 2 (over y).
Axes of the slice: x: 2, y: 2, z: 4, core: 2. Of those that a mesh axis runs over, the one named last changes fastest.
Arguments:
- hidden_in: bfloat16 [32768, 1024], P(('dp', 'mp')), may hold values from -6 to 6
- query_weight: bfloat16 [1024, 1024], replicated, may hold values from -0.1875 to 0.1875
- key_weight: bfloat16 [1024, 1024], replicated, may hold values from -0.1875 to 0.1875
- value_weight: bfloat16 [1024, 1024], replicated, may hold values from -0.1875 to 0.1875
- select_weight: bfloat16 [1024, 1024], replicated, may hold values from -0.1875 to 0.1875
- out_weight: bfloat16 [1024, 1024], replicated, may hold values from -0.1875 to 0.1875
- first_weight: bfloat16 [1024, 2816], P(None, 'mp'), may hold values from -0.1875 to 0.1875
- second_weight: bfloat16 [1024, 2816], P(None, 'mp'), may hold values from -0.1875 to 0.1875
- down_weight: bfloat16 [2816, 1024], P('mp'), may hold values from -0.109375 to 0.109375
- decay_slope: float32 [8], replicated, may hold values from 0.00012207031 to 0.5
- doc_lengths: int32 [16, 3], P('dp'), may hold values from 384 to 1024, as said below
- cotangent: bfloat16 [32768, 1024], P(('dp', 'mp')), may hold values from -6 to 6
Outputs:
- output: bfloat16 [32768, 1024], P(('dp', 'mp'))
- grad_hidden: bfloat16 [32768, 1024], P(('dp', 'mp'))
- grad_query: float32 [1024, 1024], P('dp', 'mp')
- grad_key: float32 [1024, 1024], P('dp', 'mp')
- grad_value: float32 [1024, 1024], P('dp', 'mp')
- grad_select: float32 [1024, 1024], P('dp', 'mp')
- grad_out: float32 [1024, 1024], P('dp', 'mp')
- grad_first: float32 [1024, 2816], P('dp', 'mp')
- grad_second: float32 [1024, 2816], P('dp', 'mp')
- grad_down: float32 [2816, 1024], P('mp', 'dp')
The draws below stay inside these ranges and needn't reach their ends.
Inputs may be any that keep to these rules, and one draw needn't show every extreme that they name: `doc_lengths`: row g gives the lengths of the 3 documents packed in order from the first of the group's 2048 rows; the rows after them are padding. Two of the documents have 2048 // 4 tokens and one has 1024, which one is drawn; the last document gives up 0 to 128 of its tokens to padding.
All inputs are finite; a program needn't handle non-finite values.
Results may differ from the reference program's by a relative error of at most 0.019.
Values may be sent and summed in bfloat16 or wider, within the bound.
A program may use at most 320 MiB of HBM per device.

```python
import math
from functools import partial
import jax
import jax.numpy as jnp
from jax import lax

D = 1024
HEADS = 8
HEAD = 128
FF = 2816
DOCS = 3
GROUP = 2048
TOKENS = 32768
N_DP = 16
N_MP = 2


def draw_doc_lengths(key, part):
    key = jax.random.fold_in(key, 11)
    streams = jax.random.split(key, 2)
    pattern = jax.random.randint(streams[0], (N_DP,), 0, 3)
    padding = jax.random.randint(streams[1], (N_DP,), 0, GROUP // 16 + 1)
    numbers = jnp.arange(3, dtype=jnp.int32)
    base = jnp.where(numbers[None, :] == pattern[:, None], GROUP // 2, GROUP // 4)
    last = (numbers[None, :] == 2).astype(jnp.int32)
    return (base - last * padding[:, None]).astype(jnp.int32)


def strengthened(drawn, rng, source, target, shards_of, factor):
    owner, partner = [(jnp.arange(drawn.shape[dim]) // (drawn.shape[dim] // shards_of)).reshape([-1 if axis == dim else 1 for axis in range(drawn.ndim)]) for dim in (source, target)]
    chosen = jax.random.permutation(rng, shards_of)[partner]
    strong = (owner == chosen) | (owner == (partner + shards_of // 2) % shards_of)
    return jnp.where(strong, factor * drawn, drawn)


def shard_levels(stream_key, dims, shards, least, largest):
    gain, own = 1.0, jax.random.fold_in(stream_key, 6)
    for axis_at, parts in shards:
        heights = jnp.exp(jax.random.uniform(jax.random.fold_in(own, axis_at), (parts,), jnp.float32, least / len(shards), largest / len(shards)))
        gain = gain * jnp.repeat(heights, dims[axis_at] // parts).reshape([-1 if axis == axis_at else 1 for axis in range(len(dims))])
    return gain


def bell_draw(rng, shape, deviation, most, cuts=(), kind=jnp.bfloat16):
    values = jax.random.normal(rng, shape, jnp.float32) * deviation
    if len(cuts) > 0:
        values = shard_levels(rng, shape, cuts, -0.22, 0.18) * values
    return jnp.clip(values, min=-most, max=most).astype(kind)


def bell_draw_with(rng, extent, scale, most, cuts, heavy, kind=jnp.bfloat16):
    entries = scale * jax.random.normal(rng, extent, jnp.float32)
    if cuts:
        entries = entries * shard_levels(rng, extent, cuts, -0.22, 0.18)
    return jnp.clip(strengthened(entries, jax.random.fold_in(rng, 3), *heavy), -most, most).astype(kind)


def setup_inputs(seed: int = 0) -> dict:
    key_of = jax.random.split(jax.random.key(seed), 13)
    return {
        "hidden_in": bell_draw(key_of[0], (TOKENS, D), 1.0, 6.0, ((0, 32),)),
        "query_weight": bell_draw(key_of[1], (D, D), D ** -0.5, 0.1875),
        "key_weight": bell_draw(key_of[2], (D, D), D ** -0.5, 0.1875),
        "value_weight": bell_draw(key_of[3], (D, D), D ** -0.5, 0.1875),
        "select_weight": bell_draw(key_of[4], (D, D), D ** -0.5, 0.1875),
        "out_weight": bell_draw(key_of[5], (D, D), D ** -0.5, 0.1875),
        "first_weight": bell_draw(key_of[6], (D, FF), D ** -0.5, 0.1875, ((1, 2),)),
        "second_weight": bell_draw(key_of[7], (D, FF), D ** -0.5, 0.1875, ((1, 2),)),
        "down_weight": bell_draw(key_of[8], (FF, D), FF ** -0.5, 0.109375, ((0, 2),)),
        "decay_slope": jnp.clip(jnp.exp(jax.random.uniform(key_of[9], (HEADS,), jnp.float32, math.log(0.00012207031), math.log(0.5))), 0.00012207031, 0.5),
        "doc_lengths": draw_doc_lengths(jax.random.fold_in(key_of[12], 71), 0),
        "cotangent": bell_draw_with(key_of[11], (TOKENS, D), 1.0, 6.0, ((0, 32),), (0, 1, 32, 2.75)),
    }


EPSILON = 1e-06
HIGHEST = lax.Precision.HIGHEST

@jax.custom_vjp
def low(v):
    return lax.optimization_barrier(v.astype(jnp.bfloat16)).astype(jnp.float32)

@jax.custom_vjp
def low_back(v):
    return v

def low_keep(v):
    return (low(v), None)

def low_pass(kept, grad):
    return (grad,)

def back_keep(v):
    return (v, None)

def back_low(kept, grad):
    return (low(grad),)
low.defvjp(low_keep, low_pass)
low_back.defvjp(back_keep, back_low)

def simple_norm(values):
    return values * lax.rsqrt(lax.optimization_barrier(jnp.mean(values * values, axis=-1, keepdims=True)) + EPSILON)

def product(left, right):
    return jnp.dot(left, right, precision=HIGHEST, preferred_element_type=jnp.float32)

def doc_layout(lengths, total):
    lengths = lengths.astype(jnp.int32)
    ends = jnp.cumsum(lengths).astype(jnp.int32)
    starts = (ends - lengths).astype(jnp.int32)
    places = jnp.arange(total, dtype=jnp.int32)
    segment = lax.optimization_barrier(jnp.sum((places[:, None] >= ends[None, :]).astype(jnp.int32), axis=1)).astype(jnp.int32)
    numbers = jnp.arange(DOCS, dtype=jnp.int32)
    begin = lax.optimization_barrier(jnp.sum(jnp.where(segment[:, None] == numbers[None, :], starts[None, :], 0), axis=1)).astype(jnp.int32)
    position = jnp.where(segment < DOCS, places - begin, 0).astype(jnp.int32)
    return (segment, position)

def rotate(values, position):
    freq = 10000.0 ** (-jnp.arange(HEAD, dtype=jnp.float32) / HEAD)
    phase = position.astype(jnp.float32)[:, None] * freq[None, :]
    return jnp.concatenate([values * jnp.cos(phase)[:, None, :], values * jnp.sin(phase)[:, None, :]], axis=-1)

def block_attention(slopes, carry, pieces):
    state, prior = carry
    queries, keys, values, segment = pieces
    count = segment.shape[0]
    steps_idx = jnp.arange(count, dtype=jnp.int32)
    gap = (steps_idx[:, None] - steps_idx[None, :]).astype(jnp.float32)
    live = segment < DOCS
    allowed = (gap >= 0) & (segment[:, None] == segment[None, :]) & live[:, None]
    decay_table = jnp.where(allowed[None], jnp.exp(-slopes[:, None, None] * jnp.maximum(gap, 0.0)[None]), 0.0)
    scores = jnp.einsum('thd,shd->hts', queries, keys, precision=HIGHEST) * decay_table
    result = jnp.einsum('hts,she->the', scores, values, precision=HIGHEST)
    enter = ((segment == prior) & live).astype(jnp.float32)
    fade_in = jnp.exp(-slopes[None, :] * (steps_idx[:, None] + 1).astype(jnp.float32)) * enter[:, None]
    result = result + fade_in[:, :, None] * jnp.einsum('thd,hde->the', queries, state, precision=HIGHEST)
    final = segment[count - 1]
    keep = ((final == prior) & (final < DOCS)).astype(jnp.float32)
    fade_out = jnp.exp(-slopes[None, :] * (count - 1 - steps_idx)[:, None].astype(jnp.float32)) * ((segment == final) & live).astype(jnp.float32)[:, None]
    fresh = jnp.einsum('shd,she->hde', keys * fade_out[:, :, None], values, precision=HIGHEST)
    new_state = keep * jnp.exp(-slopes * count)[:, None, None] * state + fresh
    return ((new_state, final), result)

def group_forward(weights, slopes, inputs):
    hidden, lengths = inputs
    query_weight, key_weight, value_weight, select_weight, out_weight, first_weight, second_weight, down_weight = weights
    segment, position = doc_layout(lengths, GROUP)
    normed = low(simple_norm(hidden))
    query_pre = low_back(product(normed, query_weight))
    key_pre = low_back(product(normed, key_weight))
    values = low_back(product(normed, value_weight))
    select = low_back(product(normed, select_weight))
    queries = rotate(jax.nn.silu(query_pre).reshape(GROUP, HEADS, HEAD), position)
    keys = rotate(jax.nn.silu(key_pre).reshape(GROUP, HEADS, HEAD), position)
    value_heads = values.reshape(GROUP, HEADS, HEAD)
    span = math.gcd(512, GROUP)
    blocks = GROUP // span
    pieces = (queries.reshape(blocks, span, HEADS, 2 * HEAD), keys.reshape(blocks, span, HEADS, 2 * HEAD), value_heads.reshape(blocks, span, HEADS, HEAD), segment.reshape(blocks, span))
    start_state = jnp.zeros((HEADS, 2 * HEAD, HEAD), jnp.float32)
    start_prior = jnp.array(-1, jnp.int32)
    _, results = lax.scan(jax.checkpoint(partial(block_attention, slopes)), (start_state, start_prior), pieces)
    attended = results.reshape(GROUP, D)
    mixed = low(simple_norm(attended) * select)
    branch = low_back(product(mixed, out_weight))
    middle = hidden + branch
    second_in = low(simple_norm(middle))
    inner_width = FF // N_MP
    total = jnp.zeros((GROUP, D), jnp.float32)
    for shard in range(N_MP):
        piece = low_back(second_in)
        lower = shard * inner_width
        left_part = low_back(product(piece, first_weight[:, lower:lower + inner_width]))
        right_part = low_back(product(piece, second_weight[:, lower:lower + inner_width]))
        inner = low(left_part * right_part)
        total = total + low(product(inner, down_weight[lower:lower + inner_width, :]))
    return middle + total

def reference(hidden_in, query_weight, key_weight, value_weight, select_weight, out_weight, first_weight, second_weight, down_weight, decay_slope, doc_lengths, cotangent):
    weights = tuple((weight.astype(jnp.float32) for weight in (query_weight, key_weight, value_weight, select_weight, out_weight, first_weight, second_weight, down_weight)))
    hidden = hidden_in.astype(jnp.float32).reshape(N_DP, GROUP, D)
    slopes = decay_slope.astype(jnp.float32)

    def forward(hidden_all, weight_all):
        return lax.map(jax.checkpoint(partial(group_forward, weight_all, slopes)), (hidden_all, doc_lengths))
    output, pullback = jax.vjp(forward, hidden, weights)
    grad_hidden, grad_weights = pullback(cotangent.astype(jnp.float32).reshape(N_DP, GROUP, D))
    return (output.reshape(TOKENS, D).astype(jnp.bfloat16), grad_hidden.reshape(TOKENS, D).astype(jnp.bfloat16), grad_weights[0], grad_weights[1], grad_weights[2], grad_weights[3], grad_weights[4], grad_weights[5], grad_weights[6], grad_weights[7])
```

```python
import functools

import jax
import jax.numpy as jnp
import numpy as np
from jax import lax
from jax.experimental import pallas as pl
from jax.experimental.pallas import tpu as pltpu
from jax.sharding import PartitionSpec as P

HEAD = 128
CHUNK = 256
EPSILON = 1e-06
BF16 = jnp.bfloat16
F32 = jnp.float32
VMEM_LIMIT = 58 * 1024 * 1024


def nn(left, right):
    return jnp.dot(left, right, preferred_element_type=F32)


def nt(left, right):
    return lax.dot_general(left, right, (((1,), (1,)), ((), ())), preferred_element_type=F32)


def scale_of(values):
    return lax.rsqrt(jnp.mean(values * values, axis=-1, keepdims=True) + EPSILON)


def norm_back(values, scale, upstream):
    return scale * upstream - values * (scale * scale * scale) * jnp.mean(
        values * upstream, axis=-1, keepdims=True
    )


def sigmoid(v):
    return 1.0 / (1.0 + jnp.exp(-v))


def featured(pre, cos, sin):
    act = pre * sigmoid(pre)
    return jnp.concatenate([act * cos, act * sin], axis=-1).astype(BF16)


def head_slice(h):
    return slice(h * HEAD, (h + 1) * HEAD)


def row_index(shape):
    return lax.broadcasted_iota(jnp.int32, shape, 0)


def fade_from_start(slope, width):
    return jnp.exp(-slope * (row_index((CHUNK, width)) + 1).astype(F32))


def fade_to_end(slope, width):
    return jnp.exp(-slope * (CHUNK - 1 - row_index((CHUNK, width))).astype(F32))


def decay_table(slope, transposed):
    rows = lax.broadcasted_iota(jnp.int32, (CHUNK, CHUNK), 0)
    cols = lax.broadcasted_iota(jnp.int32, (CHUNK, CHUNK), 1)
    gap = cols - rows if transposed else rows - cols
    return jnp.where(gap >= 0, jnp.exp(-slope * jnp.maximum(gap, 0).astype(F32)), 0.0)


def smem():
    return pl.BlockSpec(memory_space=pltpu.SMEM)


def anywhere():
    return pl.BlockSpec(memory_space=pl.ANY)


def whole_block(shape):
    zeros = (0,) * len(shape)
    return pl.BlockSpec(shape, lambda *_: zeros)


def params(steps=1):
    return pltpu.CompilerParams(
        vmem_limit_bytes=VMEM_LIMIT, dimension_semantics=("arbitrary",) * steps
    )


def cost(flops, arrays):
    moved = sum(int(np.prod(a.shape)) * jnp.dtype(a.dtype).itemsize for a in arrays)
    return pl.CostEstimate(flops=int(flops), bytes_accessed=moved, transcendentals=0)


def struct(shape, dtype=BF16):
    return jax.ShapeDtypeStruct(tuple(shape), dtype)


def chunk_info(lengths, offset, count):
    chunks = count // CHUNK
    ends = jnp.cumsum(lengths)
    starts = ends - lengths
    first = offset + CHUNK * jnp.arange(chunks, dtype=jnp.int32)
    begin = jnp.max(jnp.where(starts[None, :] <= first[:, None], starts[None, :], 0), axis=1)
    base = first - begin
    keep = (base > 0).astype(jnp.int32)
    before = jnp.cumprod(keep)
    after = jnp.concatenate([jnp.cumprod(keep[::-1])[::-1][1:], jnp.ones((1,), jnp.int32)])
    live = jnp.clip(ends[-1] - offset, 0, count)
    return jnp.concatenate([base, keep, before, after, live[None]]).astype(jnp.int32)


def cos_sin_tables(rows):
    freq = 10000.0 ** (-np.arange(HEAD, dtype=np.float64) / HEAD)
    phase = np.arange(rows, dtype=np.float64)[:, None] * freq[None, :]
    return jnp.asarray(np.cos(phase), F32), jnp.asarray(np.sin(phase), F32)


def keys_kernel(chunks, heads, info, slopes, hid, wk, wv, cos, sin, normed_o, turned_o, kpre_o, val_o, st_o, fin_o, state):
    c = pl.program_id(0)

    @pl.when(c == 0)
    def _():
        state[...] = jnp.zeros_like(state)

    x = hid[...].astype(F32)
    normed = (x * scale_of(x)).astype(BF16)
    normed_o[...] = normed
    turned_o[...] = normed.T.reshape(turned_o.shape)
    kpre = nn(normed, wk[...])
    kpre_o[...] = kpre.astype(BF16)
    values = nn(normed, wv[...])
    val_o[...] = values.astype(BF16)
    rows = pl.ds(pl.multiple_of(info[c], CHUNK), CHUNK)
    cs, sn = cos[rows, :], sin[rows, :]
    keep = info[chunks + c].astype(F32)
    for h in range(heads):
        slope = slopes[h]
        key = featured(kpre[:, head_slice(h)], cs, sn)
        faded = (values[:, head_slice(h)] * fade_to_end(slope, HEAD)).astype(BF16)
        old = state[h] * keep
        st_o[0, h] = old.astype(BF16)
        state[h] = jnp.exp(jnp.full((1, 2 * HEAD), -slope * CHUNK, F32)) * old + nn(faded.T, key)
    fin_o[...] = state[...].astype(BF16)


def run_keys(info, slopes, hidden, wk, wv, cos, sin, parts):
    n, d = hidden.shape
    heads, chunks = d // HEAD, n // CHUNK
    turned = (parts // 2, 2, d // parts, n)
    tile = pl.BlockSpec((CHUNK, d), lambda c: (c, 0))
    outs = [
        struct((n, d)),
        struct(turned),
        struct((n, d)),
        struct((n, d)),
        struct((chunks, heads, HEAD, 2 * HEAD)),
        struct((heads, HEAD, 2 * HEAD)),
    ]
    return pl.pallas_call(
        functools.partial(keys_kernel, chunks, heads),
        grid=(chunks,),
        in_specs=[smem(), smem(), tile, whole_block(wk.shape), whole_block(wv.shape), whole_block(cos.shape), whole_block(sin.shape)],
        out_specs=[
            tile,
            pl.BlockSpec(turned[:3] + (CHUNK,), lambda c: (0, 0, 0, c)),
            tile,
            tile,
            pl.BlockSpec((1, heads, HEAD, 2 * HEAD), lambda c: (c, 0, 0, 0)),
            whole_block((heads, HEAD, 2 * HEAD)),
        ],
        out_shape=outs,
        scratch_shapes=[pltpu.VMEM((heads, HEAD, 2 * HEAD), F32)],
        compiler_params=params(),
        cost_estimate=cost(4 * n * d * d, [hidden, wk, wv] + outs),
        name="keys_values_states",
    )(info, slopes, hidden, wk, wv, cos, sin)


def inside_kernel(chunks, heads, info, slopes, normed, wq, ws, kpre, values, st, cos, sin, qpre_o, sel_o, att_o):
    c = pl.program_id(0)
    x = normed[...]
    qpre = nn(x, wq[...])
    qpre_o[...] = qpre.astype(BF16)
    sel_o[...] = nn(x, ws[...]).astype(BF16)
    rows = pl.ds(pl.multiple_of(info[c], CHUNK), CHUNK)
    cs, sn = cos[rows, :], sin[rows, :]
    for h in range(heads):
        slope = slopes[h]
        query = featured(qpre[:, head_slice(h)], cs, sn)
        key = featured(kpre[:, head_slice(h)].astype(F32), cs, sn)
        weights = (nt(query, key) * decay_table(slope, False)).astype(BF16)
        att_o[:, head_slice(h)] = nn(weights, values[:, head_slice(h)]) + fade_from_start(
            slope, HEAD
        ) * nt(query, st[0, h])


def run_inside(info, slopes, normed, wq, ws, kpre, values, st, cos, sin):
    n, d = normed.shape
    heads, chunks = d // HEAD, n // CHUNK
    tile = pl.BlockSpec((CHUNK, d), lambda c: (c, 0))
    outs = [struct((n, d)), struct((n, d)), struct((n, d), F32)]
    return pl.pallas_call(
        functools.partial(inside_kernel, chunks, heads),
        grid=(chunks,),
        in_specs=[
            smem(),
            smem(),
            tile,
            whole_block(wq.shape),
            whole_block(ws.shape),
            tile,
            tile,
            pl.BlockSpec((1, heads, HEAD, 2 * HEAD), lambda c: (c, 0, 0, 0)),
            whole_block(cos.shape),
            whole_block(sin.shape),
        ],
        out_specs=[tile, tile, tile],
        out_shape=outs,
        compiler_params=params(),
        cost_estimate=cost(6 * n * d * d, [normed, wq, ws, kpre, values, st] + outs),
        name="queries_attention",
    )(info, slopes, normed, wq, ws, kpre, values, st, cos, sin)


def mix_kernel(chunks, heads, info, slopes, att, qpre, came, sel, wo, hid, cot, cos, sin, att_o, mixt_o, mid_o, sec_o, sect_o, cott_o, total):
    c = pl.program_id(0)
    rows = pl.ds(pl.multiple_of(info[c], CHUNK), CHUNK)
    cs, sn = cos[rows, :], sin[rows, :]
    reached = info[2 * chunks + c].astype(F32)
    lag = (c * CHUNK).astype(F32)
    alive = (row_index((CHUNK, HEAD)) + c * CHUNK < info[4 * chunks]).astype(F32)
    for h in range(heads):
        slope = slopes[h]
        query = featured(qpre[:, head_slice(h)].astype(F32), cs, sn)
        fade = jnp.exp(-slope * (row_index((CHUNK, HEAD)).astype(F32) + (lag + 1.0))) * reached
        total[:, head_slice(h)] = (att[:, head_slice(h)] + fade * nt(query, came[h])) * alive
    attended = total[...]
    att_o[...] = attended.astype(BF16)
    mixed = (attended * scale_of(attended) * sel[...].astype(F32)).astype(BF16)
    mixt_o[...] = mixed.T.reshape(mixt_o.shape)
    middle = hid[...].astype(F32) + nn(mixed, wo[...])
    mid_o[...] = middle
    second = (middle * scale_of(middle)).astype(BF16)
    sec_o[...] = second
    sect_o[...] = second.T.reshape(sect_o.shape)
    cott_o[...] = cot[...].T.reshape(cott_o.shape)


def run_mix(info, slopes, att, qpre, came, sel, wo, hidden, cot, cos, sin, parts):
    n, d = hidden.shape
    heads, chunks = d // HEAD, n // CHUNK
    turned = (parts // 2, 2, d // parts, n)
    tile = pl.BlockSpec((CHUNK, d), lambda c: (c, 0))
    turned_tile = pl.BlockSpec(turned[:3] + (CHUNK,), lambda c: (0, 0, 0, c))
    outs = [
        struct((n, d)),
        struct(turned),
        struct((n, d), F32),
        struct((n, d)),
        struct(turned),
        struct(turned),
    ]
    return pl.pallas_call(
        functools.partial(mix_kernel, chunks, heads),
        grid=(chunks,),
        in_specs=[
            smem(),
            smem(),
            tile,
            tile,
            whole_block(came.shape),
            tile,
            whole_block(wo.shape),
            tile,
            tile,
            whole_block(cos.shape),
            whole_block(sin.shape),
        ],
        out_specs=[tile, turned_tile, tile, tile, turned_tile, turned_tile],
        out_shape=outs,
        scratch_shapes=[pltpu.VMEM((CHUNK, d), F32)],
        compiler_params=params(),
        cost_estimate=cost(3 * n * d * d, [att, qpre, sel, wo, hidden, cot] + outs),
        name="carried_mixed_middle",
    )(info, slopes, att, qpre, came, sel, wo, hidden, cot, cos, sin)


def sglu_kernel(chunks, heads, peers, plan, first, last, place, info, slopes, *refs):
    refs = list(refs)
    take = lambda k: [refs.pop(0) for _ in range(k)]
    step = pl.program_id(0)
    c = chunks - 1 - step
    (sec, cot) = take(2)
    sources = take(len(plan))
    if not first:
        (term_i, part_i) = take(2)
    if last:
        (mid, sel, att, wo, qpre, cos, sin) = take(7)
    (inner_o, left_o, right_o) = take(3)
    if last:
        (out_o, gmid_o, gbr_o, gsel_o, gatt_o, et_o, e0_o) = take(7)
    else:
        (term_o, part_o) = take(2)
    (w1, w2, wd, sems) = take(4)
    if last:
        (state,) = take(1)

    def copies():
        for i, (which, low, size, slot, row, rows) in enumerate(plan):
            src, dst = sources[i], (w1, w2, wd)[which]
            if low is not None:
                src = src.at[:, pl.ds(low, size)] if which < 2 else src.at[pl.ds(low, size), :]
            if slot is not None:
                dst = dst.at[place[slot]]
                if rows is not None:
                    dst = dst.at[pl.ds(pl.multiple_of(place[row] * rows, rows), rows), :]
            yield pltpu.make_async_copy(src, dst, sems.at[i])

    @pl.when(step == 0)
    def _():
        for copy in copies():
            copy.start()
        if last:
            state[...] = jnp.zeros_like(state)
        for copy in copies():
            copy.wait()

    x, y = sec[...], cot[...]
    term = None if first else term_i[...]
    part = None if first else part_i[...].astype(F32)
    for b in range(peers):
        left = nn(x, w1[b])
        right = nn(x, w2[b])
        inner = (left * right).astype(BF16)
        inner_o[b] = inner
        upstream = nt(y, wd[b])
        grad_left = (upstream * right).astype(BF16)
        grad_right = (upstream * left).astype(BF16)
        left_o[b] = grad_left
        right_o[b] = grad_right
        new_term = nn(inner, wd[b])
        new_part = nt(grad_left, w1[b]) + nt(grad_right, w2[b])
        term = new_term if term is None else term + new_term
        part = new_part if part is None else part + new_part
    if not last:
        term_o[...] = term
        part_o[...] = part
        return
    middle = mid[...]
    out_o[...] = (middle + term).astype(BF16)
    grad_middle = y.astype(F32) + norm_back(middle, scale_of(middle), part)
    gmid_o[...] = grad_middle
    branch = grad_middle.astype(BF16)
    gbr_o[...] = branch
    grad_mixed = nt(branch, wo[...])
    attended = att[...].astype(F32)
    scale = scale_of(attended)
    gsel_o[...] = (grad_mixed * attended * scale).astype(BF16)
    alive = (row_index((CHUNK, 1)) + c * CHUNK < info[4 * chunks]).astype(F32)
    grad_att = norm_back(attended, scale, grad_mixed * sel[...].astype(F32)) * alive
    gatt_o[...] = grad_att.astype(BF16)
    rows = pl.ds(pl.multiple_of(info[c], CHUNK), CHUNK)
    cs, sn = cos[rows, :], sin[rows, :]
    keep = info[chunks + c].astype(F32)
    for h in range(heads):
        slope = slopes[h]
        query = featured(qpre[:, head_slice(h)].astype(F32), cs, sn)
        faded = (grad_att[:, head_slice(h)] * fade_from_start(slope, HEAD)).astype(BF16)
        old = state[h]
        et_o[0, h] = old.astype(BF16)
        state[h] = keep * (
            jnp.exp(jnp.full((1, 2 * HEAD), -slope * CHUNK, F32)) * old + nn(faded.T, query)
        )
    e0_o[...] = state[...].astype(BF16)


def run_sglu(place, info, slopes, second, cot, sources, plan, peers, width, before, after):
    n, d = second.shape
    heads, chunks = d // HEAD, n // CHUNK
    first, last = before is None, after is not None
    tile = pl.BlockSpec((CHUNK, d), lambda s: (chunks - 1 - s, 0))
    inputs = [second, cot] + list(sources)
    specs = [tile, tile] + [anywhere()] * len(sources)
    if not first:
        inputs += list(before)
        specs += [tile, tile]
    if last:
        mid, sel, att, wo, qpre, cos, sin = after
        inputs += [mid, sel, att, wo, qpre, cos, sin]
        specs += [tile, tile, tile, whole_block(wo.shape), tile, whole_block(cos.shape), whole_block(sin.shape)]
    hidden_tile = pl.BlockSpec((peers, CHUNK, width), lambda s: (0, chunks - 1 - s, 0))
    outs = [struct((peers, n, width))] * 3
    out_specs = [hidden_tile] * 3
    scratch = [
        pltpu.VMEM((peers, d, width), BF16),
        pltpu.VMEM((peers, d, width), BF16),
        pltpu.VMEM((peers, width, d), BF16),
        pltpu.SemaphoreType.DMA((len(plan),)),
    ]
    if last:
        outs += [
            struct((n, d)),
            struct((n, d), F32),
            struct((n, d)),
            struct((n, d)),
            struct((n, d)),
            struct((chunks, heads, HEAD, 2 * HEAD)),
            struct((heads, HEAD, 2 * HEAD)),
        ]
        out_specs += [tile] * 5 + [
            pl.BlockSpec((1, heads, HEAD, 2 * HEAD), lambda s: (chunks - 1 - s, 0, 0, 0)),
            whole_block((heads, HEAD, 2 * HEAD)),
        ]
        scratch.append(pltpu.VMEM((heads, HEAD, 2 * HEAD), F32))
    else:
        outs += [struct((n, d), F32), struct((n, d), F32)]
        out_specs += [tile, tile]
    return pl.pallas_call(
        functools.partial(sglu_kernel, chunks, heads, peers, plan, first, last),
        grid=(chunks,),
        in_specs=[smem(), smem(), smem()] + specs,
        out_specs=out_specs,
        out_shape=outs,
        scratch_shapes=scratch,
        compiler_params=params(),
        cost_estimate=cost(12 * n * d * width * peers, inputs + outs),
        name="sglu_last" if last else "sglu_first",
    )(place, info, slopes, *inputs)


def weights_kernel(items, count, added, half, *refs):
    refs = list(refs)
    lefts = refs[:count]
    rights = refs[count : count + len(items)]
    rest = refs[count + len(items) :]
    out = rest[-1]
    for t, which in enumerate(items):
        left = lefts[which][...]
        left = left.reshape(left.shape[0] * left.shape[1], left.shape[2])
        right = rights[t][...]
        total = nn(left, right).reshape(out.shape[1:])
        if added:
            total = total + rest[0][t].astype(F32)
        out[t] = total.astype(BF16)


def run_weights(half, lefts, items, rights, spec, peers, width, received=None):
    pairs, _, rows, n = lefts[0].shape
    shape = (peers, len(items), pairs, rows, width)
    block = pl.BlockSpec((None,) + shape[1:], lambda m, half: (m, 0, 0, 0, 0))
    left_spec = pl.BlockSpec((pairs, None, rows, n), lambda m, half: (0, half[0], 0, 0))
    inputs = list(lefts) + list(rights)
    specs = [left_spec] * len(lefts) + [spec] * len(rights)
    if received is not None:
        inputs.append(received)
        specs.append(block)
    out = struct(shape)
    return pl.pallas_call(
        functools.partial(weights_kernel, tuple(items), len(lefts), received is not None),
        grid_spec=pltpu.PrefetchScalarGridSpec(
            num_scalar_prefetch=1,
            grid=(peers,),
            in_specs=specs,
            out_specs=block,
        ),
        out_shape=out,
        compiler_params=params(),
        cost_estimate=cost(2 * n * pairs * rows * width * len(items) * peers, inputs + [out]),
        name="weight_gradients",
    )(half, *inputs)


def attention_back_kernel(chunks, first_head, info, slopes, qpre, kpre, values, gatt, st, came, et, left, cos, sin, gq_o, gk_o, gv_o):
    pair, c = pl.program_id(0), pl.program_id(1)
    rows = pl.ds(pl.multiple_of(info[c], CHUNK), CHUNK)
    cs, sn = cos[rows, :], sin[rows, :]
    before = info[2 * chunks + c].astype(F32)
    after = info[3 * chunks + c].astype(F32)
    span = CHUNK * c.astype(F32)
    rest = CHUNK * (chunks - 1 - c).astype(F32)
    for h in range(2):
        slope = slopes[first_head + 2 * pair + h]
        cols = head_slice(h)
        qp, kp = qpre[:, cols].astype(F32), kpre[:, cols].astype(F32)
        qs, ks = sigmoid(qp), sigmoid(kp)
        qa, ka = qp * qs, kp * ks
        query = jnp.concatenate([qa * cs, qa * sn], axis=-1).astype(BF16)
        key = jnp.concatenate([ka * cs, ka * sn], axis=-1).astype(BF16)
        value, grad = values[:, cols], gatt[:, cols]
        lane = jnp.zeros((1, 2 * HEAD), F32)
        state = st[0, h].astype(F32) + came[h].astype(F32) * (jnp.exp(lane - slope * span) * before)
        ending = et[0, h].astype(F32) + left[h].astype(F32) * (jnp.exp(lane - slope * rest) * after)
        state, ending = state.astype(BF16), ending.astype(BF16)
        table, turned = decay_table(slope, False), decay_table(slope, True)
        scores_t = (nt(key, query) * turned).astype(BF16)
        slope_s = (nt(grad, value) * table).astype(BF16)
        slope_t = (nt(value, grad) * turned).astype(BF16)
        start = fade_from_start(slope, HEAD)
        end = fade_to_end(slope, HEAD)
        grad_start = (grad.astype(F32) * start).astype(BF16)
        value_end = (value.astype(F32) * end).astype(BF16)
        dq = nn(slope_s, key) + nn(grad_start, state)
        dk = nn(slope_t, query) + nn(value_end, ending)
        dv = nn(scores_t, grad) + end * nt(key, ending)
        gv_o[:, cols] = dv.astype(BF16)
        dq = dq[:, :HEAD] * cs + dq[:, HEAD:] * sn
        dk = dk[:, :HEAD] * cs + dk[:, HEAD:] * sn
        gq_o[:, cols] = (dq * (qs * (1.0 + qp * (1.0 - qs)))).astype(BF16)
        gk_o[:, cols] = (dk * (ks * (1.0 + kp * (1.0 - ks)))).astype(BF16)


def run_attention_back(info, slopes, qpre, kpre, values, gatt, st, came, et, left, cos, sin, first_head, heads):
    n, d = qpre.shape
    chunks = n // CHUNK
    skip = first_head // 2
    tile = pl.BlockSpec((CHUNK, 2 * HEAD), lambda p, c: (c, skip + p))
    out_tile = pl.BlockSpec((CHUNK, 2 * HEAD), lambda p, c: (c, p))
    states = pl.BlockSpec((1, 2, HEAD, 2 * HEAD), lambda p, c: (c, skip + p, 0, 0))
    ends = pl.BlockSpec((2, HEAD, 2 * HEAD), lambda p, c: (skip + p, 0, 0))
    outs = [struct((n, heads * HEAD))] * 3
    return pl.pallas_call(
        functools.partial(attention_back_kernel, chunks, first_head),
        grid=(heads // 2, chunks),
        in_specs=[smem(), smem(), tile, tile, tile, tile, states, ends, states, ends, whole_block(cos.shape), whole_block(sin.shape)],
        out_specs=[out_tile] * 3,
        out_shape=outs,
        compiler_params=params(2),
        cost_estimate=cost(18 * n * 256 * 256 * heads // 2, [qpre, kpre, values, gatt, st, et] + outs),
        name="attention_backward",
    )(info, slopes, qpre, kpre, values, gatt, st, came, et, left, cos, sin)


def input_kernel(count, *refs):
    grads = refs[:count]
    weights = refs[count : 2 * count]
    hid, gmid, out = refs[2 * count :]
    total = None
    for g, w in zip(grads, weights):
        part = nt(g[...], w[...])
        total = part if total is None else total + part
    x = hid[...].astype(F32)
    out[...] = (gmid[...] + norm_back(x, scale_of(x), total)).astype(BF16)


def run_input(grads, weights, hidden, gmid):
    n, d = hidden.shape
    tile = pl.BlockSpec((CHUNK, d), lambda c: (c, 0))
    out = struct((n, d))
    return pl.pallas_call(
        functools.partial(input_kernel, len(grads)),
        grid=(n // CHUNK,),
        in_specs=[pl.BlockSpec((CHUNK, g.shape[1]), lambda c: (c, 0)) for g in grads]
        + [whole_block(w.shape) for w in weights]
        + [tile, tile],
        out_specs=tile,
        out_shape=out,
        compiler_params=params(),
        cost_estimate=cost(8 * n * d * d, list(grads) + list(weights) + [hidden, gmid, out]),
        name="input_gradient",
    )(*grads, *weights, hidden, gmid)


def across(x, axis, flip):
    size = lax.axis_size(axis)
    return lax.ppermute(x, axis, [(i, i ^ flip) for i in range(size)])


def pick(x, index, axis):
    return lax.dynamic_index_in_dim(x, index, axis, keepdims=False)


def plus(*arrays):
    total = arrays[0].astype(F32)
    for a in arrays[1:]:
        total = total + a.astype(F32)
    return total


def reduced(lefts, items, rights, spec, peers, width):
    dp, me = lax.axis_index("dp"), lax.axis_index("mp")
    core = (dp % 2).astype(jnp.int32).reshape(1)
    run = functools.partial(run_weights, lefts=lefts, items=items, rights=rights, spec=spec, peers=peers, width=width)
    if peers != 2:
        halves = [run(jnp.full((1,), k, jnp.int32)) for k in range(2)]
        full = jnp.stack(halves, axis=3)
        full = full.reshape(peers, len(items), -1, full.shape[4], width)
        mine = lax.psum_scatter(full, "dp", scatter_dimension=2, tiled=False)
        return lax.psum_scatter(mine, "mp", scatter_dimension=0, tiled=False).astype(F32)
    sent = run(1 - core)
    total = run(core, received=across(sent, "dp", 1))
    x, z = (dp // 2) % 2, dp // 4
    depth = lax.axis_size("dp") // 4
    total = total.reshape(2, len(items), depth, 2, -1, width)
    half = depth // 2
    upper, lower = total[:, :, :half], total[:, :, half:]
    from_x = across(pick(upper, 1 - x, 3), "dp", 2)
    from_y = across(pick(lower, 1 - me, 0), "mp", 1)
    upper = plus(pick(upper, x, 3), from_x).astype(BF16)
    lower = plus(pick(lower, me, 0), from_y).astype(BF16)
    from_y = across(pick(upper, 1 - me, 0), "mp", 1)
    from_x = across(pick(lower, 1 - x, 2), "dp", 2)
    upper = plus(pick(upper, me, 0), from_y).astype(BF16)
    lower = plus(pick(lower, x, 2), from_x).astype(BF16)
    line = jnp.concatenate([upper, lower], axis=1)
    parts = [pick(line, z, 1)]
    for k in range(1, depth):
        parts.append(across(pick(line, z ^ k, 1), "dp", 4 * k))
    return plus(*parts)


def per_device(
    hidden_in,
    query_weight,
    key_weight,
    value_weight,
    select_weight,
    out_weight,
    first_weight,
    second_weight,
    down_weight,
    decay_slope,
    doc_lengths,
    cotangent,
):
    count, d = hidden_in.shape
    heads, chunks = d // HEAD, count // CHUNK
    peers, parts = lax.axis_size("mp"), lax.axis_size("dp")
    dp, me = lax.axis_index("dp"), lax.axis_index("mp")
    group = count * peers
    units = first_weight.shape[1]
    lengths = doc_lengths[0].astype(jnp.int32)
    info = chunk_info(lengths, me * count, count)
    cos, sin = cos_sin_tables(group // 2)
    slopes = decay_slope

    if units % 128 == 0:
        cut = -(-units // 256) * 128
        ranges = [(0, cut), (cut, units - cut)]
    else:
        ranges = [(0, units)]

    quarter = dp % 4
    place = jnp.stack([me, 1 - me] + [quarter ^ k for k in range(4)]).astype(jnp.int32)
    plans, fetched = [], []
    for low, size in ranges:
        plan, sources = [], []
        if peers == 2:
            for which, weight in enumerate((first_weight, second_weight, down_weight)):
                rows = d // 4 if which < 2 else size // 4
                at = (quarter * rows, low) if which < 2 else (low + quarter * rows, 0)
                extent = (rows, size) if which < 2 else (rows, d)
                mine = lax.dynamic_slice(weight, at, extent)
                one = across(mine, "mp", 1)
                two = across(one, "dp", 2)
                pieces = {0: one, 2: two, 1: across(one, "dp", 1), 3: across(two, "dp", 1)}
                whole = low == 0 and size == units
                plan.append((which, None if whole else low, size, 0, None, None))
                sources.append(weight)
                for k, piece in pieces.items():
                    plan.append((which, None, None, 1, 2 + k, rows))
                    sources.append(piece)
        else:
            for which, weight in enumerate((first_weight, second_weight, down_weight)):
                weight = weight[:, low : low + size] if which < 2 else weight[low : low + size]
                plan.append((which, None, None, None, None, None))
                sources.append(lax.all_gather(weight, "mp"))
        plans.append(tuple(plan))
        fetched.append(sources)

    normed, normed_t, kpre, values, st, final = run_keys(
        info, slopes, hidden_in, key_weight, value_weight, cos, sin, parts
    )
    whole_keep = info[2 * chunks + chunks - 1].astype(F32)
    decay = jnp.exp(-slopes * count)
    if peers == 2:
        came = across(final, "mp", 1)
        came = jnp.where(me == 1, came, jnp.zeros_like(came))
    else:
        finals = lax.all_gather(final, "mp")
        keeps = lax.all_gather(whole_keep.reshape(1), "mp")[:, 0]

        def ahead(k, total):
            new = finals[k].astype(F32) + (keeps[k] * decay)[:, None, None] * total
            return jnp.where(k < me, new, total)

        came = lax.fori_loop(0, peers, ahead, jnp.zeros(final.shape, F32)).astype(BF16)
    qpre, sel, att = run_inside(
        info, slopes, normed, query_weight, select_weight, kpre, values, st, cos, sin
    )
    attended, mixed_t, middle, second, second_t, cot_t = run_mix(
        info, slopes, att, qpre, came, sel, out_weight, hidden_in, cotangent, cos, sin, parts
    )

    before = None
    pieces = []
    for i, (low, size) in enumerate(ranges):
        last = i == len(ranges) - 1
        after = (middle, sel, attended, out_weight, qpre, cos, sin) if last else None
        got = run_sglu(
            place, info, slopes, second, cotangent, fetched[i], plans[i], peers, size, before, after
        )
        inner, grad_left, grad_right = got[:3]
        if last:
            output, grad_middle, grad_branch, grad_sel, grad_att, et, leaving = got[3:]
        else:
            before = got[3:]
        spec = pl.BlockSpec((None, count, size), lambda m, half: (m, 0, 0))
        pieces.append(
            reduced(
                [second_t, cot_t], (0, 0, 1), [grad_left, grad_right, inner], spec, peers, size
            )
        )
    if peers == 2:
        left = across(leaving, "mp", 1)
        left = jnp.where(me == 0, left, jnp.zeros_like(left))
    else:
        leavings = lax.all_gather(leaving, "mp")

        def behind(step, total):
            k = peers - 1 - step
            new = leavings[k].astype(F32) + (keeps[k] * decay)[:, None, None] * total
            return jnp.where(k > me, new, total)

        left = lax.fori_loop(0, peers, behind, jnp.zeros(leaving.shape, F32)).astype(BF16)

    share = d // peers
    wide = pl.BlockSpec((count, share), lambda m, half: (0, m))
    grad_out_sel = reduced(
        [mixed_t, normed_t], (0, 1), [grad_branch, grad_sel], wide, peers, share
    )
    gq, gk, gv = run_attention_back(
        info, slopes, qpre, kpre, values, grad_att, st, came, et, left, cos, sin, 0, heads
    )
    grad_qkv = reduced([normed_t], (0, 0, 0), [gq, gk, gv], wide, peers, share)
    grad_hidden = run_input(
        [gq, gk, gv, grad_sel],
        [query_weight, key_weight, value_weight, select_weight],
        hidden_in,
        grad_middle,
    )
    sglu = pieces[0] if len(pieces) == 1 else jnp.concatenate(pieces, axis=2)
    return (
        output,
        grad_hidden,
        grad_qkv[0],
        grad_qkv[1],
        grad_qkv[2],
        grad_out_sel[1],
        grad_out_sel[0],
        sglu[0],
        sglu[1],
        jnp.transpose(sglu[2]),
    )


def solution(mesh):
    rows = P(("dp", "mp"), None)
    in_specs = (
        rows,
        P(),
        P(),
        P(),
        P(),
        P(),
        P(None, "mp"),
        P(None, "mp"),
        P("mp", None),
        P(),
        P("dp", None),
        rows,
    )
    out_specs = (rows, rows) + (P("dp", "mp"),) * 7 + (P("mp", "dp"),)
    return jax.shard_map(
        per_device, mesh=mesh, in_specs=in_specs, out_specs=out_specs, check_vma=False
    )
```

```python
import functools

import jax
import jax.numpy as jnp
import numpy as np
from jax import lax
from jax.experimental import pallas as pl
from jax.experimental.pallas import tpu as pltpu
from jax.sharding import PartitionSpec as P

HEAD = 128
CHUNK = 256
EPSILON = 1e-06
BF16 = jnp.bfloat16
F32 = jnp.float32
VMEM_LIMIT = 58 * 1024 * 1024


def nn(left, right):
    return jnp.dot(left, right, preferred_element_type=F32)


def nt(left, right):
    return lax.dot_general(left, right, (((1,), (1,)), ((), ())), preferred_element_type=F32)


def scale_of(values):
    return lax.rsqrt(jnp.mean(values * values, axis=-1, keepdims=True) + EPSILON)


def norm_back(values, scale, upstream):
    return scale * upstream - values * (scale * scale * scale) * jnp.mean(
        values * upstream, axis=-1, keepdims=True
    )


def sigmoid(v):
    return 1.0 / (1.0 + jnp.exp(-v))


def featured(pre, cos, sin):
    act = pre * sigmoid(pre)
    return jnp.concatenate([act * cos, act * sin], axis=-1).astype(BF16)


def head_slice(h):
    return slice(h * HEAD, (h + 1) * HEAD)


def row_index(shape):
    return lax.broadcasted_iota(jnp.int32, shape, 0)


def fade_from_start(slope, width):
    return jnp.exp(-slope * (row_index((CHUNK, width)) + 1).astype(F32))


def fade_to_end(slope, width):
    return jnp.exp(-slope * (CHUNK - 1 - row_index((CHUNK, width))).astype(F32))


def decay_table(slope, transposed):
    rows = lax.broadcasted_iota(jnp.int32, (CHUNK, CHUNK), 0)
    cols = lax.broadcasted_iota(jnp.int32, (CHUNK, CHUNK), 1)
    gap = cols - rows if transposed else rows - cols
    return jnp.where(gap >= 0, jnp.exp(-slope * jnp.maximum(gap, 0).astype(F32)), 0.0)


def plus(*arrays):
    total = arrays[0].astype(F32)
    for a in arrays[1:]:
        total = total + a.astype(F32)
    return total


def smem():
    return pl.BlockSpec(memory_space=pltpu.SMEM)


def anywhere():
    return pl.BlockSpec(memory_space=pl.ANY)


def whole_block(shape):
    zeros = (0,) * len(shape)
    return pl.BlockSpec(shape, lambda *_: zeros)


def cost(flops, arrays):
    moved = sum(int(np.prod(a.shape)) * jnp.dtype(a.dtype).itemsize for a in arrays)
    return pl.CostEstimate(flops=int(flops), bytes_accessed=moved, transcendentals=0)


def struct(shape, dtype=BF16):
    return jax.ShapeDtypeStruct(tuple(shape), dtype)


def flipped(index, mask):
    bit = 1
    while bit <= mask:
        if mask & bit:
            index = index + bit * (1 - 2 * lax.rem(lax.div(index, bit), 2))
        bit *= 2
    return index


def remote(src, dst, send, recv, axis, mask):
    return pltpu.make_async_remote_copy(
        src_ref=src,
        dst_ref=dst,
        send_sem=send,
        recv_sem=recv,
        device_id={axis: flipped(lax.axis_index(axis), mask)},
        device_id_type=pl.DeviceIdType.MESH,
    )


def greet(partners):
    barrier = pltpu.get_barrier_semaphore()
    for axis, mask in partners:
        pl.semaphore_signal(
            barrier,
            inc=1,
            device_id={axis: flipped(lax.axis_index(axis), mask)},
            device_id_type=pl.DeviceIdType.MESH,
        )
    pl.semaphore_wait(barrier, len(partners))


class Carry:
    def __init__(self, inputs, outs, phases):
        self.inputs, self.outs, self.phases = list(inputs), list(outs), phases
        count = sum(len(p[2]) for p in phases)
        self.scratch = [pltpu.SemaphoreType.DMA((count,)), pltpu.SemaphoreType.DMA((count,))]
        self.partners = [(c[2], c[3]) for p in phases for c in p[2]]

    def copies(self, which, ins, outs, scratch):
        at = sum(len(p[2]) for p in self.phases[:which])
        send, recv = scratch
        for k, (src, dst, axis, mask) in enumerate(self.phases[which][2]):
            yield remote(src(ins, outs), dst(ins, outs), send.at[at + k], recv.at[at + k], axis, mask)

    def before(self, step, ins, outs, scratch):
        for p, phase in enumerate(self.phases):

            @pl.when(step == phase[0])
            def _(p=p):
                for copy in self.copies(p, ins, outs, scratch):
                    copy.start()

    def after(self, step, ins, outs, scratch):
        for p, phase in enumerate(self.phases):

            @pl.when(step == phase[1])
            def _(p=p):
                for copy in self.copies(p, ins, outs, scratch):
                    copy.wait()


class Halving:
    def __init__(self, array, steps):
        self.inputs, self.steps = [array], steps
        _, depth, _, items, rows, width = array.shape
        half = depth // 2
        self.outs = [struct((depth, items, rows, width))]
        pair = pltpu.VMEM((2, half, items, rows, width), BF16)
        flat = pltpu.VMEM((half, 2, items, rows, width), BF16)
        one = pltpu.VMEM((half, items, rows, width), BF16)
        self.scratch = [pair, flat, pair, flat] + [one] * 4 + [pltpu.VMEM(self.outs[0].shape, BF16)]
        self.scratch += [pltpu.SemaphoreType.DMA((4,)), pltpu.SemaphoreType.DMA((4,)), pltpu.SemaphoreType.DMA((3,))]
        self.partners = [("dp", 2), ("mp", 1)]

    def parts(self, ins, outs, scratch):
        pk, qk, pr, qr, ps, qs, pb, qb, line, send, recv, local = scratch
        half = pb.shape[0]
        me = lax.axis_index("mp")
        x = lax.rem(lax.div(lax.axis_index("dp"), 2), 2)
        upper, lower = pl.ds(0, half), pl.ds(half, half)
        first = [
            remote(ins[0].at[:, upper, 1 - x], pr, send.at[0], recv.at[0], "dp", 2),
            remote(ins[0].at[1 - me, lower], qr, send.at[1], recv.at[1], "mp", 1),
        ]
        kept = [
            pltpu.make_async_copy(ins[0].at[:, upper, x], pk, local.at[0]),
            pltpu.make_async_copy(ins[0].at[me, lower], qk, local.at[1]),
        ]
        second = [
            remote(ps, pb, send.at[2], recv.at[2], "mp", 1),
            remote(qs, qb, send.at[3], recv.at[3], "dp", 2),
        ]
        out = pltpu.make_async_copy(line, outs[0], local.at[2])
        return first, kept, second, out

    def before(self, step, ins, outs, scratch):
        first, kept, _, _ = self.parts(ins, outs, scratch)

        @pl.when(step == self.steps[0])
        def _():
            for copy in first + kept:
                copy.start()

    def after(self, step, ins, outs, scratch):
        first, kept, second, out = self.parts(ins, outs, scratch)
        pk, qk, pr, qr, ps, qs, pb, qb, line = scratch[:9]
        half = pb.shape[0]
        me = lax.axis_index("mp")
        x = lax.rem(lax.div(lax.axis_index("dp"), 2), 2)

        @pl.when(step == self.steps[1])
        def _():
            for copy in first + kept:
                copy.wait()
            for z in range(half):
                ps[z] = plus(pk[1 - me, z], pr[1 - me, z]).astype(BF16)
                qs[z] = plus(qk[z, 1 - x], qr[z, 1 - x]).astype(BF16)
            for copy in second:
                copy.start()
            for z in range(half):
                line[z] = plus(pk[me, z], pr[me, z]).astype(BF16)
                line[half + z] = plus(qk[z, x], qr[z, x]).astype(BF16)

        @pl.when(step == self.steps[2])
        def _():
            for copy in second:
                copy.wait()
            for z in range(half):
                line[z] = plus(line[z], pb[z]).astype(BF16)
                line[half + z] = plus(line[half + z], qb[z]).astype(BF16)
            out.start()
            out.wait()


def launch(kernel, name, steps, inputs, specs, outs, out_specs, scratch, flops, guests=(), ident=None, partners=()):
    guests = list(guests)
    partners = list(partners) + [p for g in guests for p in g.partners]
    partners = sorted(set(partners))
    all_inputs = list(inputs) + [a for g in guests for a in g.inputs]
    all_specs = list(specs) + [anywhere() for g in guests for _ in g.inputs]
    all_outs = list(outs) + [a for g in guests for a in g.outs]
    all_out_specs = list(out_specs) + [anywhere() for g in guests for _ in g.outs]
    all_scratch = list(scratch) + [a for g in guests for a in g.scratch]

    def body(*refs):
        refs = list(refs)
        take = lambda k: [refs.pop(0) for _ in range(k)]
        own = take(len(inputs))
        ins = [take(len(g.inputs)) for g in guests]
        own += take(len(outs))
        gone = [take(len(g.outs)) for g in guests]
        own += take(len(scratch))
        held = [take(len(g.scratch)) for g in guests]
        step = pl.program_id(0)
        if partners:

            @pl.when(step == 0)
            def _():
                greet(partners)

        for g, i, o, s in zip(guests, ins, gone, held):
            g.before(step, i, o, s)
        kernel(*own)
        for g, i, o, s in zip(guests, ins, gone, held):
            g.after(step, i, o, s)

    extra = dict(collective_id=ident, has_side_effects=True) if partners else {}
    return pl.pallas_call(
        body,
        grid=(steps,),
        in_specs=all_specs,
        out_specs=all_out_specs,
        out_shape=all_outs,
        scratch_shapes=all_scratch,
        compiler_params=pltpu.CompilerParams(
            vmem_limit_bytes=VMEM_LIMIT, dimension_semantics=("arbitrary",), **extra
        ),
        cost_estimate=cost(flops, all_inputs + all_outs),
        name=name,
    )(*all_inputs)


def chunk_info(lengths, offset, count):
    chunks = count // CHUNK
    ends = jnp.cumsum(lengths)
    starts = ends - lengths
    first = offset + CHUNK * jnp.arange(chunks, dtype=jnp.int32)
    begin = jnp.max(jnp.where(starts[None, :] <= first[:, None], starts[None, :], 0), axis=1)
    base = first - begin
    keep = (base > 0).astype(jnp.int32)
    before = jnp.cumprod(keep)
    after = jnp.concatenate([jnp.cumprod(keep[::-1])[::-1][1:], jnp.ones((1,), jnp.int32)])
    live = jnp.clip(ends[-1] - offset, 0, count)
    return jnp.concatenate([base, keep, before, after, live[None]]).astype(jnp.int32)


def turning(info, chunks, longest):
    freq = 10000.0 ** (-np.arange(HEAD, dtype=np.float64) / HEAD)
    phase = np.arange(longest, dtype=np.float64)[:, None] * freq[None, :]
    table = jnp.asarray(np.concatenate([np.cos(phase), np.sin(phase)], axis=1), F32)
    return jnp.concatenate(
        [lax.dynamic_slice(table, (info[c], 0), (CHUNK, 2 * HEAD)) for c in range(chunks)], axis=0
    )


def keys_kernel(chunks, heads, info, slopes, hid, wk, wv, rot, normed_o, turned_o, kpre_o, val_o, st_o, fin_o, state):
    c = pl.program_id(0)

    @pl.when(c == 0)
    def _():
        state[...] = jnp.zeros_like(state)

    x = hid[...].astype(F32)
    normed = (x * scale_of(x)).astype(BF16)
    normed_o[...] = normed
    turned_o[...] = normed.T.reshape(turned_o.shape)
    kpre = nn(normed, wk[...])
    kpre_o[...] = kpre.astype(BF16)
    values = nn(normed, wv[...])
    val_o[...] = values.astype(BF16)
    cs, sn = rot[:, :HEAD], rot[:, HEAD:]
    keep = info[chunks + c].astype(F32)
    for h in range(heads):
        slope = slopes[h]
        key = featured(kpre[:, head_slice(h)], cs, sn)
        faded = (values[:, head_slice(h)] * fade_to_end(slope, HEAD)).astype(BF16)
        old = state[h] * keep
        st_o[0, h] = old.astype(BF16)
        state[h] = jnp.exp(jnp.full((1, 2 * HEAD), -slope * CHUNK, F32)) * old + nn(faded.T, key)
    fin_o[...] = state[...].astype(BF16)


def run_keys(info, slopes, hidden, wk, wv, rot, parts, **ride):
    n, d = hidden.shape
    heads, chunks = d // HEAD, n // CHUNK
    turned = (parts // 2, 2, d // parts, n)
    tile = pl.BlockSpec((CHUNK, d), lambda c: (c, 0))
    outs = [
        struct((n, d)),
        struct(turned),
        struct((n, d)),
        struct((n, d)),
        struct((chunks, heads, HEAD, 2 * HEAD)),
        struct((heads, HEAD, 2 * HEAD)),
    ]
    return launch(
        functools.partial(keys_kernel, chunks, heads),
        "keys_values_states",
        chunks,
        [info, slopes, hidden, wk, wv, rot],
        [smem(), smem(), tile, whole_block(wk.shape), whole_block(wv.shape), pl.BlockSpec((CHUNK, 2 * HEAD), lambda c: (c, 0))],
        outs,
        [
            tile,
            pl.BlockSpec(turned[:3] + (CHUNK,), lambda c: (0, 0, 0, c)),
            tile,
            tile,
            pl.BlockSpec((1, heads, HEAD, 2 * HEAD), lambda c: (c, 0, 0, 0)),
            whole_block((heads, HEAD, 2 * HEAD)),
        ],
        [pltpu.VMEM((heads, HEAD, 2 * HEAD), F32)],
        4 * n * d * d,
        **ride,
    )


def inside_kernel(chunks, heads, info, slopes, normed, wq, ws, kpre, values, st, rot, qpre_o, sel_o, att_o):
    c = pl.program_id(0)
    x = normed[...]
    qpre = nn(x, wq[...])
    qpre_o[...] = qpre.astype(BF16)
    sel_o[...] = nn(x, ws[...]).astype(BF16)
    cs, sn = rot[:, :HEAD], rot[:, HEAD:]
    for h in range(heads):
        slope = slopes[h]
        query = featured(qpre[:, head_slice(h)], cs, sn)
        key = featured(kpre[:, head_slice(h)].astype(F32), cs, sn)
        weights = (nt(query, key) * decay_table(slope, False)).astype(BF16)
        att_o[:, head_slice(h)] = nn(weights, values[:, head_slice(h)]) + fade_from_start(
            slope, HEAD
        ) * nt(query, st[0, h])


def run_inside(info, slopes, normed, wq, ws, kpre, values, st, rot, **ride):
    n, d = normed.shape
    heads, chunks = d // HEAD, n // CHUNK
    tile = pl.BlockSpec((CHUNK, d), lambda c: (c, 0))
    outs = [struct((n, d)), struct((n, d)), struct((n, d), F32)]
    return launch(
        functools.partial(inside_kernel, chunks, heads),
        "queries_attention",
        chunks,
        [info, slopes, normed, wq, ws, kpre, values, st, rot],
        [
            smem(),
            smem(),
            tile,
            whole_block(wq.shape),
            whole_block(ws.shape),
            tile,
            tile,
            pl.BlockSpec((1, heads, HEAD, 2 * HEAD), lambda c: (c, 0, 0, 0)),
            pl.BlockSpec((CHUNK, 2 * HEAD), lambda c: (c, 0)),
        ],
        outs,
        [tile, tile, tile],
        [],
        6 * n * d * d,
        **ride,
    )


def mix_kernel(chunks, heads, info, slopes, att, qpre, came, sel, wo, hid, cot, rot, att_o, mixt_o, mid_o, sec_o, sect_o, cott_o, total):
    c = pl.program_id(0)
    cs, sn = rot[:, :HEAD], rot[:, HEAD:]
    reached = info[2 * chunks + c].astype(F32)
    lag = (c * CHUNK).astype(F32)
    alive = (row_index((CHUNK, HEAD)) + c * CHUNK < info[4 * chunks]).astype(F32)
    for h in range(heads):
        slope = slopes[h]
        query = featured(qpre[:, head_slice(h)].astype(F32), cs, sn)
        fade = jnp.exp(-slope * (row_index((CHUNK, HEAD)).astype(F32) + (lag + 1.0))) * reached
        total[:, head_slice(h)] = (att[:, head_slice(h)] + fade * nt(query, came[h])) * alive
    attended = total[...]
    att_o[...] = attended.astype(BF16)
    mixed = (attended * scale_of(attended) * sel[...].astype(F32)).astype(BF16)
    mixt_o[...] = mixed.T.reshape(mixt_o.shape)
    middle = hid[...].astype(F32) + nn(mixed, wo[...])
    mid_o[...] = middle
    second = (middle * scale_of(middle)).astype(BF16)
    sec_o[...] = second
    sect_o[...] = second.T.reshape(sect_o.shape)
    cott_o[...] = cot[...].T.reshape(cott_o.shape)


def run_mix(info, slopes, att, qpre, came, sel, wo, hidden, cot, rot, parts, **ride):
    n, d = hidden.shape
    heads, chunks = d // HEAD, n // CHUNK
    turned = (parts // 2, 2, d // parts, n)
    tile = pl.BlockSpec((CHUNK, d), lambda c: (c, 0))
    turned_tile = pl.BlockSpec(turned[:3] + (CHUNK,), lambda c: (0, 0, 0, c))
    outs = [
        struct((n, d)),
        struct(turned),
        struct((n, d), F32),
        struct((n, d)),
        struct(turned),
        struct(turned),
    ]
    return launch(
        functools.partial(mix_kernel, chunks, heads),
        "carried_mixed_middle",
        chunks,
        [info, slopes, att, qpre, came, sel, wo, hidden, cot, rot],
        [
            smem(),
            smem(),
            tile,
            tile,
            whole_block(came.shape),
            tile,
            whole_block(wo.shape),
            tile,
            tile,
            pl.BlockSpec((CHUNK, 2 * HEAD), lambda c: (c, 0)),
        ],
        outs,
        [tile, turned_tile, tile, tile, turned_tile, turned_tile],
        [pltpu.VMEM((CHUNK, d), F32)],
        3 * n * d * d,
        **ride,
    )


def sglu_kernel(chunks, heads, peers, plan, count, first, last, info, slopes, *refs):
    refs = list(refs)
    take = lambda k: [refs.pop(0) for _ in range(k)]
    step = pl.program_id(0)
    sweep, c = lax.div(step, chunks), chunks - 1 - lax.rem(step, chunks)
    me = lax.axis_index("mp")
    block = lax.rem(me + sweep, peers)
    here = pl.ds(pl.multiple_of(c * CHUNK, CHUNK), CHUNK)
    (sec, cot) = take(2)
    sources = take(count)
    if not first:
        (term_i, part_i) = take(2)
    if last:
        (mid, sel, att, wo, qpre, rot) = take(6)
    (units_o,) = take(1)
    if last:
        (out_o, gmid_o, pair_o, gatt_o, et_o, e0_o) = take(6)
    else:
        (term_o, part_o) = take(2)
    (w1, w2, wd, term_s, part_s, sems) = take(6)
    if last:
        (state,) = take(1)

    def copies(own):
        for i, (which, source, inner, low, size, slot, mask, rows) in enumerate(plan):
            if (slot == 0) != own:
                continue
            src, dst = sources[source], (w1, w2, wd)[which]
            if inner is not None:
                src = src.at[inner]
            if low is not None:
                src = src.at[:, pl.ds(low, size)] if which < 2 else src.at[pl.ds(low, size), :]
            if slot is not None:
                dst = dst.at[me if slot == 0 else 1 - me]
            if rows is not None:
                at = flipped(lax.rem(lax.axis_index("dp"), 8), mask) * rows
                dst = dst.at[pl.ds(pl.multiple_of(at, 16), rows), :]
            yield pltpu.make_async_copy(src, dst, sems.at[i])

    whole = plan[0][5] is None

    @pl.when(step == 0)
    def _():
        for copy in list(copies(True)) + list(copies(False)):
            copy.start()
        if last:
            state[...] = jnp.zeros_like(state)
        for copy in copies(not whole):
            copy.wait()

    if not whole:

        @pl.when(step == chunks)
        def _():
            for copy in copies(False):
                copy.wait()

    x, y = sec[...], cot[...]
    left = nn(x, w1[block])
    right = nn(x, w2[block])
    inner = (left * right).astype(BF16)
    upstream = nt(y, wd[block])
    grad_left = (upstream * right).astype(BF16)
    grad_right = (upstream * left).astype(BF16)
    units_o[0] = grad_left
    units_o[1] = grad_right
    units_o[2] = inner
    new_term = nn(inner, wd[block])
    new_part = nt(grad_left, w1[block]) + nt(grad_right, w2[block])

    @pl.when(sweep == 0)
    def _():
        term_s[here, :] = new_term if first else new_term + term_i[...]
        part_s[here, :] = new_part if first else new_part + part_i[...]

    @pl.when(sweep > 0)
    def _():
        term_s[here, :] += new_term
        part_s[here, :] += new_part

    @pl.when(sweep == peers - 1)
    def _():
        term, part = term_s[here, :], part_s[here, :]
        if not last:
            term_o[...] = term
            part_o[...] = part
            return
        middle = mid[...]
        out_o[...] = (middle + term).astype(BF16)
        grad_middle = y.astype(F32) + norm_back(middle, scale_of(middle), part)
        gmid_o[...] = grad_middle
        branch = grad_middle.astype(BF16)
        pair_o[0] = branch
        grad_mixed = nt(branch, wo[...])
        attended = att[...].astype(F32)
        scale = scale_of(attended)
        pair_o[1] = (grad_mixed * attended * scale).astype(BF16)
        alive = (row_index((CHUNK, 1)) + c * CHUNK < info[4 * chunks]).astype(F32)
        grad_att = norm_back(attended, scale, grad_mixed * sel[...].astype(F32)) * alive
        gatt_o[...] = grad_att.astype(BF16)
        cs, sn = rot[:, :HEAD], rot[:, HEAD:]
        keep = info[chunks + c].astype(F32)
        for h in range(heads):
            slope = slopes[h]
            query = featured(qpre[:, head_slice(h)].astype(F32), cs, sn)
            faded = (grad_att[:, head_slice(h)] * fade_from_start(slope, HEAD)).astype(BF16)
            old = state[h]
            et_o[0, h] = old.astype(BF16)
            state[h] = keep * (
                jnp.exp(jnp.full((1, 2 * HEAD), -slope * CHUNK, F32)) * old + nn(faded.T, query)
            )
        e0_o[...] = state[...].astype(BF16)


def run_sglu(info, slopes, second, cot, sources, plan, peers, width, before, after, **ride):
    n, d = second.shape
    heads, chunks = d // HEAD, n // CHUNK
    first, last = before is None, after is not None
    chunk_of = lambda s: chunks - 1 - lax.rem(s, chunks)
    late = lambda s: jnp.where(s >= (peers - 1) * chunks, chunk_of(s), chunks - 1)
    early = lambda s: jnp.where(s < chunks, chunk_of(s), 0)
    tile = pl.BlockSpec((CHUNK, d), lambda s: (chunk_of(s), 0))
    late_tile = pl.BlockSpec((CHUNK, d), lambda s: (late(s), 0))
    early_tile = pl.BlockSpec((CHUNK, d), lambda s: (early(s), 0))
    inputs = [info, slopes, second, cot] + list(sources)
    specs = [smem(), smem(), tile, tile] + [anywhere()] * len(sources)
    if not first:
        inputs += list(before)
        specs += [early_tile, early_tile]
    if last:
        mid, sel, att, wo, qpre, rot = after
        inputs += [mid, sel, att, wo, qpre, rot]
        specs += [late_tile, late_tile, late_tile, whole_block(wo.shape), late_tile, pl.BlockSpec((CHUNK, 2 * HEAD), lambda s: (late(s), 0))]
    outs = [struct((3, peers, n, width))]
    out_specs = [
        pl.BlockSpec(
            (3, None, CHUNK, width),
            lambda s: (0, lax.rem(lax.axis_index("mp") + lax.div(s, chunks), peers), chunk_of(s), 0),
        )
    ]
    scratch = [
        pltpu.VMEM((peers, d, width), BF16),
        pltpu.VMEM((peers, d, width), BF16),
        pltpu.VMEM((peers, width, d), BF16),
        pltpu.VMEM((n, d), F32),
        pltpu.VMEM((n, d), F32),
        pltpu.SemaphoreType.DMA((len(plan),)),
    ]
    if last:
        outs += [
            struct((n, d)),
            struct((n, d), F32),
            struct((2, n, d)),
            struct((n, d)),
            struct((chunks, heads, HEAD, 2 * HEAD)),
            struct((heads, HEAD, 2 * HEAD)),
        ]
        out_specs += [
            late_tile,
            late_tile,
            pl.BlockSpec((2, CHUNK, d), lambda s: (0, late(s), 0)),
            late_tile,
            pl.BlockSpec((1, heads, HEAD, 2 * HEAD), lambda s: (late(s), 0, 0, 0)),
            whole_block((heads, HEAD, 2 * HEAD)),
        ]
        scratch.append(pltpu.VMEM((heads, HEAD, 2 * HEAD), F32))
    else:
        outs += [struct((n, d), F32), struct((n, d), F32)]
        out_specs += [late_tile, late_tile]
    return launch(
        functools.partial(sglu_kernel, chunks, heads, peers, plan, len(sources), first, last),
        "sglu_last" if last else "sglu_first",
        peers * chunks,
        inputs,
        specs,
        outs,
        out_specs,
        scratch,
        12 * n * d * width * peers,
        **ride,
    )


def rows_of(left):
    block = left[...]
    return block.reshape(block.shape[0] * block.shape[1], block.shape[2])


def weights_kernel(items, peers, half, *refs):
    item = lax.div(pl.program_id(0), peers)
    lefts, right, out = refs[:-2], refs[-2], refs[-1]
    for i, left in enumerate(lefts):

        @pl.when(functools.reduce(jnp.logical_or, [item == t for t, w in enumerate(items) if w == i]))
        def _(left=left):
            out[...] = nn(rows_of(left), right[...]).astype(BF16).reshape(out.shape)


def run_weights(half, lefts, items, rights, right_spec, peers, width):
    pairs, _, rows, n = lefts[0].shape
    shape = (peers, len(items), pairs, rows, width)
    out = struct(shape)
    inputs = list(lefts) + [rights]
    return pl.pallas_call(
        functools.partial(weights_kernel, items, peers),
        grid_spec=pltpu.PrefetchScalarGridSpec(
            num_scalar_prefetch=1,
            grid=(peers * len(items),),
            in_specs=[pl.BlockSpec((pairs, None, rows, n), lambda s, half: (0, half[0], 0, 0))] * len(lefts)
            + [right_spec(lambda s, half: (lax.div(s, peers), lax.rem(s, peers)))],
            out_specs=pl.BlockSpec(
                (None, None) + shape[2:], lambda s, half: (lax.rem(s, peers), lax.div(s, peers), 0, 0, 0)
            ),
        ),
        out_shape=out,
        compiler_params=pltpu.CompilerParams(vmem_limit_bytes=VMEM_LIMIT),
        name="weight_gradients",
    )(half, *inputs)


def shared_weights_kernel(items, *refs):
    count = len(set(items))
    lefts, right, out = refs[:count], refs[count], refs[count + 1]
    given, got, send, recv = refs[count + 2 :]
    step = pl.program_id(0)
    own = lax.div(step, 2 * len(items))
    k = lax.rem(step, 2 * len(items))
    item = lax.div(k, 2)
    copy = remote(given.at[k], got.at[k], send.at[k], recv.at[k], "dp", 1)

    @pl.when(own == 1)
    def _():
        copy.wait()

    for i, left in enumerate(lefts):
        chosen = functools.reduce(jnp.logical_or, [item == t for t, w in enumerate(items) if w == i])

        @pl.when(jnp.logical_and(chosen, own == 0))
        def _(left=left):
            given[k] = nn(rows_of(left), right[...]).astype(BF16)

        @pl.when(jnp.logical_and(chosen, own == 1))
        def _(left=left):
            total = nn(rows_of(left), right[...]) + got[k].astype(F32)
            out[...] = total.astype(BF16).reshape(out.shape)

    @pl.when(own == 0)
    def _():
        copy.start()


def run_shared_weights(lefts, items, rights, right_spec, width, depth, **ride):
    pairs, _, rows, n = lefts[0].shape
    kinds = len(items)
    which = lambda s: (lax.div(lax.rem(s, 2 * kinds), 2), lax.rem(s, 2))
    core = lambda: lax.rem(lax.axis_index("dp"), 2)
    share = lambda s: jnp.where(s < 2 * kinds, 1 - core(), core())
    kept = lambda s: jnp.maximum(s - 2 * kinds, 0)
    return launch(
        functools.partial(shared_weights_kernel, items),
        "weight_gradients",
        4 * kinds,
        list(lefts) + [rights],
        [pl.BlockSpec((pairs, None, rows, n), lambda s: (0, share(s), 0, 0))] * len(lefts) + [right_spec(which)],
        [struct((2, depth, 2, kinds, rows, width))],
        [
            pl.BlockSpec(
                (None, depth, 2, None, rows, width),
                lambda s: (lax.rem(kept(s), 2), 0, 0, lax.div(kept(s), 2), 0, 0),
            )
        ],
        [
            pltpu.VMEM((2 * kinds, pairs * rows, width), BF16),
            pltpu.VMEM((2 * kinds, pairs * rows, width), BF16),
            pltpu.SemaphoreType.DMA((2 * kinds,)),
            pltpu.SemaphoreType.DMA((2 * kinds,)),
        ],
        8 * n * pairs * rows * width * kinds,
        partners=[("dp", 1)],
        **ride,
    )


def attention_back_kernel(chunks, first_head, info, slopes, qpre, kpre, values, gatt, st, came, et, left, rot, grads_o):
    pair, c = lax.div(pl.program_id(0), chunks), lax.rem(pl.program_id(0), chunks)
    cs, sn = rot[:, :HEAD], rot[:, HEAD:]
    before = info[2 * chunks + c].astype(F32)
    after = info[3 * chunks + c].astype(F32)
    span = CHUNK * c.astype(F32)
    rest = CHUNK * (chunks - 1 - c).astype(F32)
    for h in range(2):
        slope = slopes[first_head + 2 * pair + h]
        cols = head_slice(h)
        qp, kp = qpre[:, cols].astype(F32), kpre[:, cols].astype(F32)
        qs, ks = sigmoid(qp), sigmoid(kp)
        qa, ka = qp * qs, kp * ks
        query = jnp.concatenate([qa * cs, qa * sn], axis=-1).astype(BF16)
        key = jnp.concatenate([ka * cs, ka * sn], axis=-1).astype(BF16)
        value, grad = values[:, cols], gatt[:, cols]
        lane = jnp.zeros((1, 2 * HEAD), F32)
        state = st[0, h].astype(F32) + came[h].astype(F32) * (jnp.exp(lane - slope * span) * before)
        ending = et[0, h].astype(F32) + left[h].astype(F32) * (jnp.exp(lane - slope * rest) * after)
        state, ending = state.astype(BF16), ending.astype(BF16)
        table, turned = decay_table(slope, False), decay_table(slope, True)
        scores_t = (nt(key, query) * turned).astype(BF16)
        slope_s = (nt(grad, value) * table).astype(BF16)
        slope_t = (nt(value, grad) * turned).astype(BF16)
        start = fade_from_start(slope, HEAD)
        end = fade_to_end(slope, HEAD)
        grad_start = (grad.astype(F32) * start).astype(BF16)
        value_end = (value.astype(F32) * end).astype(BF16)
        dq = nn(slope_s, key) + nn(grad_start, state)
        dk = nn(slope_t, query) + nn(value_end, ending)
        dv = nn(scores_t, grad) + end * nt(key, ending)
        grads_o[2, :, cols] = dv.astype(BF16)
        dq = dq[:, :HEAD] * cs + dq[:, HEAD:] * sn
        dk = dk[:, :HEAD] * cs + dk[:, HEAD:] * sn
        grads_o[0, :, cols] = (dq * (qs * (1.0 + qp * (1.0 - qs)))).astype(BF16)
        grads_o[1, :, cols] = (dk * (ks * (1.0 + kp * (1.0 - ks)))).astype(BF16)


def run_attention_back(info, slopes, qpre, kpre, values, gatt, st, came, et, left, rot, first_head, heads, **ride):
    n, d = qpre.shape
    chunks = n // CHUNK
    skip = first_head // 2
    pair = lambda s: lax.div(s, chunks)
    chunk = lambda s: lax.rem(s, chunks)
    tile = pl.BlockSpec((CHUNK, 2 * HEAD), lambda s: (chunk(s), skip + pair(s)))
    states = pl.BlockSpec((1, 2, HEAD, 2 * HEAD), lambda s: (chunk(s), skip + pair(s), 0, 0))
    ends = pl.BlockSpec((2, HEAD, 2 * HEAD), lambda s: (skip + pair(s), 0, 0))
    return launch(
        functools.partial(attention_back_kernel, chunks, first_head),
        "attention_backward",
        chunks * heads // 2,
        [info, slopes, qpre, kpre, values, gatt, st, came, et, left, rot],
        [smem(), smem(), tile, tile, tile, tile, states, ends, states, ends, pl.BlockSpec((CHUNK, 2 * HEAD), lambda s: (chunk(s), 0))],
        [struct((3, n, heads * HEAD))],
        [pl.BlockSpec((3, CHUNK, 2 * HEAD), lambda s: (0, chunk(s), pair(s)))],
        [],
        18 * n * 256 * 256 * heads // 2,
        **ride,
    )


def input_kernel(wq, wk, wv, ws, grads, pair, hid, gmid, out):
    total = nt(grads[0], wq[...]) + nt(grads[1], wk[...]) + nt(grads[2], wv[...]) + nt(pair[...], ws[...])
    x = hid[...].astype(F32)
    out[...] = (gmid[...] + norm_back(x, scale_of(x), total)).astype(BF16)


def run_input(weights, grads, pair, hidden, gmid, **ride):
    n, d = hidden.shape
    tile = pl.BlockSpec((CHUNK, d), lambda c: (c, 0))
    return launch(
        input_kernel,
        "input_gradient",
        n // CHUNK,
        list(weights) + [grads, pair, hidden, gmid],
        [whole_block(w.shape) for w in weights]
        + [
            pl.BlockSpec((3, CHUNK, d), lambda c: (0, c, 0)),
            pl.BlockSpec((None, CHUNK, d), lambda c: (1, c, 0)),
            tile,
            tile,
        ],
        [struct((n, d))],
        [tile],
        [],
        8 * n * d * d,
        **ride,
    )


def across(x, axis, flip):
    size = lax.axis_size(axis)
    return lax.ppermute(x, axis, [(i, i ^ flip) for i in range(size)])


def pick(x, index, axis):
    return lax.dynamic_index_in_dim(x, index, axis, keepdims=False)


def halved(array):
    dp, me = lax.axis_index("dp"), lax.axis_index("mp")
    x = (dp // 2) % 2
    half = array.shape[1] // 2
    p, q = array[:, :half], array[:, half:]
    p = plus(pick(p, x, 2), across(pick(p, 1 - x, 2), "dp", 2)).astype(BF16)
    q = plus(pick(q, me, 0), across(pick(q, 1 - me, 0), "mp", 1)).astype(BF16)
    p = plus(pick(p, me, 0), across(pick(p, 1 - me, 0), "mp", 1))
    q = plus(pick(q, x, 1), across(pick(q, 1 - x, 1), "dp", 2))
    return jnp.concatenate([p, q], axis=0).astype(BF16)


def spread(line):
    dp = lax.axis_index("dp")
    z = dp // 4
    return [across(pick(line, z ^ k, 0), "dp", 4 * k) for k in range(1, line.shape[0])]


def summed(line, others):
    return plus(pick(line, lax.axis_index("dp") // 4, 0), *others)


def spread_guest(line, steps):
    depth = line.shape[0]

    def source(k):
        return lambda i, o: i[0].at[flipped(lax.div(lax.axis_index("dp"), 4), k)]

    copies = [(source(k), lambda i, o, k=k: o[0].at[k - 1], "dp", 4 * k) for k in range(1, depth)]
    return Carry([line], [struct((depth - 1,) + line.shape[1:])], [(0, steps - 1, copies)])


def reduced(lefts, items, rights, spec, peers, width):
    halves = [
        run_weights(jnp.full((1,), k, jnp.int32), lefts, items, rights, spec, peers, width) for k in range(2)
    ]
    full = jnp.stack(halves, axis=3)
    full = full.reshape(peers, len(items), -1, full.shape[4], width)
    mine = lax.psum_scatter(full, "dp", scatter_dimension=2, tiled=False)
    return lax.psum_scatter(mine, "mp", scatter_dimension=0, tiled=False).astype(F32)


def per_device(
    hidden_in,
    query_weight,
    key_weight,
    value_weight,
    select_weight,
    out_weight,
    first_weight,
    second_weight,
    down_weight,
    decay_slope,
    doc_lengths,
    cotangent,
):
    count, d = hidden_in.shape
    heads, chunks = d // HEAD, count // CHUNK
    peers, parts = lax.axis_size("mp"), lax.axis_size("dp")
    me = lax.axis_index("mp")
    depth = parts // 4
    group = count * peers
    units = first_weight.shape[1]
    lengths = doc_lengths[0].astype(jnp.int32)
    info = chunk_info(lengths, me * count, count)
    rot = turning(info, chunks, group // 2)
    slopes = decay_slope
    matrices = (first_weight, second_weight, down_weight)
    riding = peers == 2

    if riding:
        cut = -(-units // 256) * 128
        ranges = [(0, cut), (cut, units - cut)]
    else:
        ranges = [(0, units)]

    def like(arrays, count=None):
        return [struct(a.shape if count is None else (count,) + a.shape) for a in arrays]

    def over_mp(g, steps):
        low, size = ranges[g]

        def source(w):
            def src(i, o):
                eighth = lax.rem(lax.axis_index("dp"), 8)
                if w < 2:
                    rows = d // 8
                    return i[w].at[pl.ds(pl.multiple_of(eighth * rows, 16), rows), pl.ds(low, size)]
                rows = size // 8
                return i[w].at[pl.ds(pl.multiple_of(low + eighth * rows, 16), rows), :]

            return src

        outs = [struct((d // 8, size)), struct((d // 8, size)), struct((size // 8, d))]
        copies = [(source(w), lambda i, o, w=w: o[w], "mp", 1) for w in range(3)]
        return Carry(matrices, outs, [(0, steps, copies)])

    def near(w):
        return [
            (lambda i, o: i[w], lambda i, o: o[w].at[0], "dp", 2),
            (lambda i, o: i[w], lambda i, o: o[w].at[1], "dp", 4),
            (lambda i, o: i[w], lambda i, o: o[w].at[2], "dp", 1),
        ]

    def far(w, src, dst, rows):
        top = -(-rows // 32) * 16
        upper, lower = pl.ds(0, top), pl.ds(top, rows - top)
        return [
            (lambda i, o: src(i, o).at[1, upper, :], lambda i, o: dst(i, o).at[0, upper, :], "dp", 2),
            (lambda i, o: src(i, o).at[0, lower, :], lambda i, o: dst(i, o).at[0, lower, :], "dp", 4),
            (lambda i, o: src(i, o).at[0], lambda i, o: dst(i, o).at[1], "dp", 1),
            (lambda i, o: src(i, o).at[1], lambda i, o: dst(i, o).at[2], "dp", 1),
        ]

    ride = dict(guests=[over_mp(0, chunks - 1)], ident=1) if riding else {}
    normed, normed_t, kpre, values, st, final, *had = run_keys(
        info, slopes, hidden_in, key_weight, value_weight, rot, parts, **ride
    )
    whole_keep = info[2 * chunks + chunks - 1].astype(F32)
    decay = jnp.exp(-slopes * count)
    ride = {}
    if riding:
        state_copy = [(lambda i, o: i[0], lambda i, o: o[0], "mp", 1)]
        near_copies = [c for w in range(3) for c in near(w)]
        ride = dict(
            guests=[
                Carry([final], like([final]), [(0, chunks - 1, state_copy)]),
                Carry(had, like(had, 3), [(0, chunks - 1, near_copies)]),
            ],
            ident=2,
        )
    qpre, sel, att, *more = run_inside(
        info, slopes, normed, query_weight, select_weight, kpre, values, st, rot, **ride
    )
    if riding:
        came, close = more[0], more[1:]
        came = jnp.where(me == 1, came, jnp.zeros_like(came))
    else:
        finals = lax.all_gather(final, "mp")
        keeps = lax.all_gather(whole_keep.reshape(1), "mp")[:, 0]

        def ahead(k, total):
            new = finals[k].astype(F32) + (keeps[k] * decay)[:, None, None] * total
            return jnp.where(k < me, new, total)

        came = lax.fori_loop(0, peers, ahead, jnp.zeros(final.shape, F32)).astype(BF16)
    ride = {}
    if riding:
        first_phase = []
        for w in range(3):
            src, dst = (lambda i, o, w=w: i[w]), (lambda i, o, w=w: o[w])
            first_phase += far(w, src, dst, close[w].shape[1])
        second_phase = [
            (lambda i, o, w=w: o[w].at[0], lambda i, o, w=w: o[3 + w], "dp", 1) for w in range(3)
        ]
        ride = dict(
            guests=[
                Carry(
                    close,
                    like(close) + like(had),
                    [(0, chunks // 2, first_phase), (chunks // 2 + 1, chunks - 1, second_phase)],
                ),
                over_mp(1, chunks - 1),
            ],
            ident=3,
        )
    attended, mixed_t, middle, second, second_t, cot_t, *more = run_mix(
        info, slopes, att, qpre, came, sel, out_weight, hidden_in, cotangent, rot, parts, **ride
    )

    def plan_of(low, size, had, close, wide, corner):
        sources = list(matrices) + list(had) + list(close) + list(wide) + list(corner)
        plan = []
        for which in range(3):
            rows = had[which].shape[0]
            plan.append((which, which, None, low, size, 0, None, None))
            pieces = [(3, None, 0), (6, 0, 2), (6, 1, 4), (6, 2, 1), (9, 0, 6), (9, 1, 3), (9, 2, 5), (12, None, 7)]
            for at, inner, mask in pieces:
                plan.append((which, at + which, inner, None, None, 1, mask, rows))
        return tuple(plan), sources

    units_spec = lambda n, size: lambda at: pl.BlockSpec(
        (None, None, n, size), lambda s, *r: at(s, *r) + (0, 0)
    )
    share = d // peers
    wide_spec = lambda at: pl.BlockSpec(
        (None, count, share), lambda s, *r: (at(s, *r)[0], 0, at(s, *r)[1])
    )
    if not riding:
        plan = tuple((w, w, None, None, None, None, None, None) for w in range(3))
        sources = [lax.all_gather(w, "mp") for w in matrices]
        after = (middle, sel, attended, out_weight, qpre, rot)
        grads, output, grad_middle, pair, grad_att, et, leaving = run_sglu(
            info, slopes, second, cotangent, sources, plan, peers, units, None, after
        )
        sglu = reduced([second_t, cot_t], (0, 0, 1), grads, units_spec(count, units), peers, units)
        leavings = lax.all_gather(leaving, "mp")

        def behind(step, total):
            k = peers - 1 - step
            new = leavings[k].astype(F32) + (keeps[k] * decay)[:, None, None] * total
            return jnp.where(k > me, new, total)

        left = lax.fori_loop(0, peers, behind, jnp.zeros(leaving.shape, F32)).astype(BF16)
        out_sel = reduced([mixed_t, normed_t], (0, 1), pair, wide_spec, peers, share)
        (qkv,) = run_attention_back(
            info, slopes, qpre, kpre, values, grad_att, st, came, et, left, rot, 0, heads
        )
        inputs = reduced([normed_t], (0, 0, 0), qkv, wide_spec, peers, share)
        (grad_hidden,) = run_input(
            [query_weight, key_weight, value_weight, select_weight], qkv, pair, hidden_in, grad_middle
        )
    else:
        wide, corner, had_b = more[:3], more[3:6], more[6:9]
        steps = peers * chunks
        plan, sources = plan_of(*ranges[0], had, close, wide, corner)
        one = [c for w in range(3) for c in near(w)]
        two = []
        for w in range(3):
            src, dst = (lambda i, o, w=w: o[w]), (lambda i, o, w=w: o[3 + w])
            two += far(w, src, dst, had_b[w].shape[0])
        three = [
            (lambda i, o, w=w: o[3 + w].at[0], lambda i, o, w=w: o[6 + w], "dp", 1) for w in range(3)
        ]
        phases = [(0, steps // 2 - 1, one), (steps // 2, steps - 2, two), (steps - 1, steps - 1, three)]
        ride = dict(
            guests=[Carry(had_b, like(had_b, 3) + like(had_b, 3) + like(had_b), phases)], ident=4
        )
        grads, term, part, *more = run_sglu(
            info, slopes, second, cotangent, sources, plan, peers, ranges[0][1], None, None, **ride
        )
        (halves_a,) = run_shared_weights(
            [second_t, cot_t], (0, 0, 1), grads, units_spec(count, ranges[0][1]), ranges[0][1], depth, ident=5
        )
        plan, sources = plan_of(*ranges[1], had_b, more[:3], more[3:6], more[6:9])
        after = (middle, sel, attended, out_weight, qpre, rot)
        ride = dict(guests=[Halving(halves_a, (0, 5, steps - 1))], ident=6)
        grads, output, grad_middle, pair, grad_att, et, leaving, line_a = run_sglu(
            info, slopes, second, cotangent, sources, plan, peers, ranges[1][1], (term, part), after, **ride
        )
        state_copy = [(lambda i, o: i[0], lambda i, o: o[0], "mp", 1)]
        ride = dict(guests=[Carry([leaving], like([leaving]), [(0, 11, state_copy)])], ident=7)
        halves_b, left = run_shared_weights(
            [second_t, cot_t], (0, 0, 1), grads, units_spec(count, ranges[1][1]), ranges[1][1], depth, **ride
        )
        left = jnp.where(me == 0, left, jnp.zeros_like(left))
        (halves_c,) = run_shared_weights([mixed_t, normed_t], (0, 1), pair, wide_spec, share, depth, ident=8)
        steps = chunks * heads // 2
        ride = dict(guests=[spread_guest(line_a, steps)], ident=9)
        qkv, other_a = run_attention_back(
            info, slopes, qpre, kpre, values, grad_att, st, came, et, left, rot, 0, heads, **ride
        )
        (halves_d,) = run_shared_weights([normed_t], (0, 0, 0), qkv, wide_spec, share, depth, ident=10)
        (grad_hidden,) = run_input(
            [query_weight, key_weight, value_weight, select_weight], qkv, pair, hidden_in, grad_middle
        )
        line_b, line_c, line_d = halved(halves_b), halved(halves_c), halved(halves_d)
        sglu_a = summed(line_a, [other_a[k] for k in range(depth - 1)])
        sglu = jnp.concatenate([sglu_a, summed(line_b, spread(line_b))], axis=2)
        out_sel = summed(line_c, spread(line_c))
        inputs = summed(line_d, spread(line_d))
    return (
        output,
        grad_hidden,
        inputs[0],
        inputs[1],
        inputs[2],
        out_sel[1],
        out_sel[0],
        sglu[0],
        sglu[1],
        jnp.transpose(sglu[2]),
    )


def solution(mesh):
    rows = P(("dp", "mp"), None)
    in_specs = (
        rows,
        P(),
        P(),
        P(),
        P(),
        P(),
        P(None, "mp"),
        P(None, "mp"),
        P("mp", None),
        P(),
        P("dp", None),
        rows,
    )
    out_specs = (rows, rows) + (P("dp", "mp"),) * 7 + (P("mp", "dp"),)
    return jax.shard_map(
        per_device, mesh=mesh, in_specs=in_specs, out_specs=out_specs, check_vma=False
    )
```

```python
import functools

import jax
import jax.numpy as jnp
import numpy as np
from jax import lax
from jax.experimental import pallas as pl
from jax.experimental.pallas import tpu as pltpu
from jax.sharding import PartitionSpec as P

HEAD = 128
CHUNK = 256
EPSILON = 1e-06
BF16 = jnp.bfloat16
F32 = jnp.float32
VMEM_LIMIT = 58 * 1024 * 1024


def nn(left, right):
    return jnp.dot(left, right, preferred_element_type=F32)


def nt(left, right):
    return lax.dot_general(left, right, (((1,), (1,)), ((), ())), preferred_element_type=F32)


def scale_of(values):
    return lax.rsqrt(jnp.mean(values * values, axis=-1, keepdims=True) + EPSILON)


def norm_back(values, scale, upstream):
    return scale * upstream - values * (scale * scale * scale) * jnp.mean(
        values * upstream, axis=-1, keepdims=True
    )


def sigmoid(v):
    return 1.0 / (1.0 + jnp.exp(-v))


def featured(pre, cos, sin):
    act = pre * sigmoid(pre)
    return jnp.concatenate([act * cos, act * sin], axis=-1).astype(BF16)


def head_slice(h):
    return slice(h * HEAD, (h + 1) * HEAD)


def row_index(shape):
    return lax.broadcasted_iota(jnp.int32, shape, 0)


def fade_from_start(slope, width):
    return jnp.exp(-slope * (row_index((CHUNK, width)) + 1).astype(F32))


def fade_to_end(slope, width):
    return jnp.exp(-slope * (CHUNK - 1 - row_index((CHUNK, width))).astype(F32))


def decay_table(slope, transposed):
    rows = lax.broadcasted_iota(jnp.int32, (CHUNK, CHUNK), 0)
    cols = lax.broadcasted_iota(jnp.int32, (CHUNK, CHUNK), 1)
    gap = cols - rows if transposed else rows - cols
    return jnp.where(gap >= 0, jnp.exp(-slope * jnp.maximum(gap, 0).astype(F32)), 0.0)


def plus(*arrays):
    total = arrays[0].astype(F32)
    for a in arrays[1:]:
        total = total + a.astype(F32)
    return total


def smem():
    return pl.BlockSpec(memory_space=pltpu.SMEM)


def anywhere():
    return pl.BlockSpec(memory_space=pl.ANY)


def once(shape):
    zeros = (0,) * len(shape)
    return pl.BlockSpec(shape, lambda *_: zeros, pipeline_mode=pl.Buffered(1))


def whole_block(shape):
    zeros = (0,) * len(shape)
    return pl.BlockSpec(shape, lambda *_: zeros)


def cost(flops, arrays):
    moved = sum(int(np.prod(a.shape)) * jnp.dtype(a.dtype).itemsize for a in arrays)
    return pl.CostEstimate(flops=int(flops), bytes_accessed=moved, transcendentals=0)


def struct(shape, dtype=BF16):
    return jax.ShapeDtypeStruct(tuple(shape), dtype)


def flipped(index, mask):
    bit = 1
    while bit <= mask:
        if mask & bit:
            index = index + bit * (1 - 2 * lax.rem(lax.div(index, bit), 2))
        bit *= 2
    return index


def remote(src, dst, send, recv, axis, mask):
    return pltpu.make_async_remote_copy(
        src_ref=src,
        dst_ref=dst,
        send_sem=send,
        recv_sem=recv,
        device_id={axis: flipped(lax.axis_index(axis), mask)},
        device_id_type=pl.DeviceIdType.MESH,
    )


def greet(partners):
    barrier = pltpu.get_barrier_semaphore()
    for axis, mask in partners:
        pl.semaphore_signal(
            barrier,
            inc=1,
            device_id={axis: flipped(lax.axis_index(axis), mask)},
            device_id_type=pl.DeviceIdType.MESH,
        )
    pl.semaphore_wait(barrier, len(partners))


class Carry:
    def __init__(self, inputs, outs, phases):
        self.inputs, self.outs, self.phases = list(inputs), list(outs), phases
        count = sum(len(p[2]) for p in phases)
        self.scratch = [pltpu.SemaphoreType.DMA((count,)), pltpu.SemaphoreType.DMA((count,))]
        self.partners = [(c[2], c[3]) for p in phases for c in p[2]]

    def copies(self, which, ins, outs, scratch):
        at = sum(len(p[2]) for p in self.phases[:which])
        send, recv = scratch
        for k, (src, dst, axis, mask) in enumerate(self.phases[which][2]):
            yield remote(src(ins, outs), dst(ins, outs), send.at[at + k], recv.at[at + k], axis, mask)

    def before(self, step, ins, outs, scratch):
        for p, phase in enumerate(self.phases):

            @pl.when(step == phase[0])
            def _(p=p):
                for copy in self.copies(p, ins, outs, scratch):
                    copy.start()

    def after(self, step, ins, outs, scratch):
        for p, phase in enumerate(self.phases):

            @pl.when(step == phase[1])
            def _(p=p):
                for copy in self.copies(p, ins, outs, scratch):
                    copy.wait()


class Reducer:
    KINDS = 8

    def __init__(self, start, blocks, items, depth, rows, delays):
        self.start, self.blocks, self.items = start, blocks, items
        self.depth, self.rows, self.delays = depth, rows, delays
        half, n, wide = depth // 2, 2 * depth * rows, 2 * HEAD
        buf = lambda *shape: pltpu.VMEM(shape, BF16)
        pair = (half, items, rows, wide)
        flat = (2, half, items, rows, HEAD)
        one = (half, items, rows, HEAD)
        self.scratch = [
            buf(2, items, n, wide),
            buf(2, items, n, wide),
            buf(4, items, n, wide),
            buf(2, *pair),
            buf(2, *pair),
            buf(blocks, *pair),
            buf(2, *flat),
            buf(2, *flat),
            buf(blocks, *flat),
            buf(2, *one),
            buf(2, *one),
            buf(blocks, *one),
            buf(2, *one),
            buf(2, *one),
            buf(blocks, *one),
            buf(2, depth, items, rows, HEAD),
            buf(blocks, depth - 1, items, rows, HEAD),
            pltpu.SemaphoreType.DMA((self.KINDS, blocks)),
            pltpu.SemaphoreType.DMA((self.KINDS, blocks)),
        ]
        self.partners = [("dp", 1), ("dp", 2), ("mp", 1)] + [("dp", 4 * k) for k in range(1, depth)]
        self.last = start + blocks - 1 + delays[3]

    def bind(self, scratch):
        self.refs = scratch
        self.given, self.kept = scratch[:2]
        self.x = lax.rem(lax.div(lax.axis_index("dp"), 2), 2)
        self.z = lax.div(lax.axis_index("dp"), 4)

    def copies(self, stage, j):
        (given, kept, got, ps, pk, pr, qs, qk, qr, ps2, pk2, pr2, qs2, qk2, qr2, line, zr, send, recv) = self.refs
        slot = lax.rem(j, 2)
        if stage == 0:
            plan = [(0, given.at[slot], got.at[lax.rem(j, 4)], "dp", 1)]
        elif stage == 1:
            plan = [(1, ps.at[slot], pr.at[j], "dp", 2), (2, qs.at[slot], qr.at[j], "mp", 1)]
        elif stage == 2:
            plan = [(3, ps2.at[slot], pr2.at[j], "mp", 1), (4, qs2.at[slot], qr2.at[j], "dp", 2)]
        else:
            plan = [
                (4 + k, line.at[slot, flipped(self.z, k)], zr.at[j, k - 1], "dp", 4 * k)
                for k in range(1, self.depth)
            ]
        return [remote(src, dst, send.at[i, j], recv.at[i, j], axis, mask) for i, src, dst, axis, mask in plan]

    def begin(self, j):
        for copy in self.copies(0, j):
            copy.start()

    def run(self, step, out):
        for stage in (4, 3, 2, 1):
            j = step - self.start - self.delays[stage - 1]

            @pl.when(jnp.logical_and(j >= 0, j < self.blocks))
            def _(stage=stage, j=j):
                for copy in self.copies(stage - 1, j):
                    copy.wait()
                self.add(stage, j, out)
                if stage < 4:
                    for copy in self.copies(stage, j):
                        copy.start()

    def add(self, stage, j, out):
        (given, kept, got, ps, pk, pr, qs, qk, qr, ps2, pk2, pr2, qs2, qk2, qr2, line, zr, send, recv) = self.refs
        slot, x, rows = lax.rem(j, 2), self.x, self.rows
        half = self.depth // 2
        if stage == 1:
            four = lax.rem(j, 4)

            def total(t, z, at):
                here = pl.ds(pl.multiple_of((2 * z + at) * rows, rows), rows)
                return plus(kept[slot, t, here, :], got[four, t, here, :]).astype(BF16)

            for z in range(half):
                for t in range(self.items):
                    ps[slot, z, t] = total(t, z, 1 - x)
                    pk[slot, z, t] = total(t, z, x)
                    for at in range(2):
                        block = total(t, half + z, at)
                        qk[slot, at, z, t] = block[:, :HEAD]
                        qs[slot, at, z, t] = block[:, HEAD:]
        elif stage == 2:
            for z in range(half):
                block = plus(pk[slot, z], pr[j, z]).astype(BF16)
                pk2[slot, z] = block[:, :, :HEAD]
                ps2[slot, z] = block[:, :, HEAD:]
                qs2[slot, z] = plus(qk[slot, 1 - x, z], qr[j, 1 - x, z]).astype(BF16)
                qk2[slot, z] = plus(qk[slot, x, z], qr[j, x, z]).astype(BF16)
        elif stage == 3:
            for z in range(half):
                line[slot, z] = plus(pk2[slot, z], pr2[j, z]).astype(BF16)
                line[slot, half + z] = plus(qk2[slot, z], qr2[j, z]).astype(BF16)
        else:
            total = plus(line[slot, self.z], *[zr[j, k] for k in range(self.depth - 1)])
            out[:, :, pl.ds(pl.multiple_of(j * HEAD, HEAD), HEAD)] = total


def launch(kernel, name, steps, inputs, specs, outs, out_specs, scratch, flops, guests=(), ident=None, partners=()):
    guests = list(guests)
    partners = list(partners) + [p for g in guests for p in g.partners]
    partners = sorted(set(partners))
    all_inputs = list(inputs) + [a for g in guests for a in g.inputs]
    all_specs = list(specs) + [anywhere() for g in guests for _ in g.inputs]
    all_outs = list(outs) + [a for g in guests for a in g.outs]
    all_out_specs = list(out_specs) + [anywhere() for g in guests for _ in g.outs]
    all_scratch = list(scratch) + [a for g in guests for a in g.scratch]

    def body(*refs):
        refs = list(refs)
        take = lambda k: [refs.pop(0) for _ in range(k)]
        own = take(len(inputs))
        ins = [take(len(g.inputs)) for g in guests]
        own += take(len(outs))
        gone = [take(len(g.outs)) for g in guests]
        own += take(len(scratch))
        held = [take(len(g.scratch)) for g in guests]
        step = pl.program_id(0)
        if partners:

            @pl.when(step == 0)
            def _():
                greet(partners)

        for g, i, o, s in zip(guests, ins, gone, held):
            g.before(step, i, o, s)
        kernel(*own)
        for g, i, o, s in zip(guests, ins, gone, held):
            g.after(step, i, o, s)

    extra = dict(collective_id=ident, has_side_effects=True) if partners else {}
    return pl.pallas_call(
        body,
        grid=(steps,),
        in_specs=all_specs,
        out_specs=all_out_specs,
        out_shape=all_outs,
        scratch_shapes=all_scratch,
        compiler_params=pltpu.CompilerParams(
            vmem_limit_bytes=VMEM_LIMIT, dimension_semantics=("arbitrary",), **extra
        ),
        cost_estimate=cost(flops, all_inputs + all_outs),
        name=name,
    )(*all_inputs)


def chunk_info(lengths, me, peers, count):
    chunks = count // CHUNK
    offset = me * count
    first = offset + CHUNK * jnp.arange(chunks, dtype=jnp.int32)
    begin, start = jnp.zeros_like(first), jnp.int32(0)
    for i in range(lengths.shape[0]):
        begin = jnp.where(first >= start, start, begin)
        start = start + lengths[i]
    base = first - begin
    keep = (base > 0).astype(jnp.int32)
    before = (begin < offset).astype(jnp.int32)
    after = ((begin[-1] <= first) & (me < peers - 1)).astype(jnp.int32)
    live = jnp.clip(start - offset, 0, count)
    return jnp.concatenate([base, keep, before, after, live[None]]).astype(jnp.int32)


def turning(info, chunks, longest):
    freq = 10000.0 ** (-np.arange(HEAD, dtype=np.float64) / HEAD)
    phase = np.arange(longest, dtype=np.float64)[:, None] * freq[None, :]
    table = jnp.asarray(np.concatenate([np.cos(phase), np.sin(phase)], axis=1), F32)
    return jnp.concatenate(
        [lax.dynamic_slice(table, (info[c], 0), (CHUNK, 2 * HEAD)) for c in range(chunks)], axis=0
    )


def keys_kernel(chunks, heads, info, slopes, hid, wk, wv, rot, normed_o, turned_o, kpre_o, val_o, st_o, fin_o, state):
    c = pl.program_id(0)

    @pl.when(c == 0)
    def _():
        state[...] = jnp.zeros_like(state)

    x = hid[...].astype(F32)
    normed = (x * scale_of(x)).astype(BF16)
    normed_o[...] = normed
    turned_o[...] = normed.T.reshape(turned_o.shape)
    kpre = nn(normed, wk[...])
    kpre_o[...] = kpre.astype(BF16)
    values = nn(normed, wv[...])
    val_o[...] = values.astype(BF16)
    cs, sn = rot[:, :HEAD], rot[:, HEAD:]
    keep = info[chunks + c].astype(F32)
    for h in range(heads):
        slope = slopes[h]
        key = featured(kpre[:, head_slice(h)], cs, sn)
        faded = (values[:, head_slice(h)] * fade_to_end(slope, HEAD)).astype(BF16)
        old = state[h] * keep
        st_o[0, h] = old.astype(BF16)
        state[h] = jnp.exp(jnp.full((1, 2 * HEAD), -slope * CHUNK, F32)) * old + nn(faded.T, key)
    fin_o[...] = state[...].astype(BF16)


def run_keys(info, slopes, hidden, wk, wv, rot, parts, **ride):
    n, d = hidden.shape
    heads, chunks = d // HEAD, n // CHUNK
    turned = (parts // 2, 2, d // parts, n)
    tile = pl.BlockSpec((CHUNK, d), lambda c: (c, 0))
    outs = [
        struct((n, d)),
        struct(turned),
        struct((n, d)),
        struct((n, d)),
        struct((chunks, heads, HEAD, 2 * HEAD)),
        struct((heads, HEAD, 2 * HEAD)),
    ]
    return launch(
        functools.partial(keys_kernel, chunks, heads),
        "keys_values_states",
        chunks,
        [info, slopes, hidden, wk, wv, rot],
        [smem(), smem(), tile, whole_block(wk.shape), whole_block(wv.shape), pl.BlockSpec((CHUNK, 2 * HEAD), lambda c: (c, 0))],
        outs,
        [
            tile,
            pl.BlockSpec(turned[:3] + (CHUNK,), lambda c: (0, 0, 0, c)),
            tile,
            tile,
            pl.BlockSpec((1, heads, HEAD, 2 * HEAD), lambda c: (c, 0, 0, 0)),
            whole_block((heads, HEAD, 2 * HEAD)),
        ],
        [pltpu.VMEM((heads, HEAD, 2 * HEAD), F32)],
        4 * n * d * d,
        **ride,
    )


def inside_kernel(chunks, heads, info, slopes, normed, wq, ws, kpre, values, st, rot, qpre_o, sel_o, att_o):
    c = pl.program_id(0)
    x = normed[...]
    qpre = nn(x, wq[...])
    qpre_o[...] = qpre.astype(BF16)
    sel_o[...] = nn(x, ws[...]).astype(BF16)
    cs, sn = rot[:, :HEAD], rot[:, HEAD:]
    for h in range(heads):
        slope = slopes[h]
        query = featured(qpre[:, head_slice(h)], cs, sn)
        key = featured(kpre[:, head_slice(h)].astype(F32), cs, sn)
        weights = (nt(query, key) * decay_table(slope, False)).astype(BF16)
        att_o[:, head_slice(h)] = nn(weights, values[:, head_slice(h)]) + fade_from_start(
            slope, HEAD
        ) * nt(query, st[0, h])


def run_inside(info, slopes, normed, wq, ws, kpre, values, st, rot, **ride):
    n, d = normed.shape
    heads, chunks = d // HEAD, n // CHUNK
    tile = pl.BlockSpec((CHUNK, d), lambda c: (c, 0))
    outs = [struct((n, d)), struct((n, d)), struct((n, d), F32)]
    return launch(
        functools.partial(inside_kernel, chunks, heads),
        "queries_attention",
        chunks,
        [info, slopes, normed, wq, ws, kpre, values, st, rot],
        [
            smem(),
            smem(),
            tile,
            whole_block(wq.shape),
            whole_block(ws.shape),
            tile,
            tile,
            pl.BlockSpec((1, heads, HEAD, 2 * HEAD), lambda c: (c, 0, 0, 0)),
            pl.BlockSpec((CHUNK, 2 * HEAD), lambda c: (c, 0)),
        ],
        outs,
        [tile, tile, tile],
        [],
        6 * n * d * d,
        **ride,
    )


def mix_kernel(chunks, heads, info, slopes, att, qpre, came, sel, wo, hid, cot, rot, att_o, mixt_o, mid_o, sec_o, sect_o, cott_o, total):
    c = pl.program_id(0)
    cs, sn = rot[:, :HEAD], rot[:, HEAD:]
    reached = info[2 * chunks + c].astype(F32)
    lag = (c * CHUNK).astype(F32)
    alive = (row_index((CHUNK, HEAD)) + c * CHUNK < info[4 * chunks]).astype(F32)
    for h in range(heads):
        slope = slopes[h]
        query = featured(qpre[:, head_slice(h)].astype(F32), cs, sn)
        fade = jnp.exp(-slope * (row_index((CHUNK, HEAD)).astype(F32) + (lag + 1.0))) * reached
        total[:, head_slice(h)] = (att[:, head_slice(h)] + fade * nt(query, came[h])) * alive
    attended = total[...]
    att_o[...] = attended.astype(BF16)
    mixed = (attended * scale_of(attended) * sel[...].astype(F32)).astype(BF16)
    mixt_o[...] = mixed.T.reshape(mixt_o.shape)
    middle = hid[...].astype(F32) + nn(mixed, wo[...])
    mid_o[...] = middle
    second = (middle * scale_of(middle)).astype(BF16)
    sec_o[...] = second
    sect_o[...] = second.T.reshape(sect_o.shape)
    cott_o[...] = cot[...].T.reshape(cott_o.shape)


def run_mix(info, slopes, att, qpre, came, sel, wo, hidden, cot, rot, parts, **ride):
    n, d = hidden.shape
    heads, chunks = d // HEAD, n // CHUNK
    turned = (parts // 2, 2, d // parts, n)
    tile = pl.BlockSpec((CHUNK, d), lambda c: (c, 0))
    turned_tile = pl.BlockSpec(turned[:3] + (CHUNK,), lambda c: (0, 0, 0, c))
    outs = [
        struct((n, d)),
        struct(turned),
        struct((n, d), F32),
        struct((n, d)),
        struct(turned),
        struct(turned),
    ]
    return launch(
        functools.partial(mix_kernel, chunks, heads),
        "carried_mixed_middle",
        chunks,
        [info, slopes, att, qpre, came, sel, wo, hidden, cot, rot],
        [
            smem(),
            smem(),
            tile,
            tile,
            whole_block(came.shape),
            tile,
            whole_block(wo.shape),
            tile,
            tile,
            pl.BlockSpec((CHUNK, 2 * HEAD), lambda c: (c, 0)),
        ],
        outs,
        [tile, turned_tile, tile, tile, turned_tile, turned_tile],
        [pltpu.VMEM((CHUNK, d), F32)],
        3 * n * d * d,
        **ride,
    )


def sglu_kernel(chunks, peers, sec, cot, w1, w2, wd, units_o, term_o, part_o):
    step = pl.program_id(0)
    here = pl.ds(pl.multiple_of(lax.rem(step, chunks) * CHUNK, CHUNK), CHUNK)
    left = nn(sec[...], w1[...])
    right = nn(sec[...], w2[...])
    inner = (left * right).astype(BF16)
    upstream = nt(cot[...], wd[...])
    grad_left = (upstream * right).astype(BF16)
    grad_right = (upstream * left).astype(BF16)
    units_o[0] = grad_left
    units_o[1] = grad_right
    units_o[2] = inner
    term = nn(inner, wd[...])
    part = nt(grad_left, w1[...]) + nt(grad_right, w2[...])

    @pl.when(step < chunks)
    def _():
        term_o[here, :] = term
        part_o[here, :] = part

    @pl.when(step >= chunks)
    def _():
        term_o[here, :] += term
        part_o[here, :] += part


def run_sglu(second, cot, w1, w2, wd):
    n, d = second.shape
    peers, _, width = w1.shape
    chunks = n // CHUNK
    tile = pl.BlockSpec((CHUNK, d), lambda s: (lax.rem(s, chunks), 0))
    block = lambda shape: pl.BlockSpec((None,) + shape, lambda s: (lax.div(s, chunks), 0, 0))
    return launch(
        functools.partial(sglu_kernel, chunks, peers),
        "sglu",
        peers * chunks,
        [second, cot, w1, w2, wd],
        [tile, tile, block((d, width)), block((d, width)), block((width, d))],
        [struct((3, peers, n, width)), struct((n, d), F32), struct((n, d), F32)],
        [
            pl.BlockSpec((3, None, CHUNK, width), lambda s: (0, lax.div(s, chunks), lax.rem(s, chunks), 0)),
            whole_block((n, d)),
            whole_block((n, d)),
        ],
        [],
        12 * n * d * width * peers,
    )


def units_kernel(geo, reducer, ride, first_weight, second_weight, down_weight, x, *refs):
    blocks, cut, d, units = geo["blocks"], geo["cut"], geo["d"], geo["units"]
    refs = list(refs)
    take = lambda k: [refs.pop(0) for _ in range(k)]
    cot_h, xt_h, cott_h = take(3)
    pieces = take(12)
    had_b = take(3)
    term_o, part_o, out = take(3)
    pieces = pieces + had_b + take(9)
    term, part, cot, xt, cott, o1, o2, od, c1, c2, cd, sems, out_sems = take(13)
    reducer.bind(take(len(reducer.scratch)))
    step = pl.program_id(0)
    ride.before(step, had_b, pieces[15:], refs)
    core = lax.rem(lax.axis_index("dp"), 2)
    eighth = lax.rem(lax.axis_index("dp"), 8)

    def fetch(g):
        size = cut if g == 0 else units - cut
        masks = [(0, None, 0), (3, 0, 2), (3, 1, 4), (3, 2, 1), (6, 0, 6), (6, 1, 3), (6, 2, 5), (9, None, 7)]
        copies = []
        for w, region in enumerate((o1, o2, od)):
            rows = d // 8 if w < 2 else size // 8
            for k, (at, inner, mask) in enumerate(masks):
                src = pieces[12 * g + at + w]
                src = src if inner is None else src.at[inner]
                here = pl.ds(pl.multiple_of(flipped(eighth, mask) * rows, 16), rows)
                dst = region.at[here, pl.ds(0, size)] if w < 2 else region.at[here, :]
                copies.append(pltpu.make_async_copy(src, dst, sems.at[g, w, k]))
        return copies

    own = [
        pltpu.make_async_copy(cot_h, cot, out_sems.at[2]),
        pltpu.make_async_copy(xt_h.at[:, 1 - core], xt.at[0], out_sems.at[3]),
        pltpu.make_async_copy(xt_h.at[:, core], xt.at[1], out_sems.at[4]),
        pltpu.make_async_copy(cott_h.at[:, 1 - core], cott.at[0], out_sems.at[5]),
        pltpu.make_async_copy(cott_h.at[:, core], cott.at[1], out_sems.at[6]),
    ]
    done = [
        pltpu.make_async_copy(term, term_o, out_sems.at[0]),
        pltpu.make_async_copy(part, part_o, out_sems.at[1]),
    ]
    turn = cut // HEAD

    @pl.when(step == 0)
    def _():
        for copy in fetch(0) + own:
            copy.start()
        term[...] = jnp.zeros_like(term)
        part[...] = jnp.zeros_like(part)
        for copy in fetch(0):
            copy.wait()

    @pl.when(step == turn)
    def _():
        for copy in fetch(1):
            copy.wait()

    @pl.when(step < blocks)
    def _():
        local = step - jnp.where(step >= turn, turn, 0)
        here = pl.ds(pl.multiple_of(local * HEAD, HEAD), HEAD)
        c1[:, :HEAD] = first_weight[...]
        c1[:, HEAD:] = o1[:, here]
        c2[:, :HEAD] = second_weight[...]
        c2[:, HEAD:] = o2[:, here]
        cd[:HEAD, :] = down_weight[...]
        cd[HEAD:, :] = od[here, :]

    @pl.when(step == turn - 1)
    def _():
        for copy in fetch(1):
            copy.start()

    @pl.when(step == 0)
    def _():
        for copy in own:
            copy.wait()

    @pl.when(step < blocks)
    def _():
        left = nn(x[...], c1[...])
        right = nn(x[...], c2[...])
        inner = (left * right).astype(BF16)
        upstream = nt(cot[...], cd[...])
        grad_left = (upstream * right).astype(BF16)
        grad_right = (upstream * left).astype(BF16)
        slot = lax.rem(step, 2)
        for k, buffer in enumerate((reducer.given, reducer.kept)):
            buffer[slot, 0] = nn(rows_of(xt, k), grad_left).astype(BF16)
            buffer[slot, 1] = nn(rows_of(xt, k), grad_right).astype(BF16)
            buffer[slot, 2] = nn(rows_of(cott, k), inner).astype(BF16)
            if k == 0:
                reducer.begin(step)
        term[...] += nn(inner, cd[...])
        part[...] += nt(grad_left, c1[...]) + nt(grad_right, c2[...])

    @pl.when(step == blocks - 1)
    def _():
        for copy in done:
            copy.start()

    ride.after(step, had_b, pieces[15:], refs)
    reducer.run(step, out)

    @pl.when(step == reducer.last)
    def _():
        for copy in done:
            copy.wait()


def rows_of(ref, k):
    block = ref[k]
    return block.reshape(block.shape[0] * block.shape[1], block.shape[2])


def run_units(matrices, second, cot, second_t, cot_t, pieces, ride, cut, depth, ident):
    n, d = second.shape
    units = matrices[0].shape[1]
    blocks = units // HEAD
    pairs, _, rows, _ = second_t.shape
    reducer = Reducer(0, blocks, 3, depth, rows, (1, 3, 5, 7))
    geo = dict(blocks=blocks, cut=cut, d=d, units=units)
    at = lambda s: jnp.minimum(s, blocks - 1)
    columns = pl.BlockSpec((d, HEAD), lambda s: (0, at(s)))
    turned = pltpu.VMEM((2, pairs, rows, n), BF16)
    size = max(cut, units - cut)
    return launch(
        functools.partial(units_kernel, geo, reducer, ride),
        "sglu_and_gradients",
        reducer.last + 1,
        list(matrices) + [second, cot, second_t, cot_t] + list(pieces) + ride.inputs,
        [columns, columns, pl.BlockSpec((HEAD, d), lambda s: (at(s), 0)), once(second.shape)]
        + [anywhere()] * (3 + len(pieces) + len(ride.inputs)),
        [struct((n, d), F32), struct((n, d), F32), struct((3, rows, units), F32)] + ride.outs,
        [anywhere(), anywhere(), whole_block((3, rows, units))] + [anywhere()] * len(ride.outs),
        [
            pltpu.VMEM((n, d), F32),
            pltpu.VMEM((n, d), F32),
            pltpu.VMEM((n, d), BF16),
            turned,
            turned,
            pltpu.VMEM((d, size), BF16),
            pltpu.VMEM((d, size), BF16),
            pltpu.VMEM((size, d), BF16),
            pltpu.VMEM((d, 2 * HEAD), BF16),
            pltpu.VMEM((d, 2 * HEAD), BF16),
            pltpu.VMEM((2 * HEAD, d), BF16),
            pltpu.SemaphoreType.DMA((2, 3, 8)),
            pltpu.SemaphoreType.DMA((7,)),
        ]
        + reducer.scratch
        + ride.scratch,
        36 * n * d * units,
        partners=reducer.partners + ride.partners,
        ident=ident,
    )[:3]


def after_kernel(chunks, heads, info, slopes, term, part, cot, mid, sel, att, wo, qpre, rot, out_o, gmid_o, pair_o, gatt_o, et_o, e0_o, state):
    step = pl.program_id(0)
    c = chunks - 1 - step

    @pl.when(step == 0)
    def _():
        state[...] = jnp.zeros_like(state)

    middle = mid[...]
    out_o[...] = (middle + term[...]).astype(BF16)
    grad_middle = cot[...].astype(F32) + norm_back(middle, scale_of(middle), part[...])
    gmid_o[...] = grad_middle
    branch = grad_middle.astype(BF16)
    pair_o[0] = branch
    grad_mixed = nt(branch, wo[...])
    attended = att[...].astype(F32)
    scale = scale_of(attended)
    pair_o[1] = (grad_mixed * attended * scale).astype(BF16)
    alive = (row_index((CHUNK, 1)) + c * CHUNK < info[4 * chunks]).astype(F32)
    grad_att = norm_back(attended, scale, grad_mixed * sel[...].astype(F32)) * alive
    gatt_o[...] = grad_att.astype(BF16)
    cs, sn = rot[:, :HEAD], rot[:, HEAD:]
    keep = info[chunks + c].astype(F32)
    for h in range(heads):
        slope = slopes[h]
        query = featured(qpre[:, head_slice(h)].astype(F32), cs, sn)
        faded = (grad_att[:, head_slice(h)] * fade_from_start(slope, HEAD)).astype(BF16)
        old = state[h]
        et_o[0, h] = old.astype(BF16)
        state[h] = keep * (
            jnp.exp(jnp.full((1, 2 * HEAD), -slope * CHUNK, F32)) * old + nn(faded.T, query)
        )
    e0_o[...] = state[...].astype(BF16)


def run_after(info, slopes, term, part, cot, mid, sel, att, wo, qpre, rot, **ride):
    n, d = cot.shape
    heads, chunks = d // HEAD, n // CHUNK
    back = lambda s: chunks - 1 - s
    tile = pl.BlockSpec((CHUNK, d), lambda s: (back(s), 0))
    return launch(
        functools.partial(after_kernel, chunks, heads),
        "output_and_row_gradients",
        chunks,
        [info, slopes, term, part, cot, mid, sel, att, wo, qpre, rot],
        [smem(), smem()]
        + [tile] * 6
        + [whole_block(wo.shape), tile, pl.BlockSpec((CHUNK, 2 * HEAD), lambda s: (back(s), 0))],
        [
            struct((n, d)),
            struct((n, d), F32),
            struct((2, n, d)),
            struct((n, d)),
            struct((chunks, heads, HEAD, 2 * HEAD)),
            struct((heads, HEAD, 2 * HEAD)),
        ],
        [
            tile,
            tile,
            pl.BlockSpec((2, CHUNK, d), lambda s: (0, back(s), 0)),
            tile,
            pl.BlockSpec((1, heads, HEAD, 2 * HEAD), lambda s: (back(s), 0, 0, 0)),
            whole_block((heads, HEAD, 2 * HEAD)),
        ],
        [pltpu.VMEM((heads, HEAD, 2 * HEAD), F32)],
        3 * n * d * d,
        **ride,
    )


def weights_kernel(items, peers, *refs):
    item = lax.div(pl.program_id(0), peers)
    lefts, right, out = refs[:-2], refs[-2], refs[-1]
    for i, left in enumerate(lefts):

        @pl.when(functools.reduce(jnp.logical_or, [item == t for t, w in enumerate(items) if w == i]))
        def _(left=left):
            block = left[...]
            block = block.reshape(-1, block.shape[-1])
            out[...] = nn(block, right[...]).astype(BF16).reshape(out.shape)


def run_weights(lefts, items, rights, right_spec, peers, width):
    pairs, _, rows, n = lefts[0].shape
    shape = (peers, len(items), pairs, 2, rows, width)
    which = lambda s: (lax.div(s, peers), lax.rem(s, peers))
    (out,) = launch(
        functools.partial(weights_kernel, items, peers),
        "weight_gradients",
        peers * len(items),
        list(lefts) + [rights],
        [whole_block(left.shape) for left in lefts] + [right_spec(which)],
        [struct(shape)],
        [pl.BlockSpec((None, None) + shape[2:], lambda s: (which(s)[1], which(s)[0], 0, 0, 0, 0))],
        [],
        4 * n * pairs * rows * width * len(items) * peers,
    )
    return out


def head_back(slope, qpre, kpre, value, grad, state, ending, cs, sn):
    qp, kp = qpre.astype(F32), kpre.astype(F32)
    qs, ks = sigmoid(qp), sigmoid(kp)
    qa, ka = qp * qs, kp * ks
    query = jnp.concatenate([qa * cs, qa * sn], axis=-1).astype(BF16)
    key = jnp.concatenate([ka * cs, ka * sn], axis=-1).astype(BF16)
    state, ending = state.astype(BF16), ending.astype(BF16)
    table, turned = decay_table(slope, False), decay_table(slope, True)
    scores_t = (nt(key, query) * turned).astype(BF16)
    slope_s = (nt(grad, value) * table).astype(BF16)
    slope_t = (nt(value, grad) * turned).astype(BF16)
    start = fade_from_start(slope, HEAD)
    end = fade_to_end(slope, HEAD)
    grad_start = (grad.astype(F32) * start).astype(BF16)
    value_end = (value.astype(F32) * end).astype(BF16)
    dq = nn(slope_s, key) + nn(grad_start, state)
    dk = nn(slope_t, query) + nn(value_end, ending)
    dv = nn(scores_t, grad) + end * nt(key, ending)
    dq = dq[:, :HEAD] * cs + dq[:, HEAD:] * sn
    dk = dk[:, :HEAD] * cs + dk[:, HEAD:] * sn
    gq = (dq * (qs * (1.0 + qp * (1.0 - qs)))).astype(BF16)
    gk = (dk * (ks * (1.0 + kp * (1.0 - ks)))).astype(BF16)
    return gq, gk, dv.astype(BF16)


def attention_back_kernel(chunks, first_head, info, slopes, qpre, kpre, values, gatt, st, came, et, left, rot, grads_o):
    pair, c = lax.div(pl.program_id(0), chunks), lax.rem(pl.program_id(0), chunks)
    cs, sn = rot[:, :HEAD], rot[:, HEAD:]
    before = info[2 * chunks + c].astype(F32)
    after = info[3 * chunks + c].astype(F32)
    span = (CHUNK * c).astype(F32)
    rest = (CHUNK * (chunks - 1 - c)).astype(F32)
    for h in range(2):
        slope = slopes[first_head + 2 * pair + h]
        cols = head_slice(h)
        lane = jnp.zeros((1, 2 * HEAD), F32)
        state = st[0, h].astype(F32) + came[h].astype(F32) * (jnp.exp(lane - slope * span) * before)
        ending = et[0, h].astype(F32) + left[h].astype(F32) * (jnp.exp(lane - slope * rest) * after)
        three = head_back(
            slope, qpre[:, cols], kpre[:, cols], values[:, cols], gatt[:, cols], state, ending, cs, sn
        )
        for i in range(3):
            grads_o[i, :, cols] = three[i]


def run_attention_back(info, slopes, qpre, kpre, values, gatt, st, came, et, left, rot, first_head, heads, **ride):
    n, d = qpre.shape
    chunks = n // CHUNK
    skip = first_head // 2
    pair = lambda s: lax.div(s, chunks)
    chunk = lambda s: lax.rem(s, chunks)
    tile = pl.BlockSpec((CHUNK, 2 * HEAD), lambda s: (chunk(s), skip + pair(s)))
    states = pl.BlockSpec((1, 2, HEAD, 2 * HEAD), lambda s: (chunk(s), skip + pair(s), 0, 0))
    ends = pl.BlockSpec((2, HEAD, 2 * HEAD), lambda s: (skip + pair(s), 0, 0))
    return launch(
        functools.partial(attention_back_kernel, chunks, first_head),
        "attention_backward",
        chunks * heads // 2,
        [info, slopes, qpre, kpre, values, gatt, st, came, et, left, rot],
        [smem(), smem(), tile, tile, tile, tile, states, ends, states, ends, pl.BlockSpec((CHUNK, 2 * HEAD), lambda s: (chunk(s), 0))],
        [struct((3, n, heads * HEAD))],
        [pl.BlockSpec((3, CHUNK, 2 * HEAD), lambda s: (0, chunk(s), pair(s)))],
        [],
        18 * n * 256 * 256 * heads // 2,
        **ride,
    )


def projections_kernel(geo, outer, inner, info, slopes, *refs):
    chunks, blocks, d, n = geo["chunks"], geo["blocks"], geo["d"], geo["n"]
    refs = list(refs)
    take = lambda k: [refs.pop(0) for _ in range(k)]
    columns = [take(2) for _ in range(4)]
    states = [take(2) for _ in range(2)]
    (came, leaving, rot, branch_a, branch_b, sel_a, sel_b, sel, hid, gmid, mixt_h, normt_h) = take(12)
    weights_h = take(4)
    hidden_o, out, out2 = take(3)
    grads, block, mixt, normt, w4, left, sems, state_sems = take(8)
    outer.bind(take(len(outer.scratch)))
    inner.bind(refs)
    step = pl.program_id(0)
    core = lax.rem(lax.axis_index("dp"), 2)
    me = lax.axis_index("mp")
    loads = [
        pltpu.make_async_copy(mixt_h.at[:, 1 - core], mixt.at[0], sems.at[0]),
        pltpu.make_async_copy(mixt_h.at[:, core], mixt.at[1], sems.at[1]),
        pltpu.make_async_copy(normt_h.at[:, 1 - core], normt.at[0], sems.at[2]),
        pltpu.make_async_copy(normt_h.at[:, core], normt.at[1], sems.at[3]),
    ]
    matrices = [pltpu.make_async_copy(w, w4.at[i], sems.at[4 + i]) for i, w in enumerate(weights_h)]
    exchange = remote(leaving, left, state_sems.at[0], state_sems.at[1], "mp", 1)

    @pl.when(step == 0)
    def _():
        exchange.start()
        for copy in loads:
            copy.start()
        for copy in matrices:
            copy.start()
        for copy in loads:
            copy.wait()

    @pl.when(step < blocks)
    def _():
        slot = lax.rem(step, 2)
        gb = jnp.concatenate([branch_a[...], branch_b[...]], axis=1)
        gs = jnp.concatenate([sel_a[...], sel_b[...]], axis=1)
        for k, buffer in enumerate((outer.given, outer.kept)):
            buffer[slot, 0] = nn(rows_of(mixt, k), gb).astype(BF16)
            buffer[slot, 1] = nn(rows_of(normt, k), gs).astype(BF16)
            if k == 0:
                outer.begin(step)

    @pl.when(step == blocks - 1)
    def _():
        exchange.wait()

    @pl.when(jnp.logical_and(step >= blocks, step < 2 * blocks))
    def _():
        j = step - blocks

        def one(c, carry):
            here = pl.ds(pl.multiple_of(c * CHUNK, CHUNK), CHUNK)
            cs, sn = rot[here, :HEAD], rot[here, HEAD:]
            before = info[2 * chunks + c].astype(F32)
            after = info[3 * chunks + c].astype(F32)
            span = (CHUNK * c).astype(F32)
            rest = (CHUNK * (chunks - 1 - c)).astype(F32)
            for side in range(2):
                h = (me if side == 0 else 1 - me) * blocks + j
                slope = slopes[h]
                qpre, kpre, values, gatt = [pair[side][here, :] for pair in columns]
                st, et = [pair[side][c, 0].astype(F32) for pair in states]
                lane = jnp.zeros((1, 2 * HEAD), F32)
                state = st + came[h].astype(F32) * (jnp.exp(lane - slope * span) * before)
                ending = et + left[h].astype(F32) * (jnp.exp(lane - slope * rest) * after)
                three = head_back(slope, qpre, kpre, values, gatt, state, ending, cs, sn)
                cols = pl.ds(pl.multiple_of(h * HEAD, HEAD), HEAD)
                for i in range(3):
                    block[i, here, head_slice(side)] = three[i]
                    grads[i, here, cols] = three[i]
            return carry

        lax.fori_loop(0, chunks, one, 0)
        slot = lax.rem(j, 2)
        for k, buffer in enumerate((inner.given, inner.kept)):
            for i in range(3):
                buffer[slot, i] = nn(rows_of(normt, k), block[i]).astype(BF16)
            if k == 0:
                inner.begin(j)

    @pl.when(step == 2 * blocks)
    def _():
        for copy in matrices:
            copy.wait()

    @pl.when(jnp.logical_and(step >= 2 * blocks, step < 2 * blocks + chunks))
    def _():
        here = pl.ds(pl.multiple_of((step - 2 * blocks) * CHUNK, CHUNK), CHUNK)
        total = nt(sel[...], w4[3])
        for i in range(3):
            total = total + nt(grads[i, here, :], w4[i])
        x = hid[...].astype(F32)
        hidden_o[...] = (gmid[...] + norm_back(x, scale_of(x), total)).astype(BF16)

    outer.run(step, out)
    inner.run(step, out2)


def run_projections(info, slopes, qpre, kpre, values, gatt, st, et, came, leaving, rot, pair, hidden, gmid, mixed_t, normed_t, weights, depth, ident):
    n, d = qpre.shape
    heads, chunks = d // HEAD, n // CHUNK
    blocks = heads // 2
    pairs, _, rows, _ = mixed_t.shape
    outer = Reducer(0, blocks, 2, depth, rows, (1, 3, 5, 7))
    inner = Reducer(blocks, blocks, 3, depth, rows, (1, 2, 4, 5))
    steps = max(outer.last, inner.last, 2 * blocks + chunks - 1) + 1
    geo = dict(chunks=chunks, blocks=blocks, d=d, n=n)
    early = lambda s: jnp.minimum(s, blocks - 1)
    mid = lambda s: jnp.clip(s - blocks, 0, blocks - 1)
    late = lambda s: jnp.clip(s - 2 * blocks, 0, chunks - 1)
    side = lambda k: blocks * (lax.axis_index("mp") if k == 0 else 1 - lax.axis_index("mp"))
    column = lambda k: pl.BlockSpec((n, HEAD), lambda s: (0, side(k) + mid(s)))
    state = lambda k: pl.BlockSpec((chunks, 1, HEAD, 2 * HEAD), lambda s: (0, side(k) + mid(s), 0, 0))
    pair_column = lambda i, k: pl.BlockSpec((None, n, HEAD), lambda s: (i, 0, side(k) + early(s)))
    tile = pl.BlockSpec((CHUNK, d), lambda s: (late(s), 0))
    turned = pltpu.VMEM((2, pairs, rows, n), BF16)
    return launch(
        functools.partial(projections_kernel, geo, outer, inner),
        "attention_backward_and_gradients",
        steps,
        [info, slopes]
        + [a for a in (qpre, kpre, values, gatt, st, et) for _ in range(2)]
        + [came, leaving, rot, pair, pair, pair, pair, pair, hidden, gmid, mixed_t, normed_t]
        + list(weights),
        [smem(), smem()]
        + [column(k) for _ in range(4) for k in range(2)]
        + [state(k) for _ in range(2) for k in range(2)]
        + [once(came.shape), anywhere(), once(rot.shape)]
        + [pair_column(i, k) for i in range(2) for k in range(2)]
        + [pl.BlockSpec((None, CHUNK, d), lambda s: (1, late(s), 0)), tile, tile]
        + [anywhere()] * 6,
        [struct((n, d)), struct((2, rows, d // 2), F32), struct((3, rows, d // 2), F32)],
        [tile, whole_block((2, rows, d // 2)), whole_block((3, rows, d // 2))],
        [
            pltpu.VMEM((3, n, d), BF16),
            pltpu.VMEM((3, n, 2 * HEAD), BF16),
            turned,
            turned,
            pltpu.VMEM((4, d, d), BF16),
            pltpu.VMEM(leaving.shape, BF16),
            pltpu.SemaphoreType.DMA((8,)),
            pltpu.SemaphoreType.DMA((2,)),
        ]
        + outer.scratch
        + inner.scratch,
        30 * n * d * d,
        partners=outer.partners,
        ident=ident,
    )


def input_kernel(wq, wk, wv, ws, grads, pair, hid, gmid, out):
    total = nt(grads[0], wq[...]) + nt(grads[1], wk[...]) + nt(grads[2], wv[...]) + nt(pair[...], ws[...])
    x = hid[...].astype(F32)
    out[...] = (gmid[...] + norm_back(x, scale_of(x), total)).astype(BF16)


def run_input(weights, grads, pair, hidden, gmid, **ride):
    n, d = hidden.shape
    tile = pl.BlockSpec((CHUNK, d), lambda c: (c, 0))
    return launch(
        input_kernel,
        "input_gradient",
        n // CHUNK,
        list(weights) + [grads, pair, hidden, gmid],
        [whole_block(w.shape) for w in weights]
        + [
            pl.BlockSpec((3, CHUNK, d), lambda c: (0, c, 0)),
            pl.BlockSpec((None, CHUNK, d), lambda c: (1, c, 0)),
            tile,
            tile,
        ],
        [struct((n, d))],
        [tile],
        [],
        8 * n * d * d,
        **ride,
    )


def reduced(lefts, items, rights, spec, peers, width):
    full = run_weights(lefts, items, rights, spec, peers, width)
    full = full.reshape(peers, len(items), -1, full.shape[4], width)
    mine = lax.psum_scatter(full, "dp", scatter_dimension=2, tiled=False)
    return lax.psum_scatter(mine, "mp", scatter_dimension=0, tiled=False).astype(F32)


def per_device(
    hidden_in,
    query_weight,
    key_weight,
    value_weight,
    select_weight,
    out_weight,
    first_weight,
    second_weight,
    down_weight,
    decay_slope,
    doc_lengths,
    cotangent,
):
    count, d = hidden_in.shape
    heads, chunks = d // HEAD, count // CHUNK
    peers, parts = lax.axis_size("mp"), lax.axis_size("dp")
    me = lax.axis_index("mp")
    depth = parts // 4
    group = count * peers
    units = first_weight.shape[1]
    lengths = doc_lengths[0].astype(jnp.int32)
    info = chunk_info(lengths, me, peers, count)
    rot = turning(info, chunks, group // 2)
    slopes = decay_slope
    matrices = (first_weight, second_weight, down_weight)
    riding = peers == 2

    if riding:
        cut = -(-units // 256) * 128
        ranges = [(0, cut), (cut, units - cut)]
    else:
        ranges = [(0, units)]

    def like(arrays, count=None):
        return [struct(a.shape if count is None else (count,) + a.shape) for a in arrays]

    def over_mp(g, steps):
        low, size = ranges[g]

        def source(w):
            def src(i, o):
                eighth = lax.rem(lax.axis_index("dp"), 8)
                if w < 2:
                    rows = d // 8
                    return i[w].at[pl.ds(pl.multiple_of(eighth * rows, 16), rows), pl.ds(low, size)]
                rows = size // 8
                return i[w].at[pl.ds(pl.multiple_of(low + eighth * rows, 16), rows), :]

            return src

        outs = [struct((d // 8, size)), struct((d // 8, size)), struct((size // 8, d))]
        copies = [(source(w), lambda i, o, w=w: o[w], "mp", 1) for w in range(3)]
        return Carry(matrices, outs, [(0, steps, copies)])

    def near(w):
        return [
            (lambda i, o: i[w], lambda i, o: o[w].at[0], "dp", 2),
            (lambda i, o: i[w], lambda i, o: o[w].at[1], "dp", 4),
            (lambda i, o: i[w], lambda i, o: o[w].at[2], "dp", 1),
        ]

    def far(w, src, dst, rows):
        top = -(-rows // 32) * 16
        upper, lower = pl.ds(0, top), pl.ds(top, rows - top)
        return [
            (lambda i, o: src(i, o).at[1, upper, :], lambda i, o: dst(i, o).at[0, upper, :], "dp", 2),
            (lambda i, o: src(i, o).at[0, lower, :], lambda i, o: dst(i, o).at[0, lower, :], "dp", 4),
            (lambda i, o: src(i, o).at[0], lambda i, o: dst(i, o).at[1], "dp", 1),
            (lambda i, o: src(i, o).at[1], lambda i, o: dst(i, o).at[2], "dp", 1),
        ]

    ride = dict(guests=[over_mp(0, chunks - 1)], ident=1) if riding else {}
    normed, normed_t, kpre, values, st, final, *had = run_keys(
        info, slopes, hidden_in, key_weight, value_weight, rot, parts, **ride
    )
    whole_keep = info[2 * chunks + chunks - 1].astype(F32)
    decay = jnp.exp(-slopes * count)
    ride = {}
    if riding:
        state_copy = [(lambda i, o: i[0], lambda i, o: o[0], "mp", 1)]
        near_copies = [c for w in range(3) for c in near(w)]
        ride = dict(
            guests=[
                Carry([final], like([final]), [(0, chunks - 1, state_copy)]),
                Carry(had, like(had, 3), [(0, chunks - 1, near_copies)]),
            ],
            ident=2,
        )
    qpre, sel, att, *more = run_inside(
        info, slopes, normed, query_weight, select_weight, kpre, values, st, rot, **ride
    )
    if riding:
        came, close = more[0], more[1:]
    else:
        finals = lax.all_gather(final, "mp")
        keeps = lax.all_gather(whole_keep.reshape(1), "mp")[:, 0]

        def ahead(k, total):
            new = finals[k].astype(F32) + (keeps[k] * decay)[:, None, None] * total
            return jnp.where(k < me, new, total)

        came = lax.fori_loop(0, peers, ahead, jnp.zeros(final.shape, F32)).astype(BF16)
    ride = {}
    if riding:
        first_phase = []
        for w in range(3):
            src, dst = (lambda i, o, w=w: i[w]), (lambda i, o, w=w: o[w])
            first_phase += far(w, src, dst, close[w].shape[1])
        second_phase = [
            (lambda i, o, w=w: o[w].at[0], lambda i, o, w=w: o[3 + w], "dp", 1) for w in range(3)
        ]
        ride = dict(
            guests=[
                Carry(
                    close,
                    like(close) + like(had),
                    [(0, chunks // 2, first_phase), (chunks // 2 + 1, chunks - 1, second_phase)],
                ),
                over_mp(1, chunks - 1),
            ],
            ident=3,
        )
    attended, mixed_t, middle, second, second_t, cot_t, *more = run_mix(
        info, slopes, att, qpre, came, sel, out_weight, hidden_in, cotangent, rot, parts, **ride
    )

    if riding:
        wide, corner, had_b = more[:3], more[3:6], more[6:9]
        one = [c for w in range(3) for c in near(w)]
        two = []
        for w in range(3):
            src, dst = (lambda i, o, w=w: o[w]), (lambda i, o, w=w: o[3 + w])
            two += far(w, src, dst, had_b[w].shape[0])
        three = [
            (lambda i, o, w=w: o[3 + w].at[0], lambda i, o, w=w: o[6 + w], "dp", 1) for w in range(3)
        ]
        turn = ranges[0][1] // HEAD
        ride = Carry(
            had_b,
            like(had_b, 3) + like(had_b, 3) + like(had_b),
            [(0, 1, one), (2, 3, two), (4, 4, three)],
        )
        pieces = list(had) + list(close) + list(wide) + list(corner)
        term, part, sglu = run_units(
            matrices, second, cotangent, second_t, cot_t, pieces, ride, ranges[0][1], depth, ident=4
        )
    else:
        sources = [lax.all_gather(w, "mp") for w in matrices]
        grads, term, part = run_sglu(second, cotangent, *sources)
        units_spec = lambda at: pl.BlockSpec((None, None, count, units), lambda s: at(s) + (0, 0))
        sglu = reduced([second_t, cot_t], (0, 0, 1), grads, units_spec, peers, units)
    output, grad_middle, pair, grad_att, et, leaving = run_after(
        info, slopes, term, part, cotangent, middle, sel, attended, out_weight, qpre, rot
    )
    inputs_weights = [query_weight, key_weight, value_weight, select_weight]
    if riding:
        grad_hidden, out_sel, inputs = run_projections(
            info, slopes, qpre, kpre, values, grad_att, st, et, came, leaving, rot, pair,
            hidden_in, grad_middle, mixed_t, normed_t, inputs_weights, depth, ident=5,
        )
    else:
        leavings = lax.all_gather(leaving, "mp")

        def behind(step, total):
            k = peers - 1 - step
            new = leavings[k].astype(F32) + (keeps[k] * decay)[:, None, None] * total
            return jnp.where(k > me, new, total)

        left = lax.fori_loop(0, peers, behind, jnp.zeros(leaving.shape, F32)).astype(BF16)
        share = d // peers
        wide_spec = lambda at: pl.BlockSpec((None, count, share), lambda s: (at(s)[0], 0, at(s)[1]))
        out_sel = reduced([mixed_t, normed_t], (0, 1), pair, wide_spec, peers, share)
        (qkv,) = run_attention_back(
            info, slopes, qpre, kpre, values, grad_att, st, came, et, left, rot, 0, heads
        )
        inputs = reduced([normed_t], (0, 0, 0), qkv, wide_spec, peers, share)
        (grad_hidden,) = run_input(inputs_weights, qkv, pair, hidden_in, grad_middle)
    return (
        output,
        grad_hidden,
        inputs[0],
        inputs[1],
        inputs[2],
        out_sel[1],
        out_sel[0],
        sglu[0],
        sglu[1],
        jnp.transpose(sglu[2]),
    )


def solution(mesh):
    rows = P(("dp", "mp"), None)
    in_specs = (
        rows,
        P(),
        P(),
        P(),
        P(),
        P(),
        P(None, "mp"),
        P(None, "mp"),
        P("mp", None),
        P(),
        P("dp", None),
        rows,
    )
    out_specs = (rows, rows) + (P("dp", "mp"),) * 7 + (P("mp", "dp"),)
    return jax.shard_map(
        per_device, mesh=mesh, in_specs=in_specs, out_specs=out_specs, check_vma=False
    )
```

```python
import functools

import jax
import jax.numpy as jnp
import numpy as np
from jax import lax
from jax.experimental import pallas as pl
from jax.experimental.pallas import tpu as pltpu
from jax.sharding import PartitionSpec as P

HEAD = 128
CHUNK = 256
EPSILON = 1e-06
BF16 = jnp.bfloat16
F32 = jnp.float32
VMEM_LIMIT = 61 * 1024 * 1024


def nn(left, right):
    return jnp.dot(left, right, preferred_element_type=F32)


def nt(left, right):
    return lax.dot_general(left, right, (((1,), (1,)), ((), ())), preferred_element_type=F32)


def scale_of(values):
    return lax.rsqrt(jnp.mean(values * values, axis=-1, keepdims=True) + EPSILON)


def norm_back(values, scale, upstream):
    return scale * upstream - values * (scale * scale * scale) * jnp.mean(
        values * upstream, axis=-1, keepdims=True
    )


def sigmoid(v):
    return 1.0 / (1.0 + jnp.exp(-v))


def featured(pre, cos, sin):
    act = pre * sigmoid(pre)
    return jnp.concatenate([act * cos, act * sin], axis=-1).astype(BF16)


def head_slice(h):
    return slice(h * HEAD, (h + 1) * HEAD)


def row_index(shape):
    return lax.broadcasted_iota(jnp.int32, shape, 0)


def fade_from_start(slope, width):
    return jnp.exp(-slope * (row_index((CHUNK, width)) + 1).astype(F32))


def fade_to_end(slope, width):
    return jnp.exp(-slope * (CHUNK - 1 - row_index((CHUNK, width))).astype(F32))


def decay_table(slope, transposed):
    rows = lax.broadcasted_iota(jnp.int32, (CHUNK, CHUNK), 0)
    cols = lax.broadcasted_iota(jnp.int32, (CHUNK, CHUNK), 1)
    gap = cols - rows if transposed else rows - cols
    return jnp.where(gap >= 0, jnp.exp(-slope * jnp.maximum(gap, 0).astype(F32)), 0.0)


def plus(*arrays):
    total = arrays[0].astype(F32)
    for a in arrays[1:]:
        total = total + a.astype(F32)
    return total


def smem():
    return pl.BlockSpec(memory_space=pltpu.SMEM)


def anywhere():
    return pl.BlockSpec(memory_space=pl.ANY)


def once(shape):
    zeros = (0,) * len(shape)
    return pl.BlockSpec(shape, lambda *_: zeros, pipeline_mode=pl.Buffered(1))


def whole_block(shape):
    zeros = (0,) * len(shape)
    return pl.BlockSpec(shape, lambda *_: zeros)


def cost(flops, arrays):
    moved = sum(int(np.prod(a.shape)) * jnp.dtype(a.dtype).itemsize for a in arrays)
    return pl.CostEstimate(flops=int(flops), bytes_accessed=moved, transcendentals=0)


def struct(shape, dtype=BF16):
    return jax.ShapeDtypeStruct(tuple(shape), dtype)


def flipped(index, mask):
    bit = 1
    while bit <= mask:
        if mask & bit:
            index = index + bit * (1 - 2 * lax.rem(lax.div(index, bit), 2))
        bit *= 2
    return index


def remote(src, dst, send, recv, axis, mask):
    return pltpu.make_async_remote_copy(
        src_ref=src,
        dst_ref=dst,
        send_sem=send,
        recv_sem=recv,
        device_id={axis: flipped(lax.axis_index(axis), mask)},
        device_id_type=pl.DeviceIdType.MESH,
    )


def greet(partners):
    barrier = pltpu.get_barrier_semaphore()
    for axis, mask in partners:
        pl.semaphore_signal(
            barrier,
            inc=1,
            device_id={axis: flipped(lax.axis_index(axis), mask)},
            device_id_type=pl.DeviceIdType.MESH,
        )
    pl.semaphore_wait(barrier, len(partners))


class Carry:
    def __init__(self, inputs, outs, phases):
        self.inputs, self.outs, self.phases = list(inputs), list(outs), phases
        count = sum(len(p[2]) for p in phases)
        self.scratch = [pltpu.SemaphoreType.DMA((count,)), pltpu.SemaphoreType.DMA((count,))]
        self.partners = [(c[2], c[3]) for p in phases for c in p[2]]

    def copies(self, which, ins, outs, scratch):
        at = sum(len(p[2]) for p in self.phases[:which])
        send, recv = scratch
        for k, (src, dst, axis, mask) in enumerate(self.phases[which][2]):
            yield remote(src(ins, outs), dst(ins, outs), send.at[at + k], recv.at[at + k], axis, mask)

    def before(self, step, ins, outs, scratch):
        for p, phase in enumerate(self.phases):

            @pl.when(step == phase[0])
            def _(p=p):
                for copy in self.copies(p, ins, outs, scratch):
                    copy.start()

    def after(self, step, ins, outs, scratch):
        for p, phase in enumerate(self.phases):

            @pl.when(step == phase[1])
            def _(p=p):
                for copy in self.copies(p, ins, outs, scratch):
                    copy.wait()


class Reducer:
    KINDS = 8

    def __init__(self, start, blocks, items, depth, rows, delays):
        self.start, self.blocks, self.items = start, blocks, items
        self.depth, self.rows, self.delays = depth, rows, delays
        half, n, wide = depth // 2, 2 * depth * rows, 2 * HEAD
        buf = lambda *shape: pltpu.VMEM(shape, BF16)
        pair = (half, items, rows, wide)
        flat = (2, half, items, rows, HEAD)
        one = (half, items, rows, HEAD)
        self.scratch = [
            buf(2, items, n, wide),
            buf(2, items, n, wide),
            buf(4, items, n, wide),
            buf(2, *pair),
            buf(2, *pair),
            buf(4, *pair),
            buf(2, *flat),
            buf(2, *flat),
            buf(4, *flat),
            buf(2, *one),
            buf(2, *one),
            buf(4, *one),
            buf(2, *one),
            buf(2, *one),
            buf(4, *one),
            buf(2, depth, items, rows, HEAD),
            buf(4, depth - 1, items, rows, HEAD),
            pltpu.SemaphoreType.DMA((self.KINDS, blocks)),
            pltpu.SemaphoreType.DMA((self.KINDS, blocks)),
        ]
        self.partners = [("dp", 1), ("dp", 2), ("mp", 1)] + [("dp", 4 * k) for k in range(1, depth)]
        self.last = start + blocks - 1 + delays[3]

    def bind(self, scratch):
        self.refs = scratch
        self.given, self.kept = scratch[:2]
        self.x = lax.rem(lax.div(lax.axis_index("dp"), 2), 2)
        self.z = lax.div(lax.axis_index("dp"), 4)

    def copies(self, stage, j):
        (given, kept, got, ps, pk, pr, qs, qk, qr, ps2, pk2, pr2, qs2, qk2, qr2, line, zr, send, recv) = self.refs
        slot, four = lax.rem(j, 2), lax.rem(j, 4)
        if stage == 0:
            plan = [(0, given.at[slot], got.at[four], "dp", 1)]
        elif stage == 1:
            plan = [(1, ps.at[slot], pr.at[four], "dp", 2), (2, qs.at[slot], qr.at[four], "mp", 1)]
        elif stage == 2:
            plan = [(3, ps2.at[slot], pr2.at[four], "mp", 1), (4, qs2.at[slot], qr2.at[four], "dp", 2)]
        else:
            plan = [
                (4 + k, line.at[slot, flipped(self.z, k)], zr.at[four, k - 1], "dp", 4 * k)
                for k in range(1, self.depth)
            ]
        return [remote(src, dst, send.at[i, j], recv.at[i, j], axis, mask) for i, src, dst, axis, mask in plan]

    def begin(self, j):
        for copy in self.copies(0, j):
            copy.start()

    def run(self, step, out):
        for stage in (4, 3, 2, 1):
            j = step - self.start - self.delays[stage - 1]

            @pl.when(jnp.logical_and(j >= 0, j < self.blocks))
            def _(stage=stage, j=j):
                for copy in self.copies(stage - 1, j):
                    copy.wait()
                self.add(stage, j, out)
                if stage < 4:
                    for copy in self.copies(stage, j):
                        copy.start()

    def add(self, stage, j, out):
        (given, kept, got, ps, pk, pr, qs, qk, qr, ps2, pk2, pr2, qs2, qk2, qr2, line, zr, send, recv) = self.refs
        slot, four, x, rows = lax.rem(j, 2), lax.rem(j, 4), self.x, self.rows
        half = self.depth // 2
        if stage == 1:

            def total(t, z, at):
                here = pl.ds(pl.multiple_of((2 * z + at) * rows, rows), rows)
                return plus(kept[slot, t, here, :], got[four, t, here, :]).astype(BF16)

            for z in range(half):
                for t in range(self.items):
                    ps[slot, z, t] = total(t, z, 1 - x)
                    pk[slot, z, t] = total(t, z, x)
                    for at in range(2):
                        block = total(t, half + z, at)
                        qk[slot, at, z, t] = block[:, :HEAD]
                        qs[slot, at, z, t] = block[:, HEAD:]
        elif stage == 2:
            for z in range(half):
                block = plus(pk[slot, z], pr[four, z]).astype(BF16)
                pk2[slot, z] = block[:, :, :HEAD]
                ps2[slot, z] = block[:, :, HEAD:]
                qs2[slot, z] = plus(qk[slot, 1 - x, z], qr[four, 1 - x, z]).astype(BF16)
                qk2[slot, z] = plus(qk[slot, x, z], qr[four, x, z]).astype(BF16)
        elif stage == 3:
            for z in range(half):
                line[slot, z] = plus(pk2[slot, z], pr2[four, z]).astype(BF16)
                line[slot, half + z] = plus(qk2[slot, z], qr2[four, z]).astype(BF16)
        else:
            total = plus(line[slot, self.z], *[zr[four, k] for k in range(self.depth - 1)])
            out[:, :, pl.ds(pl.multiple_of(j * HEAD, HEAD), HEAD)] = total


def launch(kernel, name, steps, inputs, specs, outs, out_specs, scratch, flops, guests=(), ident=None, partners=()):
    guests = list(guests)
    partners = list(partners) + [p for g in guests for p in g.partners]
    partners = sorted(set(partners))
    all_inputs = list(inputs) + [a for g in guests for a in g.inputs]
    all_specs = list(specs) + [anywhere() for g in guests for _ in g.inputs]
    all_outs = list(outs) + [a for g in guests for a in g.outs]
    all_out_specs = list(out_specs) + [anywhere() for g in guests for _ in g.outs]
    all_scratch = list(scratch) + [a for g in guests for a in g.scratch]

    def body(*refs):
        refs = list(refs)
        take = lambda k: [refs.pop(0) for _ in range(k)]
        own = take(len(inputs))
        ins = [take(len(g.inputs)) for g in guests]
        own += take(len(outs))
        gone = [take(len(g.outs)) for g in guests]
        own += take(len(scratch))
        held = [take(len(g.scratch)) for g in guests]
        step = pl.program_id(0)
        if partners:

            @pl.when(step == 0)
            def _():
                greet(partners)

        for g, i, o, s in zip(guests, ins, gone, held):
            g.before(step, i, o, s)
        kernel(*own)
        for g, i, o, s in zip(guests, ins, gone, held):
            g.after(step, i, o, s)

    extra = dict(collective_id=ident, has_side_effects=True) if partners else {}
    return pl.pallas_call(
        body,
        grid=(steps,),
        in_specs=all_specs,
        out_specs=all_out_specs,
        out_shape=all_outs,
        scratch_shapes=all_scratch,
        compiler_params=pltpu.CompilerParams(
            vmem_limit_bytes=VMEM_LIMIT, dimension_semantics=("arbitrary",), **extra
        ),
        cost_estimate=cost(flops, all_inputs + all_outs),
        name=name,
    )(*all_inputs)


def tables(longest):
    freq = 10000.0 ** (-np.arange(HEAD, dtype=np.float64) / HEAD)

    def both(places):
        phase = places[:, None] * freq[None, :]
        return jnp.asarray(np.concatenate([np.cos(phase), np.sin(phase)], axis=1), F32)

    return both(np.arange(CHUNK)), both(np.arange(0, longest, CHUNK))


class Layout:
    def __init__(self, lengths, peers, count):
        self.lengths, self.peers, self.count = lengths, peers, count
        self.me = lax.axis_index("mp")
        self.offset = self.me * count

    def begin(self, first):
        begin = start = jnp.int32(0)
        for i in range(self.lengths.shape[1]):
            begin = jnp.where(first >= start, start, begin)
            start = start + self.lengths[0, i]
        return begin

    def first(self, c):
        return self.offset + c * CHUNK

    def keep(self, c):
        return jnp.where(self.begin(self.first(c)) < self.first(c), 1.0, 0.0)

    def before(self, c):
        return jnp.where(self.begin(self.first(c)) < self.offset, 1.0, 0.0)

    def after(self, c):
        last = self.begin(self.offset + self.count - CHUNK)
        return jnp.where(last <= self.first(c), 1.0, 0.0) * jnp.where(self.me < self.peers - 1, 1.0, 0.0)

    def alive(self, c, width):
        end = jnp.int32(0)
        for i in range(self.lengths.shape[1]):
            end = end + self.lengths[0, i]
        return (row_index((CHUNK, width)) + self.first(c) < end).astype(F32)

    def angles(self, c, fine, coarse):
        base = self.first(c) - self.begin(self.first(c))
        start = jnp.zeros((1, 2 * HEAD), F32)
        for k in range(coarse.shape[0]):
            start = start + coarse[k : k + 1, :] * jnp.where(base == k * CHUNK, 1.0, 0.0)
        cb, sb = start[:, :HEAD], start[:, HEAD:]
        cf, sf = fine[:, :HEAD], fine[:, HEAD:]
        return cf * cb - sf * sb, sf * cb + cf * sb


def normed_of(hid):
    x = hid[...].astype(F32)
    return (x * scale_of(x)).astype(BF16)


def states_chunk(heads, slopes, keep, kpre, values, cs, sn, state, put):
    for h in range(heads):
        slope = slopes[h]
        key = featured(kpre[:, head_slice(h)], cs, sn)
        faded = (values[:, head_slice(h)] * fade_to_end(slope, HEAD)).astype(BF16)
        old = state[h] * keep
        put(h, old.astype(BF16))
        state[h] = jnp.exp(jnp.full((1, 2 * HEAD), -slope * CHUNK, F32)) * old + nn(faded.T, key)


def inside_chunk(heads, slopes, qpre, kpre, values, st, cs, sn, put):
    for h in range(heads):
        slope = slopes[h]
        query = featured(qpre[:, head_slice(h)], cs, sn)
        key = featured(kpre(h).astype(F32), cs, sn)
        weights = (nt(query, key) * decay_table(slope, False)).astype(BF16)
        put(h, nn(weights, values(h)) + fade_from_start(slope, HEAD) * nt(query, st(h)))


def carried_chunk(heads, slopes, layout, c, att, qpre, came, cs, sn, total):
    reached = layout.before(c)
    lag = (c * CHUNK).astype(F32)
    alive = layout.alive(c, HEAD)
    for h in range(heads):
        query = featured(qpre(h).astype(F32), cs, sn)
        fade = jnp.exp(-slopes[h] * (row_index((CHUNK, HEAD)).astype(F32) + (lag + 1.0))) * reached
        total[:, head_slice(h)] = (att(h) + fade * nt(query, came[h])) * alive


def mix_chunk(total, sel, wo, hid, att_o, mixt_o, mid_o, sec_o, sect_o):
    attended = total[...]
    att_o[...] = attended.astype(BF16)
    mixed = (attended * scale_of(attended) * sel.astype(F32)).astype(BF16)
    mixt_o[...] = mixed.T.reshape(mixt_o.shape)
    middle = hid[...].astype(F32) + nn(mixed, wo)
    mid_o[...] = middle.astype(BF16)
    second = (middle * scale_of(middle)).astype(BF16)
    sec_o[...] = second
    sect_o[...] = second.T.reshape(sect_o.shape)


def state_shape(d):
    return (d // HEAD, HEAD, 2 * HEAD)


def keys_kernel(peers, count, lengths, slopes, hid, wk, wv, fine, coarse, normed_o, turned_o, kpre_o, val_o, st_o, fin_o, state):
    c = pl.program_id(0)
    layout = Layout(lengths, peers, count)

    @pl.when(c == 0)
    def _():
        state[...] = jnp.zeros_like(state)

    normed = normed_of(hid)
    normed_o[...] = normed
    turned_o[...] = normed.T.reshape(turned_o.shape)
    kpre = nn(normed, wk[...])
    kpre_o[...] = kpre.astype(BF16)
    values = nn(normed, wv[...])
    val_o[...] = values.astype(BF16)
    cs, sn = layout.angles(c, fine, coarse)

    def put(h, value):
        st_o[0, h] = value

    states_chunk(state.shape[0], slopes, layout.keep(c), kpre, values, cs, sn, state, put)
    fin_o[...] = state[...].astype(BF16)


def run_keys(peers, lengths, slopes, hidden, wk, wv, angles, parts):
    n, d = hidden.shape
    heads, chunks = d // HEAD, n // CHUNK
    turned = (parts // 2, 2, d // parts, n)
    tile = pl.BlockSpec((CHUNK, d), lambda c: (c, 0))
    outs = [struct((n, d)), struct(turned), struct((n, d)), struct((n, d)), struct((chunks,) + state_shape(d)), struct(state_shape(d))]
    return launch(
        functools.partial(keys_kernel, peers, n),
        "keys_values_states",
        chunks,
        [lengths, slopes, hidden, wk, wv, *angles],
        [smem(), smem(), tile, whole_block(wk.shape), whole_block(wv.shape)] + [whole_block(a.shape) for a in angles],
        outs,
        [
            tile,
            pl.BlockSpec(turned[:3] + (CHUNK,), lambda c: (0, 0, 0, c)),
            tile,
            tile,
            pl.BlockSpec((1,) + state_shape(d), lambda c: (c, 0, 0, 0)),
            whole_block(state_shape(d)),
        ],
        [pltpu.VMEM(state_shape(d), F32)],
        4 * n * d * d,
    )


def inside_kernel(peers, count, lengths, slopes, normed, wq, ws, kpre, values, st, fine, coarse, qpre_o, sel_o, att_o):
    c = pl.program_id(0)
    layout = Layout(lengths, peers, count)
    x = normed[...]
    qpre = nn(x, wq[...])
    qpre_o[...] = qpre.astype(BF16)
    sel_o[...] = nn(x, ws[...]).astype(BF16)
    cs, sn = layout.angles(c, fine, coarse)

    def put(h, value):
        att_o[:, head_slice(h)] = value

    inside_chunk(
        st.shape[1],
        slopes,
        qpre,
        lambda h: kpre[:, head_slice(h)],
        lambda h: values[:, head_slice(h)],
        lambda h: st[0, h],
        cs,
        sn,
        put,
    )


def run_inside(peers, lengths, slopes, normed, wq, ws, kpre, values, st, angles):
    n, d = normed.shape
    chunks = n // CHUNK
    tile = pl.BlockSpec((CHUNK, d), lambda c: (c, 0))
    return launch(
        functools.partial(inside_kernel, peers, n),
        "queries_attention",
        chunks,
        [lengths, slopes, normed, wq, ws, kpre, values, st, *angles],
        [smem(), smem(), tile, whole_block(wq.shape), whole_block(ws.shape), tile, tile]
        + [pl.BlockSpec((1,) + state_shape(d), lambda c: (c, 0, 0, 0))]
        + [whole_block(a.shape) for a in angles],
        [struct((n, d)), struct((n, d)), struct((n, d), F32)],
        [tile, tile, tile],
        [],
        6 * n * d * d,
    )


def mix_kernel(peers, count, lengths, slopes, att, qpre, came, sel, wo, hid, cot, fine, coarse, att_o, mixt_o, mid_o, sec_o, sect_o, cott_o, total):
    c = pl.program_id(0)
    layout = Layout(lengths, peers, count)
    cs, sn = layout.angles(c, fine, coarse)
    carried_chunk(
        came.shape[0],
        slopes,
        layout,
        c,
        lambda h: att[:, head_slice(h)],
        lambda h: qpre[:, head_slice(h)],
        came,
        cs,
        sn,
        total,
    )
    mix_chunk(total, sel[...], wo[...], hid, att_o, mixt_o, mid_o, sec_o, sect_o)
    cott_o[...] = cot[...].T.reshape(cott_o.shape)


def run_mix(peers, lengths, slopes, att, qpre, came, sel, wo, hidden, cot, angles, parts):
    n, d = hidden.shape
    chunks = n // CHUNK
    turned = (parts // 2, 2, d // parts, n)
    tile = pl.BlockSpec((CHUNK, d), lambda c: (c, 0))
    turned_tile = pl.BlockSpec(turned[:3] + (CHUNK,), lambda c: (0, 0, 0, c))
    return launch(
        functools.partial(mix_kernel, peers, n),
        "carried_mixed_middle",
        chunks,
        [lengths, slopes, att, qpre, came, sel, wo, hidden, cot, *angles],
        [smem(), smem(), tile, tile, whole_block(came.shape), tile, whole_block(wo.shape), tile, tile]
        + [whole_block(a.shape) for a in angles],
        [struct((n, d)), struct(turned), struct((n, d)), struct((n, d)), struct(turned), struct(turned)],
        [tile, turned_tile, tile, tile, turned_tile, turned_tile],
        [pltpu.VMEM((CHUNK, d), F32)],
        3 * n * d * d,
    )


def forward_kernel(chunks, lengths, slopes, hid, cot, fine, coarse, *refs):
    refs = list(refs)
    take = lambda k: [refs.pop(0) for _ in range(k)]
    weights_h = take(5)
    (kpre_o, val_o, st_o, qpre_o, sel_o) = take(5)
    (turned_o, att_o, mixt_o, mid_o, sec_o, sect_o, cott_o, came_o) = take(8)
    (weights, normed, kpre, val, st, qpre, sel, att, state, final, came, total) = take(12)
    (load_sems, out_sems, state_sems) = take(3)
    heads = state.shape[0]
    step = pl.program_id(0)
    c = lax.rem(step, chunks)
    here = pl.ds(pl.multiple_of(c * CHUNK, CHUNK), CHUNK)
    layout = Layout(lengths, 2, chunks * CHUNK)
    loads = [pltpu.make_async_copy(w, weights.at[i], load_sems.at[i]) for i, w in enumerate(weights_h)]
    saves = [
        pltpu.make_async_copy(src, dst, out_sems.at[i])
        for i, (src, dst) in enumerate([(kpre, kpre_o), (val, val_o), (st, st_o), (qpre, qpre_o), (sel, sel_o)])
    ]
    exchange = remote(final, came, state_sems.at[0], state_sems.at[1], "mp", 1)

    @pl.when(step == 0)
    def _():
        for copy in loads:
            copy.start()
        state[...] = jnp.zeros_like(state)
        for copy in loads[:2]:
            copy.wait()

    @pl.when(step < chunks)
    def _():
        x = normed_of(hid)
        normed[here, :] = x
        turned_o[...] = x.T.reshape(turned_o.shape)
        keys = nn(x, weights[0])
        kpre[here, :] = keys.astype(BF16)
        values = nn(x, weights[1])
        val[here, :] = values.astype(BF16)
        cs, sn = layout.angles(c, fine, coarse)

        def put(h, value):
            st[c, h] = value

        states_chunk(heads, slopes, layout.keep(c), keys, values, cs, sn, state, put)

    @pl.when(step == chunks - 1)
    def _():
        final[...] = state[...].astype(BF16)
        exchange.start()
        for copy in saves[:3]:
            copy.start()

    @pl.when(step == chunks)
    def _():
        for copy in loads[2:4]:
            copy.wait()

    @pl.when(jnp.logical_and(step >= chunks, step < 2 * chunks))
    def _():
        x = normed[here, :]
        queries = nn(x, weights[2])
        qpre[here, :] = queries.astype(BF16)
        sel[here, :] = nn(x, weights[3]).astype(BF16)
        cs, sn = layout.angles(c, fine, coarse)

        def put(h, value):
            att[here, head_slice(h)] = value

        inside_chunk(
            heads,
            slopes,
            queries,
            lambda h: kpre[here, head_slice(h)],
            lambda h: val[here, head_slice(h)],
            lambda h: st[c, h],
            cs,
            sn,
            put,
        )
        cott_o[...] = cot[...].T.reshape(cott_o.shape)

    @pl.when(step == 2 * chunks - 1)
    def _():
        for copy in saves[3:]:
            copy.start()

    @pl.when(step == 2 * chunks)
    def _():
        loads[4].wait()
        exchange.wait()
        came_o[...] = came[...]

    @pl.when(step >= 2 * chunks)
    def _():
        cs, sn = layout.angles(c, fine, coarse)
        carried_chunk(
            heads,
            slopes,
            layout,
            c,
            lambda h: att[here, head_slice(h)],
            lambda h: qpre[here, head_slice(h)],
            came,
            cs,
            sn,
            total,
        )
        mix_chunk(total, sel[here, :], weights[4], hid, att_o, mixt_o, mid_o, sec_o, sect_o)

    @pl.when(step == 3 * chunks - 1)
    def _():
        for copy in saves:
            copy.wait()


def run_forward(lengths, slopes, hidden, cot, weights, angles, parts, guests, ident):
    n, d = hidden.shape
    chunks = n // CHUNK
    turned = (parts // 2, 2, d // parts, n)
    late = lambda s: jnp.maximum(s - 2 * chunks, 0)
    mid = lambda s: jnp.clip(s - chunks, 0, chunks - 1)
    early = lambda s: jnp.minimum(s, chunks - 1)
    tile = pl.BlockSpec((CHUNK, d), lambda s: (late(s), 0))
    turned_tile = lambda at: pl.BlockSpec(turned[:3] + (CHUNK,), lambda s: (0, 0, 0, at(s)))
    whole = pltpu.VMEM((n, d), BF16)
    return launch(
        functools.partial(forward_kernel, chunks),
        "forward_to_sglu",
        3 * chunks,
        [lengths, slopes, hidden, cot, *angles, *weights],
        [
            smem(),
            smem(),
            pl.BlockSpec((CHUNK, d), lambda s: (jnp.where(s < 2 * chunks, early(s), late(s)), 0)),
            pl.BlockSpec((CHUNK, d), lambda s: (mid(s), 0)),
        ]
        + [whole_block(a.shape) for a in angles]
        + [anywhere()] * 5,
        [struct((n, d)), struct((n, d)), struct((chunks,) + state_shape(d)), struct((n, d)), struct((n, d))]
        + [struct(turned), struct((n, d)), struct(turned), struct((n, d)), struct((n, d)), struct(turned), struct(turned)]
        + [struct(state_shape(d))],
        [anywhere()] * 5
        + [turned_tile(early), tile, turned_tile(late), tile, tile, turned_tile(late), turned_tile(mid)]
        + [whole_block(state_shape(d))],
        [
            pltpu.VMEM((5, d, d), BF16),
            whole,
            whole,
            whole,
            pltpu.VMEM((chunks,) + state_shape(d), BF16),
            whole,
            whole,
            pltpu.VMEM((n, d), F32),
            pltpu.VMEM(state_shape(d), F32),
            pltpu.VMEM(state_shape(d), BF16),
            pltpu.VMEM(state_shape(d), BF16),
            pltpu.VMEM((CHUNK, d), F32),
            pltpu.SemaphoreType.DMA((5,)),
            pltpu.SemaphoreType.DMA((5,)),
            pltpu.SemaphoreType.DMA((2,)),
        ],
        12 * n * d * d,
        guests=guests,
        ident=ident,
        partners=[("mp", 1)],
    )


def sglu_kernel(chunks, peers, sec, cot, w1, w2, wd, units_o, term_o, part_o):
    step = pl.program_id(0)
    here = pl.ds(pl.multiple_of(lax.rem(step, chunks) * CHUNK, CHUNK), CHUNK)
    left = nn(sec[...], w1[...])
    right = nn(sec[...], w2[...])
    inner = (left * right).astype(BF16)
    upstream = nt(cot[...], wd[...])
    grad_left = (upstream * right).astype(BF16)
    grad_right = (upstream * left).astype(BF16)
    units_o[0] = grad_left
    units_o[1] = grad_right
    units_o[2] = inner
    term = nn(inner, wd[...])
    part = nt(grad_left, w1[...]) + nt(grad_right, w2[...])

    @pl.when(step < chunks)
    def _():
        term_o[here, :] = term
        part_o[here, :] = part

    @pl.when(step >= chunks)
    def _():
        term_o[here, :] += term
        part_o[here, :] += part


def run_sglu(second, cot, w1, w2, wd):
    n, d = second.shape
    peers, _, width = w1.shape
    chunks = n // CHUNK
    tile = pl.BlockSpec((CHUNK, d), lambda s: (lax.rem(s, chunks), 0))
    block = lambda shape: pl.BlockSpec((None,) + shape, lambda s: (lax.div(s, chunks), 0, 0))
    return launch(
        functools.partial(sglu_kernel, chunks, peers),
        "sglu",
        peers * chunks,
        [second, cot, w1, w2, wd],
        [tile, tile, block((d, width)), block((d, width)), block((width, d))],
        [struct((3, peers, n, width)), struct((n, d), F32), struct((n, d), F32)],
        [
            pl.BlockSpec((3, None, CHUNK, width), lambda s: (0, lax.div(s, chunks), lax.rem(s, chunks), 0)),
            whole_block((n, d)),
            whole_block((n, d)),
        ],
        [],
        12 * n * d * width * peers,
    )


def units_kernel(geo, reducer, ride, lengths, slopes, first_weight, second_weight, down_weight, x, *refs):
    blocks, cut, d, units, chunks = geo["blocks"], geo["cut"], geo["d"], geo["units"], geo["chunks"]
    refs = list(refs)
    take = lambda k: [refs.pop(0) for _ in range(k)]
    (mid, sel, att, qpre, fine, coarse) = take(6)
    cot_h, xt_h, cott_h, wo_h = take(4)
    pieces = take(12)
    had_b = take(3)
    (out_o, gmid_o, gsel_o, gatt_o, et_o, e0_o, sums_o) = take(7)
    pieces = pieces + had_b + take(9)
    term, part, cot, xt, cott, o1, o2, od, c1, c2, cd, state, sums, sems, own_sems, wo_sems = take(16)
    reducer.bind(take(len(reducer.scratch)))
    step = pl.program_id(0)
    ride.before(step, had_b, pieces[15:], refs)
    core = lax.rem(lax.axis_index("dp"), 2)
    eighth = lax.rem(lax.axis_index("dp"), 8)
    heads = state.shape[0]
    layout = Layout(lengths, 2, chunks * CHUNK)

    def fetch(g):
        size = cut if g == 0 else units - cut
        masks = [(0, None, 0), (3, 0, 2), (3, 1, 4), (3, 2, 1), (6, 0, 6), (6, 1, 3), (6, 2, 5), (9, None, 7)]
        copies = []
        for w, region in enumerate((o1, o2, od)):
            rows = d // 8 if w < 2 else size // 8
            for k, (at, inner, mask) in enumerate(masks):
                src = pieces[12 * g + at + w]
                src = src if inner is None else src.at[inner]
                here = pl.ds(pl.multiple_of(flipped(eighth, mask) * rows, 16), rows)
                dst = region.at[here, pl.ds(0, size)] if w < 2 else region.at[here, :]
                copies.append(pltpu.make_async_copy(src, dst, sems.at[g, w, k]))
        return copies

    own = [
        pltpu.make_async_copy(cot_h, cot, own_sems.at[0]),
        pltpu.make_async_copy(xt_h.at[:, 1 - core], xt.at[0], own_sems.at[1]),
        pltpu.make_async_copy(xt_h.at[:, core], xt.at[1], own_sems.at[2]),
        pltpu.make_async_copy(cott_h.at[:, 1 - core], cott.at[0], own_sems.at[3]),
        pltpu.make_async_copy(cott_h.at[:, core], cott.at[1], own_sems.at[4]),
    ]
    pairs, rows = xt.shape[1], xt.shape[2]
    out_weight = [
        pltpu.make_async_copy(
            wo_h.at[pl.ds((k * pairs + i) * rows, rows), :], xt.at[k, i], wo_sems.at[k * pairs + i]
        )
        for k in range(2)
        for i in range(pairs)
    ]
    saved = pltpu.make_async_copy(sums, sums_o, own_sems.at[5])
    turn = cut // HEAD

    @pl.when(step == 0)
    def _():
        for copy in fetch(0) + own:
            copy.start()
        term[...] = jnp.zeros_like(term)
        part[...] = jnp.zeros_like(part)
        state[...] = jnp.zeros_like(state)
        for copy in fetch(0):
            copy.wait()

    @pl.when(step == turn)
    def _():
        for copy in fetch(1):
            copy.wait()

    @pl.when(step < blocks)
    def _():
        local = step - jnp.where(step >= turn, turn, 0)
        here = pl.ds(pl.multiple_of(local * HEAD, HEAD), HEAD)
        c1[:, :HEAD] = first_weight[...]
        c1[:, HEAD:] = o1[:, here]
        c2[:, :HEAD] = second_weight[...]
        c2[:, HEAD:] = o2[:, here]
        cd[:HEAD, :] = down_weight[...]
        cd[HEAD:, :] = od[here, :]

    @pl.when(step == turn - 1)
    def _():
        for copy in fetch(1):
            copy.start()

    @pl.when(step == 0)
    def _():
        for copy in own:
            copy.wait()

    @pl.when(step < blocks)
    def _():
        left = nn(x[...], c1[...])
        right = nn(x[...], c2[...])
        inner = (left * right).astype(BF16)
        upstream = nt(cot[...], cd[...])
        grad_left = (upstream * right).astype(BF16)
        grad_right = (upstream * left).astype(BF16)
        slot = lax.rem(step, 2)
        for k, buffer in enumerate((reducer.given, reducer.kept)):
            buffer[slot, 0] = nn(rows_of(xt, k), grad_left).astype(BF16)
            buffer[slot, 1] = nn(rows_of(xt, k), grad_right).astype(BF16)
            buffer[slot, 2] = nn(rows_of(cott, k), inner).astype(BF16)
            if k == 0:
                reducer.begin(step)
        term[...] += nn(inner, cd[...])
        part[...] += nt(grad_left, c1[...]) + nt(grad_right, c2[...])

    @pl.when(step == blocks - 1)
    def _():
        for copy in out_weight:
            copy.start()

    @pl.when(step == blocks)
    def _():
        for copy in out_weight:
            copy.wait()

    @pl.when(jnp.logical_and(step >= blocks, step < blocks + chunks))
    def _():
        c = chunks - 1 - (step - blocks)
        here = pl.ds(pl.multiple_of(c * CHUNK, CHUNK), CHUNK)
        cs, sn = layout.angles(c, fine, coarse)
        wo = xt[...].reshape(d, d)
        after_chunk(
            layout, c, heads, slopes, term[here, :], part[here, :], cot[here, :], mid, sel, att, wo, qpre, cs, sn,
            out_o, gmid_o, gsel_o, gatt_o, et_o, state,
        )

    @pl.when(step == blocks + chunks - 1)
    def _():
        e0_o[...] = state[...].astype(BF16)

    ride.after(step, had_b, pieces[15:], refs)
    reducer.run(step, sums)

    @pl.when(step == reducer.last)
    def _():
        saved.start()
        saved.wait()


def rows_of(ref, k):
    block = ref[k]
    return block.reshape(block.shape[0] * block.shape[1], block.shape[2])


def run_units(lengths, slopes, matrices, second, cot, second_t, cot_t, rows_in, angles, wo, pieces, ride, cut, depth, ident):
    n, d = second.shape
    chunks = n // CHUNK
    units = matrices[0].shape[1]
    blocks = units // HEAD
    pairs, _, rows, _ = second_t.shape
    reducer = Reducer(0, blocks, 3, depth, rows, (1, 3, 5, 7))
    geo = dict(blocks=blocks, cut=cut, d=d, units=units, chunks=chunks)
    at = lambda s: jnp.minimum(s, blocks - 1)
    back = lambda s: chunks - 1 - jnp.clip(s - blocks, 0, chunks - 1)
    tile = pl.BlockSpec((CHUNK, d), lambda s: (back(s), 0))
    columns = pl.BlockSpec((d, HEAD), lambda s: (0, at(s)))
    turned = pltpu.VMEM((2, pairs, rows, n), BF16)
    size = max(cut, units - cut)
    sums = (3, rows, units)
    return launch(
        functools.partial(units_kernel, geo, reducer, ride),
        "sglu_and_gradients",
        max(reducer.last, blocks + chunks - 1) + 1,
        [lengths, slopes] + list(matrices) + [second] + list(rows_in) + list(angles)
        + [cot, second_t, cot_t, wo] + list(pieces) + ride.inputs,
        [smem(), smem(), columns, columns, pl.BlockSpec((HEAD, d), lambda s: (at(s), 0)), once(second.shape)]
        + [tile] * 4
        + [once(a.shape) for a in angles]
        + [anywhere()] * (4 + len(pieces) + len(ride.inputs)),
        [struct((n, d))] * 4
        + [struct((chunks,) + state_shape(d)), struct(state_shape(d)), struct(sums, F32)]
        + ride.outs,
        [tile] * 4
        + [pl.BlockSpec((1,) + state_shape(d), lambda s: (back(s), 0, 0, 0)), whole_block(state_shape(d))]
        + [anywhere()] * (1 + len(ride.outs)),
        [
            pltpu.VMEM((n, d), F32),
            pltpu.VMEM((n, d), F32),
            pltpu.VMEM((n, d), BF16),
            turned,
            turned,
            pltpu.VMEM((d, size), BF16),
            pltpu.VMEM((d, size), BF16),
            pltpu.VMEM((size, d), BF16),
            pltpu.VMEM((d, 2 * HEAD), BF16),
            pltpu.VMEM((d, 2 * HEAD), BF16),
            pltpu.VMEM((2 * HEAD, d), BF16),
            pltpu.VMEM(state_shape(d), F32),
            pltpu.VMEM(sums, F32),
            pltpu.SemaphoreType.DMA((2, 3, 8)),
            pltpu.SemaphoreType.DMA((6,)),
            pltpu.SemaphoreType.DMA((2 * pairs,)),
        ]
        + reducer.scratch
        + ride.scratch,
        36 * n * d * units,
        partners=reducer.partners + ride.partners,
        ident=ident,
    )[:7]


def after_chunk(layout, c, heads, slopes, term, part, cot, mid, sel, att, wo, qpre, cs, sn, out_o, gmid_o, pair_o, gatt_o, et_o, state):
    middle = mid[...].astype(F32)
    out_o[...] = (middle + term).astype(BF16)
    grad_middle = cot.astype(F32) + norm_back(middle, scale_of(middle), part)
    branch = grad_middle.astype(BF16)
    gmid_o[...] = branch
    grad_mixed = nt(branch, wo)
    attended = att[...].astype(F32)
    scale = scale_of(attended)
    pair_o[...] = (grad_mixed * attended * scale).astype(BF16)
    grad_att = norm_back(attended, scale, grad_mixed * sel[...].astype(F32)) * layout.alive(c, 1)
    gatt_o[...] = grad_att.astype(BF16)
    keep = layout.keep(c)
    for h in range(heads):
        slope = slopes[h]
        query = featured(qpre[:, head_slice(h)].astype(F32), cs, sn)
        faded = (grad_att[:, head_slice(h)] * fade_from_start(slope, HEAD)).astype(BF16)
        old = state[h]
        et_o[0, h] = old.astype(BF16)
        state[h] = keep * (
            jnp.exp(jnp.full((1, 2 * HEAD), -slope * CHUNK, F32)) * old + nn(faded.T, query)
        )


def after_kernel(peers, count, lengths, slopes, term, part, cot, mid, sel, att, wo, qpre, fine, coarse, out_o, gmid_o, gsel_o, gatt_o, et_o, e0_o, state):
    step = pl.program_id(0)
    c = count // CHUNK - 1 - step
    layout = Layout(lengths, peers, count)

    @pl.when(step == 0)
    def _():
        state[...] = jnp.zeros_like(state)

    cs, sn = layout.angles(c, fine, coarse)
    after_chunk(
        layout, c, state.shape[0], slopes, term[...], part[...], cot[...], mid, sel, att, wo[...], qpre, cs, sn,
        out_o, gmid_o, gsel_o, gatt_o, et_o, state,
    )
    e0_o[...] = state[...].astype(BF16)


def run_after(peers, lengths, slopes, term, part, cot, mid, sel, att, wo, qpre, angles):
    n, d = cot.shape
    chunks = n // CHUNK
    back = lambda s: chunks - 1 - s
    tile = pl.BlockSpec((CHUNK, d), lambda s: (back(s), 0))
    return launch(
        functools.partial(after_kernel, peers, n),
        "output_and_row_gradients",
        chunks,
        [lengths, slopes, term, part, cot, mid, sel, att, wo, qpre, *angles],
        [smem(), smem()] + [tile] * 6 + [whole_block(wo.shape), tile] + [whole_block(a.shape) for a in angles],
        [struct((n, d))] * 4 + [struct((chunks,) + state_shape(d)), struct(state_shape(d))],
        [tile] * 4
        + [pl.BlockSpec((1,) + state_shape(d), lambda s: (back(s), 0, 0, 0)), whole_block(state_shape(d))],
        [pltpu.VMEM(state_shape(d), F32)],
        3 * n * d * d,
    )


def weights_kernel(items, peers, *refs):
    item = lax.div(pl.program_id(0), peers)
    lefts, right, out = refs[:-2], refs[-2], refs[-1]
    for i, left in enumerate(lefts):

        @pl.when(functools.reduce(jnp.logical_or, [item == t for t, w in enumerate(items) if w == i]))
        def _(left=left):
            block = left[...]
            block = block.reshape(-1, block.shape[-1])
            out[...] = nn(block, right[...]).astype(BF16).reshape(out.shape)


def run_weights(lefts, items, rights, right_spec, peers, width):
    pairs, _, rows, n = lefts[0].shape
    shape = (peers, len(items), pairs, 2, rows, width)
    which = lambda s: (lax.div(s, peers), lax.rem(s, peers))
    (out,) = launch(
        functools.partial(weights_kernel, items, peers),
        "weight_gradients",
        peers * len(items),
        list(lefts) + [rights],
        [whole_block(left.shape) for left in lefts] + [right_spec(which)],
        [struct(shape)],
        [pl.BlockSpec((None, None) + shape[2:], lambda s: (which(s)[1], which(s)[0], 0, 0, 0, 0))],
        [],
        4 * n * pairs * rows * width * len(items) * peers,
    )
    return out


def head_back(slope, qpre, kpre, value, grad, state, ending, cs, sn):
    qp, kp = qpre.astype(F32), kpre.astype(F32)
    qs, ks = sigmoid(qp), sigmoid(kp)
    qa, ka = qp * qs, kp * ks
    query = jnp.concatenate([qa * cs, qa * sn], axis=-1).astype(BF16)
    key = jnp.concatenate([ka * cs, ka * sn], axis=-1).astype(BF16)
    state, ending = state.astype(BF16), ending.astype(BF16)
    table, turned = decay_table(slope, False), decay_table(slope, True)
    scores_t = (nt(key, query) * turned).astype(BF16)
    slope_s = (nt(grad, value) * table).astype(BF16)
    slope_t = (nt(value, grad) * turned).astype(BF16)
    start = fade_from_start(slope, HEAD)
    end = fade_to_end(slope, HEAD)
    grad_start = (grad.astype(F32) * start).astype(BF16)
    value_end = (value.astype(F32) * end).astype(BF16)
    dq = nn(slope_s, key) + nn(grad_start, state)
    dk = nn(slope_t, query) + nn(value_end, ending)
    dv = nn(scores_t, grad) + end * nt(key, ending)
    dq = dq[:, :HEAD] * cs + dq[:, HEAD:] * sn
    dk = dk[:, :HEAD] * cs + dk[:, HEAD:] * sn
    gq = (dq * (qs * (1.0 + qp * (1.0 - qs)))).astype(BF16)
    gk = (dk * (ks * (1.0 + kp * (1.0 - ks)))).astype(BF16)
    return gq, gk, dv.astype(BF16)


def attention_back_kernel(peers, count, lengths, slopes, qpre, kpre, values, gatt, st, came, et, left, fine, coarse, grads_o):
    chunks = count // CHUNK
    layout = Layout(lengths, peers, count)
    pair, c = lax.div(pl.program_id(0), chunks), lax.rem(pl.program_id(0), chunks)
    cs, sn = layout.angles(c, fine, coarse)
    before, after = layout.before(c), layout.after(c)
    span = (CHUNK * c).astype(F32)
    rest = (CHUNK * (chunks - 1 - c)).astype(F32)
    for h in range(2):
        slope = slopes[2 * pair + h]
        cols = head_slice(h)
        lane = jnp.zeros((1, 2 * HEAD), F32)
        state = st[0, h].astype(F32) + came[h].astype(F32) * (jnp.exp(lane - slope * span) * before)
        ending = et[0, h].astype(F32) + left[h].astype(F32) * (jnp.exp(lane - slope * rest) * after)
        three = head_back(
            slope, qpre[:, cols], kpre[:, cols], values[:, cols], gatt[:, cols], state, ending, cs, sn
        )
        for i in range(3):
            grads_o[i, :, cols] = three[i]


def run_attention_back(peers, lengths, slopes, qpre, kpre, values, gatt, st, came, et, left, angles):
    n, d = qpre.shape
    chunks = n // CHUNK
    pair = lambda s: lax.div(s, chunks)
    chunk = lambda s: lax.rem(s, chunks)
    tile = pl.BlockSpec((CHUNK, 2 * HEAD), lambda s: (chunk(s), pair(s)))
    states = pl.BlockSpec((1, 2, HEAD, 2 * HEAD), lambda s: (chunk(s), pair(s), 0, 0))
    ends = pl.BlockSpec((2, HEAD, 2 * HEAD), lambda s: (pair(s), 0, 0))
    return launch(
        functools.partial(attention_back_kernel, peers, n),
        "attention_backward",
        chunks * d // (2 * HEAD),
        [lengths, slopes, qpre, kpre, values, gatt, st, came, et, left, *angles],
        [smem(), smem(), tile, tile, tile, tile, states, ends, states, ends] + [whole_block(a.shape) for a in angles],
        [struct((3, n, d))],
        [pl.BlockSpec((3, CHUNK, 2 * HEAD), lambda s: (0, chunk(s), pair(s)))],
        [],
        18 * n * 256 * d,
    )


def projections_kernel(geo, outer, inner, lengths, slopes, *refs):
    chunks, blocks, d, n = geo["chunks"], geo["blocks"], geo["d"], geo["n"]
    refs = list(refs)
    take = lambda k: [refs.pop(0) for _ in range(k)]
    columns = [take(2) for _ in range(4)]
    states = [take(2) for _ in range(2)]
    (came, leaving, fine, coarse, branch_a, branch_b, sel_a, sel_b, sel, hid, gmid, mixt_h, normt_h) = take(13)
    weights_h = take(4)
    hidden_o, out, out2 = take(3)
    grads, block, mixt, normt, w4, left, sems, state_sems = take(8)
    outer.bind(take(len(outer.scratch)))
    inner.bind(refs)
    step = pl.program_id(0)
    core = lax.rem(lax.axis_index("dp"), 2)
    me = lax.axis_index("mp")
    layout = Layout(lengths, 2, n)
    loads = [
        pltpu.make_async_copy(mixt_h.at[:, 1 - core], mixt.at[0], sems.at[0]),
        pltpu.make_async_copy(mixt_h.at[:, core], mixt.at[1], sems.at[1]),
        pltpu.make_async_copy(normt_h.at[:, 1 - core], normt.at[0], sems.at[2]),
        pltpu.make_async_copy(normt_h.at[:, core], normt.at[1], sems.at[3]),
    ]
    matrices = [pltpu.make_async_copy(w, w4.at[i], sems.at[4 + i]) for i, w in enumerate(weights_h)]

    def exchange(j):
        pair = []
        for k in range(2):
            h = k * blocks + j
            pair.append(remote(leaving.at[h], left.at[h], state_sems.at[0, h], state_sems.at[1, h], "mp", 1))
        return pair

    @pl.when(step == 0)
    def _():
        for j in range(blocks):
            for copy in exchange(j):
                copy.start()
        for copy in loads:
            copy.start()
        for copy in matrices:
            copy.start()
        for copy in loads:
            copy.wait()

    @pl.when(step < blocks)
    def _():
        slot = lax.rem(step, 2)
        gb = jnp.concatenate([branch_a[...], branch_b[...]], axis=1)
        gs = jnp.concatenate([sel_a[...], sel_b[...]], axis=1)
        for k, buffer in enumerate((outer.given, outer.kept)):
            buffer[slot, 0] = nn(rows_of(mixt, k), gb).astype(BF16)
            buffer[slot, 1] = nn(rows_of(normt, k), gs).astype(BF16)
            if k == 0:
                outer.begin(step)

    @pl.when(jnp.logical_and(step >= blocks, step < 2 * blocks))
    def _():
        j = step - blocks
        for copy in exchange(j):
            copy.wait()

        def one(c, carry):
            here = pl.ds(pl.multiple_of(c * CHUNK, CHUNK), CHUNK)
            cs, sn = layout.angles(c, fine, coarse)
            before, after = layout.before(c), layout.after(c)
            span = (CHUNK * c).astype(F32)
            rest = (CHUNK * (chunks - 1 - c)).astype(F32)
            for side in range(2):
                h = (me if side == 0 else 1 - me) * blocks + j
                slope = slopes[h]
                qpre, kpre, values, gatt = [pair[side][here, :] for pair in columns]
                st, et = [pair[side][c, 0].astype(F32) for pair in states]
                lane = jnp.zeros((1, 2 * HEAD), F32)
                state = st + came[h].astype(F32) * (jnp.exp(lane - slope * span) * before)
                ending = et + left[h].astype(F32) * (jnp.exp(lane - slope * rest) * after)
                three = head_back(slope, qpre, kpre, values, gatt, state, ending, cs, sn)
                cols = pl.ds(pl.multiple_of(h * HEAD, HEAD), HEAD)
                for i in range(3):
                    block[i, here, head_slice(side)] = three[i]
                    grads[i, here, cols] = three[i]
            return carry

        lax.fori_loop(0, chunks, one, 0)
        slot = lax.rem(j, 2)
        for k, buffer in enumerate((inner.given, inner.kept)):
            for i in range(3):
                buffer[slot, i] = nn(rows_of(normt, k), block[i]).astype(BF16)
            if k == 0:
                inner.begin(j)

    @pl.when(step == 2 * blocks)
    def _():
        for copy in matrices:
            copy.wait()

    @pl.when(jnp.logical_and(step >= 2 * blocks, step < 2 * blocks + chunks))
    def _():
        here = pl.ds(pl.multiple_of((step - 2 * blocks) * CHUNK, CHUNK), CHUNK)
        total = nt(sel[...], w4[3])
        for i in range(3):
            total = total + nt(grads[i, here, :], w4[i])
        x = hid[...].astype(F32)
        hidden_o[...] = (gmid[...].astype(F32) + norm_back(x, scale_of(x), total)).astype(BF16)

    outer.run(step, out)
    inner.run(step, out2)


def run_projections(lengths, slopes, qpre, kpre, values, gatt, st, et, came, leaving, angles, gsel, hidden, gmid, mixed_t, normed_t, weights, depth, ident):
    n, d = qpre.shape
    heads, chunks = d // HEAD, n // CHUNK
    blocks = heads // 2
    pairs, _, rows, _ = mixed_t.shape
    outer = Reducer(0, blocks, 2, depth, rows, (1, 3, 5, 7))
    inner = Reducer(blocks, blocks, 3, depth, rows, (1, 2, 4, 5))
    steps = max(outer.last, inner.last, 2 * blocks + chunks - 1) + 1
    geo = dict(chunks=chunks, blocks=blocks, d=d, n=n)
    early = lambda s: jnp.minimum(s, blocks - 1)
    mid = lambda s: jnp.clip(s - blocks, 0, blocks - 1)
    late = lambda s: jnp.clip(s - 2 * blocks, 0, chunks - 1)
    side = lambda k: blocks * (lax.axis_index("mp") if k == 0 else 1 - lax.axis_index("mp"))
    column = lambda k: pl.BlockSpec((n, HEAD), lambda s: (0, side(k) + mid(s)))
    state = lambda k: pl.BlockSpec((chunks, 1, HEAD, 2 * HEAD), lambda s: (0, side(k) + mid(s), 0, 0))
    early_column = lambda k: pl.BlockSpec((n, HEAD), lambda s: (0, side(k) + early(s)))
    tile = pl.BlockSpec((CHUNK, d), lambda s: (late(s), 0))
    turned = pltpu.VMEM((2, pairs, rows, n), BF16)
    return launch(
        functools.partial(projections_kernel, geo, outer, inner),
        "attention_backward_and_gradients",
        steps,
        [lengths, slopes]
        + [a for a in (qpre, kpre, values, gatt, st, et) for _ in range(2)]
        + [came, leaving, *angles, gmid, gmid, gsel, gsel, gsel, hidden, gmid, mixed_t, normed_t]
        + list(weights),
        [smem(), smem()]
        + [column(k) for _ in range(4) for k in range(2)]
        + [state(k) for _ in range(2) for k in range(2)]
        + [once(came.shape), anywhere()]
        + [once(a.shape) for a in angles]
        + [early_column(k) for _ in range(2) for k in range(2)]
        + [tile, tile, tile]
        + [anywhere()] * 6,
        [struct((n, d)), struct((2, rows, d // 2), F32), struct((3, rows, d // 2), F32)],
        [tile, whole_block((2, rows, d // 2)), whole_block((3, rows, d // 2))],
        [
            pltpu.VMEM((3, n, d), BF16),
            pltpu.VMEM((3, n, 2 * HEAD), BF16),
            turned,
            turned,
            pltpu.VMEM((4, d, d), BF16),
            pltpu.VMEM(leaving.shape, BF16),
            pltpu.SemaphoreType.DMA((8,)),
            pltpu.SemaphoreType.DMA((2, heads)),
        ]
        + outer.scratch
        + inner.scratch,
        30 * n * d * d,
        partners=outer.partners,
        ident=ident,
    )


def input_kernel(wq, wk, wv, ws, grads, gsel, hid, gmid, out):
    total = nt(grads[0], wq[...]) + nt(grads[1], wk[...]) + nt(grads[2], wv[...]) + nt(gsel[...], ws[...])
    x = hid[...].astype(F32)
    out[...] = (gmid[...].astype(F32) + norm_back(x, scale_of(x), total)).astype(BF16)


def run_input(weights, grads, gsel, hidden, gmid):
    n, d = hidden.shape
    tile = pl.BlockSpec((CHUNK, d), lambda c: (c, 0))
    return launch(
        input_kernel,
        "input_gradient",
        n // CHUNK,
        list(weights) + [grads, gsel, hidden, gmid],
        [whole_block(w.shape) for w in weights]
        + [
            pl.BlockSpec((3, CHUNK, d), lambda c: (0, c, 0)),
            tile,
            tile,
            tile,
        ],
        [struct((n, d))],
        [tile],
        [],
        8 * n * d * d,
    )


def reduced(lefts, items, rights, spec, peers, width):
    full = run_weights(lefts, items, rights, spec, peers, width)
    full = full.reshape(peers, len(items), -1, full.shape[4], width)
    mine = lax.psum_scatter(full, "dp", scatter_dimension=2, tiled=False)
    return lax.psum_scatter(mine, "mp", scatter_dimension=0, tiled=False).astype(F32)


def per_device(
    hidden_in,
    query_weight,
    key_weight,
    value_weight,
    select_weight,
    out_weight,
    first_weight,
    second_weight,
    down_weight,
    decay_slope,
    doc_lengths,
    cotangent,
):
    count, d = hidden_in.shape
    heads, chunks = d // HEAD, count // CHUNK
    peers, parts = lax.axis_size("mp"), lax.axis_size("dp")
    me = lax.axis_index("mp")
    depth = parts // 4
    group = count * peers
    units = first_weight.shape[1]
    lengths = doc_lengths.astype(jnp.int32)
    angles = tables(group // 2)
    slopes = decay_slope
    matrices = (first_weight, second_weight, down_weight)
    riding = peers == 2

    if riding:
        cut = -(-units // 256) * 128
        ranges = [(0, cut), (cut, units - cut)]
    else:
        ranges = [(0, units)]

    def like(arrays, count=None):
        return [struct(a.shape if count is None else (count,) + a.shape) for a in arrays]

    def over_mp(g):
        low, size = ranges[g]

        def source(w):
            def src(i, o):
                eighth = lax.rem(lax.axis_index("dp"), 8)
                if w < 2:
                    rows = d // 8
                    return i[w].at[pl.ds(pl.multiple_of(eighth * rows, 16), rows), pl.ds(low, size)]
                rows = size // 8
                return i[w].at[pl.ds(pl.multiple_of(low + eighth * rows, 16), rows), :]

            return src

        outs = [struct((d // 8, size)), struct((d // 8, size)), struct((size // 8, d))]
        return outs, [(source(w), lambda i, o, w=w: o[w], "mp", 1) for w in range(3)]

    def near(src, dst):
        return [
            (lambda i, o: src(i, o), lambda i, o: dst(i, o).at[0], "dp", 2),
            (lambda i, o: src(i, o), lambda i, o: dst(i, o).at[1], "dp", 4),
            (lambda i, o: src(i, o), lambda i, o: dst(i, o).at[2], "dp", 1),
        ]

    def far(src, dst, rows):
        top = -(-rows // 32) * 16
        upper, lower = pl.ds(0, top), pl.ds(top, rows - top)
        return [
            (lambda i, o: src(i, o).at[1, upper, :], lambda i, o: dst(i, o).at[0, upper, :], "dp", 2),
            (lambda i, o: src(i, o).at[0, lower, :], lambda i, o: dst(i, o).at[0, lower, :], "dp", 4),
            (lambda i, o: src(i, o).at[0], lambda i, o: dst(i, o).at[1], "dp", 1),
            (lambda i, o: src(i, o).at[1], lambda i, o: dst(i, o).at[2], "dp", 1),
        ]

    def onward(pieces, out, at):
        ref = lambda k: lambda i, o: o[k]
        one, two, three = [], [], []
        for w in range(3):
            one += near(pieces(w), ref(at + w))
            two += far(ref(at + w), ref(at + 3 + w), out[w].shape[0])
            three.append((lambda i, o, w=w: o[at + 3 + w].at[0], ref(at + 6 + w), "dp", 1))
        return like(out, 3) + like(out, 3) + like(out), [one, two, three]

    if riding:
        outs, copies = over_mp(0)
        more, phases = onward(lambda w: lambda i, o: o[w], outs, 3)
        outs_b, copies_b = over_mp(1)
        spans = [(0, chunks), (chunks + 1, 2 * chunks), (2 * chunks + 1, 3 * chunks - 2), (3 * chunks - 1,) * 2]
        guests = [
            Carry(matrices, outs + more, [span + (c,) for span, c in zip(spans, [copies] + phases)]),
            Carry(matrices, outs_b, [(chunks + 2, 3 * chunks - 1, copies_b)]),
        ]
        weights = [key_weight, value_weight, query_weight, select_weight, out_weight]
        kpre, values, st, qpre, sel, normed_t, attended, mixed_t, middle, second, second_t, cot_t, came, *got = run_forward(
            lengths, slopes, hidden_in, cotangent, weights, angles, parts, guests, ident=1
        )
    else:
        normed, normed_t, kpre, values, st, final = run_keys(
            peers, lengths, slopes, hidden_in, key_weight, value_weight, angles, parts
        )
        begin, start, last = jnp.int32(0), jnp.int32(0), (me + 1) * count - CHUNK
        for i in range(lengths.shape[1]):
            begin = jnp.where(last >= start, start, begin)
            start = start + lengths[0, i]
        passes = (begin < me * count).astype(F32)
        decay = jnp.exp(-slopes * count)
        finals = lax.all_gather(final, "mp")
        keeps = lax.all_gather(passes.reshape(1), "mp")[:, 0]

        def ahead(k, total):
            new = finals[k].astype(F32) + (keeps[k] * decay)[:, None, None] * total
            return jnp.where(k < me, new, total)

        came = lax.fori_loop(0, peers, ahead, jnp.zeros(final.shape, F32)).astype(BF16)
        qpre, sel, att = run_inside(
            peers, lengths, slopes, normed, query_weight, select_weight, kpre, values, st, angles
        )
        attended, mixed_t, middle, second, second_t, cot_t = run_mix(
            peers, lengths, slopes, att, qpre, came, sel, out_weight, hidden_in, cotangent, angles, parts
        )

    if riding:
        had_b = got[12:15]
        more, phases = onward(lambda w: lambda i, o: i[w], had_b, 0)
        ride = Carry(had_b, more, [(0, 1, phases[0]), (2, 3, phases[1]), (4, 4, phases[2])])
        output, grad_middle, grad_sel, grad_att, et, leaving, sglu = run_units(
            lengths, slopes, matrices, second, cotangent, second_t, cot_t, [middle, sel, attended, qpre],
            angles, out_weight, got[:12], ride, ranges[0][1], depth, ident=2,
        )
    else:
        sources = [lax.all_gather(w, "mp") for w in matrices]
        grads, term, part = run_sglu(second, cotangent, *sources)
        units_spec = lambda at: pl.BlockSpec((None, None, count, units), lambda s: at(s) + (0, 0))
        sglu = reduced([second_t, cot_t], (0, 0, 1), grads, units_spec, peers, units)
        output, grad_middle, grad_sel, grad_att, et, leaving = run_after(
            peers, lengths, slopes, term, part, cotangent, middle, sel, attended, out_weight, qpre, angles
        )
    inputs_weights = [query_weight, key_weight, value_weight, select_weight]
    if riding:
        grad_hidden, out_sel, inputs = run_projections(
            lengths, slopes, qpre, kpre, values, grad_att, st, et, came, leaving, angles, grad_sel,
            hidden_in, grad_middle, mixed_t, normed_t, inputs_weights, depth, ident=3,
        )
    else:
        leavings = lax.all_gather(leaving, "mp")

        def behind(step, total):
            k = peers - 1 - step
            new = leavings[k].astype(F32) + (keeps[k] * decay)[:, None, None] * total
            return jnp.where(k > me, new, total)

        left = lax.fori_loop(0, peers, behind, jnp.zeros(leaving.shape, F32)).astype(BF16)
        share = d // peers
        wide_spec = lambda at: pl.BlockSpec((None, count, share), lambda s: (at(s)[0], 0, at(s)[1]))
        pair = jnp.stack([grad_middle, grad_sel])
        out_sel = reduced([mixed_t, normed_t], (0, 1), pair, wide_spec, peers, share)
        (qkv,) = run_attention_back(
            peers, lengths, slopes, qpre, kpre, values, grad_att, st, came, et, left, angles
        )
        inputs = reduced([normed_t], (0, 0, 0), qkv, wide_spec, peers, share)
        (grad_hidden,) = run_input(inputs_weights, qkv, grad_sel, hidden_in, grad_middle)
    return (
        output,
        grad_hidden,
        inputs[0],
        inputs[1],
        inputs[2],
        out_sel[1],
        out_sel[0],
        sglu[0],
        sglu[1],
        jnp.transpose(sglu[2]),
    )


def solution(mesh):
    rows = P(("dp", "mp"), None)
    in_specs = (
        rows,
        P(),
        P(),
        P(),
        P(),
        P(),
        P(None, "mp"),
        P(None, "mp"),
        P("mp", None),
        P(),
        P("dp", None),
        rows,
    )
    out_specs = (rows, rows) + (P("dp", "mp"),) * 7 + (P("mp", "dp"),)
    return jax.shard_map(
        per_device, mesh=mesh, in_specs=in_specs, out_specs=out_specs, check_vma=False
    )
```

```python
import functools

import jax
import jax.numpy as jnp
import numpy as np
from jax import lax
from jax.experimental import pallas as pl
from jax.experimental.pallas import tpu as pltpu
from jax.sharding import PartitionSpec as P

HEAD = 128
CHUNK = 256
EPSILON = 1e-06
BF16 = jnp.bfloat16
F32 = jnp.float32
VMEM_LIMIT = 62 * 1024 * 1024


def nn(left, right):
    return jnp.dot(left, right, preferred_element_type=F32)


def nt(left, right):
    return lax.dot_general(left, right, (((1,), (1,)), ((), ())), preferred_element_type=F32)


def scale_of(values):
    return lax.rsqrt(jnp.mean(values * values, axis=-1, keepdims=True) + EPSILON)


def norm_back(values, scale, upstream):
    return scale * upstream - values * (scale * scale * scale) * jnp.mean(
        values * upstream, axis=-1, keepdims=True
    )


def sigmoid(v):
    return 0.5 * jnp.tanh(0.5 * v) + 0.5


def featured(pre, cos, sin):
    act = pre * sigmoid(pre)
    return jnp.concatenate([act * cos, act * sin], axis=-1).astype(BF16)


def head_slice(h):
    return slice(h * HEAD, (h + 1) * HEAD)


def turned_shape(d, n):
    return (2, d // 2, n)


def put_turned(ref, value, parts):
    turned = value.T
    rows = turned.shape[0] // parts
    for i in range(parts):
        ref[i % 2, (i // 2) * rows : (i // 2 + 1) * rows, :] = turned[i * rows : (i + 1) * rows, :]


def feature_slice(h):
    return slice(2 * h * HEAD, 2 * (h + 1) * HEAD)


def row_index(shape):
    return lax.broadcasted_iota(jnp.int32, shape, 0)


def fade_from_start(slope, width):
    return jnp.exp(-slope * (row_index((CHUNK, width)) + 1).astype(F32))


def fade_to_end(slope, width):
    return jnp.exp(-slope * (CHUNK - 1 - row_index((CHUNK, width))).astype(F32))


def decay_table(slope, transposed):
    rows = lax.broadcasted_iota(jnp.int32, (CHUNK, CHUNK), 0)
    cols = lax.broadcasted_iota(jnp.int32, (CHUNK, CHUNK), 1)
    gap = cols - rows if transposed else rows - cols
    return jnp.where(gap >= 0, jnp.exp(-slope * jnp.maximum(gap, 0).astype(F32)), 0.0)


def plus(*arrays):
    total = arrays[0].astype(F32)
    for a in arrays[1:]:
        total = total + a.astype(F32)
    return total


def smem():
    return pl.BlockSpec(memory_space=pltpu.SMEM)


def anywhere():
    return pl.BlockSpec(memory_space=pl.ANY)


def once(shape):
    zeros = (0,) * len(shape)
    return pl.BlockSpec(shape, lambda *_: zeros, pipeline_mode=pl.Buffered(1))


def whole_block(shape):
    zeros = (0,) * len(shape)
    return pl.BlockSpec(shape, lambda *_: zeros)


def cost(flops, arrays):
    moved = sum(int(np.prod(a.shape)) * jnp.dtype(a.dtype).itemsize for a in arrays)
    return pl.CostEstimate(flops=int(flops), bytes_accessed=moved, transcendentals=0)


def struct(shape, dtype=BF16):
    return jax.ShapeDtypeStruct(tuple(shape), dtype)


def flipped(index, mask):
    bit = 1
    while bit <= mask:
        if mask & bit:
            index = index + bit * (1 - 2 * lax.rem(lax.div(index, bit), 2))
        bit *= 2
    return index


def remote(src, dst, send, recv, axis, mask):
    return pltpu.make_async_remote_copy(
        src_ref=src,
        dst_ref=dst,
        send_sem=send,
        recv_sem=recv,
        device_id={axis: flipped(lax.axis_index(axis), mask)},
        device_id_type=pl.DeviceIdType.MESH,
    )


def greet(partners):
    barrier = pltpu.get_barrier_semaphore()
    for axis, mask in partners:
        pl.semaphore_signal(
            barrier,
            inc=1,
            device_id={axis: flipped(lax.axis_index(axis), mask)},
            device_id_type=pl.DeviceIdType.MESH,
        )
    pl.semaphore_wait(barrier, len(partners))


class Carry:
    def __init__(self, inputs, outs, phases):
        self.inputs, self.outs, self.phases = list(inputs), list(outs), phases
        count = sum(len(p[2]) for p in phases)
        self.scratch = [pltpu.SemaphoreType.DMA((count,)), pltpu.SemaphoreType.DMA((count,))]
        self.partners = [(c[2], c[3]) for p in phases for c in p[2]]

    def copies(self, which, ins, outs, scratch):
        at = sum(len(p[2]) for p in self.phases[:which])
        send, recv = scratch
        for k, (src, dst, axis, mask) in enumerate(self.phases[which][2]):
            yield remote(src(ins, outs), dst(ins, outs), send.at[at + k], recv.at[at + k], axis, mask)

    def before(self, step, ins, outs, scratch):
        for p, phase in enumerate(self.phases):

            @pl.when(step == phase[0])
            def _(p=p):
                for copy in self.copies(p, ins, outs, scratch):
                    copy.start()

    def after(self, step, ins, outs, scratch):
        for p, phase in enumerate(self.phases):

            @pl.when(step == phase[1])
            def _(p=p):
                for copy in self.copies(p, ins, outs, scratch):
                    copy.wait()


class Reducer:
    KINDS = 8

    def __init__(self, start, blocks, items, depth, rows, delays, slots, order, over_x):
        self.start, self.blocks, self.items = start, blocks, items
        self.slots, self.order = slots, order
        self.made = 2 if delays[0] else 1
        self.depth, self.rows, self.delays = depth, rows, delays
        self.upper = [(t, z) for t in range(items) for z in range(over_x[t])]
        self.lower = [(t, z) for t in range(items) for z in range(over_x[t], depth)]
        n, wide = 2 * depth * rows, 2 * HEAD
        buf = lambda *shape: pltpu.VMEM(shape, BF16)
        up, low = len(self.upper), len(self.lower)
        pair, flat = (up, rows, wide), (2, low, rows, HEAD)
        self.scratch = [
            buf(self.made, items, n, wide),
            buf(self.made, items, n, wide),
            buf(4 if delays[0] else 2, items, n, wide),
            buf(slots, *pair),
            buf(slots, *pair),
            buf(4, *pair),
            buf(slots, *flat),
            buf(slots, *flat),
            buf(4, *flat),
            buf(slots, up, rows, HEAD),
            buf(slots, up, rows, HEAD),
            buf(4, up, rows, HEAD),
            buf(slots, low, rows, HEAD),
            buf(slots, low, rows, HEAD),
            buf(4, low, rows, HEAD),
            buf(slots, depth, items, rows, HEAD),
            buf(4, depth - 1, items, rows, HEAD),
            pltpu.SemaphoreType.DMA((self.KINDS, blocks)),
            pltpu.SemaphoreType.DMA((self.KINDS, blocks)),
        ]
        self.partners = [("dp", 1), ("dp", 2), ("mp", 1)] + [("dp", 4 * k) for k in range(1, depth)]
        self.last = start + blocks - 1 + delays[3]

    def bind(self, scratch):
        self.refs = scratch
        self.given, self.kept = scratch[:2]
        self.x = lax.rem(lax.div(lax.axis_index("dp"), 2), 2)
        self.z = lax.div(lax.axis_index("dp"), 4)

    def copies(self, stage, j):
        (given, kept, got, ps, pk, pr, qs, qk, qr, ps2, pk2, pr2, qs2, qk2, qr2, line, zr, send, recv) = self.refs
        slot, four = lax.rem(j, self.slots), lax.rem(j, 4)
        if stage == 0:
            plan = [(0, given.at[lax.rem(j, self.made)], got.at[lax.rem(j, got.shape[0])], "dp", 1)]
        elif stage == 1:
            plan = [(1, ps.at[slot], pr.at[four], "dp", 2), (2, qs.at[slot], qr.at[four], "mp", 1)]
        elif stage == 2:
            plan = [(3, ps2.at[slot], pr2.at[four], "mp", 1), (4, qs2.at[slot], qr2.at[four], "dp", 2)]
        else:
            plan = [
                (4 + k, line.at[slot, flipped(self.z, k)], zr.at[four, k - 1], "dp", 4 * k)
                for k in range(1, self.depth)
            ]
        return [remote(src, dst, send.at[i, j], recv.at[i, j], axis, mask) for i, src, dst, axis, mask in plan]

    def begin(self, j):
        for copy in self.copies(0, j):
            copy.start()

    def run(self, step, out):
        for stage in self.order:
            j = step - self.start - self.delays[stage - 1]

            @pl.when(jnp.logical_and(j >= 0, j < self.blocks))
            def _(stage=stage, j=j):
                for copy in self.copies(stage - 1, j):
                    copy.wait()
                self.add(stage, j, out)
                if stage < 4:
                    for copy in self.copies(stage, j):
                        copy.start()

    def add(self, stage, j, out):
        (given, kept, got, ps, pk, pr, qs, qk, qr, ps2, pk2, pr2, qs2, qk2, qr2, line, zr, send, recv) = self.refs
        slot, four, x, rows = lax.rem(j, self.slots), lax.rem(j, 4), self.x, self.rows
        if stage == 1:
            two, came = lax.rem(j, self.made), lax.rem(j, got.shape[0])

            def total(t, z, at):
                here = pl.ds(pl.multiple_of((2 * z + at) * rows, rows), rows)
                return kept[two, t, here, :] + got[came, t, here, :]

            for i, (t, z) in enumerate(self.upper):
                ps[slot, i] = total(t, z, 1 - x)
                pk[slot, i] = total(t, z, x)
            for i, (t, z) in enumerate(self.lower):
                for at in range(2):
                    block = total(t, z, at)
                    qk[slot, at, i] = block[:, :HEAD]
                    qs[slot, at, i] = block[:, HEAD:]
        elif stage == 2:
            for i in range(len(self.upper)):
                block = pk[slot, i] + pr[four, i]
                pk2[slot, i] = block[:, :HEAD]
                ps2[slot, i] = block[:, HEAD:]
            for i in range(len(self.lower)):
                qs2[slot, i] = qk[slot, 1 - x, i] + qr[four, 1 - x, i]
                qk2[slot, i] = qk[slot, x, i] + qr[four, x, i]
        elif stage == 3:
            for i, (t, z) in enumerate(self.upper):
                line[slot, z, t] = pk2[slot, i] + pr2[four, i]
            for i, (t, z) in enumerate(self.lower):
                line[slot, z, t] = qk2[slot, i] + qr2[four, i]
        else:
            total = plus(line[slot, self.z], *[zr[four, k] for k in range(self.depth - 1)])
            out[:, :, pl.ds(pl.multiple_of(j * HEAD, HEAD), HEAD)] = total


def launch(kernel, name, steps, inputs, specs, outs, out_specs, scratch, flops, guests=(), ident=None, partners=()):
    guests = list(guests)
    partners = list(partners) + [p for g in guests for p in g.partners]
    partners = sorted(set(partners))
    all_inputs = list(inputs) + [a for g in guests for a in g.inputs]
    all_specs = list(specs) + [anywhere() for g in guests for _ in g.inputs]
    all_outs = list(outs) + [a for g in guests for a in g.outs]
    all_out_specs = list(out_specs) + [anywhere() for g in guests for _ in g.outs]
    all_scratch = list(scratch) + [a for g in guests for a in g.scratch]

    def body(*refs):
        refs = list(refs)
        take = lambda k: [refs.pop(0) for _ in range(k)]
        own = take(len(inputs))
        ins = [take(len(g.inputs)) for g in guests]
        own += take(len(outs))
        gone = [take(len(g.outs)) for g in guests]
        own += take(len(scratch))
        held = [take(len(g.scratch)) for g in guests]
        step = pl.program_id(0)
        if partners:

            @pl.when(step == 0)
            def _():
                greet(partners)

        for g, i, o, s in zip(guests, ins, gone, held):
            g.before(step, i, o, s)
        kernel(*own)
        for g, i, o, s in zip(guests, ins, gone, held):
            g.after(step, i, o, s)

    extra = dict(collective_id=ident, has_side_effects=True) if partners else {}
    return pl.pallas_call(
        body,
        grid=(steps,),
        in_specs=all_specs,
        out_specs=all_out_specs,
        out_shape=all_outs,
        scratch_shapes=all_scratch,
        compiler_params=pltpu.CompilerParams(
            vmem_limit_bytes=VMEM_LIMIT, dimension_semantics=("arbitrary",), **extra
        ),
        cost_estimate=cost(flops, all_inputs + all_outs),
        name=name,
    )(*all_inputs)


def tables(longest):
    freq = 10000.0 ** (-np.arange(HEAD, dtype=np.float64) / HEAD)

    def both(places):
        phase = places[:, None] * freq[None, :]
        return jnp.asarray(np.concatenate([np.cos(phase), np.sin(phase)], axis=1), F32)

    return both(np.arange(CHUNK)), both(np.arange(0, longest, CHUNK))


class Layout:
    def __init__(self, lengths, peers, count):
        self.lengths, self.peers, self.count = lengths, peers, count
        self.me = lax.axis_index("mp")
        self.offset = self.me * count

    def begin(self, first):
        begin = start = jnp.int32(0)
        for i in range(self.lengths.shape[1]):
            begin = jnp.where(first >= start, start, begin)
            start = start + self.lengths[0, i]
        return begin

    def first(self, c):
        return self.offset + c * CHUNK

    def keep(self, c):
        return jnp.where(self.begin(self.first(c)) < self.first(c), 1.0, 0.0)

    def before(self, c):
        return jnp.where(self.begin(self.first(c)) < self.offset, 1.0, 0.0)

    def after(self, c):
        last = self.begin(self.offset + self.count - CHUNK)
        return jnp.where(last <= self.first(c), 1.0, 0.0) * jnp.where(self.me < self.peers - 1, 1.0, 0.0)

    def alive(self, c, width):
        end = jnp.int32(0)
        for i in range(self.lengths.shape[1]):
            end = end + self.lengths[0, i]
        return (row_index((CHUNK, width)) + self.first(c) < end).astype(F32)

    def angles(self, c, fine, coarse):
        base = self.first(c) - self.begin(self.first(c))
        start = jnp.zeros((1, 2 * HEAD), F32)
        for k in range(coarse.shape[0]):
            start = start + coarse[k : k + 1, :] * jnp.where(base == k * CHUNK, 1.0, 0.0)
        cb, sb = start[:, :HEAD], start[:, HEAD:]
        cf, sf = fine[:, :HEAD], fine[:, HEAD:]
        return cf * cb - sf * sb, sf * cb + cf * sb


def normed_of(hid):
    x = hid[...].astype(F32)
    return (x * scale_of(x)).astype(BF16)


def states_chunk(heads, slopes, keep, key, values, state, put):
    for h in range(heads):
        slope = slopes[h]
        faded = (values[:, head_slice(h)] * fade_to_end(slope, HEAD)).astype(BF16)
        old = state[h] * keep
        put(h, old.astype(BF16))
        state[h] = jnp.exp(jnp.full((1, 2 * HEAD), -slope * CHUNK, F32)) * old + nn(faded.T, key(h))


def inside_chunk(heads, slopes, query, key, values, st, table, put):
    for h in range(heads):
        asked = query(h)
        weights = (nt(asked, key(h)) * table(h)).astype(BF16)
        put(h, nn(weights, values(h)) + fade_from_start(slopes[h], HEAD) * nt(asked, st(h)))


def carried_chunk(heads, slopes, layout, c, att, query, came, total):
    reached = layout.before(c)
    lag = (c * CHUNK).astype(F32)
    alive = layout.alive(c, HEAD)
    for h in range(heads):
        fade = jnp.exp(-slopes[h] * (row_index((CHUNK, HEAD)).astype(F32) + (lag + 1.0))) * reached
        total[:, head_slice(h)] = (att(h) + fade * nt(query(h), came[h])) * alive


def mix_chunk(parts, total, sel, wo, hid, att_o, mixt_o, mid_o, sec_o, sect_o):
    attended = total[...]
    att_o[...] = attended.astype(BF16)
    mixed = (attended * scale_of(attended) * sel.astype(F32)).astype(BF16)
    put_turned(mixt_o, mixed, parts)
    middle = hid[...].astype(F32) + nn(mixed, wo)
    mid_o[...] = middle.astype(BF16)
    second = (middle * scale_of(middle)).astype(BF16)
    sec_o[...] = second
    put_turned(sect_o, second, parts)


def state_shape(d):
    return (d // HEAD, HEAD, 2 * HEAD)


def keys_kernel(peers, parts, count, lengths, slopes, hid, wk, wv, fine, coarse, normed_o, turned_o, kpre_o, val_o, st_o, fin_o, state):
    c = pl.program_id(0)
    layout = Layout(lengths, peers, count)

    @pl.when(c == 0)
    def _():
        state[...] = jnp.zeros_like(state)

    normed = normed_of(hid)
    normed_o[...] = normed
    put_turned(turned_o, normed, parts)
    kpre = nn(normed, wk[...])
    kpre_o[...] = kpre.astype(BF16)
    values = nn(normed, wv[...])
    val_o[...] = values.astype(BF16)
    cs, sn = layout.angles(c, fine, coarse)

    def put(h, value):
        st_o[0, h] = value

    key = lambda h: featured(kpre[:, head_slice(h)], cs, sn)
    states_chunk(state.shape[0], slopes, layout.keep(c), key, values, state, put)
    fin_o[...] = state[...].astype(BF16)


def run_keys(peers, lengths, slopes, hidden, wk, wv, angles, parts):
    n, d = hidden.shape
    heads, chunks = d // HEAD, n // CHUNK
    turned = turned_shape(d, n)
    tile = pl.BlockSpec((CHUNK, d), lambda c: (c, 0))
    outs = [struct((n, d)), struct(turned), struct((n, d)), struct((n, d)), struct((chunks,) + state_shape(d)), struct(state_shape(d))]
    return launch(
        functools.partial(keys_kernel, peers, parts, n),
        "keys_values_states",
        chunks,
        [lengths, slopes, hidden, wk, wv, *angles],
        [smem(), smem(), tile, whole_block(wk.shape), whole_block(wv.shape)] + [whole_block(a.shape) for a in angles],
        outs,
        [
            tile,
            pl.BlockSpec(turned[:2] + (CHUNK,), lambda c: (0, 0, c)),
            tile,
            tile,
            pl.BlockSpec((1,) + state_shape(d), lambda c: (c, 0, 0, 0)),
            whole_block(state_shape(d)),
        ],
        [pltpu.VMEM(state_shape(d), F32)],
        4 * n * d * d,
    )


def inside_kernel(peers, count, lengths, slopes, normed, wq, ws, kpre, values, st, fine, coarse, qpre_o, sel_o, att_o):
    c = pl.program_id(0)
    layout = Layout(lengths, peers, count)
    x = normed[...]
    qpre = nn(x, wq[...])
    qpre_o[...] = qpre.astype(BF16)
    sel_o[...] = nn(x, ws[...]).astype(BF16)
    cs, sn = layout.angles(c, fine, coarse)

    def put(h, value):
        att_o[:, head_slice(h)] = value

    inside_chunk(
        st.shape[1],
        slopes,
        lambda h: featured(qpre[:, head_slice(h)], cs, sn),
        lambda h: featured(kpre[:, head_slice(h)].astype(F32), cs, sn),
        lambda h: values[:, head_slice(h)],
        lambda h: st[0, h],
        lambda h: decay_table(slopes[h], False),
        put,
    )


def run_inside(peers, lengths, slopes, normed, wq, ws, kpre, values, st, angles):
    n, d = normed.shape
    chunks = n // CHUNK
    tile = pl.BlockSpec((CHUNK, d), lambda c: (c, 0))
    return launch(
        functools.partial(inside_kernel, peers, n),
        "queries_attention",
        chunks,
        [lengths, slopes, normed, wq, ws, kpre, values, st, *angles],
        [smem(), smem(), tile, whole_block(wq.shape), whole_block(ws.shape), tile, tile]
        + [pl.BlockSpec((1,) + state_shape(d), lambda c: (c, 0, 0, 0))]
        + [whole_block(a.shape) for a in angles],
        [struct((n, d)), struct((n, d)), struct((n, d), F32)],
        [tile, tile, tile],
        [],
        6 * n * d * d,
    )


def mix_kernel(peers, parts, count, lengths, slopes, att, qpre, came, sel, wo, hid, cot, fine, coarse, att_o, mixt_o, mid_o, sec_o, sect_o, cott_o, total):
    c = pl.program_id(0)
    layout = Layout(lengths, peers, count)
    cs, sn = layout.angles(c, fine, coarse)
    carried_chunk(
        came.shape[0],
        slopes,
        layout,
        c,
        lambda h: att[:, head_slice(h)],
        lambda h: featured(qpre[:, head_slice(h)].astype(F32), cs, sn),
        came,
        total,
    )
    mix_chunk(parts, total, sel[...], wo[...], hid, att_o, mixt_o, mid_o, sec_o, sect_o)
    put_turned(cott_o, cot[...], parts)


def run_mix(peers, lengths, slopes, att, qpre, came, sel, wo, hidden, cot, angles, parts):
    n, d = hidden.shape
    chunks = n // CHUNK
    turned = turned_shape(d, n)
    tile = pl.BlockSpec((CHUNK, d), lambda c: (c, 0))
    turned_tile = pl.BlockSpec(turned[:2] + (CHUNK,), lambda c: (0, 0, c))
    return launch(
        functools.partial(mix_kernel, peers, parts, n),
        "carried_mixed_middle",
        chunks,
        [lengths, slopes, att, qpre, came, sel, wo, hidden, cot, *angles],
        [smem(), smem(), tile, tile, whole_block(came.shape), tile, whole_block(wo.shape), tile, tile]
        + [whole_block(a.shape) for a in angles],
        [struct((n, d)), struct(turned), struct((n, d)), struct((n, d)), struct(turned), struct(turned)],
        [tile, turned_tile, tile, tile, turned_tile, turned_tile],
        [pltpu.VMEM((CHUNK, d), F32)],
        3 * n * d * d,
    )


def forward_kernel(chunks, parts, lengths, slopes, hid, cot, fine, coarse, *refs):
    refs = list(refs)
    take = lambda k: [refs.pop(0) for _ in range(k)]
    weights_h = take(5)
    (kpre_o, val_o, st_o, qpre_o, sel_o) = take(5)
    (turned_o, att_o, mixt_o, mid_o, sec_o, sect_o, cott_o, came_o) = take(8)
    (weights, normed, kpre, val, st, qpre, sel, att, state, final, came, total, keyed, asked, table) = take(15)
    (load_sems, out_sems, state_sems) = take(3)
    heads = state.shape[0]
    step = pl.program_id(0)
    c = lax.rem(step, chunks)
    here = pl.ds(pl.multiple_of(c * CHUNK, CHUNK), CHUNK)
    layout = Layout(lengths, 2, chunks * CHUNK)
    loads = [pltpu.make_async_copy(w, weights.at[i], load_sems.at[i]) for i, w in enumerate(weights_h)]
    saves = [
        pltpu.make_async_copy(src, dst, out_sems.at[i])
        for i, (src, dst) in enumerate([(kpre, kpre_o), (val, val_o), (st, st_o), (qpre, qpre_o), (sel, sel_o)])
    ]
    exchange = remote(final, came, state_sems.at[0], state_sems.at[1], "mp", 1)

    @pl.when(step == 0)
    def _():
        for copy in loads:
            copy.start()
        state[...] = jnp.zeros_like(state)
        for copy in loads[:2]:
            copy.wait()

    @pl.when(step < chunks)
    def _():
        x = normed_of(hid)
        normed[here, :] = x
        put_turned(turned_o, x, parts)
        keys = nn(x, weights[0])
        kpre[here, :] = keys.astype(BF16)
        values = nn(x, weights[1])
        val[here, :] = values.astype(BF16)
        cs, sn = layout.angles(c, fine, coarse)

        def put(h, value):
            st[c, h] = value

        def key(h):
            value = featured(keys[:, head_slice(h)], cs, sn)
            keyed[here, feature_slice(h)] = value
            return value

        states_chunk(heads, slopes, layout.keep(c), key, values, state, put)

    @pl.when(step == chunks - 1)
    def _():
        final[...] = state[...].astype(BF16)
        exchange.start()
        for copy in saves[:3]:
            copy.start()

    @pl.when(step == chunks)
    def _():
        for h in range(heads):
            table[h] = decay_table(slopes[h], False)
        for copy in loads[2:4]:
            copy.wait()

    @pl.when(jnp.logical_and(step >= chunks, step < 2 * chunks))
    def _():
        x = normed[here, :]
        queries = nn(x, weights[2])
        qpre[here, :] = queries.astype(BF16)
        sel[here, :] = nn(x, weights[3]).astype(BF16)
        cs, sn = layout.angles(c, fine, coarse)

        def put(h, value):
            att[here, head_slice(h)] = value

        def query(h):
            value = featured(queries[:, head_slice(h)], cs, sn)
            asked[here, feature_slice(h)] = value
            return value

        inside_chunk(
            heads,
            slopes,
            query,
            lambda h: keyed[here, feature_slice(h)],
            lambda h: val[here, head_slice(h)],
            lambda h: st[c, h],
            lambda h: table[h],
            put,
        )
        put_turned(cott_o, cot[...], parts)

    @pl.when(step == 2 * chunks - 1)
    def _():
        for copy in saves[3:]:
            copy.start()

    @pl.when(step == 2 * chunks)
    def _():
        loads[4].wait()
        exchange.wait()
        came_o[...] = came[...]

    @pl.when(step >= 2 * chunks)
    def _():
        carried_chunk(
            heads,
            slopes,
            layout,
            c,
            lambda h: att[here, head_slice(h)],
            lambda h: asked[here, feature_slice(h)],
            came,
            total,
        )
        mix_chunk(parts, total, sel[here, :], weights[4], hid, att_o, mixt_o, mid_o, sec_o, sect_o)

    @pl.when(step == 3 * chunks - 1)
    def _():
        for copy in saves:
            copy.wait()


def run_forward(lengths, slopes, hidden, cot, weights, angles, parts, guests, ident):
    n, d = hidden.shape
    chunks = n // CHUNK
    turned = turned_shape(d, n)
    late = lambda s: jnp.maximum(s - 2 * chunks, 0)
    mid = lambda s: jnp.clip(s - chunks, 0, chunks - 1)
    early = lambda s: jnp.minimum(s, chunks - 1)
    tile = pl.BlockSpec((CHUNK, d), lambda s: (late(s), 0))
    turned_tile = lambda at: pl.BlockSpec(turned[:2] + (CHUNK,), lambda s: (0, 0, at(s)))
    whole = pltpu.VMEM((n, d), BF16)
    return launch(
        functools.partial(forward_kernel, chunks, parts),
        "forward_to_sglu",
        3 * chunks,
        [lengths, slopes, hidden, cot, *angles, *weights],
        [
            smem(),
            smem(),
            pl.BlockSpec((CHUNK, d), lambda s: (jnp.where(s < 2 * chunks, early(s), late(s)), 0)),
            pl.BlockSpec((CHUNK, d), lambda s: (mid(s), 0)),
        ]
        + [whole_block(a.shape) for a in angles]
        + [anywhere()] * 5,
        [struct((n, d)), struct((n, d)), struct((chunks,) + state_shape(d)), struct((n, d)), struct((n, d))]
        + [struct(turned), struct((n, d)), struct(turned), struct((n, d)), struct((n, d)), struct(turned), struct(turned)]
        + [struct(state_shape(d))],
        [anywhere()] * 5
        + [turned_tile(early), tile, turned_tile(late), tile, tile, turned_tile(late), turned_tile(mid)]
        + [whole_block(state_shape(d))],
        [
            pltpu.VMEM((5, d, d), BF16),
            whole,
            whole,
            whole,
            pltpu.VMEM((chunks,) + state_shape(d), BF16),
            whole,
            whole,
            pltpu.VMEM((n, d), F32),
            pltpu.VMEM(state_shape(d), F32),
            pltpu.VMEM(state_shape(d), BF16),
            pltpu.VMEM(state_shape(d), BF16),
            pltpu.VMEM((CHUNK, d), F32),
            pltpu.VMEM((n, 2 * d), BF16),
            pltpu.VMEM((n, 2 * d), BF16),
            pltpu.VMEM((d // HEAD, CHUNK, CHUNK), F32),
            pltpu.SemaphoreType.DMA((5,)),
            pltpu.SemaphoreType.DMA((5,)),
            pltpu.SemaphoreType.DMA((2,)),
        ],
        12 * n * d * d,
        guests=guests,
        ident=ident,
        partners=[("mp", 1)],
    )


def sglu_kernel(chunks, peers, sec, cot, w1, w2, wd, units_o, term_o, part_o):
    step = pl.program_id(0)
    here = pl.ds(pl.multiple_of(lax.rem(step, chunks) * CHUNK, CHUNK), CHUNK)
    left = nn(sec[...], w1[...])
    right = nn(sec[...], w2[...])
    inner = (left * right).astype(BF16)
    upstream = nt(cot[...], wd[...])
    grad_left = (upstream * right).astype(BF16)
    grad_right = (upstream * left).astype(BF16)
    units_o[0] = grad_left
    units_o[1] = grad_right
    units_o[2] = inner
    term = nn(inner, wd[...])
    part = nt(grad_left, w1[...]) + nt(grad_right, w2[...])

    @pl.when(step < chunks)
    def _():
        term_o[here, :] = term
        part_o[here, :] = part

    @pl.when(step >= chunks)
    def _():
        term_o[here, :] += term
        part_o[here, :] += part


def run_sglu(second, cot, w1, w2, wd):
    n, d = second.shape
    peers, _, width = w1.shape
    chunks = n // CHUNK
    tile = pl.BlockSpec((CHUNK, d), lambda s: (lax.rem(s, chunks), 0))
    block = lambda shape: pl.BlockSpec((None,) + shape, lambda s: (lax.div(s, chunks), 0, 0))
    return launch(
        functools.partial(sglu_kernel, chunks, peers),
        "sglu",
        peers * chunks,
        [second, cot, w1, w2, wd],
        [tile, tile, block((d, width)), block((d, width)), block((width, d))],
        [struct((3, peers, n, width)), struct((n, d), F32), struct((n, d), F32)],
        [
            pl.BlockSpec((3, None, CHUNK, width), lambda s: (0, lax.div(s, chunks), lax.rem(s, chunks), 0)),
            whole_block((n, d)),
            whole_block((n, d)),
        ],
        [],
        12 * n * d * width * peers,
    )


def units_kernel(geo, reducer, ride, lengths, slopes, fine, coarse, *refs):
    blocks, cut, d, units, chunks = geo["blocks"], geo["cut"], geo["d"], geo["units"], geo["chunks"]
    refs = list(refs)
    take = lambda k: [refs.pop(0) for _ in range(k)]
    weights_h = take(3)
    (x_h, cot_h, xt_h, cott_h, wo_h) = take(5)
    rows_h = take(4)
    pieces = take(12)
    had_b = take(3)
    rows_out = take(4)
    (et_o, e0_o, sums_o) = take(3)
    pieces = pieces + had_b + take(9)
    (term, part, x, cot, xt, cott, o1, o2, od, c12, cd, inner, grads, state, e0, sums) = take(16)
    (tiles, made, ends) = take(3)
    (sems, own_sems, block_sems, tile_sems, made_sems) = take(5)
    reducer.bind(take(len(reducer.scratch)))
    step = pl.program_id(0)
    ride.before(step, had_b, pieces[15:], refs)
    core = lax.rem(lax.axis_index("dp"), 2)
    eighth = lax.rem(lax.axis_index("dp"), 8)
    heads = state.shape[0]
    layout = Layout(lengths, 2, chunks * CHUNK)

    def fetch(g):
        size = cut if g == 0 else units - cut
        masks = [(0, None, 0), (3, 0, 2), (3, 1, 4), (3, 2, 1), (6, 0, 6), (6, 1, 3), (6, 2, 5), (9, None, 7)]
        copies = []
        for w, region in enumerate((o1, o2, od)):
            rows = d // 8 if w < 2 else size // 8
            for k, (at, inner, mask) in enumerate(masks):
                src = pieces[12 * g + at + w]
                src = src if inner is None else src.at[inner]
                here = pl.ds(pl.multiple_of(flipped(eighth, mask) * rows, 16), rows)
                dst = region.at[here, pl.ds(0, size)] if w < 2 else region.at[here, :]
                copies.append(pltpu.make_async_copy(src, dst, sems.at[g, w, k]))
        return copies

    own = [
        pltpu.make_async_copy(x_h, x, own_sems.at[6]),
        pltpu.make_async_copy(cot_h, cot, own_sems.at[0]),
        pltpu.make_async_copy(xt_h.at[1 - core], xt.at[pl.ds(0, d // 2), :], own_sems.at[1]),
        pltpu.make_async_copy(xt_h.at[core], xt.at[pl.ds(d // 2, d // 2), :], own_sems.at[2]),
        pltpu.make_async_copy(cott_h.at[1 - core], cott.at[pl.ds(0, d // 2), :], own_sems.at[3]),
        pltpu.make_async_copy(cott_h.at[core], cott.at[pl.ds(d // 2, d // 2), :], own_sems.at[4]),
    ]
    out_weight = pltpu.make_async_copy(wo_h, xt, own_sems.at[7])
    saved = pltpu.make_async_copy(sums, sums_o, own_sems.at[5])
    leaving = pltpu.make_async_copy(e0, e0_o, own_sems.at[8])

    def own_block(j):
        slot, here = lax.rem(j, 2), pl.ds(pl.multiple_of(j * HEAD, HEAD), HEAD)
        return [
            pltpu.make_async_copy(weights_h[0].at[:, here], c12.at[slot, :, pl.ds(0, HEAD)], block_sems.at[slot, 0]),
            pltpu.make_async_copy(
                weights_h[1].at[:, here], c12.at[slot, :, pl.ds(2 * HEAD, HEAD)], block_sems.at[slot, 1]
            ),
            pltpu.make_async_copy(weights_h[2].at[here, :], cd.at[slot, pl.ds(0, HEAD), :], block_sems.at[slot, 2]),
        ]

    def rows_at(i):
        return pl.ds(pl.multiple_of((chunks - 1 - i) * CHUNK, CHUNK), CHUNK)

    def tile(i):
        slot = lax.rem(i, 2)
        return [
            pltpu.make_async_copy(src.at[rows_at(i), :], tiles.at[slot, k], tile_sems.at[slot, k])
            for k, src in enumerate(rows_h)
        ]

    def results(i):
        slot = lax.rem(i, 2)
        return [
            pltpu.make_async_copy(made.at[slot, k], dst.at[rows_at(i), :], made_sems.at[slot, k])
            for k, dst in enumerate(rows_out)
        ] + [pltpu.make_async_copy(ends.at[slot], et_o.at[chunks - 1 - i], made_sems.at[slot, 4])]

    turn = cut // HEAD

    @pl.when(step == 0)
    def _():
        for copy in own_block(0) + fetch(0) + own:
            copy.start()
        term[...] = jnp.zeros_like(term)
        part[...] = jnp.zeros_like(part)
        state[...] = jnp.zeros_like(state)
        for copy in fetch(0):
            copy.wait()

    @pl.when(step == turn)
    def _():
        for copy in fetch(1):
            copy.wait()

    @pl.when(step < blocks)
    def _():
        local = step - jnp.where(step >= turn, turn, 0)
        here = pl.ds(pl.multiple_of(local * HEAD, HEAD), HEAD)
        at = lax.rem(step, 2)
        c12[at, :, HEAD : 2 * HEAD] = o1[:, here]
        c12[at, :, 3 * HEAD :] = o2[:, here]
        cd[at, HEAD:, :] = od[here, :]
        for copy in own_block(step):
            copy.wait()

    @pl.when(step < blocks - 1)
    def _():
        for copy in own_block(step + 1):
            copy.start()

    @pl.when(step == turn - 1)
    def _():
        for copy in fetch(1):
            copy.start()

    @pl.when(step == 0)
    def _():
        for copy in own:
            copy.wait()

    @pl.when(step < blocks)
    def _():
        wide, at = 2 * HEAD, lax.rem(step, 2)
        for k in range(chunks):
            here = slice(k * CHUNK, (k + 1) * CHUNK)
            both = nn(x[here, :], c12[at])
            left, right = both[:, :wide], both[:, wide:]
            upstream = nt(cot[here, :], cd[at])
            inner[here, :] = (left * right).astype(BF16)
            grads[here, :wide] = (upstream * right).astype(BF16)
            grads[here, wide:] = (upstream * left).astype(BF16)
        slot = 0
        both = nn(xt[...], grads[...]).astype(BF16)
        down = nn(cott[...], inner[...]).astype(BF16)
        for k, buffer in enumerate((reducer.given, reducer.kept)):
            here = slice(k * (d // 2), (k + 1) * (d // 2))
            buffer[slot, 0] = both[here, :wide]
            buffer[slot, 1] = both[here, wide:]
            buffer[slot, 2] = down[here, :]
            if k == 0:
                reducer.begin(step)
        term[...] += nn(inner[...], cd[at])
        part[...] += nt(grads[...], c12[at])

    @pl.when(step == blocks - 1)
    def _():
        out_weight.start()
        for copy in tile(0):
            copy.start()

    @pl.when(step == blocks)
    def _():
        out_weight.wait()

    @pl.when(jnp.logical_and(step >= blocks, step < blocks + chunks))
    def _():
        i = step - blocks
        c, slot = chunks - 1 - i, lax.rem(i, 2)
        here = pl.ds(pl.multiple_of(c * CHUNK, CHUNK), CHUNK)
        for copy in tile(i):
            copy.wait()

        @pl.when(i < chunks - 1)
        def _():
            for copy in tile(i + 1):
                copy.start()

        @pl.when(i >= 2)
        def _():
            for copy in results(i - 2):
                copy.wait()

        cs, sn = layout.angles(c, fine, coarse)
        mid, sel, att, qpre = [tiles.at[slot, k] for k in range(4)]
        after_chunk(
            layout, c, heads, slopes, term[here, :], part[here, :], cot[here, :], mid, sel, att, xt[...], qpre, cs, sn,
            *[made.at[slot, k] for k in range(4)], ends.at[pl.ds(slot, 1)], state,
        )
        for copy in results(i):
            copy.start()

    @pl.when(step == blocks + chunks - 1)
    def _():
        e0[...] = state[...].astype(BF16)
        leaving.start()

    ride.after(step, had_b, pieces[15:], refs)
    reducer.run(step, sums)

    @pl.when(step == reducer.last)
    def _():
        saved.start()
        for i in range(chunks - 2, chunks):
            for copy in results(i):
                copy.wait()
        leaving.wait()
        saved.wait()


def run_units(lengths, slopes, matrices, second, cot, second_t, cot_t, rows_in, angles, wo, pieces, ride, cut, depth, ident):
    n, d = second.shape
    chunks = n // CHUNK
    units = matrices[0].shape[1]
    blocks = units // HEAD
    rows = d // (4 * depth)
    reducer = Reducer(0, blocks, 3, depth, rows, (0, 2, 4, 6), 2, (4, 3, 2, 1), (1, 1, 2))
    geo = dict(blocks=blocks, cut=cut, d=d, units=units, chunks=chunks)
    turned = pltpu.VMEM((d, n), BF16)
    size = max(cut, units - cut)
    sums = (3, rows, units)
    return launch(
        functools.partial(units_kernel, geo, reducer, ride),
        "sglu_and_gradients",
        max(reducer.last, blocks + chunks - 1) + 1,
        [lengths, slopes, *angles]
        + list(matrices)
        + [second, cot, second_t, cot_t, wo]
        + list(rows_in)
        + list(pieces)
        + ride.inputs,
        [smem(), smem()] + [once(a.shape) for a in angles] + [anywhere()] * (12 + len(pieces) + len(ride.inputs)),
        [struct((n, d))] * 4
        + [struct((chunks,) + state_shape(d)), struct(state_shape(d)), struct(sums, F32)]
        + ride.outs,
        [anywhere()] * (7 + len(ride.outs)),
        [
            pltpu.VMEM((n, d), F32),
            pltpu.VMEM((n, d), F32),
            pltpu.VMEM((n, d), BF16),
            pltpu.VMEM((n, d), BF16),
            turned,
            turned,
            pltpu.VMEM((d, size), BF16),
            pltpu.VMEM((d, size), BF16),
            pltpu.VMEM((size, d), BF16),
            pltpu.VMEM((2, d, 4 * HEAD), BF16),
            pltpu.VMEM((2, 2 * HEAD, d), BF16),
            pltpu.VMEM((n, 2 * HEAD), BF16),
            pltpu.VMEM((n, 4 * HEAD), BF16),
            pltpu.VMEM(state_shape(d), F32),
            pltpu.VMEM(state_shape(d), BF16),
            pltpu.VMEM(sums, F32),
            pltpu.VMEM((2, 4, CHUNK, d), BF16),
            pltpu.VMEM((2, 4, CHUNK, d), BF16),
            pltpu.VMEM((2,) + state_shape(d), BF16),
            pltpu.SemaphoreType.DMA((2, 3, 8)),
            pltpu.SemaphoreType.DMA((9,)),
            pltpu.SemaphoreType.DMA((2, 3)),
            pltpu.SemaphoreType.DMA((2, 4)),
            pltpu.SemaphoreType.DMA((2, 5)),
        ]
        + reducer.scratch
        + ride.scratch,
        36 * n * d * units,
        partners=reducer.partners + ride.partners,
        ident=ident,
    )[:7]


def after_chunk(layout, c, heads, slopes, term, part, cot, mid, sel, att, wo, qpre, cs, sn, out_o, gmid_o, pair_o, gatt_o, et_o, state):
    middle = mid[...].astype(F32)
    out_o[...] = (middle + term).astype(BF16)
    grad_middle = cot.astype(F32) + norm_back(middle, scale_of(middle), part)
    branch = grad_middle.astype(BF16)
    gmid_o[...] = branch
    grad_mixed = nt(branch, wo)
    attended = att[...].astype(F32)
    scale = scale_of(attended)
    pair_o[...] = (grad_mixed * attended * scale).astype(BF16)
    grad_att = norm_back(attended, scale, grad_mixed * sel[...].astype(F32)) * layout.alive(c, 1)
    gatt_o[...] = grad_att.astype(BF16)
    keep = layout.keep(c)
    for h in range(heads):
        slope = slopes[h]
        query = featured(qpre[:, head_slice(h)].astype(F32), cs, sn)
        faded = (grad_att[:, head_slice(h)] * fade_from_start(slope, HEAD)).astype(BF16)
        old = state[h]
        et_o[0, h] = old.astype(BF16)
        state[h] = keep * (
            jnp.exp(jnp.full((1, 2 * HEAD), -slope * CHUNK, F32)) * old + nn(faded.T, query)
        )


def after_kernel(peers, count, lengths, slopes, term, part, cot, mid, sel, att, wo, qpre, fine, coarse, out_o, gmid_o, gsel_o, gatt_o, et_o, e0_o, state):
    step = pl.program_id(0)
    c = count // CHUNK - 1 - step
    layout = Layout(lengths, peers, count)

    @pl.when(step == 0)
    def _():
        state[...] = jnp.zeros_like(state)

    cs, sn = layout.angles(c, fine, coarse)
    after_chunk(
        layout, c, state.shape[0], slopes, term[...], part[...], cot[...], mid, sel, att, wo[...], qpre, cs, sn,
        out_o, gmid_o, gsel_o, gatt_o, et_o, state,
    )
    e0_o[...] = state[...].astype(BF16)


def run_after(peers, lengths, slopes, term, part, cot, mid, sel, att, wo, qpre, angles):
    n, d = cot.shape
    chunks = n // CHUNK
    back = lambda s: chunks - 1 - s
    tile = pl.BlockSpec((CHUNK, d), lambda s: (back(s), 0))
    return launch(
        functools.partial(after_kernel, peers, n),
        "output_and_row_gradients",
        chunks,
        [lengths, slopes, term, part, cot, mid, sel, att, wo, qpre, *angles],
        [smem(), smem()] + [tile] * 6 + [whole_block(wo.shape), tile] + [whole_block(a.shape) for a in angles],
        [struct((n, d))] * 4 + [struct((chunks,) + state_shape(d)), struct(state_shape(d))],
        [tile] * 4
        + [pl.BlockSpec((1,) + state_shape(d), lambda s: (back(s), 0, 0, 0)), whole_block(state_shape(d))],
        [pltpu.VMEM(state_shape(d), F32)],
        3 * n * d * d,
    )


def weights_kernel(items, peers, *refs):
    item = lax.div(pl.program_id(0), peers)
    lefts, right, out = refs[:-2], refs[-2], refs[-1]
    for i, left in enumerate(lefts):

        @pl.when(functools.reduce(jnp.logical_or, [item == t for t, w in enumerate(items) if w == i]))
        def _(left=left):
            block = left[...]
            block = block.reshape(-1, block.shape[-1])
            out[...] = nn(block, right[...]).astype(BF16)


def run_weights(lefts, items, rights, right_spec, peers, width):
    _, half, n = lefts[0].shape
    shape = (peers, len(items), 2 * half, width)
    which = lambda s: (lax.div(s, peers), lax.rem(s, peers))
    (out,) = launch(
        functools.partial(weights_kernel, items, peers),
        "weight_gradients",
        peers * len(items),
        list(lefts) + [rights],
        [whole_block(left.shape) for left in lefts] + [right_spec(which)],
        [struct(shape)],
        [pl.BlockSpec((None, None) + shape[2:], lambda s: (which(s)[1], which(s)[0], 0, 0))],
        [],
        4 * n * half * width * len(items) * peers,
    )
    return out


def head_back(slope, table, turned, qpre, kpre, value, grad, state, ending, cs, sn):
    qp, kp = qpre.astype(F32), kpre.astype(F32)
    qs, ks = sigmoid(qp), sigmoid(kp)
    qa, ka = qp * qs, kp * ks
    query = jnp.concatenate([qa * cs, qa * sn], axis=-1).astype(BF16)
    key = jnp.concatenate([ka * cs, ka * sn], axis=-1).astype(BF16)
    state, ending = state.astype(BF16), ending.astype(BF16)
    scores_t = (nt(key, query) * turned).astype(BF16)
    slope_s = (nt(grad, value) * table).astype(BF16)
    slope_t = (nt(value, grad) * turned).astype(BF16)
    start = fade_from_start(slope, HEAD)
    end = fade_to_end(slope, HEAD)
    grad_start = (grad.astype(F32) * start).astype(BF16)
    value_end = (value.astype(F32) * end).astype(BF16)
    dq = nn(slope_s, key) + nn(grad_start, state)
    dk = nn(slope_t, query) + nn(value_end, ending)
    dv = nn(scores_t, grad) + end * nt(key, ending)
    dq = dq[:, :HEAD] * cs + dq[:, HEAD:] * sn
    dk = dk[:, :HEAD] * cs + dk[:, HEAD:] * sn
    gq = (dq * (qs * (1.0 + qp * (1.0 - qs)))).astype(BF16)
    gk = (dk * (ks * (1.0 + kp * (1.0 - ks)))).astype(BF16)
    return gq, gk, dv.astype(BF16)


def attention_back_kernel(peers, count, lengths, slopes, qpre, kpre, values, gatt, st, came, et, left, fine, coarse, grads_o):
    chunks = count // CHUNK
    layout = Layout(lengths, peers, count)
    pair, c = lax.div(pl.program_id(0), chunks), lax.rem(pl.program_id(0), chunks)
    cs, sn = layout.angles(c, fine, coarse)
    before, after = layout.before(c), layout.after(c)
    span = (CHUNK * c).astype(F32)
    rest = (CHUNK * (chunks - 1 - c)).astype(F32)
    for h in range(2):
        slope = slopes[2 * pair + h]
        cols = head_slice(h)
        lane = jnp.zeros((1, 2 * HEAD), F32)
        state = st[0, h].astype(F32) + came[h].astype(F32) * (jnp.exp(lane - slope * span) * before)
        ending = et[0, h].astype(F32) + left[h].astype(F32) * (jnp.exp(lane - slope * rest) * after)
        table, turned = decay_table(slope, False), decay_table(slope, True)
        three = head_back(
            slope, table, turned, qpre[:, cols], kpre[:, cols], values[:, cols], gatt[:, cols], state, ending, cs, sn
        )
        for i in range(3):
            grads_o[i, :, cols] = three[i]


def run_attention_back(peers, lengths, slopes, qpre, kpre, values, gatt, st, came, et, left, angles):
    n, d = qpre.shape
    chunks = n // CHUNK
    pair = lambda s: lax.div(s, chunks)
    chunk = lambda s: lax.rem(s, chunks)
    tile = pl.BlockSpec((CHUNK, 2 * HEAD), lambda s: (chunk(s), pair(s)))
    states = pl.BlockSpec((1, 2, HEAD, 2 * HEAD), lambda s: (chunk(s), pair(s), 0, 0))
    ends = pl.BlockSpec((2, HEAD, 2 * HEAD), lambda s: (pair(s), 0, 0))
    return launch(
        functools.partial(attention_back_kernel, peers, n),
        "attention_backward",
        chunks * d // (2 * HEAD),
        [lengths, slopes, qpre, kpre, values, gatt, st, came, et, left, *angles],
        [smem(), smem(), tile, tile, tile, tile, states, ends, states, ends] + [whole_block(a.shape) for a in angles],
        [struct((3, n, d))],
        [pl.BlockSpec((3, CHUNK, 2 * HEAD), lambda s: (0, chunk(s), pair(s)))],
        [],
        18 * n * 256 * d,
    )


def projections_kernel(geo, outer, inner, lengths, slopes, *refs):
    chunks, blocks, d, n = geo["chunks"], geo["blocks"], geo["d"], geo["n"]
    refs = list(refs)
    take = lambda k: [refs.pop(0) for _ in range(k)]
    arrays_h = take(6)
    (came_h, leaving, fine, coarse, gsel_h, hid_h, gmid_h, mixt_h, normt_h) = take(9)
    weights_h = take(4)
    hidden_o, out, out2 = take(3)
    (qpre, kpre, val, gatt, st, et, came, gsel, gmid) = take(9)
    grads, block, decays, mixt, normt, left, sems, late_sems, state_sems = take(9)
    outer.bind(take(len(outer.scratch)))
    inner.bind(refs)
    step = pl.program_id(0)
    core = lax.rem(lax.axis_index("dp"), 2)
    me = lax.axis_index("mp")
    layout = Layout(lengths, 2, n)
    loads = [
        pltpu.make_async_copy(gmid_h, gmid, sems.at[4]),
        pltpu.make_async_copy(mixt_h.at[1 - core], mixt.at[pl.ds(0, d // 2), :], sems.at[0]),
        pltpu.make_async_copy(mixt_h.at[core], mixt.at[pl.ds(d // 2, d // 2), :], sems.at[1]),
        pltpu.make_async_copy(gsel_h, gsel, sems.at[5]),
        pltpu.make_async_copy(normt_h.at[1 - core], normt.at[pl.ds(0, d // 2), :], sems.at[2]),
        pltpu.make_async_copy(normt_h.at[core], normt.at[pl.ds(d // 2, d // 2), :], sems.at[3]),
    ]
    more = [
        pltpu.make_async_copy(src, dst, sems.at[6 + i])
        for i, (src, dst) in enumerate(zip(arrays_h + [came_h], (qpre, kpre, val, gatt, st, et, came)))
    ]
    select = pltpu.make_async_copy(weights_h[3], mixt, sems.at[13])

    def replaced(j):
        copies = []
        for side in range(2):
            cols = pl.ds(pl.multiple_of(((me if side == 0 else 1 - me) * blocks + j) * HEAD, HEAD), HEAD)
            for i, (src, dst) in enumerate(zip(weights_h[:3] + [hid_h], (qpre, kpre, gatt, val))):
                copies.append(pltpu.make_async_copy(src.at[:, cols], dst.at[:, cols], late_sems.at[j, side, i]))
        return copies

    def exchange(j):
        pair = []
        for k in range(2):
            h = k * blocks + j
            pair.append(remote(leaving.at[h], left.at[h], state_sems.at[0, h], state_sems.at[1, h], "mp", 1))
        return pair

    @pl.when(step == 0)
    def _():
        for j in range(blocks):
            for copy in exchange(j):
                copy.start()
        for copy in loads + more:
            copy.start()
        for copy in loads:
            copy.wait()

    @pl.when(step < blocks)
    def _():
        slot = lax.rem(step, 2)
        mine = pl.ds(pl.multiple_of((me * blocks + step) * HEAD, HEAD), HEAD)
        theirs = pl.ds(pl.multiple_of(((1 - me) * blocks + step) * HEAD, HEAD), HEAD)
        gb = jnp.concatenate([gmid[:, mine], gmid[:, theirs]], axis=1)
        gs = jnp.concatenate([gsel[:, mine], gsel[:, theirs]], axis=1)
        made = [nn(mixt[...], gb).astype(BF16), nn(normt[...], gs).astype(BF16)]
        for k, buffer in enumerate((outer.given, outer.kept)):
            for i in range(2):
                buffer[slot, i] = made[i][k * (d // 2) : (k + 1) * (d // 2), :]
            if k == 0:
                outer.begin(step)

    @pl.when(jnp.logical_and(step >= blocks, step < 2 * blocks))
    def _():
        j = step - blocks
        for copy in exchange(j):
            copy.wait()
        for side in range(2):
            slope = slopes[(me if side == 0 else 1 - me) * blocks + j]
            for k in range(2):
                decays[side, k] = decay_table(slope, k == 1)

        def one(c, carry):
            here = pl.ds(pl.multiple_of(c * CHUNK, CHUNK), CHUNK)
            cs, sn = layout.angles(c, fine, coarse)
            before, after = layout.before(c), layout.after(c)
            span = (CHUNK * c).astype(F32)
            rest = (CHUNK * (chunks - 1 - c)).astype(F32)
            for side in range(2):
                h = (me if side == 0 else 1 - me) * blocks + j
                slope = slopes[h]
                cols = pl.ds(pl.multiple_of(h * HEAD, HEAD), HEAD)
                four = [ref[here, cols] for ref in (qpre, kpre, val, gatt)]
                lane = jnp.zeros((1, 2 * HEAD), F32)
                state = st[c, h].astype(F32) + came[h].astype(F32) * (jnp.exp(lane - slope * span) * before)
                ending = et[c, h].astype(F32) + left[h].astype(F32) * (jnp.exp(lane - slope * rest) * after)
                three = head_back(
                    slope, decays[side, 0], decays[side, 1], *four, state, ending, cs, sn
                )
                for i in range(3):
                    block[here, head_slice(2 * i + side)] = three[i]
                    grads[i, here, cols] = three[i]
            return carry

        lax.fori_loop(0, chunks, one, 0)
        slot = lax.rem(j, 2)
        made = nn(normt[...], block[...]).astype(BF16)
        for k, buffer in enumerate((inner.given, inner.kept)):
            for i in range(3):
                buffer[slot, i] = made[k * (d // 2) : (k + 1) * (d // 2), feature_slice(i)]
            if k == 0:
                inner.begin(j)
        for copy in replaced(j):
            copy.start()

    @pl.when(step == blocks - 1)
    def _():
        select.start()
        for copy in more:
            copy.wait()

    @pl.when(step == 2 * blocks)
    def _():
        select.wait()
        for j in range(blocks):
            for copy in replaced(j):
                copy.wait()

    @pl.when(jnp.logical_and(step >= 2 * blocks, step < 2 * blocks + chunks))
    def _():
        here = pl.ds(pl.multiple_of((step - 2 * blocks) * CHUNK, CHUNK), CHUNK)
        total = nt(gsel[here, :], mixt[...])
        for i, w in enumerate((qpre, kpre, gatt)):
            total = total + nt(grads[i, here, :], w[...])
        x = val[here, :].astype(F32)
        hidden_o[...] = (gmid[here, :].astype(F32) + norm_back(x, scale_of(x), total)).astype(BF16)

    outer.run(step, out)
    inner.run(step, out2)


def run_projections(lengths, slopes, qpre, kpre, values, gatt, st, et, came, leaving, angles, gsel, hidden, gmid, mixed_t, normed_t, weights, depth, ident):
    n, d = qpre.shape
    heads, chunks = d // HEAD, n // CHUNK
    blocks = heads // 2
    rows = d // (4 * depth)
    outer = Reducer(0, blocks, 2, depth, rows, (1, 4, 5, 6), 4, (1, 2, 3, 4), (2, 2))
    inner = Reducer(blocks, blocks, 3, depth, rows, (1, 2, 3, 4), 4, (1, 2, 3, 4), (2, 2, 2))
    steps = max(outer.last, inner.last, 2 * blocks + chunks - 1) + 1
    geo = dict(chunks=chunks, blocks=blocks, d=d, n=n)
    late = lambda s: jnp.clip(s - 2 * blocks, 0, chunks - 1)
    whole = pltpu.VMEM((n, d), BF16)
    states = pltpu.VMEM((chunks,) + state_shape(d), BF16)
    one = pltpu.VMEM(state_shape(d), BF16)
    turned = pltpu.VMEM((d, n), BF16)
    return launch(
        functools.partial(projections_kernel, geo, outer, inner),
        "attention_backward_and_gradients",
        steps,
        [lengths, slopes, qpre, kpre, values, gatt, st, et, came, leaving, *angles]
        + [gsel, hidden, gmid, mixed_t, normed_t]
        + list(weights),
        [smem(), smem()] + [anywhere()] * 8 + [once(a.shape) for a in angles] + [anywhere()] * 9,
        [struct((n, d)), struct((2, rows, d // 2), F32), struct((3, rows, d // 2), F32)],
        [
            pl.BlockSpec((CHUNK, d), lambda s: (late(s), 0)),
            whole_block((2, rows, d // 2)),
            whole_block((3, rows, d // 2)),
        ],
        [whole] * 4
        + [states, states, one, whole, whole]
        + [
            pltpu.VMEM((3, n, d), BF16),
            pltpu.VMEM((n, 6 * HEAD), BF16),
            pltpu.VMEM((2, 2, CHUNK, CHUNK), F32),
            turned,
            turned,
            one,
            pltpu.SemaphoreType.DMA((14,)),
            pltpu.SemaphoreType.DMA((blocks, 2, 4)),
            pltpu.SemaphoreType.DMA((2, heads)),
        ]
        + outer.scratch
        + inner.scratch,
        30 * n * d * d,
        partners=outer.partners,
        ident=ident,
    )


def input_kernel(wq, wk, wv, ws, grads, gsel, hid, gmid, out):
    total = nt(grads[0], wq[...]) + nt(grads[1], wk[...]) + nt(grads[2], wv[...]) + nt(gsel[...], ws[...])
    x = hid[...].astype(F32)
    out[...] = (gmid[...].astype(F32) + norm_back(x, scale_of(x), total)).astype(BF16)


def run_input(weights, grads, gsel, hidden, gmid):
    n, d = hidden.shape
    tile = pl.BlockSpec((CHUNK, d), lambda c: (c, 0))
    return launch(
        input_kernel,
        "input_gradient",
        n // CHUNK,
        list(weights) + [grads, gsel, hidden, gmid],
        [whole_block(w.shape) for w in weights]
        + [
            pl.BlockSpec((3, CHUNK, d), lambda c: (0, c, 0)),
            tile,
            tile,
            tile,
        ],
        [struct((n, d))],
        [tile],
        [],
        8 * n * d * d,
    )


def reduced(lefts, items, rights, spec, peers, width):
    full = run_weights(lefts, items, rights, spec, peers, width)
    parts = lax.axis_size("dp")
    full = full.reshape(peers, len(items), 2, parts // 2, -1, width)
    full = jnp.swapaxes(full, 2, 3).reshape(peers, len(items), parts, -1, width)
    mine = lax.psum_scatter(full, "dp", scatter_dimension=2, tiled=False)
    return lax.psum_scatter(mine, "mp", scatter_dimension=0, tiled=False).astype(F32)


def per_device(
    hidden_in,
    query_weight,
    key_weight,
    value_weight,
    select_weight,
    out_weight,
    first_weight,
    second_weight,
    down_weight,
    decay_slope,
    doc_lengths,
    cotangent,
):
    count, d = hidden_in.shape
    heads, chunks = d // HEAD, count // CHUNK
    peers, parts = lax.axis_size("mp"), lax.axis_size("dp")
    me = lax.axis_index("mp")
    depth = parts // 4
    group = count * peers
    units = first_weight.shape[1]
    lengths = doc_lengths.astype(jnp.int32)
    angles = tables(group // 2)
    slopes = decay_slope
    matrices = (first_weight, second_weight, down_weight)
    riding = peers == 2

    if riding:
        cut = units // 256 * 128
        ranges = [(0, cut), (cut, units - cut)]
    else:
        ranges = [(0, units)]

    def like(arrays, count=None):
        return [struct(a.shape if count is None else (count,) + a.shape) for a in arrays]

    def over_mp(g):
        low, size = ranges[g]

        def source(w):
            def src(i, o):
                eighth = lax.rem(lax.axis_index("dp"), 8)
                if w < 2:
                    rows = d // 8
                    return i[w].at[pl.ds(pl.multiple_of(eighth * rows, 16), rows), pl.ds(low, size)]
                rows = size // 8
                return i[w].at[pl.ds(pl.multiple_of(low + eighth * rows, 16), rows), :]

            return src

        outs = [struct((d // 8, size)), struct((d // 8, size)), struct((size // 8, d))]
        return outs, [(source(w), lambda i, o, w=w: o[w], "mp", 1) for w in range(3)]

    def near(src, dst):
        return [
            (lambda i, o: src(i, o), lambda i, o: dst(i, o).at[0], "dp", 2),
            (lambda i, o: src(i, o), lambda i, o: dst(i, o).at[1], "dp", 4),
            (lambda i, o: src(i, o), lambda i, o: dst(i, o).at[2], "dp", 1),
        ]

    def far(src, dst, rows, balanced):
        top = -(-rows // 32) * 16 if balanced else 0
        upper, lower = pl.ds(0, top), pl.ds(top, rows - top)
        over_x = (lambda i, o: src(i, o).at[1, upper, :], lambda i, o: dst(i, o).at[0, upper, :], "dp", 2)
        return ([over_x] if balanced else []) + [
            (lambda i, o: src(i, o).at[0, lower, :], lambda i, o: dst(i, o).at[0, lower, :], "dp", 4),
            (lambda i, o: src(i, o).at[0], lambda i, o: dst(i, o).at[1], "dp", 1),
            (lambda i, o: src(i, o).at[1], lambda i, o: dst(i, o).at[2], "dp", 1),
        ]

    def onward(pieces, out, at, balanced):
        ref = lambda k: lambda i, o: o[k]
        one, two, three = [], [], []
        for w in range(3):
            one += near(pieces(w), ref(at + w))
            two += far(ref(at + w), ref(at + 3 + w), out[w].shape[0], balanced)
            three.append((lambda i, o, w=w: o[at + 3 + w].at[0], ref(at + 6 + w), "dp", 1))
        return like(out, 3) + like(out, 3) + like(out), [one, two, three]

    if riding:
        outs, copies = over_mp(0)
        more, phases = onward(lambda w: lambda i, o: o[w], outs, 3, True)
        outs_b, copies_b = over_mp(1)
        spans = [(0, chunks), (chunks + 1, 2 * chunks), (2 * chunks + 1, 3 * chunks - 2), (3 * chunks - 1,) * 2]
        guests = [
            Carry(matrices, outs + more, [span + (c,) for span, c in zip(spans, [copies] + phases)]),
            Carry(matrices, outs_b, [(chunks + 2, 3 * chunks - 1, copies_b)]),
        ]
        weights = [key_weight, value_weight, query_weight, select_weight, out_weight]
        kpre, values, st, qpre, sel, normed_t, attended, mixed_t, middle, second, second_t, cot_t, came, *got = run_forward(
            lengths, slopes, hidden_in, cotangent, weights, angles, parts, guests, ident=1
        )
    else:
        normed, normed_t, kpre, values, st, final = run_keys(
            peers, lengths, slopes, hidden_in, key_weight, value_weight, angles, parts
        )
        begin, start, last = jnp.int32(0), jnp.int32(0), (me + 1) * count - CHUNK
        for i in range(lengths.shape[1]):
            begin = jnp.where(last >= start, start, begin)
            start = start + lengths[0, i]
        passes = (begin < me * count).astype(F32)
        decay = jnp.exp(-slopes * count)
        finals = lax.all_gather(final, "mp")
        keeps = lax.all_gather(passes.reshape(1), "mp")[:, 0]

        def ahead(k, total):
            new = finals[k].astype(F32) + (keeps[k] * decay)[:, None, None] * total
            return jnp.where(k < me, new, total)

        came = lax.fori_loop(0, peers, ahead, jnp.zeros(final.shape, F32)).astype(BF16)
        qpre, sel, att = run_inside(
            peers, lengths, slopes, normed, query_weight, select_weight, kpre, values, st, angles
        )
        attended, mixed_t, middle, second, second_t, cot_t = run_mix(
            peers, lengths, slopes, att, qpre, came, sel, out_weight, hidden_in, cotangent, angles, parts
        )

    if riding:
        had_b = got[12:15]
        more, phases = onward(lambda w: lambda i, o: i[w], had_b, 0, True)
        ride = Carry(had_b, more, [(0, 1, phases[0]), (2, 2, phases[1]), (3, 3, phases[2])])
        output, grad_middle, grad_sel, grad_att, et, leaving, sglu = run_units(
            lengths, slopes, matrices, second, cotangent, second_t, cot_t, [middle, sel, attended, qpre],
            angles, out_weight, got[:12], ride, ranges[0][1], depth, ident=2,
        )
    else:
        sources = [lax.all_gather(w, "mp") for w in matrices]
        grads, term, part = run_sglu(second, cotangent, *sources)
        units_spec = lambda at: pl.BlockSpec((None, None, count, units), lambda s: at(s) + (0, 0))
        sglu = reduced([second_t, cot_t], (0, 0, 1), grads, units_spec, peers, units)
        output, grad_middle, grad_sel, grad_att, et, leaving = run_after(
            peers, lengths, slopes, term, part, cotangent, middle, sel, attended, out_weight, qpre, angles
        )
    inputs_weights = [query_weight, key_weight, value_weight, select_weight]
    if riding:
        grad_hidden, out_sel, inputs = run_projections(
            lengths, slopes, qpre, kpre, values, grad_att, st, et, came, leaving, angles, grad_sel,
            hidden_in, grad_middle, mixed_t, normed_t, inputs_weights, depth, ident=3,
        )
    else:
        leavings = lax.all_gather(leaving, "mp")

        def behind(step, total):
            k = peers - 1 - step
            new = leavings[k].astype(F32) + (keeps[k] * decay)[:, None, None] * total
            return jnp.where(k > me, new, total)

        left = lax.fori_loop(0, peers, behind, jnp.zeros(leaving.shape, F32)).astype(BF16)
        share = d // peers
        wide_spec = lambda at: pl.BlockSpec((None, count, share), lambda s: (at(s)[0], 0, at(s)[1]))
        pair = jnp.stack([grad_middle, grad_sel])
        out_sel = reduced([mixed_t, normed_t], (0, 1), pair, wide_spec, peers, share)
        (qkv,) = run_attention_back(
            peers, lengths, slopes, qpre, kpre, values, grad_att, st, came, et, left, angles
        )
        inputs = reduced([normed_t], (0, 0, 0), qkv, wide_spec, peers, share)
        (grad_hidden,) = run_input(inputs_weights, qkv, grad_sel, hidden_in, grad_middle)
    return (
        output,
        grad_hidden,
        inputs[0],
        inputs[1],
        inputs[2],
        out_sel[1],
        out_sel[0],
        sglu[0],
        sglu[1],
        jnp.transpose(sglu[2]),
    )


def solution(mesh):
    rows = P(("dp", "mp"), None)
    in_specs = (
        rows,
        P(),
        P(),
        P(),
        P(),
        P(),
        P(None, "mp"),
        P(None, "mp"),
        P("mp", None),
        P(),
        P("dp", None),
        rows,
    )
    out_specs = (rows, rows) + (P("dp", "mp"),) * 7 + (P("mp", "dp"),)
    return jax.shard_map(
        per_device, mesh=mesh, in_specs=in_specs, out_specs=out_specs, check_vma=False
    )
```

```python
import functools

import jax
import jax.numpy as jnp
import numpy as np
from jax import lax
from jax.experimental import pallas as pl
from jax.experimental.pallas import tpu as pltpu
from jax.sharding import PartitionSpec as P

HEAD = 128
CHUNK = 256
EPSILON = 1e-06
BF16 = jnp.bfloat16
F32 = jnp.float32
VMEM_LIMIT = 62 * 1024 * 1024


def nn(left, right):
    return jnp.dot(left, right, preferred_element_type=F32)


def nt(left, right):
    return lax.dot_general(left, right, (((1,), (1,)), ((), ())), preferred_element_type=F32)


def scale_of(values):
    return lax.rsqrt(jnp.mean(values * values, axis=-1, keepdims=True) + EPSILON)


def norm_back(values, scale, upstream):
    return scale * upstream - values * (scale * scale * scale) * jnp.mean(
        values * upstream, axis=-1, keepdims=True
    )


def sigmoid(v):
    return 0.5 * jnp.tanh(0.5 * v) + 0.5


def featured(pre, cos, sin):
    act = pre * sigmoid(pre)
    return jnp.concatenate([act * cos, act * sin], axis=-1).astype(BF16)


def head_slice(h):
    return slice(h * HEAD, (h + 1) * HEAD)


def turned_shape(d, n):
    return (2, d // 2, n)


def put_turned(ref, value, parts):
    turned = value.T
    rows = turned.shape[0] // parts
    for i in range(parts):
        ref[i % 2, (i // 2) * rows : (i // 2 + 1) * rows, :] = turned[i * rows : (i + 1) * rows, :]


def feature_slice(h):
    return slice(2 * h * HEAD, 2 * (h + 1) * HEAD)


def row_index(shape):
    return lax.broadcasted_iota(jnp.int32, shape, 0)


def fade_from_start(slope, width):
    return jnp.exp(-slope * (row_index((CHUNK, width)) + 1).astype(F32))


def fade_to_end(slope, width):
    return jnp.exp(-slope * (CHUNK - 1 - row_index((CHUNK, width))).astype(F32))


def decay_table(slope, transposed):
    rows = lax.broadcasted_iota(jnp.int32, (CHUNK, CHUNK), 0)
    cols = lax.broadcasted_iota(jnp.int32, (CHUNK, CHUNK), 1)
    gap = cols - rows if transposed else rows - cols
    return jnp.where(gap >= 0, jnp.exp(-slope * jnp.maximum(gap, 0).astype(F32)), 0.0)


def plus(*arrays):
    total = arrays[0].astype(F32)
    for a in arrays[1:]:
        total = total + a.astype(F32)
    return total


def smem():
    return pl.BlockSpec(memory_space=pltpu.SMEM)


def anywhere():
    return pl.BlockSpec(memory_space=pl.ANY)


def once(shape):
    zeros = (0,) * len(shape)
    return pl.BlockSpec(shape, lambda *_: zeros, pipeline_mode=pl.Buffered(1))


def whole_block(shape):
    zeros = (0,) * len(shape)
    return pl.BlockSpec(shape, lambda *_: zeros)


def cost(flops, arrays):
    moved = sum(int(np.prod(a.shape)) * jnp.dtype(a.dtype).itemsize for a in arrays)
    return pl.CostEstimate(flops=int(flops), bytes_accessed=moved, transcendentals=0)


def struct(shape, dtype=BF16):
    return jax.ShapeDtypeStruct(tuple(shape), dtype)


def flipped(index, mask):
    bit = 1
    while bit <= mask:
        if mask & bit:
            index = index + bit * (1 - 2 * lax.rem(lax.div(index, bit), 2))
        bit *= 2
    return index


def remote(src, dst, send, recv, axis, mask, where=None):
    return pltpu.make_async_remote_copy(
        src_ref=src,
        dst_ref=dst,
        send_sem=send,
        recv_sem=recv,
        device_id={axis: flipped(lax.axis_index(axis), mask) if where is None else where},
        device_id_type=pl.DeviceIdType.MESH,
    )


def greet(partners):
    barrier = pltpu.get_barrier_semaphore()
    for axis, mask in partners:
        pl.semaphore_signal(
            barrier,
            inc=1,
            device_id={axis: flipped(lax.axis_index(axis), mask)},
            device_id_type=pl.DeviceIdType.MESH,
        )
    pl.semaphore_wait(barrier, len(partners))


class Carry:
    def __init__(self, inputs, outs, phases):
        self.inputs, self.outs, self.phases = list(inputs), list(outs), phases
        count = sum(len(p[2]) for p in phases)
        self.scratch = [pltpu.SemaphoreType.DMA((count,)), pltpu.SemaphoreType.DMA((count,))]
        self.partners = [(c[2], c[3]) for p in phases for c in p[2]]

    def copies(self, which, ins, outs, scratch):
        at = sum(len(p[2]) for p in self.phases[:which])
        send, recv = scratch
        for k, (src, dst, axis, mask) in enumerate(self.phases[which][2]):
            yield remote(src(ins, outs), dst(ins, outs), send.at[at + k], recv.at[at + k], axis, mask)

    def before(self, step, ins, outs, scratch):
        for p, phase in enumerate(self.phases):

            @pl.when(step == phase[0])
            def _(p=p):
                for copy in self.copies(p, ins, outs, scratch):
                    copy.start()

    def after(self, step, ins, outs, scratch):
        for p, phase in enumerate(self.phases):

            @pl.when(step == phase[1])
            def _(p=p):
                for copy in self.copies(p, ins, outs, scratch):
                    copy.wait()


class Reducer:
    KINDS = 8

    def __init__(self, start, blocks, items, depth, rows, delays, slots, order, over_x, offset=0):
        self.offset = offset
        self.start, self.blocks, self.items = start, blocks, items
        self.slots, self.order = slots, order
        self.made = 2 if delays[0] else 1
        self.depth, self.rows, self.delays = depth, rows, delays
        self.upper = [(t, z) for t in range(items) for z in range(over_x[t])]
        self.lower = [(t, z) for t in range(items) for z in range(over_x[t], depth)]
        n, wide = 2 * depth * rows, 2 * HEAD
        buf = lambda *shape: pltpu.VMEM(shape, BF16)
        up, low = len(self.upper), len(self.lower)
        pair, flat = (up, rows, wide), (2, low, rows, HEAD)
        self.scratch = [
            buf(self.made, items, n, wide),
            buf(self.made, items, n, wide),
            buf(4 if delays[0] else 2, items, n, wide),
            buf(slots, *pair),
            buf(slots, *pair),
            buf(4, *pair),
            buf(slots, *flat),
            buf(slots, *flat),
            buf(4, *flat),
            buf(slots, up, rows, HEAD),
            buf(slots, up, rows, HEAD),
            buf(4, up, rows, HEAD),
            buf(slots, low, rows, HEAD),
            buf(slots, low, rows, HEAD),
            buf(4, low, rows, HEAD),
            buf(slots, depth, items, rows, HEAD),
            buf(4, depth - 1, items, rows, HEAD),
            pltpu.SemaphoreType.DMA((self.KINDS, blocks)),
            pltpu.SemaphoreType.DMA((self.KINDS, blocks)),
        ]
        self.partners = [("dp", 1), ("dp", 2), ("mp", 1)] + [("dp", 4 * k) for k in range(1, depth)]
        self.last = start + blocks - 1 + delays[3]

    def bind(self, scratch, places):
        self.refs = scratch
        self.given, self.kept = scratch[:2]
        self.x, self.z, self.where, self.partner_z = places

    @staticmethod
    def places(depth):
        dp, me = lax.axis_index("dp"), lax.axis_index("mp")
        z = lax.div(dp, 4)
        x = lax.div(dp - 4 * z, 2)
        core = dp - 4 * z - 2 * x
        where = {("dp", 1): dp + 1 - 2 * core, ("dp", 2): dp + 2 - 4 * x, ("mp", 1): 1 - me}
        partner_z = {}
        for k in range(1, depth):
            partner_z[k] = flipped(z, k)
            where["dp", 4 * k] = dp + 4 * (partner_z[k] - z)
        return x, z, where, partner_z

    def copies(self, stage, j):
        (given, kept, got, ps, pk, pr, qs, qk, qr, ps2, pk2, pr2, qs2, qk2, qr2, line, zr, send, recv) = self.refs
        slot, four = lax.rem(j, self.slots), lax.rem(j, 4)
        if stage == 0:
            plan = [(0, given.at[lax.rem(j, self.made)], got.at[lax.rem(j, got.shape[0])], "dp", 1)]
        elif stage == 1:
            plan = [(1, ps.at[slot], pr.at[four], "dp", 2), (2, qs.at[slot], qr.at[four], "mp", 1)]
        elif stage == 2:
            plan = [(3, ps2.at[slot], pr2.at[four], "mp", 1), (4, qs2.at[slot], qr2.at[four], "dp", 2)]
        else:
            plan = [
                (4 + k, line.at[slot, self.partner_z[k]], zr.at[four, k - 1], "dp", 4 * k)
                for k in range(1, self.depth)
            ]
        return [
            remote(src, dst, send.at[i, j], recv.at[i, j], axis, mask, self.where[axis, mask])
            for i, src, dst, axis, mask in plan
        ]

    def begin(self, j):
        for copy in self.copies(0, j):
            copy.start()

    def run(self, step, out):
        for stage in self.order:
            j = step - self.start - self.delays[stage - 1]

            @pl.when(jnp.logical_and(j >= 0, j < self.blocks))
            def _(stage=stage, j=j):
                for copy in self.copies(stage - 1, j):
                    copy.wait()
                self.add(stage, j, out)
                if stage < 4:
                    for copy in self.copies(stage, j):
                        copy.start()

    def add(self, stage, j, out):
        (given, kept, got, ps, pk, pr, qs, qk, qr, ps2, pk2, pr2, qs2, qk2, qr2, line, zr, send, recv) = self.refs
        slot, four, x, rows = lax.rem(j, self.slots), lax.rem(j, 4), self.x, self.rows
        if stage == 1:
            two, came = lax.rem(j, self.made), lax.rem(j, got.shape[0])

            def total(t, z, at):
                here = pl.ds(pl.multiple_of((2 * z + at) * rows, rows), rows)
                return kept[two, t, here, :] + got[came, t, here, :]

            for i, (t, z) in enumerate(self.upper):
                ps[slot, i] = total(t, z, 1 - x)
                pk[slot, i] = total(t, z, x)
            for i, (t, z) in enumerate(self.lower):
                for at in range(2):
                    block = total(t, z, at)
                    qk[slot, at, i] = block[:, :HEAD]
                    qs[slot, at, i] = block[:, HEAD:]
        elif stage == 2:
            for i in range(len(self.upper)):
                block = pk[slot, i] + pr[four, i]
                pk2[slot, i] = block[:, :HEAD]
                ps2[slot, i] = block[:, HEAD:]
            for i in range(len(self.lower)):
                qs2[slot, i] = qk[slot, 1 - x, i] + qr[four, 1 - x, i]
                qk2[slot, i] = qk[slot, x, i] + qr[four, x, i]
        elif stage == 3:
            for i, (t, z) in enumerate(self.upper):
                line[slot, z, t] = pk2[slot, i] + pr2[four, i]
            for i, (t, z) in enumerate(self.lower):
                line[slot, z, t] = qk2[slot, i] + qr2[four, i]
        else:
            total = plus(line[slot, self.z], *[zr[four, k] for k in range(self.depth - 1)])
            out[:, :, pl.ds(pl.multiple_of((self.offset + j) * HEAD, HEAD), HEAD)] = total


def launch(kernel, name, steps, inputs, specs, outs, out_specs, scratch, flops, guests=(), ident=None, partners=()):
    guests = list(guests)
    partners = list(partners) + [p for g in guests for p in g.partners]
    partners = sorted(set(partners))
    all_inputs = list(inputs) + [a for g in guests for a in g.inputs]
    all_specs = list(specs) + [anywhere() for g in guests for _ in g.inputs]
    all_outs = list(outs) + [a for g in guests for a in g.outs]
    all_out_specs = list(out_specs) + [anywhere() for g in guests for _ in g.outs]
    all_scratch = list(scratch) + [a for g in guests for a in g.scratch]

    def body(*refs):
        refs = list(refs)
        take = lambda k: [refs.pop(0) for _ in range(k)]
        own = take(len(inputs))
        ins = [take(len(g.inputs)) for g in guests]
        own += take(len(outs))
        gone = [take(len(g.outs)) for g in guests]
        own += take(len(scratch))
        held = [take(len(g.scratch)) for g in guests]
        step = pl.program_id(0)
        if partners:

            @pl.when(step == 0)
            def _():
                greet(partners)

        for g, i, o, s in zip(guests, ins, gone, held):
            g.before(step, i, o, s)
        kernel(*own)
        for g, i, o, s in zip(guests, ins, gone, held):
            g.after(step, i, o, s)

    extra = dict(collective_id=ident, has_side_effects=True) if partners else {}
    return pl.pallas_call(
        body,
        grid=(steps,),
        in_specs=all_specs,
        out_specs=all_out_specs,
        out_shape=all_outs,
        scratch_shapes=all_scratch,
        compiler_params=pltpu.CompilerParams(
            vmem_limit_bytes=VMEM_LIMIT, dimension_semantics=("arbitrary",), **extra
        ),
        cost_estimate=cost(flops, all_inputs + all_outs),
        name=name,
    )(*all_inputs)


def tables(longest):
    freq = 10000.0 ** (-np.arange(HEAD, dtype=np.float64) / HEAD)

    def both(places):
        phase = places[:, None] * freq[None, :]
        return jnp.asarray(np.concatenate([np.cos(phase), np.sin(phase)], axis=1), F32)

    return both(np.arange(CHUNK)), both(np.arange(0, longest, CHUNK))


class Layout:
    def __init__(self, lengths, peers, count):
        self.lengths, self.peers, self.count = lengths, peers, count
        self.me = lax.axis_index("mp")
        self.offset = self.me * count

    def begin(self, first):
        begin = start = jnp.int32(0)
        for i in range(self.lengths.shape[1]):
            begin = jnp.where(first >= start, start, begin)
            start = start + self.lengths[0, i]
        return begin

    def first(self, c):
        return self.offset + c * CHUNK

    def keep(self, c):
        return jnp.where(self.begin(self.first(c)) < self.first(c), 1.0, 0.0)

    def before(self, c):
        return jnp.where(self.begin(self.first(c)) < self.offset, 1.0, 0.0)

    def after(self, c):
        last = self.begin(self.offset + self.count - CHUNK)
        return jnp.where(last <= self.first(c), 1.0, 0.0) * jnp.where(self.me < self.peers - 1, 1.0, 0.0)

    def alive(self, c, width):
        end = jnp.int32(0)
        for i in range(self.lengths.shape[1]):
            end = end + self.lengths[0, i]
        return (row_index((CHUNK, width)) + self.first(c) < end).astype(F32)

    def angles(self, c, fine, coarse):
        base = self.first(c) - self.begin(self.first(c))
        start = jnp.zeros((1, 2 * HEAD), F32)
        for k in range(coarse.shape[0]):
            start = start + coarse[k : k + 1, :] * jnp.where(base == k * CHUNK, 1.0, 0.0)
        cb, sb = start[:, :HEAD], start[:, HEAD:]
        cf, sf = fine[:, :HEAD], fine[:, HEAD:]
        return cf * cb - sf * sb, sf * cb + cf * sb


def normed_of(hid):
    x = hid[...].astype(F32)
    return (x * scale_of(x)).astype(BF16)


def states_chunk(heads, slopes, keep, key, values, state, put):
    for h in range(heads):
        slope = slopes[h]
        faded = (values[:, head_slice(h)] * fade_to_end(slope, HEAD)).astype(BF16)
        old = state[h] * keep
        put(h, old.astype(BF16))
        state[h] = jnp.exp(jnp.full((1, 2 * HEAD), -slope * CHUNK, F32)) * old + nn(faded.T, key(h))


def inside_chunk(heads, slopes, query, key, values, st, table, put):
    for h in range(heads):
        asked = query(h)
        weights = (nt(asked, key(h)) * table(h)).astype(BF16)
        put(h, nn(weights, values(h)) + fade_from_start(slopes[h], HEAD) * nt(asked, st(h)))


def carried_chunk(heads, slopes, layout, c, att, query, came, total):
    reached = layout.before(c)
    lag = (c * CHUNK).astype(F32)
    alive = layout.alive(c, HEAD)
    for h in range(heads):
        fade = jnp.exp(-slopes[h] * (row_index((CHUNK, HEAD)).astype(F32) + (lag + 1.0))) * reached
        total[:, head_slice(h)] = (att(h) + fade * nt(query(h), came[h])) * alive


def mix_chunk(parts, total, sel, wo, hid, att_o, mixt_o, mid_o, sec_o, sect_o):
    attended = total[...]
    att_o[...] = attended.astype(BF16)
    mixed = (attended * scale_of(attended) * sel.astype(F32)).astype(BF16)
    put_turned(mixt_o, mixed, parts)
    middle = hid[...].astype(F32) + nn(mixed, wo)
    mid_o[...] = middle.astype(BF16)
    second = (middle * scale_of(middle)).astype(BF16)
    sec_o[...] = second
    put_turned(sect_o, second, parts)


def state_shape(d):
    return (d // HEAD, HEAD, 2 * HEAD)


def keys_kernel(peers, parts, count, lengths, slopes, hid, wk, wv, fine, coarse, normed_o, turned_o, kpre_o, val_o, st_o, fin_o, state):
    c = pl.program_id(0)
    layout = Layout(lengths, peers, count)

    @pl.when(c == 0)
    def _():
        state[...] = jnp.zeros_like(state)

    normed = normed_of(hid)
    normed_o[...] = normed
    put_turned(turned_o, normed, parts)
    kpre = nn(normed, wk[...])
    kpre_o[...] = kpre.astype(BF16)
    values = nn(normed, wv[...])
    val_o[...] = values.astype(BF16)
    cs, sn = layout.angles(c, fine, coarse)

    def put(h, value):
        st_o[0, h] = value

    key = lambda h: featured(kpre[:, head_slice(h)], cs, sn)
    states_chunk(state.shape[0], slopes, layout.keep(c), key, values, state, put)
    fin_o[...] = state[...].astype(BF16)


def run_keys(peers, lengths, slopes, hidden, wk, wv, angles, parts):
    n, d = hidden.shape
    heads, chunks = d // HEAD, n // CHUNK
    turned = turned_shape(d, n)
    tile = pl.BlockSpec((CHUNK, d), lambda c: (c, 0))
    outs = [struct((n, d)), struct(turned), struct((n, d)), struct((n, d)), struct((chunks,) + state_shape(d)), struct(state_shape(d))]
    return launch(
        functools.partial(keys_kernel, peers, parts, n),
        "keys_values_states",
        chunks,
        [lengths, slopes, hidden, wk, wv, *angles],
        [smem(), smem(), tile, whole_block(wk.shape), whole_block(wv.shape)] + [whole_block(a.shape) for a in angles],
        outs,
        [
            tile,
            pl.BlockSpec(turned[:2] + (CHUNK,), lambda c: (0, 0, c)),
            tile,
            tile,
            pl.BlockSpec((1,) + state_shape(d), lambda c: (c, 0, 0, 0)),
            whole_block(state_shape(d)),
        ],
        [pltpu.VMEM(state_shape(d), F32)],
        4 * n * d * d,
    )


def inside_kernel(peers, count, lengths, slopes, normed, wq, ws, kpre, values, st, fine, coarse, qpre_o, sel_o, att_o):
    c = pl.program_id(0)
    layout = Layout(lengths, peers, count)
    x = normed[...]
    qpre = nn(x, wq[...])
    qpre_o[...] = qpre.astype(BF16)
    sel_o[...] = nn(x, ws[...]).astype(BF16)
    cs, sn = layout.angles(c, fine, coarse)

    def put(h, value):
        att_o[:, head_slice(h)] = value

    inside_chunk(
        st.shape[1],
        slopes,
        lambda h: featured(qpre[:, head_slice(h)], cs, sn),
        lambda h: featured(kpre[:, head_slice(h)].astype(F32), cs, sn),
        lambda h: values[:, head_slice(h)],
        lambda h: st[0, h],
        lambda h: decay_table(slopes[h], False),
        put,
    )


def run_inside(peers, lengths, slopes, normed, wq, ws, kpre, values, st, angles):
    n, d = normed.shape
    chunks = n // CHUNK
    tile = pl.BlockSpec((CHUNK, d), lambda c: (c, 0))
    return launch(
        functools.partial(inside_kernel, peers, n),
        "queries_attention",
        chunks,
        [lengths, slopes, normed, wq, ws, kpre, values, st, *angles],
        [smem(), smem(), tile, whole_block(wq.shape), whole_block(ws.shape), tile, tile]
        + [pl.BlockSpec((1,) + state_shape(d), lambda c: (c, 0, 0, 0))]
        + [whole_block(a.shape) for a in angles],
        [struct((n, d)), struct((n, d)), struct((n, d), F32)],
        [tile, tile, tile],
        [],
        6 * n * d * d,
    )


def mix_kernel(peers, parts, count, lengths, slopes, att, qpre, came, sel, wo, hid, cot, fine, coarse, att_o, mixt_o, mid_o, sec_o, sect_o, cott_o, total):
    c = pl.program_id(0)
    layout = Layout(lengths, peers, count)
    cs, sn = layout.angles(c, fine, coarse)
    carried_chunk(
        came.shape[0],
        slopes,
        layout,
        c,
        lambda h: att[:, head_slice(h)],
        lambda h: featured(qpre[:, head_slice(h)].astype(F32), cs, sn),
        came,
        total,
    )
    mix_chunk(parts, total, sel[...], wo[...], hid, att_o, mixt_o, mid_o, sec_o, sect_o)
    put_turned(cott_o, cot[...], parts)


def run_mix(peers, lengths, slopes, att, qpre, came, sel, wo, hidden, cot, angles, parts):
    n, d = hidden.shape
    chunks = n // CHUNK
    turned = turned_shape(d, n)
    tile = pl.BlockSpec((CHUNK, d), lambda c: (c, 0))
    turned_tile = pl.BlockSpec(turned[:2] + (CHUNK,), lambda c: (0, 0, c))
    return launch(
        functools.partial(mix_kernel, peers, parts, n),
        "carried_mixed_middle",
        chunks,
        [lengths, slopes, att, qpre, came, sel, wo, hidden, cot, *angles],
        [smem(), smem(), tile, tile, whole_block(came.shape), tile, whole_block(wo.shape), tile, tile]
        + [whole_block(a.shape) for a in angles],
        [struct((n, d)), struct(turned), struct((n, d)), struct((n, d)), struct(turned), struct(turned)],
        [tile, turned_tile, tile, tile, turned_tile, turned_tile],
        [pltpu.VMEM((CHUNK, d), F32)],
        3 * n * d * d,
    )


def forward_kernel(chunks, parts, lengths, slopes, hid, cot, fine, coarse, *refs):
    refs = list(refs)
    take = lambda k: [refs.pop(0) for _ in range(k)]
    weights_h = take(5)
    (kpre_o, val_o, st_o, qpre_o, sel_o) = take(5)
    (turned_o, att_o, mixt_o, mid_o, sec_o, sect_o, cott_o, came_o) = take(8)
    (weights, normed, kpre, val, st, qpre, sel, att, state, final, came, total, keyed, asked, table) = take(15)
    (load_sems, out_sems, state_sems) = take(3)
    heads = state.shape[0]
    step = pl.program_id(0)
    c = lax.rem(step, chunks)
    here = pl.ds(pl.multiple_of(c * CHUNK, CHUNK), CHUNK)
    layout = Layout(lengths, 2, chunks * CHUNK)
    loads = [pltpu.make_async_copy(w, weights.at[i], load_sems.at[i]) for i, w in enumerate(weights_h)]
    saves = [
        pltpu.make_async_copy(src, dst, out_sems.at[i])
        for i, (src, dst) in enumerate([(kpre, kpre_o), (val, val_o), (st, st_o), (qpre, qpre_o), (sel, sel_o)])
    ]
    exchange = remote(final, came, state_sems.at[0], state_sems.at[1], "mp", 1)

    @pl.when(step == 0)
    def _():
        for copy in loads:
            copy.start()
        state[...] = jnp.zeros_like(state)
        for copy in loads[:2]:
            copy.wait()

    @pl.when(step < chunks)
    def _():
        x = normed_of(hid)
        normed[here, :] = x
        put_turned(turned_o, x, parts)
        keys = nn(x, weights[0])
        kpre[here, :] = keys.astype(BF16)
        values = nn(x, weights[1])
        val[here, :] = values.astype(BF16)
        cs, sn = layout.angles(c, fine, coarse)

        def put(h, value):
            st[c, h] = value

        def key(h):
            value = featured(keys[:, head_slice(h)], cs, sn)
            keyed[here, feature_slice(h)] = value
            return value

        states_chunk(heads, slopes, layout.keep(c), key, values, state, put)

    @pl.when(step == chunks - 1)
    def _():
        final[...] = state[...].astype(BF16)
        exchange.start()
        for copy in saves[:3]:
            copy.start()

    @pl.when(step == chunks)
    def _():
        for h in range(heads):
            table[h] = decay_table(slopes[h], False)
        for copy in loads[2:4]:
            copy.wait()

    @pl.when(jnp.logical_and(step >= chunks, step < 2 * chunks))
    def _():
        x = normed[here, :]
        queries = nn(x, weights[2])
        qpre[here, :] = queries.astype(BF16)
        sel[here, :] = nn(x, weights[3]).astype(BF16)
        cs, sn = layout.angles(c, fine, coarse)

        def put(h, value):
            att[here, head_slice(h)] = value

        def query(h):
            value = featured(queries[:, head_slice(h)], cs, sn)
            asked[here, feature_slice(h)] = value
            return value

        inside_chunk(
            heads,
            slopes,
            query,
            lambda h: keyed[here, feature_slice(h)],
            lambda h: val[here, head_slice(h)],
            lambda h: st[c, h],
            lambda h: table[h],
            put,
        )
        put_turned(cott_o, cot[...], parts)

    @pl.when(step == 2 * chunks - 1)
    def _():
        for copy in saves[3:]:
            copy.start()

    @pl.when(step == 2 * chunks)
    def _():
        loads[4].wait()
        exchange.wait()
        came_o[...] = came[...]

    @pl.when(step >= 2 * chunks)
    def _():
        carried_chunk(
            heads,
            slopes,
            layout,
            c,
            lambda h: att[here, head_slice(h)],
            lambda h: asked[here, feature_slice(h)],
            came,
            total,
        )
        mix_chunk(parts, total, sel[here, :], weights[4], hid, att_o, mixt_o, mid_o, sec_o, sect_o)

    @pl.when(step == 3 * chunks - 1)
    def _():
        for copy in saves:
            copy.wait()


def run_forward(lengths, slopes, hidden, cot, weights, angles, parts, guests, ident):
    n, d = hidden.shape
    chunks = n // CHUNK
    turned = turned_shape(d, n)
    late = lambda s: jnp.maximum(s - 2 * chunks, 0)
    mid = lambda s: jnp.clip(s - chunks, 0, chunks - 1)
    early = lambda s: jnp.minimum(s, chunks - 1)
    tile = pl.BlockSpec((CHUNK, d), lambda s: (late(s), 0))
    turned_tile = lambda at: pl.BlockSpec(turned[:2] + (CHUNK,), lambda s: (0, 0, at(s)))
    whole = pltpu.VMEM((n, d), BF16)
    return launch(
        functools.partial(forward_kernel, chunks, parts),
        "forward_to_sglu",
        3 * chunks,
        [lengths, slopes, hidden, cot, *angles, *weights],
        [
            smem(),
            smem(),
            pl.BlockSpec((CHUNK, d), lambda s: (jnp.where(s < 2 * chunks, early(s), late(s)), 0)),
            pl.BlockSpec((CHUNK, d), lambda s: (mid(s), 0)),
        ]
        + [whole_block(a.shape) for a in angles]
        + [anywhere()] * 5,
        [struct((n, d)), struct((n, d)), struct((chunks,) + state_shape(d)), struct((n, d)), struct((n, d))]
        + [struct(turned), struct((n, d)), struct(turned), struct((n, d)), struct((n, d)), struct(turned), struct(turned)]
        + [struct(state_shape(d))],
        [anywhere()] * 5
        + [turned_tile(early), tile, turned_tile(late), tile, tile, turned_tile(late), turned_tile(mid)]
        + [whole_block(state_shape(d))],
        [
            pltpu.VMEM((5, d, d), BF16),
            whole,
            whole,
            whole,
            pltpu.VMEM((chunks,) + state_shape(d), BF16),
            whole,
            whole,
            pltpu.VMEM((n, d), F32),
            pltpu.VMEM(state_shape(d), F32),
            pltpu.VMEM(state_shape(d), BF16),
            pltpu.VMEM(state_shape(d), BF16),
            pltpu.VMEM((CHUNK, d), F32),
            pltpu.VMEM((n, 2 * d), BF16),
            pltpu.VMEM((n, 2 * d), BF16),
            pltpu.VMEM((d // HEAD, CHUNK, CHUNK), F32),
            pltpu.SemaphoreType.DMA((5,)),
            pltpu.SemaphoreType.DMA((5,)),
            pltpu.SemaphoreType.DMA((2,)),
        ],
        12 * n * d * d,
        guests=guests,
        ident=ident,
        partners=[("mp", 1)],
    )


def sglu_kernel(chunks, peers, sec, cot, w1, w2, wd, units_o, term_o, part_o):
    step = pl.program_id(0)
    here = pl.ds(pl.multiple_of(lax.rem(step, chunks) * CHUNK, CHUNK), CHUNK)
    left = nn(sec[...], w1[...])
    right = nn(sec[...], w2[...])
    inner = (left * right).astype(BF16)
    upstream = nt(cot[...], wd[...])
    grad_left = (upstream * right).astype(BF16)
    grad_right = (upstream * left).astype(BF16)
    units_o[0] = grad_left
    units_o[1] = grad_right
    units_o[2] = inner
    term = nn(inner, wd[...])
    part = nt(grad_left, w1[...]) + nt(grad_right, w2[...])

    @pl.when(step < chunks)
    def _():
        term_o[here, :] = term
        part_o[here, :] = part

    @pl.when(step >= chunks)
    def _():
        term_o[here, :] += term
        part_o[here, :] += part


def run_sglu(second, cot, w1, w2, wd):
    n, d = second.shape
    peers, _, width = w1.shape
    chunks = n // CHUNK
    tile = pl.BlockSpec((CHUNK, d), lambda s: (lax.rem(s, chunks), 0))
    block = lambda shape: pl.BlockSpec((None,) + shape, lambda s: (lax.div(s, chunks), 0, 0))
    return launch(
        functools.partial(sglu_kernel, chunks, peers),
        "sglu",
        peers * chunks,
        [second, cot, w1, w2, wd],
        [tile, tile, block((d, width)), block((d, width)), block((width, d))],
        [struct((3, peers, n, width)), struct((n, d), F32), struct((n, d), F32)],
        [
            pl.BlockSpec((3, None, CHUNK, width), lambda s: (0, lax.div(s, chunks), lax.rem(s, chunks), 0)),
            whole_block((n, d)),
            whole_block((n, d)),
        ],
        [],
        12 * n * d * width * peers,
    )


def units_kernel(geo, reducers, ride, lengths, slopes, fine, coarse, *refs):
    blocks, cut, d, units, chunks = geo["blocks"], geo["cut"], geo["d"], geo["units"], geo["chunks"]
    refs = list(refs)
    take = lambda k: [refs.pop(0) for _ in range(k)]
    weights_h = take(3)
    (x_h, cot_h, xt_h, cott_h, wo_h) = take(5)
    rows_h = take(4)
    pieces = take(12)
    had_b = take(3)
    rows_out = take(4)
    (et_o, left_o, sums_o) = take(3)
    pieces = pieces + had_b + take(9)
    (term, part, x, cot, xt, cott, o1, o2, od, c12, cd, inner, grads, state, e0, sums) = take(16)
    (left,) = take(1)
    (tiles, made, ends) = take(3)
    (sems, own_sems, block_sems, tile_sems, made_sems) = take(5)
    places = Reducer.places(reducers[0].depth)
    for reducer in reducers:
        reducer.bind(take(len(reducer.scratch)), places)
    step = pl.program_id(0)
    ride.before(step, had_b, pieces[15:], refs)
    core = lax.rem(lax.axis_index("dp"), 2)
    eighth = lax.rem(lax.axis_index("dp"), 8)
    heads = state.shape[0]
    layout = Layout(lengths, 2, chunks * CHUNK)

    def fetch(g, parts=slice(0, 8)):
        size = cut if g == 0 else units - cut
        masks = [(0, None, 0), (3, 0, 2), (3, 1, 4), (3, 2, 1), (6, 0, 6), (6, 1, 3), (6, 2, 5), (9, None, 7)]
        copies = []
        for w, region in enumerate((o1, o2, od)):
            rows = d // 8 if w < 2 else size // 8
            for k, (at, inner, mask) in list(enumerate(masks))[parts]:
                src = pieces[12 * g + at + w]
                src = src if inner is None else src.at[inner]
                here = pl.ds(pl.multiple_of(flipped(eighth, mask) * rows, 16), rows)
                dst = region.at[here, pl.ds(0, size)] if w < 2 else region.at[here, :]
                copies.append(pltpu.make_async_copy(src, dst, sems.at[g, w, k]))
        return copies

    own = [
        pltpu.make_async_copy(x_h, x, own_sems.at[6]),
        pltpu.make_async_copy(cot_h, cot, own_sems.at[0]),
        pltpu.make_async_copy(xt_h.at[1 - core], xt.at[pl.ds(0, d // 2), :], own_sems.at[1]),
        pltpu.make_async_copy(xt_h.at[core], xt.at[pl.ds(d // 2, d // 2), :], own_sems.at[2]),
        pltpu.make_async_copy(cott_h.at[1 - core], cott.at[pl.ds(0, d // 2), :], own_sems.at[3]),
        pltpu.make_async_copy(cott_h.at[core], cott.at[pl.ds(d // 2, d // 2), :], own_sems.at[4]),
    ]
    out_weight = pltpu.make_async_copy(wo_h, xt, own_sems.at[7])
    saved = pltpu.make_async_copy(sums, sums_o, own_sems.at[5])
    arrived = pltpu.make_async_copy(left, left_o, own_sems.at[8])
    exchange = remote(e0, left, own_sems.at[9], own_sems.at[10], "mp", 1)

    def own_block(j):
        slot, here = lax.rem(j, 2), pl.ds(pl.multiple_of(j * HEAD, HEAD), HEAD)
        return [
            pltpu.make_async_copy(weights_h[0].at[:, here], c12.at[slot, :, pl.ds(0, HEAD)], block_sems.at[slot, 0]),
            pltpu.make_async_copy(
                weights_h[1].at[:, here], c12.at[slot, :, pl.ds(2 * HEAD, HEAD)], block_sems.at[slot, 1]
            ),
            pltpu.make_async_copy(weights_h[2].at[here, :], cd.at[slot, pl.ds(0, HEAD), :], block_sems.at[slot, 2]),
        ]

    def rows_at(i):
        return pl.ds(pl.multiple_of((chunks - 1 - i) * CHUNK, CHUNK), CHUNK)

    def tile(i):
        slot = lax.rem(i, 2)
        return [
            pltpu.make_async_copy(src.at[rows_at(i), :], tiles.at[slot, k], tile_sems.at[slot, k])
            for k, src in enumerate(rows_h)
        ]

    def results(i):
        slot = lax.rem(i, 2)
        return [
            pltpu.make_async_copy(made.at[slot, k], dst.at[rows_at(i), :], made_sems.at[slot, k])
            for k, dst in enumerate(rows_out)
        ] + [pltpu.make_async_copy(ends.at[slot], et_o.at[chunks - 1 - i], made_sems.at[slot, 4])]

    turn = cut // HEAD

    @pl.when(step == 0)
    def _():
        for copy in own_block(0) + fetch(0) + own:
            copy.start()
        term[...] = jnp.zeros_like(term)
        part[...] = jnp.zeros_like(part)
        state[...] = jnp.zeros_like(state)
        for copy in fetch(0):
            copy.wait()

    @pl.when(step == turn)
    def _():
        for copy in fetch(1, slice(7, 8)):
            copy.start()
        for copy in fetch(1):
            copy.wait()

    @pl.when(step < blocks)
    def _():
        local = step - jnp.where(step >= turn, turn, 0)
        here = pl.ds(pl.multiple_of(local * HEAD, HEAD), HEAD)
        at = lax.rem(step, 2)
        c12[at, :, HEAD : 2 * HEAD] = o1[:, here]
        c12[at, :, 3 * HEAD :] = o2[:, here]
        cd[at, HEAD:, :] = od[here, :]
        for copy in own_block(step):
            copy.wait()

    @pl.when(step < blocks - 1)
    def _():
        for copy in own_block(step + 1):
            copy.start()

    @pl.when(step == turn - 1)
    def _():
        for copy in fetch(1, slice(0, 7)):
            copy.start()

    @pl.when(step == 0)
    def _():
        for copy in own[:2]:
            copy.wait()

    @pl.when(step < blocks)
    def _():
        wide, at = 2 * HEAD, lax.rem(step, 2)
        for k in range(chunks):
            here = slice(k * CHUNK, (k + 1) * CHUNK)
            both = nn(x[here, :], c12[at])
            left, right = both[:, :wide], both[:, wide:]
            upstream = nt(cot[here, :], cd[at])
            inner[here, :] = (left * right).astype(BF16)
            grads[here, :wide] = (upstream * right).astype(BF16)
            grads[here, wide:] = (upstream * left).astype(BF16)

        @pl.when(step == 0)
        def _():
            for copy in own[2:]:
                copy.wait()

        for reducer in reducers:

            @pl.when(jnp.logical_and(step >= reducer.start, step < reducer.start + reducer.blocks))
            def _(reducer=reducer):
                both = nn(xt[...], grads[...]).astype(BF16)
                down = nn(cott[...], inner[...]).astype(BF16)
                for k, buffer in enumerate((reducer.given, reducer.kept)):
                    here = slice(k * (d // 2), (k + 1) * (d // 2))
                    buffer[0, 0] = both[here, :wide]
                    buffer[0, 1] = both[here, wide:]
                    buffer[0, 2] = down[here, :]
                    if k == 0:
                        reducer.begin(step - reducer.start)

        term[...] += nn(inner[...], cd[at])
        part[...] += nt(grads[...], c12[at])

    @pl.when(step == blocks - 1)
    def _():
        out_weight.start()
        for copy in tile(0):
            copy.start()

    @pl.when(step == blocks)
    def _():
        out_weight.wait()

    @pl.when(jnp.logical_and(step >= blocks, step < blocks + chunks))
    def _():
        i = step - blocks
        c, slot = chunks - 1 - i, lax.rem(i, 2)
        here = pl.ds(pl.multiple_of(c * CHUNK, CHUNK), CHUNK)
        for copy in tile(i):
            copy.wait()

        @pl.when(i < chunks - 1)
        def _():
            for copy in tile(i + 1):
                copy.start()

        @pl.when(i >= 2)
        def _():
            for copy in results(i - 2):
                copy.wait()

        cs, sn = layout.angles(c, fine, coarse)
        mid, sel, att, qpre = [tiles.at[slot, k] for k in range(4)]
        after_chunk(
            layout, c, heads, slopes, term[here, :], part[here, :], cot[here, :], mid, sel, att, xt[...], qpre, cs, sn,
            *[made.at[slot, k] for k in range(4)], ends.at[pl.ds(slot, 1)], state,
        )
        for copy in results(i):
            copy.start()

    @pl.when(step == blocks + chunks - 1)
    def _():
        e0[...] = state[...].astype(BF16)
        exchange.start()

    ride.after(step, had_b, pieces[15:], refs)
    for reducer in reducers:
        reducer.run(step, sums)

    @pl.when(step == reducers[-1].last)
    def _():
        saved.start()
        exchange.wait()
        arrived.start()
        for i in range(chunks - 2, chunks):
            for copy in results(i):
                copy.wait()
        arrived.wait()
        saved.wait()


def run_units(lengths, slopes, matrices, second, cot, second_t, cot_t, rows_in, angles, wo, pieces, ride, cut, depth, ident):
    n, d = second.shape
    chunks = n // CHUNK
    units = matrices[0].shape[1]
    blocks = units // HEAD
    rows = d // (4 * depth)
    turn = cut // HEAD
    reducers = [
        Reducer(0, turn, 3, depth, rows, (0, 2, 4, 6), 2, (4, 3, 2, 1), (1, 1, 1)),
        Reducer(turn, blocks - turn, 3, depth, rows, (0, 2, 4, 6), 2, (4, 3, 2, 1), (2, 2, 2), turn),
    ]
    geo = dict(blocks=blocks, cut=cut, d=d, units=units, chunks=chunks)
    turned = pltpu.VMEM((d, n), BF16)
    size = max(cut, units - cut)
    sums = (3, rows, units)
    return launch(
        functools.partial(units_kernel, geo, reducers, ride),
        "sglu_and_gradients",
        max(reducers[-1].last, blocks + chunks - 1) + 1,
        [lengths, slopes, *angles]
        + list(matrices)
        + [second, cot, second_t, cot_t, wo]
        + list(rows_in)
        + list(pieces)
        + ride.inputs,
        [smem(), smem()] + [once(a.shape) for a in angles] + [anywhere()] * (12 + len(pieces) + len(ride.inputs)),
        [struct((n, d))] * 4
        + [struct((chunks,) + state_shape(d)), struct(state_shape(d)), struct(sums, F32)]
        + ride.outs,
        [anywhere()] * (7 + len(ride.outs)),
        [
            pltpu.VMEM((n, d), F32),
            pltpu.VMEM((n, d), F32),
            pltpu.VMEM((n, d), BF16),
            pltpu.VMEM((n, d), BF16),
            turned,
            turned,
            pltpu.VMEM((d, size), BF16),
            pltpu.VMEM((d, size), BF16),
            pltpu.VMEM((size, d), BF16),
            pltpu.VMEM((2, d, 4 * HEAD), BF16),
            pltpu.VMEM((2, 2 * HEAD, d), BF16),
            pltpu.VMEM((n, 2 * HEAD), BF16),
            pltpu.VMEM((n, 4 * HEAD), BF16),
            pltpu.VMEM(state_shape(d), F32),
            pltpu.VMEM(state_shape(d), BF16),
            pltpu.VMEM(sums, F32),
            pltpu.VMEM(state_shape(d), BF16),
            pltpu.VMEM((2, 4, CHUNK, d), BF16),
            pltpu.VMEM((2, 4, CHUNK, d), BF16),
            pltpu.VMEM((2,) + state_shape(d), BF16),
            pltpu.SemaphoreType.DMA((2, 3, 8)),
            pltpu.SemaphoreType.DMA((11,)),
            pltpu.SemaphoreType.DMA((2, 3)),
            pltpu.SemaphoreType.DMA((2, 4)),
            pltpu.SemaphoreType.DMA((2, 5)),
        ]
        + [a for reducer in reducers for a in reducer.scratch]
        + ride.scratch,
        36 * n * d * units,
        partners=reducers[0].partners + ride.partners,
        ident=ident,
    )[:7]


def after_chunk(layout, c, heads, slopes, term, part, cot, mid, sel, att, wo, qpre, cs, sn, out_o, gmid_o, pair_o, gatt_o, et_o, state):
    middle = mid[...].astype(F32)
    out_o[...] = (middle + term).astype(BF16)
    grad_middle = cot.astype(F32) + norm_back(middle, scale_of(middle), part)
    branch = grad_middle.astype(BF16)
    gmid_o[...] = branch
    grad_mixed = nt(branch, wo)
    attended = att[...].astype(F32)
    scale = scale_of(attended)
    pair_o[...] = (grad_mixed * attended * scale).astype(BF16)
    grad_att = norm_back(attended, scale, grad_mixed * sel[...].astype(F32)) * layout.alive(c, 1)
    gatt_o[...] = grad_att.astype(BF16)
    keep = layout.keep(c)
    for h in range(heads):
        slope = slopes[h]
        query = featured(qpre[:, head_slice(h)].astype(F32), cs, sn)
        faded = (grad_att[:, head_slice(h)] * fade_from_start(slope, HEAD)).astype(BF16)
        old = state[h]
        et_o[0, h] = old.astype(BF16)
        state[h] = keep * (
            jnp.exp(jnp.full((1, 2 * HEAD), -slope * CHUNK, F32)) * old + nn(faded.T, query)
        )


def after_kernel(peers, count, lengths, slopes, term, part, cot, mid, sel, att, wo, qpre, fine, coarse, out_o, gmid_o, gsel_o, gatt_o, et_o, e0_o, state):
    step = pl.program_id(0)
    c = count // CHUNK - 1 - step
    layout = Layout(lengths, peers, count)

    @pl.when(step == 0)
    def _():
        state[...] = jnp.zeros_like(state)

    cs, sn = layout.angles(c, fine, coarse)
    after_chunk(
        layout, c, state.shape[0], slopes, term[...], part[...], cot[...], mid, sel, att, wo[...], qpre, cs, sn,
        out_o, gmid_o, gsel_o, gatt_o, et_o, state,
    )
    e0_o[...] = state[...].astype(BF16)


def run_after(peers, lengths, slopes, term, part, cot, mid, sel, att, wo, qpre, angles):
    n, d = cot.shape
    chunks = n // CHUNK
    back = lambda s: chunks - 1 - s
    tile = pl.BlockSpec((CHUNK, d), lambda s: (back(s), 0))
    return launch(
        functools.partial(after_kernel, peers, n),
        "output_and_row_gradients",
        chunks,
        [lengths, slopes, term, part, cot, mid, sel, att, wo, qpre, *angles],
        [smem(), smem()] + [tile] * 6 + [whole_block(wo.shape), tile] + [whole_block(a.shape) for a in angles],
        [struct((n, d))] * 4 + [struct((chunks,) + state_shape(d)), struct(state_shape(d))],
        [tile] * 4
        + [pl.BlockSpec((1,) + state_shape(d), lambda s: (back(s), 0, 0, 0)), whole_block(state_shape(d))],
        [pltpu.VMEM(state_shape(d), F32)],
        3 * n * d * d,
    )


def weights_kernel(items, peers, *refs):
    item = lax.div(pl.program_id(0), peers)
    lefts, right, out = refs[:-2], refs[-2], refs[-1]
    for i, left in enumerate(lefts):

        @pl.when(functools.reduce(jnp.logical_or, [item == t for t, w in enumerate(items) if w == i]))
        def _(left=left):
            block = left[...]
            block = block.reshape(-1, block.shape[-1])
            out[...] = nn(block, right[...]).astype(BF16)


def run_weights(lefts, items, rights, right_spec, peers, width):
    _, half, n = lefts[0].shape
    shape = (peers, len(items), 2 * half, width)
    which = lambda s: (lax.div(s, peers), lax.rem(s, peers))
    (out,) = launch(
        functools.partial(weights_kernel, items, peers),
        "weight_gradients",
        peers * len(items),
        list(lefts) + [rights],
        [whole_block(left.shape) for left in lefts] + [right_spec(which)],
        [struct(shape)],
        [pl.BlockSpec((None, None) + shape[2:], lambda s: (which(s)[1], which(s)[0], 0, 0))],
        [],
        4 * n * half * width * len(items) * peers,
    )
    return out


def head_back(slope, table, turned, qpre, kpre, value, grad, state, ending, cs, sn):
    qp, kp = qpre.astype(F32), kpre.astype(F32)
    qs, ks = sigmoid(qp), sigmoid(kp)
    qa, ka = qp * qs, kp * ks
    query = jnp.concatenate([qa * cs, qa * sn], axis=-1).astype(BF16)
    key = jnp.concatenate([ka * cs, ka * sn], axis=-1).astype(BF16)
    state, ending = state.astype(BF16), ending.astype(BF16)
    scores_t = (nt(key, query) * turned).astype(BF16)
    slope_s = (nt(grad, value) * table).astype(BF16)
    slope_t = (nt(value, grad) * turned).astype(BF16)
    start = fade_from_start(slope, HEAD)
    end = fade_to_end(slope, HEAD)
    grad_start = (grad.astype(F32) * start).astype(BF16)
    value_end = (value.astype(F32) * end).astype(BF16)
    dq = nn(slope_s, key) + nn(grad_start, state)
    dk = nn(slope_t, query) + nn(value_end, ending)
    dv = nn(scores_t, grad) + end * nt(key, ending)
    dq = dq[:, :HEAD] * cs + dq[:, HEAD:] * sn
    dk = dk[:, :HEAD] * cs + dk[:, HEAD:] * sn
    gq = (dq * (qs * (1.0 + qp * (1.0 - qs)))).astype(BF16)
    gk = (dk * (ks * (1.0 + kp * (1.0 - ks)))).astype(BF16)
    return gq, gk, dv.astype(BF16)


def attention_back_kernel(peers, count, lengths, slopes, qpre, kpre, values, gatt, st, came, et, left, fine, coarse, grads_o):
    chunks = count // CHUNK
    layout = Layout(lengths, peers, count)
    pair, c = lax.div(pl.program_id(0), chunks), lax.rem(pl.program_id(0), chunks)
    cs, sn = layout.angles(c, fine, coarse)
    before, after = layout.before(c), layout.after(c)
    span = (CHUNK * c).astype(F32)
    rest = (CHUNK * (chunks - 1 - c)).astype(F32)
    for h in range(2):
        slope = slopes[2 * pair + h]
        cols = head_slice(h)
        lane = jnp.zeros((1, 2 * HEAD), F32)
        state = st[0, h].astype(F32) + came[h].astype(F32) * (jnp.exp(lane - slope * span) * before)
        ending = et[0, h].astype(F32) + left[h].astype(F32) * (jnp.exp(lane - slope * rest) * after)
        table, turned = decay_table(slope, False), decay_table(slope, True)
        three = head_back(
            slope, table, turned, qpre[:, cols], kpre[:, cols], values[:, cols], gatt[:, cols], state, ending, cs, sn
        )
        for i in range(3):
            grads_o[i, :, cols] = three[i]


def run_attention_back(peers, lengths, slopes, qpre, kpre, values, gatt, st, came, et, left, angles):
    n, d = qpre.shape
    chunks = n // CHUNK
    pair = lambda s: lax.div(s, chunks)
    chunk = lambda s: lax.rem(s, chunks)
    tile = pl.BlockSpec((CHUNK, 2 * HEAD), lambda s: (chunk(s), pair(s)))
    states = pl.BlockSpec((1, 2, HEAD, 2 * HEAD), lambda s: (chunk(s), pair(s), 0, 0))
    ends = pl.BlockSpec((2, HEAD, 2 * HEAD), lambda s: (pair(s), 0, 0))
    return launch(
        functools.partial(attention_back_kernel, peers, n),
        "attention_backward",
        chunks * d // (2 * HEAD),
        [lengths, slopes, qpre, kpre, values, gatt, st, came, et, left, *angles],
        [smem(), smem(), tile, tile, tile, tile, states, ends, states, ends] + [whole_block(a.shape) for a in angles],
        [struct((3, n, d))],
        [pl.BlockSpec((3, CHUNK, 2 * HEAD), lambda s: (0, chunk(s), pair(s)))],
        [],
        18 * n * 256 * d,
    )


def projections_kernel(geo, outer, inner, lengths, slopes, *refs):
    chunks, blocks, d, n = geo["chunks"], geo["blocks"], geo["d"], geo["n"]
    refs = list(refs)
    take = lambda k: [refs.pop(0) for _ in range(k)]
    arrays_h = take(6)
    (came_h, left_h, fine, coarse, gsel_h, hid_h, gmid_h, mixt_h, normt_h) = take(9)
    weights_h = take(4)
    hidden_o, out, out2 = take(3)
    (qpre, kpre, val, gatt, st, et, came, gsel, gmid) = take(9)
    grads, block, decays, mixt, normt, left, sems, late_sems = take(8)
    places = Reducer.places(outer.depth)
    outer.bind(take(len(outer.scratch)), places)
    inner.bind(refs, places)
    step = pl.program_id(0)
    core = lax.rem(lax.axis_index("dp"), 2)
    me = lax.axis_index("mp")
    layout = Layout(lengths, 2, n)
    loads = [
        pltpu.make_async_copy(gmid_h, gmid, sems.at[4]),
        pltpu.make_async_copy(mixt_h.at[1 - core], mixt.at[pl.ds(0, d // 2), :], sems.at[0]),
        pltpu.make_async_copy(mixt_h.at[core], mixt.at[pl.ds(d // 2, d // 2), :], sems.at[1]),
        pltpu.make_async_copy(gsel_h, gsel, sems.at[5]),
        pltpu.make_async_copy(normt_h.at[1 - core], normt.at[pl.ds(0, d // 2), :], sems.at[2]),
        pltpu.make_async_copy(normt_h.at[core], normt.at[pl.ds(d // 2, d // 2), :], sems.at[3]),
    ]
    more = [
        pltpu.make_async_copy(src, dst, sems.at[6 + i])
        for i, (src, dst) in enumerate(zip(arrays_h + [came_h, left_h], (qpre, kpre, val, gatt, st, et, came, left)))
    ]
    select = pltpu.make_async_copy(weights_h[3], mixt, sems.at[14])

    def replaced(j):
        copies = []
        for side in range(2):
            cols = pl.ds(pl.multiple_of(((me if side == 0 else 1 - me) * blocks + j) * HEAD, HEAD), HEAD)
            for i, (src, dst) in enumerate(zip(weights_h[:3] + [hid_h], (qpre, kpre, gatt, val))):
                copies.append(pltpu.make_async_copy(src.at[:, cols], dst.at[:, cols], late_sems.at[j, side, i]))
        return copies

    @pl.when(step == 0)
    def _():
        for copy in loads + more:
            copy.start()
        for copy in loads[:3]:
            copy.wait()

    @pl.when(step < blocks)
    def _():
        slot = lax.rem(step, 2)
        mine = pl.ds(pl.multiple_of((me * blocks + step) * HEAD, HEAD), HEAD)
        theirs = pl.ds(pl.multiple_of(((1 - me) * blocks + step) * HEAD, HEAD), HEAD)
        gb = jnp.concatenate([gmid[:, mine], gmid[:, theirs]], axis=1)
        first = nn(mixt[...], gb).astype(BF16)

        @pl.when(step == 0)
        def _():
            for copy in loads[3:]:
                copy.wait()

        gs = jnp.concatenate([gsel[:, mine], gsel[:, theirs]], axis=1)
        made = [first, nn(normt[...], gs).astype(BF16)]
        for k, buffer in enumerate((outer.given, outer.kept)):
            for i in range(2):
                buffer[slot, i] = made[i][k * (d // 2) : (k + 1) * (d // 2), :]
            if k == 0:
                outer.begin(step)

    @pl.when(jnp.logical_and(step >= blocks, step < 2 * blocks))
    def _():
        j = step - blocks
        for side in range(2):
            slope = slopes[(me if side == 0 else 1 - me) * blocks + j]
            for k in range(2):
                decays[side, k] = decay_table(slope, k == 1)

        def one(c, carry):
            here = pl.ds(pl.multiple_of(c * CHUNK, CHUNK), CHUNK)
            cs, sn = layout.angles(c, fine, coarse)
            before, after = layout.before(c), layout.after(c)
            span = (CHUNK * c).astype(F32)
            rest = (CHUNK * (chunks - 1 - c)).astype(F32)
            for side in range(2):
                h = (me if side == 0 else 1 - me) * blocks + j
                slope = slopes[h]
                cols = pl.ds(pl.multiple_of(h * HEAD, HEAD), HEAD)
                four = [ref[here, cols] for ref in (qpre, kpre, val, gatt)]
                lane = jnp.zeros((1, 2 * HEAD), F32)
                state = st[c, h].astype(F32) + came[h].astype(F32) * (jnp.exp(lane - slope * span) * before)
                ending = et[c, h].astype(F32) + left[h].astype(F32) * (jnp.exp(lane - slope * rest) * after)
                three = head_back(
                    slope, decays[side, 0], decays[side, 1], *four, state, ending, cs, sn
                )
                for i in range(3):
                    block[here, head_slice(2 * i + side)] = three[i]
                    grads[i, here, cols] = three[i]
            return carry

        lax.fori_loop(0, chunks, one, 0)
        slot = lax.rem(j, 2)
        made = nn(normt[...], block[...]).astype(BF16)
        for k, buffer in enumerate((inner.given, inner.kept)):
            for i in range(3):
                buffer[slot, i] = made[k * (d // 2) : (k + 1) * (d // 2), feature_slice(i)]
            if k == 0:
                inner.begin(j)
        for copy in replaced(j):
            copy.start()

    @pl.when(step == blocks - 1)
    def _():
        select.start()
        for copy in more:
            copy.wait()

    @pl.when(step == 2 * blocks)
    def _():
        select.wait()
        for j in range(blocks):
            for copy in replaced(j):
                copy.wait()

    @pl.when(jnp.logical_and(step >= 2 * blocks, step < 2 * blocks + chunks))
    def _():
        here = pl.ds(pl.multiple_of((step - 2 * blocks) * CHUNK, CHUNK), CHUNK)
        total = nt(gsel[here, :], mixt[...])
        for i, w in enumerate((qpre, kpre, gatt)):
            total = total + nt(grads[i, here, :], w[...])
        x = val[here, :].astype(F32)
        hidden_o[...] = (gmid[here, :].astype(F32) + norm_back(x, scale_of(x), total)).astype(BF16)

    outer.run(step, out)
    inner.run(step, out2)


def run_projections(lengths, slopes, qpre, kpre, values, gatt, st, et, came, left, angles, gsel, hidden, gmid, mixed_t, normed_t, weights, depth, ident):
    n, d = qpre.shape
    heads, chunks = d // HEAD, n // CHUNK
    blocks = heads // 2
    rows = d // (4 * depth)
    outer = Reducer(0, blocks, 2, depth, rows, (1, 4, 5, 6), 4, (1, 2, 3, 4), (2, 2))
    inner = Reducer(blocks, blocks, 3, depth, rows, (1, 2, 3, 4), 4, (1, 2, 3, 4), (2, 2, 2))
    steps = max(outer.last, inner.last, 2 * blocks + chunks - 1) + 1
    geo = dict(chunks=chunks, blocks=blocks, d=d, n=n)
    late = lambda s: jnp.clip(s - 2 * blocks, 0, chunks - 1)
    whole = pltpu.VMEM((n, d), BF16)
    states = pltpu.VMEM((chunks,) + state_shape(d), BF16)
    one = pltpu.VMEM(state_shape(d), BF16)
    turned = pltpu.VMEM((d, n), BF16)
    return launch(
        functools.partial(projections_kernel, geo, outer, inner),
        "attention_backward_and_gradients",
        steps,
        [lengths, slopes, qpre, kpre, values, gatt, st, et, came, left, *angles]
        + [gsel, hidden, gmid, mixed_t, normed_t]
        + list(weights),
        [smem(), smem()] + [anywhere()] * 8 + [once(a.shape) for a in angles] + [anywhere()] * 9,
        [struct((n, d)), struct((2, rows, d // 2), F32), struct((3, rows, d // 2), F32)],
        [
            pl.BlockSpec((CHUNK, d), lambda s: (late(s), 0)),
            whole_block((2, rows, d // 2)),
            whole_block((3, rows, d // 2)),
        ],
        [whole] * 4
        + [states, states, one, whole, whole]
        + [
            pltpu.VMEM((3, n, d), BF16),
            pltpu.VMEM((n, 6 * HEAD), BF16),
            pltpu.VMEM((2, 2, CHUNK, CHUNK), F32),
            turned,
            turned,
            one,
            pltpu.SemaphoreType.DMA((15,)),
            pltpu.SemaphoreType.DMA((blocks, 2, 4)),
        ]
        + outer.scratch
        + inner.scratch,
        30 * n * d * d,
        partners=outer.partners,
        ident=ident,
    )


def input_kernel(wq, wk, wv, ws, grads, gsel, hid, gmid, out):
    total = nt(grads[0], wq[...]) + nt(grads[1], wk[...]) + nt(grads[2], wv[...]) + nt(gsel[...], ws[...])
    x = hid[...].astype(F32)
    out[...] = (gmid[...].astype(F32) + norm_back(x, scale_of(x), total)).astype(BF16)


def run_input(weights, grads, gsel, hidden, gmid):
    n, d = hidden.shape
    tile = pl.BlockSpec((CHUNK, d), lambda c: (c, 0))
    return launch(
        input_kernel,
        "input_gradient",
        n // CHUNK,
        list(weights) + [grads, gsel, hidden, gmid],
        [whole_block(w.shape) for w in weights]
        + [
            pl.BlockSpec((3, CHUNK, d), lambda c: (0, c, 0)),
            tile,
            tile,
            tile,
        ],
        [struct((n, d))],
        [tile],
        [],
        8 * n * d * d,
    )


def reduced(lefts, items, rights, spec, peers, width):
    full = run_weights(lefts, items, rights, spec, peers, width)
    parts = lax.axis_size("dp")
    full = full.reshape(peers, len(items), 2, parts // 2, -1, width)
    full = jnp.swapaxes(full, 2, 3).reshape(peers, len(items), parts, -1, width)
    mine = lax.psum_scatter(full, "dp", scatter_dimension=2, tiled=False)
    return lax.psum_scatter(mine, "mp", scatter_dimension=0, tiled=False).astype(F32)


def per_device(
    hidden_in,
    query_weight,
    key_weight,
    value_weight,
    select_weight,
    out_weight,
    first_weight,
    second_weight,
    down_weight,
    decay_slope,
    doc_lengths,
    cotangent,
):
    count, d = hidden_in.shape
    heads, chunks = d // HEAD, count // CHUNK
    peers, parts = lax.axis_size("mp"), lax.axis_size("dp")
    me = lax.axis_index("mp")
    depth = parts // 4
    group = count * peers
    units = first_weight.shape[1]
    lengths = doc_lengths.astype(jnp.int32)
    angles = tables(group // 2)
    slopes = decay_slope
    matrices = (first_weight, second_weight, down_weight)
    riding = peers == 2

    if riding:
        cut = units // 256 * 128
        ranges = [(0, cut), (cut, units - cut)]
    else:
        ranges = [(0, units)]

    def like(arrays, count=None):
        return [struct(a.shape if count is None else (count,) + a.shape) for a in arrays]

    def over_mp(g):
        low, size = ranges[g]

        def source(w):
            def src(i, o):
                eighth = lax.rem(lax.axis_index("dp"), 8)
                if w < 2:
                    rows = d // 8
                    return i[w].at[pl.ds(pl.multiple_of(eighth * rows, 16), rows), pl.ds(low, size)]
                rows = size // 8
                return i[w].at[pl.ds(pl.multiple_of(low + eighth * rows, 16), rows), :]

            return src

        outs = [struct((d // 8, size)), struct((d // 8, size)), struct((size // 8, d))]
        return outs, [(source(w), lambda i, o, w=w: o[w], "mp", 1) for w in range(3)]

    def near(src, dst):
        return [
            (lambda i, o: src(i, o), lambda i, o: dst(i, o).at[0], "dp", 2),
            (lambda i, o: src(i, o), lambda i, o: dst(i, o).at[1], "dp", 4),
            (lambda i, o: src(i, o), lambda i, o: dst(i, o).at[2], "dp", 1),
        ]

    def far(src, dst, rows, balanced):
        top = -(-rows // 32) * 16 if balanced else 0
        upper, lower = pl.ds(0, top), pl.ds(top, rows - top)
        over_x = (lambda i, o: src(i, o).at[1, upper, :], lambda i, o: dst(i, o).at[0, upper, :], "dp", 2)
        return ([over_x] if balanced else []) + [
            (lambda i, o: src(i, o).at[0, lower, :], lambda i, o: dst(i, o).at[0, lower, :], "dp", 4),
            (lambda i, o: src(i, o).at[0], lambda i, o: dst(i, o).at[1], "dp", 1),
            (lambda i, o: src(i, o).at[1], lambda i, o: dst(i, o).at[2], "dp", 1),
        ]

    def onward(pieces, out, at, balanced):
        ref = lambda k: lambda i, o: o[k]
        one, two, three = [], [], []
        for w in range(3):
            one += near(pieces(w), ref(at + w))
            two += far(ref(at + w), ref(at + 3 + w), out[w].shape[0], balanced)
            three.append((lambda i, o, w=w: o[at + 3 + w].at[0], ref(at + 6 + w), "dp", 1))
        return like(out, 3) + like(out, 3) + like(out), [one, two, three]

    if riding:
        outs, copies = over_mp(0)
        more, phases = onward(lambda w: lambda i, o: o[w], outs, 3, True)
        outs_b, copies_b = over_mp(1)
        spans = [(0, chunks), (chunks + 1, 2 * chunks), (2 * chunks + 1, 3 * chunks - 2), (3 * chunks - 1,) * 2]
        guests = [
            Carry(matrices, outs + more, [span + (c,) for span, c in zip(spans, [copies] + phases)]),
            Carry(matrices, outs_b, [(chunks + 2, 3 * chunks - 1, copies_b)]),
        ]
        weights = [key_weight, value_weight, query_weight, select_weight, out_weight]
        kpre, values, st, qpre, sel, normed_t, attended, mixed_t, middle, second, second_t, cot_t, came, *got = run_forward(
            lengths, slopes, hidden_in, cotangent, weights, angles, parts, guests, ident=1
        )
    else:
        normed, normed_t, kpre, values, st, final = run_keys(
            peers, lengths, slopes, hidden_in, key_weight, value_weight, angles, parts
        )
        begin, start, last = jnp.int32(0), jnp.int32(0), (me + 1) * count - CHUNK
        for i in range(lengths.shape[1]):
            begin = jnp.where(last >= start, start, begin)
            start = start + lengths[0, i]
        passes = (begin < me * count).astype(F32)
        decay = jnp.exp(-slopes * count)
        finals = lax.all_gather(final, "mp")
        keeps = lax.all_gather(passes.reshape(1), "mp")[:, 0]

        def ahead(k, total):
            new = finals[k].astype(F32) + (keeps[k] * decay)[:, None, None] * total
            return jnp.where(k < me, new, total)

        came = lax.fori_loop(0, peers, ahead, jnp.zeros(final.shape, F32)).astype(BF16)
        qpre, sel, att = run_inside(
            peers, lengths, slopes, normed, query_weight, select_weight, kpre, values, st, angles
        )
        attended, mixed_t, middle, second, second_t, cot_t = run_mix(
            peers, lengths, slopes, att, qpre, came, sel, out_weight, hidden_in, cotangent, angles, parts
        )

    if riding:
        had_b = got[12:15]
        more, phases = onward(lambda w: lambda i, o: i[w], had_b, 0, True)
        ride = Carry(had_b, more, [(0, 1, phases[0]), (2, 3, phases[1]), (4, 4, phases[2])])
        output, grad_middle, grad_sel, grad_att, et, left, sglu = run_units(
            lengths, slopes, matrices, second, cotangent, second_t, cot_t, [middle, sel, attended, qpre],
            angles, out_weight, got[:12], ride, ranges[0][1], depth, ident=2,
        )
    else:
        sources = [lax.all_gather(w, "mp") for w in matrices]
        grads, term, part = run_sglu(second, cotangent, *sources)
        units_spec = lambda at: pl.BlockSpec((None, None, count, units), lambda s: at(s) + (0, 0))
        sglu = reduced([second_t, cot_t], (0, 0, 1), grads, units_spec, peers, units)
        output, grad_middle, grad_sel, grad_att, et, leaving = run_after(
            peers, lengths, slopes, term, part, cotangent, middle, sel, attended, out_weight, qpre, angles
        )
    inputs_weights = [query_weight, key_weight, value_weight, select_weight]
    if riding:
        grad_hidden, out_sel, inputs = run_projections(
            lengths, slopes, qpre, kpre, values, grad_att, st, et, came, left, angles, grad_sel,
            hidden_in, grad_middle, mixed_t, normed_t, inputs_weights, depth, ident=3,
        )
    else:
        leavings = lax.all_gather(leaving, "mp")

        def behind(step, total):
            k = peers - 1 - step
            new = leavings[k].astype(F32) + (keeps[k] * decay)[:, None, None] * total
            return jnp.where(k > me, new, total)

        left = lax.fori_loop(0, peers, behind, jnp.zeros(leaving.shape, F32)).astype(BF16)
        share = d // peers
        wide_spec = lambda at: pl.BlockSpec((None, count, share), lambda s: (at(s)[0], 0, at(s)[1]))
        pair = jnp.stack([grad_middle, grad_sel])
        out_sel = reduced([mixed_t, normed_t], (0, 1), pair, wide_spec, peers, share)
        (qkv,) = run_attention_back(
            peers, lengths, slopes, qpre, kpre, values, grad_att, st, came, et, left, angles
        )
        inputs = reduced([normed_t], (0, 0, 0), qkv, wide_spec, peers, share)
        (grad_hidden,) = run_input(inputs_weights, qkv, grad_sel, hidden_in, grad_middle)
    return (
        output,
        grad_hidden,
        inputs[0],
        inputs[1],
        inputs[2],
        out_sel[1],
        out_sel[0],
        sglu[0],
        sglu[1],
        jnp.transpose(sglu[2]),
    )


def solution(mesh):
    rows = P(("dp", "mp"), None)
    in_specs = (
        rows,
        P(),
        P(),
        P(),
        P(),
        P(),
        P(None, "mp"),
        P(None, "mp"),
        P("mp", None),
        P(),
        P("dp", None),
        rows,
    )
    out_specs = (rows, rows) + (P("dp", "mp"),) * 7 + (P("mp", "dp"),)
    return jax.shard_map(
        per_device, mesh=mesh, in_specs=in_specs, out_specs=out_specs, check_vma=False
    )
```

```python
import functools

import jax
import jax.numpy as jnp
import numpy as np
from jax import lax
from jax.experimental import pallas as pl
from jax.experimental.pallas import tpu as pltpu
from jax.sharding import PartitionSpec as P

HEAD = 128
CHUNK = 256
EPSILON = 1e-06
BF16 = jnp.bfloat16
F32 = jnp.float32
VMEM_LIMIT = 62 * 1024 * 1024


def nn(left, right):
    return jnp.dot(left, right, preferred_element_type=F32)


def nt(left, right):
    return lax.dot_general(left, right, (((1,), (1,)), ((), ())), preferred_element_type=F32)


def scale_of(values):
    return lax.rsqrt(jnp.mean(values * values, axis=-1, keepdims=True) + EPSILON)


def norm_back(values, scale, upstream):
    return scale * upstream - values * (scale * scale * scale) * jnp.mean(
        values * upstream, axis=-1, keepdims=True
    )


def sigmoid(v):
    return 0.5 * jnp.tanh(0.5 * v) + 0.5


def featured(pre, cos, sin):
    act = pre * sigmoid(pre)
    return jnp.concatenate([act * cos, act * sin], axis=-1).astype(BF16)


def head_slice(h):
    return slice(h * HEAD, (h + 1) * HEAD)


def turned_shape(d, n):
    return (2, d // 2, n)


def put_turned(ref, value, parts):
    turned = value.T
    rows = turned.shape[0] // parts
    for i in range(parts):
        ref[i % 2, (i // 2) * rows : (i // 2 + 1) * rows, :] = turned[i * rows : (i + 1) * rows, :]


def put_turned_at(ref, value, parts, cols):
    turned = value.T
    half, rows = turned.shape[0] // 2, turned.shape[0] // parts
    for i in range(parts):
        at = (i % 2) * half + (i // 2) * rows
        ref[at : at + rows, cols] = turned[i * rows : (i + 1) * rows, :]


def feature_slice(h):
    return slice(2 * h * HEAD, 2 * (h + 1) * HEAD)


def row_index(shape):
    return lax.broadcasted_iota(jnp.int32, shape, 0)


def fade_from_start(slope, width):
    return jnp.exp(-slope * (row_index((CHUNK, width)) + 1).astype(F32))


def fade_to_end(slope, width):
    return jnp.exp(-slope * (CHUNK - 1 - row_index((CHUNK, width))).astype(F32))


def decay_table(slope, transposed):
    rows = lax.broadcasted_iota(jnp.int32, (CHUNK, CHUNK), 0)
    cols = lax.broadcasted_iota(jnp.int32, (CHUNK, CHUNK), 1)
    gap = cols - rows if transposed else rows - cols
    return jnp.where(gap >= 0, jnp.exp(-slope * jnp.maximum(gap, 0).astype(F32)), 0.0)


def plus(*arrays):
    total = arrays[0].astype(F32)
    for a in arrays[1:]:
        total = total + a.astype(F32)
    return total


def smem():
    return pl.BlockSpec(memory_space=pltpu.SMEM)


def anywhere():
    return pl.BlockSpec(memory_space=pl.ANY)


def once(shape):
    zeros = (0,) * len(shape)
    return pl.BlockSpec(shape, lambda *_: zeros, pipeline_mode=pl.Buffered(1))


def whole_block(shape):
    zeros = (0,) * len(shape)
    return pl.BlockSpec(shape, lambda *_: zeros)


def cost(flops, arrays):
    moved = sum(int(np.prod(a.shape)) * jnp.dtype(a.dtype).itemsize for a in arrays)
    return pl.CostEstimate(flops=int(flops), bytes_accessed=moved, transcendentals=0)


def struct(shape, dtype=BF16):
    return jax.ShapeDtypeStruct(tuple(shape), dtype)


def flipped(index, mask):
    bit = 1
    while bit <= mask:
        if mask & bit:
            index = index + bit * (1 - 2 * lax.rem(lax.div(index, bit), 2))
        bit *= 2
    return index


def remote(src, dst, send, recv, axis, mask, where=None):
    return pltpu.make_async_remote_copy(
        src_ref=src,
        dst_ref=dst,
        send_sem=send,
        recv_sem=recv,
        device_id={axis: flipped(lax.axis_index(axis), mask) if where is None else where},
        device_id_type=pl.DeviceIdType.MESH,
    )


def greet(partners):
    barrier = pltpu.get_barrier_semaphore()
    for axis, mask in partners:
        pl.semaphore_signal(
            barrier,
            inc=1,
            device_id={axis: flipped(lax.axis_index(axis), mask)},
            device_id_type=pl.DeviceIdType.MESH,
        )
    pl.semaphore_wait(barrier, len(partners))


class Carry:
    def __init__(self, inputs, outs, phases):
        self.inputs, self.outs, self.phases = list(inputs), list(outs), phases
        count = sum(len(p[2]) for p in phases)
        self.scratch = [pltpu.SemaphoreType.DMA((count,)), pltpu.SemaphoreType.DMA((count,))]
        self.partners = [(c[2], c[3]) for p in phases for c in p[2]]

    def copies(self, which, ins, outs, scratch):
        at = sum(len(p[2]) for p in self.phases[:which])
        send, recv = scratch
        for k, (src, dst, axis, mask) in enumerate(self.phases[which][2]):
            yield remote(src(ins, outs), dst(ins, outs), send.at[at + k], recv.at[at + k], axis, mask)

    def before(self, step, ins, outs, scratch):
        for p, phase in enumerate(self.phases):

            @pl.when(step == phase[0])
            def _(p=p):
                for copy in self.copies(p, ins, outs, scratch):
                    copy.start()

    def after(self, step, ins, outs, scratch):
        for p, phase in enumerate(self.phases):

            @pl.when(step == phase[1])
            def _(p=p):
                for copy in self.copies(p, ins, outs, scratch):
                    copy.wait()


class Reducer:
    KINDS = 8

    def __init__(self, start, blocks, items, depth, rows, delays, slots, order, over_x, offset=0):
        self.offset = offset
        self.start, self.blocks, self.items = start, blocks, items
        self.slots, self.order = slots, order
        self.made = 2 if delays[0] else 1
        self.depth, self.rows, self.delays = depth, rows, delays
        self.upper = [(t, z) for t in range(items) for z in range(over_x[t])]
        self.lower = [(t, z) for t in range(items) for z in range(over_x[t], depth)]
        n, wide = 2 * depth * rows, 2 * HEAD
        buf = lambda *shape: pltpu.VMEM(shape, BF16)
        up, low = len(self.upper), len(self.lower)
        pair, flat = (up, rows, wide), (2, low, rows, HEAD)
        self.scratch = [
            buf(self.made, items, n, wide),
            buf(self.made, items, n, wide),
            buf(4 if delays[0] else 2, items, n, wide),
            buf(slots, *pair),
            buf(slots, *pair),
            buf(4, *pair),
            buf(slots, *flat),
            buf(slots, *flat),
            buf(4, *flat),
            buf(slots, up, rows, HEAD),
            buf(slots, up, rows, HEAD),
            buf(4, up, rows, HEAD),
            buf(slots, low, rows, HEAD),
            buf(slots, low, rows, HEAD),
            buf(4, low, rows, HEAD),
            buf(slots, depth, items, rows, HEAD),
            buf(4, depth - 1, items, rows, HEAD),
            pltpu.SemaphoreType.DMA((self.KINDS, blocks)),
            pltpu.SemaphoreType.DMA((self.KINDS, blocks)),
        ]
        self.partners = [("dp", 1), ("dp", 2), ("mp", 1)] + [("dp", 4 * k) for k in range(1, depth)]
        self.last = start + blocks - 1 + delays[3]

    def bind(self, scratch, places):
        self.refs = scratch
        self.given, self.kept = scratch[:2]
        self.x, self.z, self.where, self.partner_z = places

    @staticmethod
    def places(depth):
        dp, me = lax.axis_index("dp"), lax.axis_index("mp")
        z = lax.div(dp, 4)
        x = lax.div(dp - 4 * z, 2)
        core = dp - 4 * z - 2 * x
        where = {("dp", 1): dp + 1 - 2 * core, ("dp", 2): dp + 2 - 4 * x, ("mp", 1): 1 - me}
        partner_z = {}
        for k in range(1, depth):
            partner_z[k] = flipped(z, k)
            where["dp", 4 * k] = dp + 4 * (partner_z[k] - z)
        return x, z, where, partner_z

    def copies(self, stage, j):
        (given, kept, got, ps, pk, pr, qs, qk, qr, ps2, pk2, pr2, qs2, qk2, qr2, line, zr, send, recv) = self.refs
        slot, four = lax.rem(j, self.slots), lax.rem(j, 4)
        if stage == 0:
            plan = [(0, given.at[lax.rem(j, self.made)], got.at[lax.rem(j, got.shape[0])], "dp", 1)]
        elif stage == 1:
            plan = [(1, ps.at[slot], pr.at[four], "dp", 2), (2, qs.at[slot], qr.at[four], "mp", 1)]
        elif stage == 2:
            plan = [(3, ps2.at[slot], pr2.at[four], "mp", 1), (4, qs2.at[slot], qr2.at[four], "dp", 2)]
        else:
            plan = [
                (4 + k, line.at[slot, self.partner_z[k]], zr.at[four, k - 1], "dp", 4 * k)
                for k in range(1, self.depth)
            ]
        return [
            remote(src, dst, send.at[i, j], recv.at[i, j], axis, mask, self.where[axis, mask])
            for i, src, dst, axis, mask in plan
        ]

    def begin(self, j):
        for copy in self.copies(0, j):
            copy.start()

    def run(self, step, out):
        for stage in self.order:
            j = step - self.start - self.delays[stage - 1]

            @pl.when(jnp.logical_and(j >= 0, j < self.blocks))
            def _(stage=stage, j=j):
                for copy in self.copies(stage - 1, j):
                    copy.wait()
                self.add(stage, j, out)
                if stage < 4:
                    for copy in self.copies(stage, j):
                        copy.start()

    def add(self, stage, j, out):
        (given, kept, got, ps, pk, pr, qs, qk, qr, ps2, pk2, pr2, qs2, qk2, qr2, line, zr, send, recv) = self.refs
        slot, four, x, rows = lax.rem(j, self.slots), lax.rem(j, 4), self.x, self.rows
        if stage == 1:
            two, came = lax.rem(j, self.made), lax.rem(j, got.shape[0])

            def total(t, z, at):
                here = pl.ds(pl.multiple_of((2 * z + at) * rows, rows), rows)
                return kept[two, t, here, :] + got[came, t, here, :]

            for i, (t, z) in enumerate(self.upper):
                ps[slot, i] = total(t, z, 1 - x)
                pk[slot, i] = total(t, z, x)
            for i, (t, z) in enumerate(self.lower):
                for at in range(2):
                    block = total(t, z, at)
                    qk[slot, at, i] = block[:, :HEAD]
                    qs[slot, at, i] = block[:, HEAD:]
        elif stage == 2:
            for i in range(len(self.upper)):
                block = pk[slot, i] + pr[four, i]
                pk2[slot, i] = block[:, :HEAD]
                ps2[slot, i] = block[:, HEAD:]
            for i in range(len(self.lower)):
                qs2[slot, i] = qk[slot, 1 - x, i] + qr[four, 1 - x, i]
                qk2[slot, i] = qk[slot, x, i] + qr[four, x, i]
        elif stage == 3:
            for i, (t, z) in enumerate(self.upper):
                line[slot, z, t] = pk2[slot, i] + pr2[four, i]
            for i, (t, z) in enumerate(self.lower):
                line[slot, z, t] = qk2[slot, i] + qr2[four, i]
        else:
            total = plus(line[slot, self.z], *[zr[four, k] for k in range(self.depth - 1)])
            out[:, :, pl.ds(pl.multiple_of((self.offset + j) * HEAD, HEAD), HEAD)] = total


def launch(kernel, name, steps, inputs, specs, outs, out_specs, scratch, flops, guests=(), ident=None, partners=()):
    guests = list(guests)
    partners = list(partners) + [p for g in guests for p in g.partners]
    partners = sorted(set(partners))
    all_inputs = list(inputs) + [a for g in guests for a in g.inputs]
    all_specs = list(specs) + [anywhere() for g in guests for _ in g.inputs]
    all_outs = list(outs) + [a for g in guests for a in g.outs]
    all_out_specs = list(out_specs) + [anywhere() for g in guests for _ in g.outs]
    all_scratch = list(scratch) + [a for g in guests for a in g.scratch]

    def body(*refs):
        refs = list(refs)
        take = lambda k: [refs.pop(0) for _ in range(k)]
        own = take(len(inputs))
        ins = [take(len(g.inputs)) for g in guests]
        own += take(len(outs))
        gone = [take(len(g.outs)) for g in guests]
        own += take(len(scratch))
        held = [take(len(g.scratch)) for g in guests]
        step = pl.program_id(0)
        if partners:

            @pl.when(step == 0)
            def _():
                greet(partners)

        for g, i, o, s in zip(guests, ins, gone, held):
            g.before(step, i, o, s)
        kernel(*own)
        for g, i, o, s in zip(guests, ins, gone, held):
            g.after(step, i, o, s)

    extra = dict(collective_id=ident, has_side_effects=True) if partners else {}
    return pl.pallas_call(
        body,
        grid=(steps,),
        in_specs=all_specs,
        out_specs=all_out_specs,
        out_shape=all_outs,
        scratch_shapes=all_scratch,
        compiler_params=pltpu.CompilerParams(
            vmem_limit_bytes=VMEM_LIMIT, dimension_semantics=("arbitrary",), **extra
        ),
        cost_estimate=cost(flops, all_inputs + all_outs),
        name=name,
    )(*all_inputs)


def tables(longest):
    freq = 10000.0 ** (-np.arange(HEAD, dtype=np.float64) / HEAD)

    def both(places):
        phase = places[:, None] * freq[None, :]
        return jnp.asarray(np.concatenate([np.cos(phase), np.sin(phase)], axis=1), F32)

    return both(np.arange(CHUNK)), both(np.arange(0, longest, CHUNK))


class Layout:
    def __init__(self, lengths, peers, count):
        self.lengths, self.peers, self.count = lengths, peers, count
        self.me = lax.axis_index("mp")
        self.offset = self.me * count

    def begin(self, first):
        begin = start = jnp.int32(0)
        for i in range(self.lengths.shape[1]):
            begin = jnp.where(first >= start, start, begin)
            start = start + self.lengths[0, i]
        return begin

    def first(self, c):
        return self.offset + c * CHUNK

    def keep(self, c):
        return jnp.where(self.begin(self.first(c)) < self.first(c), 1.0, 0.0)

    def before(self, c):
        return jnp.where(self.begin(self.first(c)) < self.offset, 1.0, 0.0)

    def after(self, c):
        last = self.begin(self.offset + self.count - CHUNK)
        return jnp.where(last <= self.first(c), 1.0, 0.0) * jnp.where(self.me < self.peers - 1, 1.0, 0.0)

    def alive(self, c, width):
        end = jnp.int32(0)
        for i in range(self.lengths.shape[1]):
            end = end + self.lengths[0, i]
        return (row_index((CHUNK, width)) + self.first(c) < end).astype(F32)

    def angles(self, c, fine, coarse):
        base = self.first(c) - self.begin(self.first(c))
        start = jnp.zeros((1, 2 * HEAD), F32)
        for k in range(coarse.shape[0]):
            start = start + coarse[k : k + 1, :] * jnp.where(base == k * CHUNK, 1.0, 0.0)
        cb, sb = start[:, :HEAD], start[:, HEAD:]
        cf, sf = fine[:, :HEAD], fine[:, HEAD:]
        return cf * cb - sf * sb, sf * cb + cf * sb


def normed_of(hid):
    x = hid[...].astype(F32)
    return (x * scale_of(x)).astype(BF16)


def states_chunk(heads, slopes, keep, key, values, state, put):
    for h in range(heads):
        slope = slopes[h]
        faded = (values[:, head_slice(h)] * fade_to_end(slope, HEAD)).astype(BF16)
        old = state[h] * keep
        put(h, old.astype(BF16))
        state[h] = jnp.exp(jnp.full((1, 2 * HEAD), -slope * CHUNK, F32)) * old + nn(faded.T, key(h))


def inside_chunk(heads, slopes, query, key, values, st, table, put):
    for h in range(heads):
        asked = query(h)
        weights = (nt(asked, key(h)) * table(h)).astype(BF16)
        put(h, nn(weights, values(h)) + fade_from_start(slopes[h], HEAD) * nt(asked, st(h)))


def carried_chunk(heads, slopes, layout, c, att, query, came, total):
    reached = layout.before(c)
    lag = (c * CHUNK).astype(F32)
    alive = layout.alive(c, HEAD)
    for h in range(heads):
        fade = jnp.exp(-slopes[h] * (row_index((CHUNK, HEAD)).astype(F32) + (lag + 1.0))) * reached
        total[:, head_slice(h)] = (att(h) + fade * nt(query(h), came[h])) * alive


def mix_chunk(total, sel, wo, hid, put):
    attended = total[...]
    mixed = (attended * scale_of(attended) * sel.astype(F32)).astype(BF16)
    middle = hid.astype(F32) + nn(mixed, wo)
    second = (middle * scale_of(middle)).astype(BF16)
    put(attended.astype(BF16), mixed, middle.astype(BF16), second)


def state_shape(d):
    return (d // HEAD, HEAD, 2 * HEAD)


def keys_kernel(peers, parts, count, lengths, slopes, hid, wk, wv, fine, coarse, normed_o, turned_o, kpre_o, val_o, st_o, fin_o, state):
    c = pl.program_id(0)
    layout = Layout(lengths, peers, count)

    @pl.when(c == 0)
    def _():
        state[...] = jnp.zeros_like(state)

    normed = normed_of(hid)
    normed_o[...] = normed
    put_turned(turned_o, normed, parts)
    kpre = nn(normed, wk[...])
    kpre_o[...] = kpre.astype(BF16)
    values = nn(normed, wv[...])
    val_o[...] = values.astype(BF16)
    cs, sn = layout.angles(c, fine, coarse)

    def put(h, value):
        st_o[0, h] = value

    key = lambda h: featured(kpre[:, head_slice(h)], cs, sn)
    states_chunk(state.shape[0], slopes, layout.keep(c), key, values, state, put)
    fin_o[...] = state[...].astype(BF16)


def run_keys(peers, lengths, slopes, hidden, wk, wv, angles, parts):
    n, d = hidden.shape
    heads, chunks = d // HEAD, n // CHUNK
    turned = turned_shape(d, n)
    tile = pl.BlockSpec((CHUNK, d), lambda c: (c, 0))
    outs = [struct((n, d)), struct(turned), struct((n, d)), struct((n, d)), struct((chunks,) + state_shape(d)), struct(state_shape(d))]
    return launch(
        functools.partial(keys_kernel, peers, parts, n),
        "keys_values_states",
        chunks,
        [lengths, slopes, hidden, wk, wv, *angles],
        [smem(), smem(), tile, whole_block(wk.shape), whole_block(wv.shape)] + [whole_block(a.shape) for a in angles],
        outs,
        [
            tile,
            pl.BlockSpec(turned[:2] + (CHUNK,), lambda c: (0, 0, c)),
            tile,
            tile,
            pl.BlockSpec((1,) + state_shape(d), lambda c: (c, 0, 0, 0)),
            whole_block(state_shape(d)),
        ],
        [pltpu.VMEM(state_shape(d), F32)],
        4 * n * d * d,
    )


def inside_kernel(peers, count, lengths, slopes, normed, wq, ws, kpre, values, st, fine, coarse, qpre_o, sel_o, att_o):
    c = pl.program_id(0)
    layout = Layout(lengths, peers, count)
    x = normed[...]
    qpre = nn(x, wq[...])
    qpre_o[...] = qpre.astype(BF16)
    sel_o[...] = nn(x, ws[...]).astype(BF16)
    cs, sn = layout.angles(c, fine, coarse)

    def put(h, value):
        att_o[:, head_slice(h)] = value

    inside_chunk(
        st.shape[1],
        slopes,
        lambda h: featured(qpre[:, head_slice(h)], cs, sn),
        lambda h: featured(kpre[:, head_slice(h)].astype(F32), cs, sn),
        lambda h: values[:, head_slice(h)],
        lambda h: st[0, h],
        lambda h: decay_table(slopes[h], False),
        put,
    )


def run_inside(peers, lengths, slopes, normed, wq, ws, kpre, values, st, angles):
    n, d = normed.shape
    chunks = n // CHUNK
    tile = pl.BlockSpec((CHUNK, d), lambda c: (c, 0))
    return launch(
        functools.partial(inside_kernel, peers, n),
        "queries_attention",
        chunks,
        [lengths, slopes, normed, wq, ws, kpre, values, st, *angles],
        [smem(), smem(), tile, whole_block(wq.shape), whole_block(ws.shape), tile, tile]
        + [pl.BlockSpec((1,) + state_shape(d), lambda c: (c, 0, 0, 0))]
        + [whole_block(a.shape) for a in angles],
        [struct((n, d)), struct((n, d)), struct((n, d), F32)],
        [tile, tile, tile],
        [],
        6 * n * d * d,
    )


def mix_kernel(peers, parts, count, lengths, slopes, att, qpre, came, sel, wo, hid, cot, fine, coarse, att_o, mixt_o, mid_o, sec_o, sect_o, cott_o, total):
    c = pl.program_id(0)
    layout = Layout(lengths, peers, count)
    cs, sn = layout.angles(c, fine, coarse)
    carried_chunk(
        came.shape[0],
        slopes,
        layout,
        c,
        lambda h: att[:, head_slice(h)],
        lambda h: featured(qpre[:, head_slice(h)].astype(F32), cs, sn),
        came,
        total,
    )

    def put(attended, mixed, middle, second):
        att_o[...] = attended
        put_turned(mixt_o, mixed, parts)
        mid_o[...] = middle
        sec_o[...] = second
        put_turned(sect_o, second, parts)

    mix_chunk(total, sel[...], wo[...], hid[...], put)
    put_turned(cott_o, cot[...], parts)


def run_mix(peers, lengths, slopes, att, qpre, came, sel, wo, hidden, cot, angles, parts):
    n, d = hidden.shape
    chunks = n // CHUNK
    turned = turned_shape(d, n)
    tile = pl.BlockSpec((CHUNK, d), lambda c: (c, 0))
    turned_tile = pl.BlockSpec(turned[:2] + (CHUNK,), lambda c: (0, 0, c))
    return launch(
        functools.partial(mix_kernel, peers, parts, n),
        "carried_mixed_middle",
        chunks,
        [lengths, slopes, att, qpre, came, sel, wo, hidden, cot, *angles],
        [smem(), smem(), tile, tile, whole_block(came.shape), tile, whole_block(wo.shape), tile, tile]
        + [whole_block(a.shape) for a in angles],
        [struct((n, d)), struct(turned), struct((n, d)), struct((n, d)), struct(turned), struct(turned)],
        [tile, turned_tile, tile, tile, turned_tile, turned_tile],
        [pltpu.VMEM((CHUNK, d), F32)],
        3 * n * d * d,
    )


def forward_kernel(chunks, parts, lengths, slopes, fine, coarse, *refs):
    refs = list(refs)
    take = lambda k: [refs.pop(0) for _ in range(k)]
    hid_h, cot_h = take(2)
    weights_h = take(5)
    (kpre_o, val_o, st_o, qpre_o, sel_o) = take(5)
    (turned_o, att_o, mixt_o, mid_o, sec_o, sect_o, cott_o, came_o) = take(8)
    (weights, normed, kpre, val, st, qpre, sel, att, state, final, came, total, keyed, asked, table) = take(15)
    (hid, cot, normt, cott) = take(4)
    (load_sems, out_sems, state_sems, chunk_sems) = take(4)
    heads = state.shape[0]
    step = pl.program_id(0)
    c = lax.rem(step, chunks)
    here = pl.ds(pl.multiple_of(c * CHUNK, CHUNK), CHUNK)
    layout = Layout(lengths, 2, chunks * CHUNK)
    loads = [pltpu.make_async_copy(w, weights.at[i], load_sems.at[i]) for i, w in enumerate(weights_h)]
    saves = [
        pltpu.make_async_copy(src, dst, out_sems.at[i])
        for i, (src, dst) in enumerate([(kpre, kpre_o), (val, val_o), (st, st_o), (qpre, qpre_o), (sel, sel_o)])
    ]
    exchange = remote(final, came, state_sems.at[0], state_sems.at[1], "mp", 1)
    d = hid.shape[1]
    half = d // 2
    rows_in = [
        pltpu.make_async_copy(hid_h, hid, load_sems.at[5]),
        pltpu.make_async_copy(cot_h, cot, load_sems.at[6]),
    ]

    def both_halves(src, dst, at):
        return [
            pltpu.make_async_copy(src.at[pl.ds(k * half, half), :], dst.at[k], out_sems.at[at + k]) for k in range(2)
        ]

    turned = both_halves(normt, turned_o, 5)
    turned_cot = both_halves(cott, cott_o, 7)
    arrived = pltpu.make_async_copy(came, came_o, out_sems.at[9])

    def finished(c):
        here = pl.ds(pl.multiple_of(c * CHUNK, CHUNK), CHUNK)
        copies = [
            pltpu.make_async_copy(src.at[here, :], dst.at[here, :], chunk_sems.at[c, i])
            for i, (src, dst) in enumerate([(kpre, att_o), (val, mid_o), (normed, sec_o)])
        ]
        for i, dst in enumerate((mixt_o, sect_o)):
            cols = pl.ds(pl.multiple_of(i * d + c * CHUNK, CHUNK), CHUNK)
            for k in range(2):
                src = keyed.at[pl.ds(k * half, half), cols]
                copies.append(pltpu.make_async_copy(src, dst.at[k, :, here], chunk_sems.at[c, 3 + 2 * i + k]))
        return copies

    @pl.when(step == 0)
    def _():
        for copy in rows_in[:1] + loads + rows_in[1:]:
            copy.start()
        state[...] = jnp.zeros_like(state)
        for copy in rows_in[:1] + loads[:2]:
            copy.wait()

    @pl.when(step < chunks)
    def _():
        x = normed_of(hid.at[here, :])
        normed[here, :] = x
        put_turned_at(normt, x, parts, here)
        keys = nn(x, weights[0])
        kpre[here, :] = keys.astype(BF16)
        values = nn(x, weights[1])
        val[here, :] = values.astype(BF16)
        cs, sn = layout.angles(c, fine, coarse)

        def put(h, value):
            st[c, h] = value

        def key(h):
            value = featured(keys[:, head_slice(h)], cs, sn)
            keyed[here, feature_slice(h)] = value
            return value

        states_chunk(heads, slopes, layout.keep(c), key, values, state, put)

    @pl.when(step == chunks - 1)
    def _():
        final[...] = state[...].astype(BF16)
        exchange.start()
        for copy in saves[:3] + turned:
            copy.start()

    @pl.when(step == chunks)
    def _():
        for h in range(heads):
            table[h] = decay_table(slopes[h], False)
        for copy in loads[2:4] + rows_in[1:]:
            copy.wait()

    @pl.when(jnp.logical_and(step >= chunks, step < 2 * chunks))
    def _():
        x = normed[here, :]
        queries = nn(x, weights[2])
        qpre[here, :] = queries.astype(BF16)
        sel[here, :] = nn(x, weights[3]).astype(BF16)
        cs, sn = layout.angles(c, fine, coarse)

        def put(h, value):
            att[here, head_slice(h)] = value

        def query(h):
            value = featured(queries[:, head_slice(h)], cs, sn)
            asked[here, feature_slice(h)] = value
            return value

        inside_chunk(
            heads,
            slopes,
            query,
            lambda h: keyed[here, feature_slice(h)],
            lambda h: val[here, head_slice(h)],
            lambda h: st[c, h],
            lambda h: table[h],
            put,
        )
        put_turned_at(cott, cot[here, :], parts, here)

    @pl.when(step == 2 * chunks - 1)
    def _():
        for copy in saves[3:] + turned_cot:
            copy.start()
        for copy in saves[:3]:
            copy.wait()

    @pl.when(step == 2 * chunks)
    def _():
        loads[4].wait()
        exchange.wait()
        arrived.start()

    @pl.when(step >= 2 * chunks)
    def _():
        carried_chunk(
            heads,
            slopes,
            layout,
            c,
            lambda h: att[here, head_slice(h)],
            lambda h: asked[here, feature_slice(h)],
            came,
            total,
        )

        def put(attended, mixed, middle, second):
            kpre[here, :] = attended
            val[here, :] = middle
            normed[here, :] = second
            put_turned_at(keyed, mixed, parts, here)
            put_turned_at(keyed, second, parts, pl.ds(pl.multiple_of(d + c * CHUNK, CHUNK), CHUNK))

        mix_chunk(total, sel[here, :], weights[4], hid[here, :], put)
        for copy in finished(c):
            copy.start()

    @pl.when(step == 3 * chunks - 1)
    def _():
        for copy in saves[3:] + turned + turned_cot + [arrived]:
            copy.wait()
        for i in range(chunks):
            for copy in finished(i):
                copy.wait()


def run_forward(lengths, slopes, hidden, cot, weights, angles, parts, guests, ident):
    n, d = hidden.shape
    chunks = n // CHUNK
    turned = turned_shape(d, n)
    whole = pltpu.VMEM((n, d), BF16)
    return launch(
        functools.partial(forward_kernel, chunks, parts),
        "forward_to_sglu",
        3 * chunks,
        [lengths, slopes, *angles, hidden, cot, *weights],
        [smem(), smem()] + [once(a.shape) for a in angles] + [anywhere()] * 7,
        [struct((n, d)), struct((n, d)), struct((chunks,) + state_shape(d)), struct((n, d)), struct((n, d))]
        + [struct(turned), struct((n, d)), struct(turned), struct((n, d)), struct((n, d)), struct(turned), struct(turned)]
        + [struct(state_shape(d))],
        [anywhere()] * 13,
        [
            pltpu.VMEM((5, d, d), BF16),
            whole,
            whole,
            whole,
            pltpu.VMEM((chunks,) + state_shape(d), BF16),
            whole,
            whole,
            pltpu.VMEM((n, d), F32),
            pltpu.VMEM(state_shape(d), F32),
            pltpu.VMEM(state_shape(d), BF16),
            pltpu.VMEM(state_shape(d), BF16),
            pltpu.VMEM((CHUNK, d), F32),
            pltpu.VMEM((n, 2 * d), BF16),
            pltpu.VMEM((n, 2 * d), BF16),
            pltpu.VMEM((d // HEAD, CHUNK, CHUNK), F32),
            whole,
            whole,
            pltpu.VMEM((d, n), BF16),
            pltpu.VMEM((d, n), BF16),
            pltpu.SemaphoreType.DMA((7,)),
            pltpu.SemaphoreType.DMA((10,)),
            pltpu.SemaphoreType.DMA((2,)),
            pltpu.SemaphoreType.DMA((chunks, 7)),
        ],
        12 * n * d * d,
        guests=guests,
        ident=ident,
        partners=[("mp", 1)],
    )


def sglu_kernel(chunks, peers, sec, cot, w1, w2, wd, units_o, term_o, part_o):
    step = pl.program_id(0)
    here = pl.ds(pl.multiple_of(lax.rem(step, chunks) * CHUNK, CHUNK), CHUNK)
    left = nn(sec[...], w1[...])
    right = nn(sec[...], w2[...])
    inner = (left * right).astype(BF16)
    upstream = nt(cot[...], wd[...])
    grad_left = (upstream * right).astype(BF16)
    grad_right = (upstream * left).astype(BF16)
    units_o[0] = grad_left
    units_o[1] = grad_right
    units_o[2] = inner
    term = nn(inner, wd[...])
    part = nt(grad_left, w1[...]) + nt(grad_right, w2[...])

    @pl.when(step < chunks)
    def _():
        term_o[here, :] = term
        part_o[here, :] = part

    @pl.when(step >= chunks)
    def _():
        term_o[here, :] += term
        part_o[here, :] += part


def run_sglu(second, cot, w1, w2, wd):
    n, d = second.shape
    peers, _, width = w1.shape
    chunks = n // CHUNK
    tile = pl.BlockSpec((CHUNK, d), lambda s: (lax.rem(s, chunks), 0))
    block = lambda shape: pl.BlockSpec((None,) + shape, lambda s: (lax.div(s, chunks), 0, 0))
    return launch(
        functools.partial(sglu_kernel, chunks, peers),
        "sglu",
        peers * chunks,
        [second, cot, w1, w2, wd],
        [tile, tile, block((d, width)), block((d, width)), block((width, d))],
        [struct((3, peers, n, width)), struct((n, d), F32), struct((n, d), F32)],
        [
            pl.BlockSpec((3, None, CHUNK, width), lambda s: (0, lax.div(s, chunks), lax.rem(s, chunks), 0)),
            whole_block((n, d)),
            whole_block((n, d)),
        ],
        [],
        12 * n * d * width * peers,
    )


def units_kernel(geo, reducers, ride, lengths, slopes, fine, coarse, *refs):
    blocks, cut, d, units, chunks = geo["blocks"], geo["cut"], geo["d"], geo["units"], geo["chunks"]
    refs = list(refs)
    take = lambda k: [refs.pop(0) for _ in range(k)]
    weights_h = take(3)
    (x_h, cot_h, xt_h, cott_h, wo_h) = take(5)
    rows_h = take(4)
    pieces = take(12)
    had_b = take(3)
    rows_out = take(4)
    (et_o, left_o, sums_o) = take(3)
    pieces = pieces + had_b + take(9)
    (term, part, x, cot, xt, cott, o1, o2, od, c12, cd, inner, grads, state, e0, sums) = take(16)
    (left,) = take(1)
    (tiles, made, ends) = take(3)
    (sems, own_sems, block_sems, tile_sems, made_sems) = take(5)
    places = Reducer.places(reducers[0].depth)
    for reducer in reducers:
        reducer.bind(take(len(reducer.scratch)), places)
    step = pl.program_id(0)
    ride.before(step, had_b, pieces[15:], refs)
    core = lax.rem(lax.axis_index("dp"), 2)
    eighth = lax.rem(lax.axis_index("dp"), 8)
    heads = state.shape[0]
    layout = Layout(lengths, 2, chunks * CHUNK)

    def fetch(g, parts=slice(0, 8)):
        size = cut if g == 0 else units - cut
        masks = [(0, None, 0), (3, 0, 2), (3, 1, 4), (3, 2, 1), (6, 0, 6), (6, 1, 3), (6, 2, 5), (9, None, 7)]
        copies = []
        for w, region in enumerate((o1, o2, od)):
            rows = d // 8 if w < 2 else size // 8
            for k, (at, inner, mask) in list(enumerate(masks))[parts]:
                src = pieces[12 * g + at + w]
                src = src if inner is None else src.at[inner]
                here = pl.ds(pl.multiple_of(flipped(eighth, mask) * rows, 16), rows)
                dst = region.at[here, pl.ds(0, size)] if w < 2 else region.at[here, :]
                copies.append(pltpu.make_async_copy(src, dst, sems.at[g, w, k]))
        return copies

    own = [
        pltpu.make_async_copy(x_h, x, own_sems.at[6]),
        pltpu.make_async_copy(cot_h, cot, own_sems.at[0]),
        pltpu.make_async_copy(xt_h.at[1 - core], xt.at[pl.ds(0, d // 2), :], own_sems.at[1]),
        pltpu.make_async_copy(xt_h.at[core], xt.at[pl.ds(d // 2, d // 2), :], own_sems.at[2]),
        pltpu.make_async_copy(cott_h.at[1 - core], cott.at[pl.ds(0, d // 2), :], own_sems.at[3]),
        pltpu.make_async_copy(cott_h.at[core], cott.at[pl.ds(d // 2, d // 2), :], own_sems.at[4]),
    ]
    out_weight = pltpu.make_async_copy(wo_h, xt, own_sems.at[7])
    saved = pltpu.make_async_copy(sums, sums_o, own_sems.at[5])
    arrived = pltpu.make_async_copy(left, left_o, own_sems.at[8])
    exchange = remote(e0, left, own_sems.at[9], own_sems.at[10], "mp", 1)

    def own_block(j):
        slot, here = lax.rem(j, 2), pl.ds(pl.multiple_of(j * HEAD, HEAD), HEAD)
        return [
            pltpu.make_async_copy(weights_h[0].at[:, here], c12.at[slot, :, pl.ds(0, HEAD)], block_sems.at[slot, 0]),
            pltpu.make_async_copy(
                weights_h[1].at[:, here], c12.at[slot, :, pl.ds(2 * HEAD, HEAD)], block_sems.at[slot, 1]
            ),
            pltpu.make_async_copy(weights_h[2].at[here, :], cd.at[slot, pl.ds(0, HEAD), :], block_sems.at[slot, 2]),
        ]

    def rows_at(i):
        return pl.ds(pl.multiple_of((chunks - 1 - i) * CHUNK, CHUNK), CHUNK)

    def tile(i):
        slot = lax.rem(i, 2)
        return [
            pltpu.make_async_copy(src.at[rows_at(i), :], tiles.at[slot, k], tile_sems.at[slot, k])
            for k, src in enumerate(rows_h)
        ]

    def results(i):
        slot = lax.rem(i, 2)
        return [
            pltpu.make_async_copy(made.at[slot, k], dst.at[rows_at(i), :], made_sems.at[slot, k])
            for k, dst in enumerate(rows_out)
        ] + [pltpu.make_async_copy(ends.at[slot], et_o.at[chunks - 1 - i], made_sems.at[slot, 4])]

    turn = cut // HEAD

    @pl.when(step == 0)
    def _():
        for copy in own_block(0) + fetch(0) + own:
            copy.start()
        term[...] = jnp.zeros_like(term)
        part[...] = jnp.zeros_like(part)
        state[...] = jnp.zeros_like(state)
        for copy in fetch(0):
            copy.wait()

    @pl.when(step == turn)
    def _():
        for copy in fetch(1, slice(7, 8)):
            copy.start()
        for copy in fetch(1):
            copy.wait()

    @pl.when(step < blocks)
    def _():
        local = step - jnp.where(step >= turn, turn, 0)
        here = pl.ds(pl.multiple_of(local * HEAD, HEAD), HEAD)
        at = lax.rem(step, 2)
        c12[at, :, HEAD : 2 * HEAD] = o1[:, here]
        c12[at, :, 3 * HEAD :] = o2[:, here]
        cd[at, HEAD:, :] = od[here, :]
        for copy in own_block(step):
            copy.wait()

    @pl.when(step < blocks - 1)
    def _():
        for copy in own_block(step + 1):
            copy.start()

    @pl.when(step == turn - 1)
    def _():
        for copy in fetch(1, slice(0, 7)):
            copy.start()

    @pl.when(step == 0)
    def _():
        for copy in own[:2]:
            copy.wait()

    @pl.when(step < blocks)
    def _():
        wide, at = 2 * HEAD, lax.rem(step, 2)
        for k in range(chunks):
            here = slice(k * CHUNK, (k + 1) * CHUNK)
            both = nn(x[here, :], c12[at])
            left, right = both[:, :wide], both[:, wide:]
            upstream = nt(cot[here, :], cd[at])
            inner[here, :] = (left * right).astype(BF16)
            grads[here, :wide] = (upstream * right).astype(BF16)
            grads[here, wide:] = (upstream * left).astype(BF16)

        @pl.when(step == 0)
        def _():
            for copy in own[2:]:
                copy.wait()

        for reducer in reducers:

            @pl.when(jnp.logical_and(step >= reducer.start, step < reducer.start + reducer.blocks))
            def _(reducer=reducer):
                both = nn(xt[...], grads[...]).astype(BF16)
                down = nn(cott[...], inner[...]).astype(BF16)
                for k, buffer in enumerate((reducer.given, reducer.kept)):
                    here = slice(k * (d // 2), (k + 1) * (d // 2))
                    buffer[0, 0] = both[here, :wide]
                    buffer[0, 1] = both[here, wide:]
                    buffer[0, 2] = down[here, :]
                    if k == 0:
                        reducer.begin(step - reducer.start)

        term[...] += nn(inner[...], cd[at])
        part[...] += nt(grads[...], c12[at])

    @pl.when(step == blocks - 1)
    def _():
        out_weight.start()
        for copy in tile(0):
            copy.start()

    @pl.when(step == blocks)
    def _():
        out_weight.wait()

    @pl.when(jnp.logical_and(step >= blocks, step < blocks + chunks))
    def _():
        i = step - blocks
        c, slot = chunks - 1 - i, lax.rem(i, 2)
        here = pl.ds(pl.multiple_of(c * CHUNK, CHUNK), CHUNK)
        for copy in tile(i):
            copy.wait()

        @pl.when(i < chunks - 1)
        def _():
            for copy in tile(i + 1):
                copy.start()

        @pl.when(i >= 2)
        def _():
            for copy in results(i - 2):
                copy.wait()

        cs, sn = layout.angles(c, fine, coarse)
        mid, sel, att, qpre = [tiles.at[slot, k] for k in range(4)]
        after_chunk(
            layout, c, heads, slopes, term[here, :], part[here, :], cot[here, :], mid, sel, att, xt[...], qpre, cs, sn,
            *[made.at[slot, k] for k in range(4)], ends.at[pl.ds(slot, 1)], state,
        )
        for copy in results(i):
            copy.start()

    @pl.when(step == blocks + chunks - 1)
    def _():
        e0[...] = state[...].astype(BF16)
        exchange.start()

    ride.after(step, had_b, pieces[15:], refs)
    for reducer in reducers:
        reducer.run(step, sums)

    @pl.when(step == reducers[-1].last)
    def _():
        saved.start()
        exchange.wait()
        arrived.start()
        for i in range(chunks - 2, chunks):
            for copy in results(i):
                copy.wait()
        arrived.wait()
        saved.wait()


def run_units(lengths, slopes, matrices, second, cot, second_t, cot_t, rows_in, angles, wo, pieces, ride, cut, depth, ident):
    n, d = second.shape
    chunks = n // CHUNK
    units = matrices[0].shape[1]
    blocks = units // HEAD
    rows = d // (4 * depth)
    turn = cut // HEAD
    reducers = [
        Reducer(0, turn, 3, depth, rows, (0, 2, 4, 6), 2, (4, 3, 2, 1), (1, 1, 1)),
        Reducer(turn, blocks - turn, 3, depth, rows, (0, 2, 4, 6), 2, (4, 3, 2, 1), (2, 2, 2), turn),
    ]
    geo = dict(blocks=blocks, cut=cut, d=d, units=units, chunks=chunks)
    turned = pltpu.VMEM((d, n), BF16)
    size = max(cut, units - cut)
    sums = (3, rows, units)
    return launch(
        functools.partial(units_kernel, geo, reducers, ride),
        "sglu_and_gradients",
        max(reducers[-1].last, blocks + chunks - 1) + 1,
        [lengths, slopes, *angles]
        + list(matrices)
        + [second, cot, second_t, cot_t, wo]
        + list(rows_in)
        + list(pieces)
        + ride.inputs,
        [smem(), smem()] + [once(a.shape) for a in angles] + [anywhere()] * (12 + len(pieces) + len(ride.inputs)),
        [struct((n, d))] * 4
        + [struct((chunks,) + state_shape(d)), struct(state_shape(d)), struct(sums, F32)]
        + ride.outs,
        [anywhere()] * (7 + len(ride.outs)),
        [
            pltpu.VMEM((n, d), F32),
            pltpu.VMEM((n, d), F32),
            pltpu.VMEM((n, d), BF16),
            pltpu.VMEM((n, d), BF16),
            turned,
            turned,
            pltpu.VMEM((d, size), BF16),
            pltpu.VMEM((d, size), BF16),
            pltpu.VMEM((size, d), BF16),
            pltpu.VMEM((2, d, 4 * HEAD), BF16),
            pltpu.VMEM((2, 2 * HEAD, d), BF16),
            pltpu.VMEM((n, 2 * HEAD), BF16),
            pltpu.VMEM((n, 4 * HEAD), BF16),
            pltpu.VMEM(state_shape(d), F32),
            pltpu.VMEM(state_shape(d), BF16),
            pltpu.VMEM(sums, F32),
            pltpu.VMEM(state_shape(d), BF16),
            pltpu.VMEM((2, 4, CHUNK, d), BF16),
            pltpu.VMEM((2, 4, CHUNK, d), BF16),
            pltpu.VMEM((2,) + state_shape(d), BF16),
            pltpu.SemaphoreType.DMA((2, 3, 8)),
            pltpu.SemaphoreType.DMA((11,)),
            pltpu.SemaphoreType.DMA((2, 3)),
            pltpu.SemaphoreType.DMA((2, 4)),
            pltpu.SemaphoreType.DMA((2, 5)),
        ]
        + [a for reducer in reducers for a in reducer.scratch]
        + ride.scratch,
        36 * n * d * units,
        partners=reducers[0].partners + ride.partners,
        ident=ident,
    )[:7]


def after_chunk(layout, c, heads, slopes, term, part, cot, mid, sel, att, wo, qpre, cs, sn, out_o, gmid_o, pair_o, gatt_o, et_o, state):
    middle = mid[...].astype(F32)
    out_o[...] = (middle + term).astype(BF16)
    grad_middle = cot.astype(F32) + norm_back(middle, scale_of(middle), part)
    branch = grad_middle.astype(BF16)
    gmid_o[...] = branch
    grad_mixed = nt(branch, wo)
    attended = att[...].astype(F32)
    scale = scale_of(attended)
    pair_o[...] = (grad_mixed * attended * scale).astype(BF16)
    grad_att = norm_back(attended, scale, grad_mixed * sel[...].astype(F32)) * layout.alive(c, 1)
    gatt_o[...] = grad_att.astype(BF16)
    keep = layout.keep(c)
    for h in range(heads):
        slope = slopes[h]
        query = featured(qpre[:, head_slice(h)].astype(F32), cs, sn)
        faded = (grad_att[:, head_slice(h)] * fade_from_start(slope, HEAD)).astype(BF16)
        old = state[h]
        et_o[0, h] = old.astype(BF16)
        state[h] = keep * (
            jnp.exp(jnp.full((1, 2 * HEAD), -slope * CHUNK, F32)) * old + nn(faded.T, query)
        )


def after_kernel(peers, count, lengths, slopes, term, part, cot, mid, sel, att, wo, qpre, fine, coarse, out_o, gmid_o, gsel_o, gatt_o, et_o, e0_o, state):
    step = pl.program_id(0)
    c = count // CHUNK - 1 - step
    layout = Layout(lengths, peers, count)

    @pl.when(step == 0)
    def _():
        state[...] = jnp.zeros_like(state)

    cs, sn = layout.angles(c, fine, coarse)
    after_chunk(
        layout, c, state.shape[0], slopes, term[...], part[...], cot[...], mid, sel, att, wo[...], qpre, cs, sn,
        out_o, gmid_o, gsel_o, gatt_o, et_o, state,
    )
    e0_o[...] = state[...].astype(BF16)


def run_after(peers, lengths, slopes, term, part, cot, mid, sel, att, wo, qpre, angles):
    n, d = cot.shape
    chunks = n // CHUNK
    back = lambda s: chunks - 1 - s
    tile = pl.BlockSpec((CHUNK, d), lambda s: (back(s), 0))
    return launch(
        functools.partial(after_kernel, peers, n),
        "output_and_row_gradients",
        chunks,
        [lengths, slopes, term, part, cot, mid, sel, att, wo, qpre, *angles],
        [smem(), smem()] + [tile] * 6 + [whole_block(wo.shape), tile] + [whole_block(a.shape) for a in angles],
        [struct((n, d))] * 4 + [struct((chunks,) + state_shape(d)), struct(state_shape(d))],
        [tile] * 4
        + [pl.BlockSpec((1,) + state_shape(d), lambda s: (back(s), 0, 0, 0)), whole_block(state_shape(d))],
        [pltpu.VMEM(state_shape(d), F32)],
        3 * n * d * d,
    )


def weights_kernel(items, peers, *refs):
    item = lax.div(pl.program_id(0), peers)
    lefts, right, out = refs[:-2], refs[-2], refs[-1]
    for i, left in enumerate(lefts):

        @pl.when(functools.reduce(jnp.logical_or, [item == t for t, w in enumerate(items) if w == i]))
        def _(left=left):
            block = left[...]
            block = block.reshape(-1, block.shape[-1])
            out[...] = nn(block, right[...]).astype(BF16)


def run_weights(lefts, items, rights, right_spec, peers, width):
    _, half, n = lefts[0].shape
    shape = (peers, len(items), 2 * half, width)
    which = lambda s: (lax.div(s, peers), lax.rem(s, peers))
    (out,) = launch(
        functools.partial(weights_kernel, items, peers),
        "weight_gradients",
        peers * len(items),
        list(lefts) + [rights],
        [whole_block(left.shape) for left in lefts] + [right_spec(which)],
        [struct(shape)],
        [pl.BlockSpec((None, None) + shape[2:], lambda s: (which(s)[1], which(s)[0], 0, 0))],
        [],
        4 * n * half * width * len(items) * peers,
    )
    return out


def head_back(slope, table, turned, qpre, kpre, value, grad, state, ending, cs, sn):
    qp, kp = qpre.astype(F32), kpre.astype(F32)
    qs, ks = sigmoid(qp), sigmoid(kp)
    qa, ka = qp * qs, kp * ks
    query = jnp.concatenate([qa * cs, qa * sn], axis=-1).astype(BF16)
    key = jnp.concatenate([ka * cs, ka * sn], axis=-1).astype(BF16)
    state, ending = state.astype(BF16), ending.astype(BF16)
    scores_t = (nt(key, query) * turned).astype(BF16)
    slope_s = (nt(grad, value) * table).astype(BF16)
    slope_t = (nt(value, grad) * turned).astype(BF16)
    start = fade_from_start(slope, HEAD)
    end = fade_to_end(slope, HEAD)
    grad_start = (grad.astype(F32) * start).astype(BF16)
    value_end = (value.astype(F32) * end).astype(BF16)
    dq = nn(slope_s, key) + nn(grad_start, state)
    dk = nn(slope_t, query) + nn(value_end, ending)
    dv = nn(scores_t, grad) + end * nt(key, ending)
    dq = dq[:, :HEAD] * cs + dq[:, HEAD:] * sn
    dk = dk[:, :HEAD] * cs + dk[:, HEAD:] * sn
    gq = (dq * (qs * (1.0 + qp * (1.0 - qs)))).astype(BF16)
    gk = (dk * (ks * (1.0 + kp * (1.0 - ks)))).astype(BF16)
    return gq, gk, dv.astype(BF16)


def attention_back_kernel(peers, count, lengths, slopes, qpre, kpre, values, gatt, st, came, et, left, fine, coarse, grads_o):
    chunks = count // CHUNK
    layout = Layout(lengths, peers, count)
    pair, c = lax.div(pl.program_id(0), chunks), lax.rem(pl.program_id(0), chunks)
    cs, sn = layout.angles(c, fine, coarse)
    before, after = layout.before(c), layout.after(c)
    span = (CHUNK * c).astype(F32)
    rest = (CHUNK * (chunks - 1 - c)).astype(F32)
    for h in range(2):
        slope = slopes[2 * pair + h]
        cols = head_slice(h)
        lane = jnp.zeros((1, 2 * HEAD), F32)
        state = st[0, h].astype(F32) + came[h].astype(F32) * (jnp.exp(lane - slope * span) * before)
        ending = et[0, h].astype(F32) + left[h].astype(F32) * (jnp.exp(lane - slope * rest) * after)
        table, turned = decay_table(slope, False), decay_table(slope, True)
        three = head_back(
            slope, table, turned, qpre[:, cols], kpre[:, cols], values[:, cols], gatt[:, cols], state, ending, cs, sn
        )
        for i in range(3):
            grads_o[i, :, cols] = three[i]


def run_attention_back(peers, lengths, slopes, qpre, kpre, values, gatt, st, came, et, left, angles):
    n, d = qpre.shape
    chunks = n // CHUNK
    pair = lambda s: lax.div(s, chunks)
    chunk = lambda s: lax.rem(s, chunks)
    tile = pl.BlockSpec((CHUNK, 2 * HEAD), lambda s: (chunk(s), pair(s)))
    states = pl.BlockSpec((1, 2, HEAD, 2 * HEAD), lambda s: (chunk(s), pair(s), 0, 0))
    ends = pl.BlockSpec((2, HEAD, 2 * HEAD), lambda s: (pair(s), 0, 0))
    return launch(
        functools.partial(attention_back_kernel, peers, n),
        "attention_backward",
        chunks * d // (2 * HEAD),
        [lengths, slopes, qpre, kpre, values, gatt, st, came, et, left, *angles],
        [smem(), smem(), tile, tile, tile, tile, states, ends, states, ends] + [whole_block(a.shape) for a in angles],
        [struct((3, n, d))],
        [pl.BlockSpec((3, CHUNK, 2 * HEAD), lambda s: (0, chunk(s), pair(s)))],
        [],
        18 * n * 256 * d,
    )


def projections_kernel(geo, outer, inner, lengths, slopes, *refs):
    chunks, blocks, d, n = geo["chunks"], geo["blocks"], geo["d"], geo["n"]
    refs = list(refs)
    take = lambda k: [refs.pop(0) for _ in range(k)]
    arrays_h = take(6)
    (came_h, left_h, fine, coarse, gsel_h, hid_h, gmid_h, mixt_h, normt_h) = take(9)
    weights_h = take(4)
    hidden_o, out, out2 = take(3)
    (qpre, kpre, val, gatt, st, et, came, gsel, gmid) = take(9)
    grads, block, decays, mixt, normt, left, sems, late_sems = take(8)
    places = Reducer.places(outer.depth)
    outer.bind(take(len(outer.scratch)), places)
    inner.bind(refs, places)
    step = pl.program_id(0)
    core = lax.rem(lax.axis_index("dp"), 2)
    me = lax.axis_index("mp")
    layout = Layout(lengths, 2, n)
    loads = [
        pltpu.make_async_copy(gmid_h, gmid, sems.at[4]),
        pltpu.make_async_copy(mixt_h.at[1 - core], mixt.at[pl.ds(0, d // 2), :], sems.at[0]),
        pltpu.make_async_copy(mixt_h.at[core], mixt.at[pl.ds(d // 2, d // 2), :], sems.at[1]),
        pltpu.make_async_copy(gsel_h, gsel, sems.at[5]),
        pltpu.make_async_copy(normt_h.at[1 - core], normt.at[pl.ds(0, d // 2), :], sems.at[2]),
        pltpu.make_async_copy(normt_h.at[core], normt.at[pl.ds(d // 2, d // 2), :], sems.at[3]),
    ]
    more = [
        pltpu.make_async_copy(src, dst, sems.at[6 + i])
        for i, (src, dst) in enumerate(zip(arrays_h + [came_h, left_h], (qpre, kpre, val, gatt, st, et, came, left)))
    ]
    select = pltpu.make_async_copy(weights_h[3], mixt, sems.at[14])

    def replaced(j):
        copies = []
        for side in range(2):
            cols = pl.ds(pl.multiple_of(((me if side == 0 else 1 - me) * blocks + j) * HEAD, HEAD), HEAD)
            for i, (src, dst) in enumerate(zip(weights_h[:3] + [hid_h], (qpre, kpre, gatt, val))):
                copies.append(pltpu.make_async_copy(src.at[:, cols], dst.at[:, cols], late_sems.at[j, side, i]))
        return copies

    @pl.when(step == 0)
    def _():
        for copy in loads + more:
            copy.start()
        for copy in loads[:3]:
            copy.wait()

    @pl.when(step < blocks)
    def _():
        slot = lax.rem(step, 2)
        mine = pl.ds(pl.multiple_of((me * blocks + step) * HEAD, HEAD), HEAD)
        theirs = pl.ds(pl.multiple_of(((1 - me) * blocks + step) * HEAD, HEAD), HEAD)
        gb = jnp.concatenate([gmid[:, mine], gmid[:, theirs]], axis=1)
        first = nn(mixt[...], gb).astype(BF16)

        @pl.when(step == 0)
        def _():
            for copy in loads[3:]:
                copy.wait()

        gs = jnp.concatenate([gsel[:, mine], gsel[:, theirs]], axis=1)
        made = [first, nn(normt[...], gs).astype(BF16)]
        for k, buffer in enumerate((outer.given, outer.kept)):
            for i in range(2):
                buffer[slot, i] = made[i][k * (d // 2) : (k + 1) * (d // 2), :]
            if k == 0:
                outer.begin(step)

    @pl.when(jnp.logical_and(step >= blocks, step < 2 * blocks))
    def _():
        j = step - blocks
        for side in range(2):
            slope = slopes[(me if side == 0 else 1 - me) * blocks + j]
            for k in range(2):
                decays[side, k] = decay_table(slope, k == 1)

        def one(c, carry):
            here = pl.ds(pl.multiple_of(c * CHUNK, CHUNK), CHUNK)
            cs, sn = layout.angles(c, fine, coarse)
            before, after = layout.before(c), layout.after(c)
            span = (CHUNK * c).astype(F32)
            rest = (CHUNK * (chunks - 1 - c)).astype(F32)
            for side in range(2):
                h = (me if side == 0 else 1 - me) * blocks + j
                slope = slopes[h]
                cols = pl.ds(pl.multiple_of(h * HEAD, HEAD), HEAD)
                four = [ref[here, cols] for ref in (qpre, kpre, val, gatt)]
                lane = jnp.zeros((1, 2 * HEAD), F32)
                state = st[c, h].astype(F32) + came[h].astype(F32) * (jnp.exp(lane - slope * span) * before)
                ending = et[c, h].astype(F32) + left[h].astype(F32) * (jnp.exp(lane - slope * rest) * after)
                three = head_back(
                    slope, decays[side, 0], decays[side, 1], *four, state, ending, cs, sn
                )
                for i in range(3):
                    block[here, head_slice(2 * i + side)] = three[i]
                    grads[i, here, cols] = three[i]
            return carry

        lax.fori_loop(0, chunks, one, 0)
        slot = lax.rem(j, 2)
        made = nn(normt[...], block[...]).astype(BF16)
        for k, buffer in enumerate((inner.given, inner.kept)):
            for i in range(3):
                buffer[slot, i] = made[k * (d // 2) : (k + 1) * (d // 2), feature_slice(i)]
            if k == 0:
                inner.begin(j)
        for copy in replaced(j):
            copy.start()

    @pl.when(step == blocks - 1)
    def _():
        select.start()
        for copy in more:
            copy.wait()

    @pl.when(step == 2 * blocks)
    def _():
        select.wait()
        for j in range(blocks):
            for copy in replaced(j):
                copy.wait()

    @pl.when(jnp.logical_and(step >= 2 * blocks, step < 2 * blocks + chunks))
    def _():
        here = pl.ds(pl.multiple_of((step - 2 * blocks) * CHUNK, CHUNK), CHUNK)
        total = nt(gsel[here, :], mixt[...])
        for i, w in enumerate((qpre, kpre, gatt)):
            total = total + nt(grads[i, here, :], w[...])
        x = val[here, :].astype(F32)
        hidden_o[...] = (gmid[here, :].astype(F32) + norm_back(x, scale_of(x), total)).astype(BF16)

    outer.run(step, out)
    inner.run(step, out2)


def run_projections(lengths, slopes, qpre, kpre, values, gatt, st, et, came, left, angles, gsel, hidden, gmid, mixed_t, normed_t, weights, depth, ident):
    n, d = qpre.shape
    heads, chunks = d // HEAD, n // CHUNK
    blocks = heads // 2
    rows = d // (4 * depth)
    outer = Reducer(0, blocks, 2, depth, rows, (1, 4, 5, 6), 4, (1, 2, 3, 4), (2, 2))
    inner = Reducer(blocks, blocks, 3, depth, rows, (1, 2, 3, 4), 4, (1, 2, 3, 4), (2, 2, 2))
    steps = max(outer.last, inner.last, 2 * blocks + chunks - 1) + 1
    geo = dict(chunks=chunks, blocks=blocks, d=d, n=n)
    late = lambda s: jnp.clip(s - 2 * blocks, 0, chunks - 1)
    whole = pltpu.VMEM((n, d), BF16)
    states = pltpu.VMEM((chunks,) + state_shape(d), BF16)
    one = pltpu.VMEM(state_shape(d), BF16)
    turned = pltpu.VMEM((d, n), BF16)
    return launch(
        functools.partial(projections_kernel, geo, outer, inner),
        "attention_backward_and_gradients",
        steps,
        [lengths, slopes, qpre, kpre, values, gatt, st, et, came, left, *angles]
        + [gsel, hidden, gmid, mixed_t, normed_t]
        + list(weights),
        [smem(), smem()] + [anywhere()] * 8 + [once(a.shape) for a in angles] + [anywhere()] * 9,
        [struct((n, d)), struct((2, rows, d // 2), F32), struct((3, rows, d // 2), F32)],
        [
            pl.BlockSpec((CHUNK, d), lambda s: (late(s), 0)),
            whole_block((2, rows, d // 2)),
            whole_block((3, rows, d // 2)),
        ],
        [whole] * 4
        + [states, states, one, whole, whole]
        + [
            pltpu.VMEM((3, n, d), BF16),
            pltpu.VMEM((n, 6 * HEAD), BF16),
            pltpu.VMEM((2, 2, CHUNK, CHUNK), F32),
            turned,
            turned,
            one,
            pltpu.SemaphoreType.DMA((15,)),
            pltpu.SemaphoreType.DMA((blocks, 2, 4)),
        ]
        + outer.scratch
        + inner.scratch,
        30 * n * d * d,
        partners=outer.partners,
        ident=ident,
    )


def input_kernel(wq, wk, wv, ws, grads, gsel, hid, gmid, out):
    total = nt(grads[0], wq[...]) + nt(grads[1], wk[...]) + nt(grads[2], wv[...]) + nt(gsel[...], ws[...])
    x = hid[...].astype(F32)
    out[...] = (gmid[...].astype(F32) + norm_back(x, scale_of(x), total)).astype(BF16)


def run_input(weights, grads, gsel, hidden, gmid):
    n, d = hidden.shape
    tile = pl.BlockSpec((CHUNK, d), lambda c: (c, 0))
    return launch(
        input_kernel,
        "input_gradient",
        n // CHUNK,
        list(weights) + [grads, gsel, hidden, gmid],
        [whole_block(w.shape) for w in weights]
        + [
            pl.BlockSpec((3, CHUNK, d), lambda c: (0, c, 0)),
            tile,
            tile,
            tile,
        ],
        [struct((n, d))],
        [tile],
        [],
        8 * n * d * d,
    )


def reduced(lefts, items, rights, spec, peers, width):
    full = run_weights(lefts, items, rights, spec, peers, width)
    parts = lax.axis_size("dp")
    full = full.reshape(peers, len(items), 2, parts // 2, -1, width)
    full = jnp.swapaxes(full, 2, 3).reshape(peers, len(items), parts, -1, width)
    mine = lax.psum_scatter(full, "dp", scatter_dimension=2, tiled=False)
    return lax.psum_scatter(mine, "mp", scatter_dimension=0, tiled=False).astype(F32)


def per_device(
    hidden_in,
    query_weight,
    key_weight,
    value_weight,
    select_weight,
    out_weight,
    first_weight,
    second_weight,
    down_weight,
    decay_slope,
    doc_lengths,
    cotangent,
):
    count, d = hidden_in.shape
    heads, chunks = d // HEAD, count // CHUNK
    peers, parts = lax.axis_size("mp"), lax.axis_size("dp")
    me = lax.axis_index("mp")
    depth = parts // 4
    group = count * peers
    units = first_weight.shape[1]
    lengths = doc_lengths.astype(jnp.int32)
    angles = tables(group // 2)
    slopes = decay_slope
    matrices = (first_weight, second_weight, down_weight)
    riding = peers == 2

    if riding:
        cut = units // 256 * 128
        ranges = [(0, cut), (cut, units - cut)]
    else:
        ranges = [(0, units)]

    def like(arrays, count=None):
        return [struct(a.shape if count is None else (count,) + a.shape) for a in arrays]

    def over_mp(g):
        low, size = ranges[g]

        def source(w):
            def src(i, o):
                eighth = lax.rem(lax.axis_index("dp"), 8)
                if w < 2:
                    rows = d // 8
                    return i[w].at[pl.ds(pl.multiple_of(eighth * rows, 16), rows), pl.ds(low, size)]
                rows = size // 8
                return i[w].at[pl.ds(pl.multiple_of(low + eighth * rows, 16), rows), :]

            return src

        outs = [struct((d // 8, size)), struct((d // 8, size)), struct((size // 8, d))]
        return outs, [(source(w), lambda i, o, w=w: o[w], "mp", 1) for w in range(3)]

    def near(src, dst):
        return [
            (lambda i, o: src(i, o), lambda i, o: dst(i, o).at[0], "dp", 2),
            (lambda i, o: src(i, o), lambda i, o: dst(i, o).at[1], "dp", 4),
            (lambda i, o: src(i, o), lambda i, o: dst(i, o).at[2], "dp", 1),
        ]

    def far(src, dst, rows, balanced):
        top = -(-rows // 32) * 16 if balanced else 0
        upper, lower = pl.ds(0, top), pl.ds(top, rows - top)
        over_x = (lambda i, o: src(i, o).at[1, upper, :], lambda i, o: dst(i, o).at[0, upper, :], "dp", 2)
        return ([over_x] if balanced else []) + [
            (lambda i, o: src(i, o).at[0, lower, :], lambda i, o: dst(i, o).at[0, lower, :], "dp", 4),
            (lambda i, o: src(i, o).at[0], lambda i, o: dst(i, o).at[1], "dp", 1),
            (lambda i, o: src(i, o).at[1], lambda i, o: dst(i, o).at[2], "dp", 1),
        ]

    def onward(pieces, out, at, balanced):
        ref = lambda k: lambda i, o: o[k]
        one, two, three = [], [], []
        for w in range(3):
            one += near(pieces(w), ref(at + w))
            two += far(ref(at + w), ref(at + 3 + w), out[w].shape[0], balanced)
            three.append((lambda i, o, w=w: o[at + 3 + w].at[0], ref(at + 6 + w), "dp", 1))
        return like(out, 3) + like(out, 3) + like(out), [one, two, three]

    if riding:
        outs, copies = over_mp(0)
        more, phases = onward(lambda w: lambda i, o: o[w], outs, 3, True)
        outs_b, copies_b = over_mp(1)
        spans = [(0, chunks), (chunks + 1, 2 * chunks), (2 * chunks + 1, 3 * chunks - 2), (3 * chunks - 1,) * 2]
        guests = [
            Carry(matrices, outs + more, [span + (c,) for span, c in zip(spans, [copies] + phases)]),
            Carry(matrices, outs_b, [(chunks + 2, 3 * chunks - 1, copies_b)]),
        ]
        weights = [key_weight, value_weight, query_weight, select_weight, out_weight]
        kpre, values, st, qpre, sel, normed_t, attended, mixed_t, middle, second, second_t, cot_t, came, *got = run_forward(
            lengths, slopes, hidden_in, cotangent, weights, angles, parts, guests, ident=1
        )
    else:
        normed, normed_t, kpre, values, st, final = run_keys(
            peers, lengths, slopes, hidden_in, key_weight, value_weight, angles, parts
        )
        begin, start, last = jnp.int32(0), jnp.int32(0), (me + 1) * count - CHUNK
        for i in range(lengths.shape[1]):
            begin = jnp.where(last >= start, start, begin)
            start = start + lengths[0, i]
        passes = (begin < me * count).astype(F32)
        decay = jnp.exp(-slopes * count)
        finals = lax.all_gather(final, "mp")
        keeps = lax.all_gather(passes.reshape(1), "mp")[:, 0]

        def ahead(k, total):
            new = finals[k].astype(F32) + (keeps[k] * decay)[:, None, None] * total
            return jnp.where(k < me, new, total)

        came = lax.fori_loop(0, peers, ahead, jnp.zeros(final.shape, F32)).astype(BF16)
        qpre, sel, att = run_inside(
            peers, lengths, slopes, normed, query_weight, select_weight, kpre, values, st, angles
        )
        attended, mixed_t, middle, second, second_t, cot_t = run_mix(
            peers, lengths, slopes, att, qpre, came, sel, out_weight, hidden_in, cotangent, angles, parts
        )

    if riding:
        had_b = got[12:15]
        more, phases = onward(lambda w: lambda i, o: i[w], had_b, 0, True)
        ride = Carry(had_b, more, [(0, 1, phases[0]), (2, 3, phases[1]), (4, 4, phases[2])])
        output, grad_middle, grad_sel, grad_att, et, left, sglu = run_units(
            lengths, slopes, matrices, second, cotangent, second_t, cot_t, [middle, sel, attended, qpre],
            angles, out_weight, got[:12], ride, ranges[0][1], depth, ident=2,
        )
    else:
        sources = [lax.all_gather(w, "mp") for w in matrices]
        grads, term, part = run_sglu(second, cotangent, *sources)
        units_spec = lambda at: pl.BlockSpec((None, None, count, units), lambda s: at(s) + (0, 0))
        sglu = reduced([second_t, cot_t], (0, 0, 1), grads, units_spec, peers, units)
        output, grad_middle, grad_sel, grad_att, et, leaving = run_after(
            peers, lengths, slopes, term, part, cotangent, middle, sel, attended, out_weight, qpre, angles
        )
    inputs_weights = [query_weight, key_weight, value_weight, select_weight]
    if riding:
        grad_hidden, out_sel, inputs = run_projections(
            lengths, slopes, qpre, kpre, values, grad_att, st, et, came, left, angles, grad_sel,
            hidden_in, grad_middle, mixed_t, normed_t, inputs_weights, depth, ident=3,
        )
    else:
        leavings = lax.all_gather(leaving, "mp")

        def behind(step, total):
            k = peers - 1 - step
            new = leavings[k].astype(F32) + (keeps[k] * decay)[:, None, None] * total
            return jnp.where(k > me, new, total)

        left = lax.fori_loop(0, peers, behind, jnp.zeros(leaving.shape, F32)).astype(BF16)
        share = d // peers
        wide_spec = lambda at: pl.BlockSpec((None, count, share), lambda s: (at(s)[0], 0, at(s)[1]))
        pair = jnp.stack([grad_middle, grad_sel])
        out_sel = reduced([mixed_t, normed_t], (0, 1), pair, wide_spec, peers, share)
        (qkv,) = run_attention_back(
            peers, lengths, slopes, qpre, kpre, values, grad_att, st, came, et, left, angles
        )
        inputs = reduced([normed_t], (0, 0, 0), qkv, wide_spec, peers, share)
        (grad_hidden,) = run_input(inputs_weights, qkv, grad_sel, hidden_in, grad_middle)
    return (
        output,
        grad_hidden,
        inputs[0],
        inputs[1],
        inputs[2],
        out_sel[1],
        out_sel[0],
        sglu[0],
        sglu[1],
        jnp.transpose(sglu[2]),
    )


def solution(mesh):
    rows = P(("dp", "mp"), None)
    in_specs = (
        rows,
        P(),
        P(),
        P(),
        P(),
        P(),
        P(None, "mp"),
        P(None, "mp"),
        P("mp", None),
        P(),
        P("dp", None),
        rows,
    )
    out_specs = (rows, rows) + (P("dp", "mp"),) * 7 + (P("mp", "dp"),)
    return jax.shard_map(
        per_device, mesh=mesh, in_specs=in_specs, out_specs=out_specs, check_vma=False
    )
```

```python
import functools

import jax
import jax.numpy as jnp
import numpy as np
from jax import lax
from jax.experimental import pallas as pl
from jax.experimental.pallas import tpu as pltpu
from jax.sharding import PartitionSpec as P

HEAD = 128
CHUNK = 256
EPSILON = 1e-06
BF16 = jnp.bfloat16
F32 = jnp.float32
VMEM_LIMIT = 62 * 1024 * 1024


def nn(left, right):
    return jnp.dot(left, right, preferred_element_type=F32)


def nt(left, right):
    return lax.dot_general(left, right, (((1,), (1,)), ((), ())), preferred_element_type=F32)


def scale_of(values):
    return lax.rsqrt(jnp.mean(values * values, axis=-1, keepdims=True) + EPSILON)


def norm_back(values, scale, upstream):
    return scale * upstream - values * (scale * scale * scale) * jnp.mean(
        values * upstream, axis=-1, keepdims=True
    )


def sigmoid(v):
    return 0.5 * jnp.tanh(0.5 * v) + 0.5


def featured(pre, cos, sin):
    act = pre * sigmoid(pre)
    return jnp.concatenate([act * cos, act * sin], axis=-1).astype(BF16)


def head_slice(h):
    return slice(h * HEAD, (h + 1) * HEAD)


def turned_shape(d, n):
    return (2, d // 2, n)


def put_turned(ref, value, parts):
    turned = value.T
    rows = turned.shape[0] // parts
    for i in range(parts):
        ref[i % 2, (i // 2) * rows : (i // 2 + 1) * rows, :] = turned[i * rows : (i + 1) * rows, :]


def put_turned_at(ref, value, parts, cols):
    turned = value.T
    half, rows = turned.shape[0] // 2, turned.shape[0] // parts
    for i in range(parts):
        at = (i % 2) * half + (i // 2) * rows
        ref[at : at + rows, cols] = turned[i * rows : (i + 1) * rows, :]


def feature_slice(h):
    return slice(2 * h * HEAD, 2 * (h + 1) * HEAD)


def row_index(shape):
    return lax.broadcasted_iota(jnp.int32, shape, 0)


def fade_from_start(slope, width):
    return jnp.exp(-slope * (row_index((CHUNK, width)) + 1).astype(F32))


def fade_to_end(slope, width):
    return jnp.exp(-slope * (CHUNK - 1 - row_index((CHUNK, width))).astype(F32))


def decay_table(slope, transposed):
    rows = lax.broadcasted_iota(jnp.int32, (CHUNK, CHUNK), 0)
    cols = lax.broadcasted_iota(jnp.int32, (CHUNK, CHUNK), 1)
    gap = cols - rows if transposed else rows - cols
    return jnp.where(gap >= 0, jnp.exp(-slope * jnp.maximum(gap, 0).astype(F32)), 0.0)


def plus(*arrays):
    total = arrays[0].astype(F32)
    for a in arrays[1:]:
        total = total + a.astype(F32)
    return total


def smem():
    return pl.BlockSpec(memory_space=pltpu.SMEM)


def anywhere():
    return pl.BlockSpec(memory_space=pl.ANY)


def once(shape):
    zeros = (0,) * len(shape)
    return pl.BlockSpec(shape, lambda *_: zeros, pipeline_mode=pl.Buffered(1))


def whole_block(shape):
    zeros = (0,) * len(shape)
    return pl.BlockSpec(shape, lambda *_: zeros)


def cost(flops, arrays):
    moved = sum(int(np.prod(a.shape)) * jnp.dtype(a.dtype).itemsize for a in arrays)
    return pl.CostEstimate(flops=int(flops), bytes_accessed=moved, transcendentals=0)


def struct(shape, dtype=BF16):
    return jax.ShapeDtypeStruct(tuple(shape), dtype)


def flipped(index, mask):
    bit = 1
    while bit <= mask:
        if mask & bit:
            index = index + bit * (1 - 2 * lax.rem(lax.div(index, bit), 2))
        bit *= 2
    return index


def remote(src, dst, send, recv, axis, mask, where=None):
    return pltpu.make_async_remote_copy(
        src_ref=src,
        dst_ref=dst,
        send_sem=send,
        recv_sem=recv,
        device_id={axis: flipped(lax.axis_index(axis), mask) if where is None else where},
        device_id_type=pl.DeviceIdType.MESH,
    )


def greet(partners):
    barrier = pltpu.get_barrier_semaphore()
    for axis, mask in partners:
        pl.semaphore_signal(
            barrier,
            inc=1,
            device_id={axis: flipped(lax.axis_index(axis), mask)},
            device_id_type=pl.DeviceIdType.MESH,
        )
    pl.semaphore_wait(barrier, len(partners))


class Carry:
    def __init__(self, inputs, outs, phases):
        self.inputs, self.outs, self.phases = list(inputs), list(outs), phases
        count = sum(len(p[2]) for p in phases)
        self.scratch = [pltpu.SemaphoreType.DMA((count,)), pltpu.SemaphoreType.DMA((count,))]
        self.partners = [(c[2], c[3]) for p in phases for c in p[2]]

    def copies(self, which, ins, outs, scratch):
        at = sum(len(p[2]) for p in self.phases[:which])
        send, recv = scratch
        for k, (src, dst, axis, mask) in enumerate(self.phases[which][2]):
            yield remote(src(ins, outs), dst(ins, outs), send.at[at + k], recv.at[at + k], axis, mask)

    def before(self, step, ins, outs, scratch):
        for p, phase in enumerate(self.phases):

            @pl.when(step == phase[0])
            def _(p=p):
                for copy in self.copies(p, ins, outs, scratch):
                    copy.start()

    def after(self, step, ins, outs, scratch):
        for p, phase in enumerate(self.phases):

            @pl.when(step == phase[1])
            def _(p=p):
                for copy in self.copies(p, ins, outs, scratch):
                    copy.wait()


class Reducer:
    KINDS = 8

    def __init__(self, start, blocks, items, depth, rows, delays, slots, order, over_x, offset=0):
        self.offset = offset
        self.start, self.blocks, self.items = start, blocks, items
        self.slots, self.order = slots, order
        self.made = 2 if delays[0] else 1
        self.depth, self.rows, self.delays = depth, rows, delays
        self.upper = [(t, z) for t in range(items) for z in range(over_x[t])]
        self.lower = [(t, z) for t in range(items) for z in range(over_x[t], depth)]
        n, wide = 2 * depth * rows, 2 * HEAD
        buf = lambda *shape: pltpu.VMEM(shape, BF16)
        up, low = len(self.upper), len(self.lower)
        pair, flat = (up, rows, wide), (2, low, rows, HEAD)
        self.scratch = [
            buf(self.made, items, n, wide),
            buf(self.made, items, n, wide),
            buf(4 if delays[0] else 2, items, n, wide),
            buf(slots, *pair),
            buf(slots, *pair),
            buf(4, *pair),
            buf(slots, *flat),
            buf(slots, *flat),
            buf(4, *flat),
            buf(slots, up, rows, HEAD),
            buf(slots, up, rows, HEAD),
            buf(4, up, rows, HEAD),
            buf(slots, low, rows, HEAD),
            buf(slots, low, rows, HEAD),
            buf(4, low, rows, HEAD),
            buf(slots, depth, items, rows, HEAD),
            buf(4, depth - 1, items, rows, HEAD),
            pltpu.SemaphoreType.DMA((self.KINDS, blocks)),
            pltpu.SemaphoreType.DMA((self.KINDS, blocks)),
        ]
        self.partners = [("dp", 1), ("dp", 2), ("mp", 1)] + [("dp", 4 * k) for k in range(1, depth)]
        self.last = start + blocks - 1 + delays[3]

    def bind(self, scratch, places):
        self.refs = scratch
        self.given, self.kept = scratch[:2]
        self.x, self.z, self.where, self.partner_z = places

    @staticmethod
    def places(depth):
        dp, me = lax.axis_index("dp"), lax.axis_index("mp")
        z = lax.div(dp, 4)
        x = lax.div(dp - 4 * z, 2)
        core = dp - 4 * z - 2 * x
        where = {("dp", 1): dp + 1 - 2 * core, ("dp", 2): dp + 2 - 4 * x, ("mp", 1): 1 - me}
        partner_z = {}
        for k in range(1, depth):
            partner_z[k] = flipped(z, k)
            where["dp", 4 * k] = dp + 4 * (partner_z[k] - z)
        return x, z, where, partner_z

    def copies(self, stage, j):
        (given, kept, got, ps, pk, pr, qs, qk, qr, ps2, pk2, pr2, qs2, qk2, qr2, line, zr, send, recv) = self.refs
        slot, four = lax.rem(j, self.slots), lax.rem(j, 4)
        if stage == 0:
            plan = [(0, given.at[lax.rem(j, self.made)], got.at[lax.rem(j, got.shape[0])], "dp", 1)]
        elif stage == 1:
            plan = [(1, ps.at[slot], pr.at[four], "dp", 2), (2, qs.at[slot], qr.at[four], "mp", 1)]
        elif stage == 2:
            plan = [(3, ps2.at[slot], pr2.at[four], "mp", 1), (4, qs2.at[slot], qr2.at[four], "dp", 2)]
        else:
            plan = [
                (4 + k, line.at[slot, self.partner_z[k]], zr.at[four, k - 1], "dp", 4 * k)
                for k in range(1, self.depth)
            ]
        return [
            remote(src, dst, send.at[i, j], recv.at[i, j], axis, mask, self.where[axis, mask])
            for i, src, dst, axis, mask in plan
        ]

    def begin(self, j):
        for copy in self.copies(0, j):
            copy.start()

    def run(self, step, out):
        for stage in self.order:
            j = step - self.start - self.delays[stage - 1]

            @pl.when(jnp.logical_and(j >= 0, j < self.blocks))
            def _(stage=stage, j=j):
                for copy in self.copies(stage - 1, j):
                    copy.wait()
                self.add(stage, j, out)
                if stage < 4:
                    for copy in self.copies(stage, j):
                        copy.start()

    def add(self, stage, j, out):
        (given, kept, got, ps, pk, pr, qs, qk, qr, ps2, pk2, pr2, qs2, qk2, qr2, line, zr, send, recv) = self.refs
        slot, four, x, rows = lax.rem(j, self.slots), lax.rem(j, 4), self.x, self.rows
        if stage == 1:
            two, came = lax.rem(j, self.made), lax.rem(j, got.shape[0])

            def total(t, z, at):
                here = pl.ds(pl.multiple_of((2 * z + at) * rows, rows), rows)
                return kept[two, t, here, :] + got[came, t, here, :]

            for i, (t, z) in enumerate(self.upper):
                ps[slot, i] = total(t, z, 1 - x)
                pk[slot, i] = total(t, z, x)
            for i, (t, z) in enumerate(self.lower):
                for at in range(2):
                    block = total(t, z, at)
                    qk[slot, at, i] = block[:, :HEAD]
                    qs[slot, at, i] = block[:, HEAD:]
        elif stage == 2:
            for i in range(len(self.upper)):
                block = pk[slot, i] + pr[four, i]
                pk2[slot, i] = block[:, :HEAD]
                ps2[slot, i] = block[:, HEAD:]
            for i in range(len(self.lower)):
                qs2[slot, i] = qk[slot, 1 - x, i] + qr[four, 1 - x, i]
                qk2[slot, i] = qk[slot, x, i] + qr[four, x, i]
        elif stage == 3:
            for i, (t, z) in enumerate(self.upper):
                line[slot, z, t] = pk2[slot, i] + pr2[four, i]
            for i, (t, z) in enumerate(self.lower):
                line[slot, z, t] = qk2[slot, i] + qr2[four, i]
        else:
            total = plus(line[slot, self.z], *[zr[four, k] for k in range(self.depth - 1)])
            out[:, :, pl.ds(pl.multiple_of((self.offset + j) * HEAD, HEAD), HEAD)] = total


def launch(kernel, name, steps, inputs, specs, outs, out_specs, scratch, flops, guests=(), ident=None, partners=()):
    guests = list(guests)
    partners = list(partners) + [p for g in guests for p in g.partners]
    partners = sorted(set(partners))
    all_inputs = list(inputs) + [a for g in guests for a in g.inputs]
    all_specs = list(specs) + [anywhere() for g in guests for _ in g.inputs]
    all_outs = list(outs) + [a for g in guests for a in g.outs]
    all_out_specs = list(out_specs) + [anywhere() for g in guests for _ in g.outs]
    all_scratch = list(scratch) + [a for g in guests for a in g.scratch]

    def body(*refs):
        refs = list(refs)
        take = lambda k: [refs.pop(0) for _ in range(k)]
        own = take(len(inputs))
        ins = [take(len(g.inputs)) for g in guests]
        own += take(len(outs))
        gone = [take(len(g.outs)) for g in guests]
        own += take(len(scratch))
        held = [take(len(g.scratch)) for g in guests]
        step = pl.program_id(0)
        if partners:

            @pl.when(step == 0)
            def _():
                greet(partners)

        for g, i, o, s in zip(guests, ins, gone, held):
            g.before(step, i, o, s)
        kernel(*own)
        for g, i, o, s in zip(guests, ins, gone, held):
            g.after(step, i, o, s)

    extra = dict(collective_id=ident, has_side_effects=True) if partners else {}
    return pl.pallas_call(
        body,
        grid=(steps,),
        in_specs=all_specs,
        out_specs=all_out_specs,
        out_shape=all_outs,
        scratch_shapes=all_scratch,
        compiler_params=pltpu.CompilerParams(
            vmem_limit_bytes=VMEM_LIMIT, dimension_semantics=("arbitrary",), **extra
        ),
        cost_estimate=cost(flops, all_inputs + all_outs),
        name=name,
    )(*all_inputs)


def tables(longest):
    freq = 10000.0 ** (-np.arange(HEAD, dtype=np.float64) / HEAD)

    def both(places):
        phase = places[:, None] * freq[None, :]
        return jnp.asarray(np.concatenate([np.cos(phase), np.sin(phase)], axis=1), F32)

    return both(np.arange(CHUNK)), both(np.arange(0, longest, CHUNK))


class Layout:
    def __init__(self, lengths, peers, count):
        self.lengths, self.peers, self.count = lengths, peers, count
        self.me = lax.axis_index("mp")
        self.offset = self.me * count

    def begin(self, first):
        begin = start = jnp.int32(0)
        for i in range(self.lengths.shape[1]):
            begin = jnp.where(first >= start, start, begin)
            start = start + self.lengths[0, i]
        return begin

    def first(self, c):
        return self.offset + c * CHUNK

    def keep(self, c):
        return jnp.where(self.begin(self.first(c)) < self.first(c), 1.0, 0.0)

    def before(self, c):
        return jnp.where(self.begin(self.first(c)) < self.offset, 1.0, 0.0)

    def after(self, c):
        last = self.begin(self.offset + self.count - CHUNK)
        return jnp.where(last <= self.first(c), 1.0, 0.0) * jnp.where(self.me < self.peers - 1, 1.0, 0.0)

    def alive(self, c, width):
        end = jnp.int32(0)
        for i in range(self.lengths.shape[1]):
            end = end + self.lengths[0, i]
        return (row_index((CHUNK, width)) + self.first(c) < end).astype(F32)

    def angles(self, c, fine, coarse):
        base = self.first(c) - self.begin(self.first(c))
        start = jnp.zeros((1, 2 * HEAD), F32)
        for k in range(coarse.shape[0]):
            start = start + coarse[k : k + 1, :] * jnp.where(base == k * CHUNK, 1.0, 0.0)
        cb, sb = start[:, :HEAD], start[:, HEAD:]
        cf, sf = fine[:, :HEAD], fine[:, HEAD:]
        return cf * cb - sf * sb, sf * cb + cf * sb


def normed_of(hid):
    x = hid[...].astype(F32)
    return (x * scale_of(x)).astype(BF16)


def states_chunk(heads, slopes, keep, key, values, state, put):
    for h in range(heads):
        slope = slopes[h]
        faded = (values[:, head_slice(h)] * fade_to_end(slope, HEAD)).astype(BF16)
        old = state[h] * keep
        put(h, old.astype(BF16))
        state[h] = jnp.exp(jnp.full((1, 2 * HEAD), -slope * CHUNK, F32)) * old + nn(faded.T, key(h))


def inside_chunk(heads, slopes, query, key, values, st, table, put):
    for h in range(heads):
        asked = query(h)
        weights = (nt(asked, key(h)) * table(h)).astype(BF16)
        put(h, nn(weights, values(h)) + fade_from_start(slopes[h], HEAD) * nt(asked, st(h)))


def carried_chunk(heads, slopes, layout, c, att, query, came, total):
    reached = layout.before(c)
    lag = (c * CHUNK).astype(F32)
    alive = layout.alive(c, HEAD)
    for h in range(heads):
        fade = jnp.exp(-slopes[h] * (row_index((CHUNK, HEAD)).astype(F32) + (lag + 1.0))) * reached
        total[:, head_slice(h)] = (att(h) + fade * nt(query(h), came[h])) * alive


def mix_chunk(total, sel, wo, hid, put):
    attended = total[...]
    mixed = (attended * scale_of(attended) * sel.astype(F32)).astype(BF16)
    middle = hid.astype(F32) + nn(mixed, wo)
    second = (middle * scale_of(middle)).astype(BF16)
    put(attended.astype(BF16), mixed, middle.astype(BF16), second)


def state_shape(d):
    return (d // HEAD, HEAD, 2 * HEAD)


def keys_kernel(peers, parts, count, lengths, slopes, hid, wk, wv, fine, coarse, normed_o, turned_o, kpre_o, val_o, st_o, fin_o, state):
    c = pl.program_id(0)
    layout = Layout(lengths, peers, count)

    @pl.when(c == 0)
    def _():
        state[...] = jnp.zeros_like(state)

    normed = normed_of(hid)
    normed_o[...] = normed
    put_turned(turned_o, normed, parts)
    kpre = nn(normed, wk[...])
    kpre_o[...] = kpre.astype(BF16)
    values = nn(normed, wv[...])
    val_o[...] = values.astype(BF16)
    cs, sn = layout.angles(c, fine, coarse)

    def put(h, value):
        st_o[0, h] = value

    key = lambda h: featured(kpre[:, head_slice(h)], cs, sn)
    states_chunk(state.shape[0], slopes, layout.keep(c), key, values, state, put)
    fin_o[...] = state[...].astype(BF16)


def run_keys(peers, lengths, slopes, hidden, wk, wv, angles, parts):
    n, d = hidden.shape
    heads, chunks = d // HEAD, n // CHUNK
    turned = turned_shape(d, n)
    tile = pl.BlockSpec((CHUNK, d), lambda c: (c, 0))
    outs = [struct((n, d)), struct(turned), struct((n, d)), struct((n, d)), struct((chunks,) + state_shape(d)), struct(state_shape(d))]
    return launch(
        functools.partial(keys_kernel, peers, parts, n),
        "keys_values_states",
        chunks,
        [lengths, slopes, hidden, wk, wv, *angles],
        [smem(), smem(), tile, whole_block(wk.shape), whole_block(wv.shape)] + [whole_block(a.shape) for a in angles],
        outs,
        [
            tile,
            pl.BlockSpec(turned[:2] + (CHUNK,), lambda c: (0, 0, c)),
            tile,
            tile,
            pl.BlockSpec((1,) + state_shape(d), lambda c: (c, 0, 0, 0)),
            whole_block(state_shape(d)),
        ],
        [pltpu.VMEM(state_shape(d), F32)],
        4 * n * d * d,
    )


def inside_kernel(peers, count, lengths, slopes, normed, wq, ws, kpre, values, st, fine, coarse, qpre_o, sel_o, att_o):
    c = pl.program_id(0)
    layout = Layout(lengths, peers, count)
    x = normed[...]
    qpre = nn(x, wq[...])
    qpre_o[...] = qpre.astype(BF16)
    sel_o[...] = nn(x, ws[...]).astype(BF16)
    cs, sn = layout.angles(c, fine, coarse)

    def put(h, value):
        att_o[:, head_slice(h)] = value

    inside_chunk(
        st.shape[1],
        slopes,
        lambda h: featured(qpre[:, head_slice(h)], cs, sn),
        lambda h: featured(kpre[:, head_slice(h)].astype(F32), cs, sn),
        lambda h: values[:, head_slice(h)],
        lambda h: st[0, h],
        lambda h: decay_table(slopes[h], False),
        put,
    )


def run_inside(peers, lengths, slopes, normed, wq, ws, kpre, values, st, angles):
    n, d = normed.shape
    chunks = n // CHUNK
    tile = pl.BlockSpec((CHUNK, d), lambda c: (c, 0))
    return launch(
        functools.partial(inside_kernel, peers, n),
        "queries_attention",
        chunks,
        [lengths, slopes, normed, wq, ws, kpre, values, st, *angles],
        [smem(), smem(), tile, whole_block(wq.shape), whole_block(ws.shape), tile, tile]
        + [pl.BlockSpec((1,) + state_shape(d), lambda c: (c, 0, 0, 0))]
        + [whole_block(a.shape) for a in angles],
        [struct((n, d)), struct((n, d)), struct((n, d), F32)],
        [tile, tile, tile],
        [],
        6 * n * d * d,
    )


def mix_kernel(peers, parts, count, lengths, slopes, att, qpre, came, sel, wo, hid, cot, fine, coarse, att_o, mixt_o, mid_o, sec_o, sect_o, cott_o, total):
    c = pl.program_id(0)
    layout = Layout(lengths, peers, count)
    cs, sn = layout.angles(c, fine, coarse)
    carried_chunk(
        came.shape[0],
        slopes,
        layout,
        c,
        lambda h: att[:, head_slice(h)],
        lambda h: featured(qpre[:, head_slice(h)].astype(F32), cs, sn),
        came,
        total,
    )

    def put(attended, mixed, middle, second):
        att_o[...] = attended
        put_turned(mixt_o, mixed, parts)
        mid_o[...] = middle
        sec_o[...] = second
        put_turned(sect_o, second, parts)

    mix_chunk(total, sel[...], wo[...], hid[...], put)
    put_turned(cott_o, cot[...], parts)


def run_mix(peers, lengths, slopes, att, qpre, came, sel, wo, hidden, cot, angles, parts):
    n, d = hidden.shape
    chunks = n // CHUNK
    turned = turned_shape(d, n)
    tile = pl.BlockSpec((CHUNK, d), lambda c: (c, 0))
    turned_tile = pl.BlockSpec(turned[:2] + (CHUNK,), lambda c: (0, 0, c))
    return launch(
        functools.partial(mix_kernel, peers, parts, n),
        "carried_mixed_middle",
        chunks,
        [lengths, slopes, att, qpre, came, sel, wo, hidden, cot, *angles],
        [smem(), smem(), tile, tile, whole_block(came.shape), tile, whole_block(wo.shape), tile, tile]
        + [whole_block(a.shape) for a in angles],
        [struct((n, d)), struct(turned), struct((n, d)), struct((n, d)), struct(turned), struct(turned)],
        [tile, turned_tile, tile, tile, turned_tile, turned_tile],
        [pltpu.VMEM((CHUNK, d), F32)],
        3 * n * d * d,
    )


def forward_kernel(chunks, parts, lengths, slopes, fine, coarse, *refs):
    refs = list(refs)
    take = lambda k: [refs.pop(0) for _ in range(k)]
    hid_h, cot_h = take(2)
    weights_h = take(5)
    (kpre_o, val_o, st_o, qpre_o, sel_o) = take(5)
    (turned_o, att_o, mixt_o, mid_o, sec_o, sect_o, cott_o, came_o) = take(8)
    (weights, normed, kpre, val, st, qpre, sel, att, state, final, came, total, keyed, asked, table) = take(15)
    (hid, cot, normt, cott) = take(4)
    (load_sems, out_sems, state_sems, chunk_sems) = take(4)
    heads = state.shape[0]
    step = pl.program_id(0)
    c = lax.rem(step, chunks)
    here = pl.ds(pl.multiple_of(c * CHUNK, CHUNK), CHUNK)
    layout = Layout(lengths, 2, chunks * CHUNK)
    loads = [pltpu.make_async_copy(w, weights.at[i], load_sems.at[i]) for i, w in enumerate(weights_h)]
    saves = [
        pltpu.make_async_copy(src, dst, out_sems.at[i])
        for i, (src, dst) in enumerate([(kpre, kpre_o), (val, val_o), (st, st_o), (qpre, qpre_o), (sel, sel_o)])
    ]
    exchange = remote(final, came, state_sems.at[0], state_sems.at[1], "mp", 1)
    d = hid.shape[1]
    half = d // 2
    rows_in = [
        pltpu.make_async_copy(hid_h, hid, load_sems.at[5]),
        pltpu.make_async_copy(cot_h, cot, load_sems.at[6]),
    ]

    def both_halves(src, dst, at):
        return [
            pltpu.make_async_copy(src.at[pl.ds(k * half, half), :], dst.at[k], out_sems.at[at + k]) for k in range(2)
        ]

    turned = both_halves(normt, turned_o, 5)
    turned_cot = both_halves(cott, cott_o, 7)
    arrived = pltpu.make_async_copy(came, came_o, out_sems.at[9])

    def finished(c):
        here = pl.ds(pl.multiple_of(c * CHUNK, CHUNK), CHUNK)
        copies = [
            pltpu.make_async_copy(src.at[here, :], dst.at[here, :], chunk_sems.at[c, i])
            for i, (src, dst) in enumerate([(kpre, att_o), (val, mid_o), (normed, sec_o)])
        ]
        for i, dst in enumerate((mixt_o, sect_o)):
            cols = pl.ds(pl.multiple_of(i * d + c * CHUNK, CHUNK), CHUNK)
            for k in range(2):
                src = keyed.at[pl.ds(k * half, half), cols]
                copies.append(pltpu.make_async_copy(src, dst.at[k, :, here], chunk_sems.at[c, 3 + 2 * i + k]))
        return copies

    @pl.when(step == 0)
    def _():
        for copy in rows_in[:1] + loads[:2]:
            copy.start()
        state[...] = jnp.zeros_like(state)
        for copy in rows_in[:1] + loads[:2]:
            copy.wait()
        for copy in loads[2:] + rows_in[1:]:
            copy.start()

    @pl.when(step < chunks)
    def _():
        x = normed_of(hid.at[here, :])
        normed[here, :] = x
        put_turned_at(normt, x, parts, here)
        keys = nn(x, weights[0])
        kpre[here, :] = keys.astype(BF16)
        values = nn(x, weights[1])
        val[here, :] = values.astype(BF16)
        cs, sn = layout.angles(c, fine, coarse)

        def put(h, value):
            st[c, h] = value

        def key(h):
            value = featured(keys[:, head_slice(h)], cs, sn)
            keyed[here, feature_slice(h)] = value
            return value

        states_chunk(heads, slopes, layout.keep(c), key, values, state, put)

    @pl.when(step == chunks - 1)
    def _():
        final[...] = state[...].astype(BF16)
        exchange.start()
        for copy in saves[:3] + turned:
            copy.start()

    @pl.when(step == chunks)
    def _():
        for h in range(heads):
            table[h] = decay_table(slopes[h], False)
        for copy in loads[2:4] + rows_in[1:]:
            copy.wait()

    @pl.when(jnp.logical_and(step >= chunks, step < 2 * chunks))
    def _():
        x = normed[here, :]
        queries = nn(x, weights[2])
        qpre[here, :] = queries.astype(BF16)
        sel[here, :] = nn(x, weights[3]).astype(BF16)
        cs, sn = layout.angles(c, fine, coarse)

        def put(h, value):
            att[here, head_slice(h)] = value

        def query(h):
            value = featured(queries[:, head_slice(h)], cs, sn)
            asked[here, feature_slice(h)] = value
            return value

        inside_chunk(
            heads,
            slopes,
            query,
            lambda h: keyed[here, feature_slice(h)],
            lambda h: val[here, head_slice(h)],
            lambda h: st[c, h],
            lambda h: table[h],
            put,
        )
        put_turned_at(cott, cot[here, :], parts, here)

    @pl.when(step == 2 * chunks - 1)
    def _():
        for copy in saves[3:] + turned_cot:
            copy.start()
        for copy in saves[:3]:
            copy.wait()

    @pl.when(step == 2 * chunks)
    def _():
        loads[4].wait()
        exchange.wait()
        arrived.start()

    @pl.when(step >= 2 * chunks)
    def _():
        carried_chunk(
            heads,
            slopes,
            layout,
            c,
            lambda h: att[here, head_slice(h)],
            lambda h: asked[here, feature_slice(h)],
            came,
            total,
        )

        def put(attended, mixed, middle, second):
            kpre[here, :] = attended
            val[here, :] = middle
            normed[here, :] = second
            put_turned_at(keyed, mixed, parts, here)
            put_turned_at(keyed, second, parts, pl.ds(pl.multiple_of(d + c * CHUNK, CHUNK), CHUNK))

        mix_chunk(total, sel[here, :], weights[4], hid[here, :], put)
        for copy in finished(c):
            copy.start()

    @pl.when(step == 3 * chunks - 1)
    def _():
        for copy in saves[3:] + turned + turned_cot + [arrived]:
            copy.wait()
        for i in range(chunks):
            for copy in finished(i):
                copy.wait()


def run_forward(lengths, slopes, hidden, cot, weights, angles, parts, guests, ident):
    n, d = hidden.shape
    chunks = n // CHUNK
    turned = turned_shape(d, n)
    whole = pltpu.VMEM((n, d), BF16)
    return launch(
        functools.partial(forward_kernel, chunks, parts),
        "forward_to_sglu",
        3 * chunks,
        [lengths, slopes, *angles, hidden, cot, *weights],
        [smem(), smem()] + [once(a.shape) for a in angles] + [anywhere()] * 7,
        [struct((n, d)), struct((n, d)), struct((chunks,) + state_shape(d)), struct((n, d)), struct((n, d))]
        + [struct(turned), struct((n, d)), struct(turned), struct((n, d)), struct((n, d)), struct(turned), struct(turned)]
        + [struct(state_shape(d))],
        [anywhere()] * 13,
        [
            pltpu.VMEM((5, d, d), BF16),
            whole,
            whole,
            whole,
            pltpu.VMEM((chunks,) + state_shape(d), BF16),
            whole,
            whole,
            pltpu.VMEM((n, d), F32),
            pltpu.VMEM(state_shape(d), F32),
            pltpu.VMEM(state_shape(d), BF16),
            pltpu.VMEM(state_shape(d), BF16),
            pltpu.VMEM((CHUNK, d), F32),
            pltpu.VMEM((n, 2 * d), BF16),
            pltpu.VMEM((n, 2 * d), BF16),
            pltpu.VMEM((d // HEAD, CHUNK, CHUNK), F32),
            whole,
            whole,
            pltpu.VMEM((d, n), BF16),
            pltpu.VMEM((d, n), BF16),
            pltpu.SemaphoreType.DMA((7,)),
            pltpu.SemaphoreType.DMA((10,)),
            pltpu.SemaphoreType.DMA((2,)),
            pltpu.SemaphoreType.DMA((chunks, 7)),
        ],
        12 * n * d * d,
        guests=guests,
        ident=ident,
        partners=[("mp", 1)],
    )


def sglu_kernel(chunks, peers, sec, cot, w1, w2, wd, units_o, term_o, part_o):
    step = pl.program_id(0)
    here = pl.ds(pl.multiple_of(lax.rem(step, chunks) * CHUNK, CHUNK), CHUNK)
    left = nn(sec[...], w1[...])
    right = nn(sec[...], w2[...])
    inner = (left * right).astype(BF16)
    upstream = nt(cot[...], wd[...])
    grad_left = (upstream * right).astype(BF16)
    grad_right = (upstream * left).astype(BF16)
    units_o[0] = grad_left
    units_o[1] = grad_right
    units_o[2] = inner
    term = nn(inner, wd[...])
    part = nt(grad_left, w1[...]) + nt(grad_right, w2[...])

    @pl.when(step < chunks)
    def _():
        term_o[here, :] = term
        part_o[here, :] = part

    @pl.when(step >= chunks)
    def _():
        term_o[here, :] += term
        part_o[here, :] += part


def run_sglu(second, cot, w1, w2, wd):
    n, d = second.shape
    peers, _, width = w1.shape
    chunks = n // CHUNK
    tile = pl.BlockSpec((CHUNK, d), lambda s: (lax.rem(s, chunks), 0))
    block = lambda shape: pl.BlockSpec((None,) + shape, lambda s: (lax.div(s, chunks), 0, 0))
    return launch(
        functools.partial(sglu_kernel, chunks, peers),
        "sglu",
        peers * chunks,
        [second, cot, w1, w2, wd],
        [tile, tile, block((d, width)), block((d, width)), block((width, d))],
        [struct((3, peers, n, width)), struct((n, d), F32), struct((n, d), F32)],
        [
            pl.BlockSpec((3, None, CHUNK, width), lambda s: (0, lax.div(s, chunks), lax.rem(s, chunks), 0)),
            whole_block((n, d)),
            whole_block((n, d)),
        ],
        [],
        12 * n * d * width * peers,
    )


def units_kernel(geo, reducers, ride, lengths, slopes, fine, coarse, *refs):
    blocks, cut, d, units, chunks = geo["blocks"], geo["cut"], geo["d"], geo["units"], geo["chunks"]
    refs = list(refs)
    take = lambda k: [refs.pop(0) for _ in range(k)]
    weights_h = take(3)
    (x_h, cot_h, xt_h, cott_h, wo_h) = take(5)
    rows_h = take(4)
    pieces = take(12)
    had_b = take(3)
    rows_out = take(4)
    (et_o, left_o, sums_o) = take(3)
    pieces = pieces + had_b + take(9)
    (term, part, x, cot, xt, cott, o1, o2, od, c12, cd, inner, grads, state, e0, sums) = take(16)
    (left,) = take(1)
    (tiles, made, ends) = take(3)
    (sems, own_sems, block_sems, tile_sems, made_sems) = take(5)
    places = Reducer.places(reducers[0].depth)
    for reducer in reducers:
        reducer.bind(take(len(reducer.scratch)), places)
    step = pl.program_id(0)
    ride.before(step, had_b, pieces[15:], refs)
    core = lax.rem(lax.axis_index("dp"), 2)
    eighth = lax.rem(lax.axis_index("dp"), 8)
    heads = state.shape[0]
    layout = Layout(lengths, 2, chunks * CHUNK)

    def fetch(g, parts=slice(0, 8)):
        size = cut if g == 0 else units - cut
        masks = [(0, None, 0), (3, 0, 2), (3, 1, 4), (3, 2, 1), (6, 0, 6), (6, 1, 3), (6, 2, 5), (9, None, 7)]
        copies = []
        for w, region in enumerate((o1, o2, od)):
            rows = d // 8 if w < 2 else size // 8
            for k, (at, inner, mask) in list(enumerate(masks))[parts]:
                src = pieces[12 * g + at + w]
                src = src if inner is None else src.at[inner]
                here = pl.ds(pl.multiple_of(flipped(eighth, mask) * rows, 16), rows)
                dst = region.at[here, pl.ds(0, size)] if w < 2 else region.at[here, :]
                copies.append(pltpu.make_async_copy(src, dst, sems.at[g, w, k]))
        return copies

    own = [
        pltpu.make_async_copy(x_h, x, own_sems.at[6]),
        pltpu.make_async_copy(cot_h, cot, own_sems.at[0]),
        pltpu.make_async_copy(xt_h.at[1 - core], xt.at[pl.ds(0, d // 2), :], own_sems.at[1]),
        pltpu.make_async_copy(xt_h.at[core], xt.at[pl.ds(d // 2, d // 2), :], own_sems.at[2]),
        pltpu.make_async_copy(cott_h.at[1 - core], cott.at[pl.ds(0, d // 2), :], own_sems.at[3]),
        pltpu.make_async_copy(cott_h.at[core], cott.at[pl.ds(d // 2, d // 2), :], own_sems.at[4]),
    ]
    out_weight = pltpu.make_async_copy(wo_h, xt, own_sems.at[7])
    saved = pltpu.make_async_copy(sums, sums_o, own_sems.at[5])
    arrived = pltpu.make_async_copy(left, left_o, own_sems.at[8])
    exchange = remote(e0, left, own_sems.at[9], own_sems.at[10], "mp", 1)

    def own_block(j):
        slot, here = lax.rem(j, 2), pl.ds(pl.multiple_of(j * HEAD, HEAD), HEAD)
        return [
            pltpu.make_async_copy(weights_h[0].at[:, here], c12.at[slot, :, pl.ds(0, HEAD)], block_sems.at[slot, 0]),
            pltpu.make_async_copy(
                weights_h[1].at[:, here], c12.at[slot, :, pl.ds(2 * HEAD, HEAD)], block_sems.at[slot, 1]
            ),
            pltpu.make_async_copy(weights_h[2].at[here, :], cd.at[slot, pl.ds(0, HEAD), :], block_sems.at[slot, 2]),
        ]

    def rows_at(i):
        return pl.ds(pl.multiple_of((chunks - 1 - i) * CHUNK, CHUNK), CHUNK)

    def tile(i):
        slot = lax.rem(i, 2)
        return [
            pltpu.make_async_copy(src.at[rows_at(i), :], tiles.at[slot, k], tile_sems.at[slot, k])
            for k, src in enumerate(rows_h)
        ]

    def results(i):
        slot = lax.rem(i, 2)
        return [
            pltpu.make_async_copy(made.at[slot, k], dst.at[rows_at(i), :], made_sems.at[slot, k])
            for k, dst in enumerate(rows_out)
        ] + [pltpu.make_async_copy(ends.at[slot], et_o.at[chunks - 1 - i], made_sems.at[slot, 4])]

    turn = cut // HEAD

    @pl.when(step == 0)
    def _():
        for copy in own_block(0) + fetch(0) + own[:2]:
            copy.start()
        term[...] = jnp.zeros_like(term)
        part[...] = jnp.zeros_like(part)
        state[...] = jnp.zeros_like(state)
        for copy in fetch(0):
            copy.wait()

    @pl.when(step == turn)
    def _():
        for copy in fetch(1, slice(7, 8)):
            copy.start()
        for copy in fetch(1):
            copy.wait()

    @pl.when(step < blocks)
    def _():
        local = step - jnp.where(step >= turn, turn, 0)
        here = pl.ds(pl.multiple_of(local * HEAD, HEAD), HEAD)
        at = lax.rem(step, 2)
        c12[at, :, HEAD : 2 * HEAD] = o1[:, here]
        c12[at, :, 3 * HEAD :] = o2[:, here]
        cd[at, HEAD:, :] = od[here, :]
        for copy in own_block(step):
            copy.wait()

    @pl.when(step < blocks - 1)
    def _():
        for copy in own_block(step + 1):
            copy.start()

    @pl.when(step == turn - 1)
    def _():
        for copy in fetch(1, slice(0, 7)):
            copy.start()

    @pl.when(step == 0)
    def _():
        for copy in own[:2]:
            copy.wait()
        for copy in own[2:]:
            copy.start()

    @pl.when(step < blocks)
    def _():
        wide, at = 2 * HEAD, lax.rem(step, 2)
        for k in range(chunks):
            here = slice(k * CHUNK, (k + 1) * CHUNK)
            both = nn(x[here, :], c12[at])
            left, right = both[:, :wide], both[:, wide:]
            upstream = nt(cot[here, :], cd[at])
            inner[here, :] = (left * right).astype(BF16)
            grads[here, :wide] = (upstream * right).astype(BF16)
            grads[here, wide:] = (upstream * left).astype(BF16)

        @pl.when(step == 0)
        def _():
            for copy in own[2:]:
                copy.wait()

        for reducer in reducers:

            @pl.when(jnp.logical_and(step >= reducer.start, step < reducer.start + reducer.blocks))
            def _(reducer=reducer):
                both = nn(xt[...], grads[...]).astype(BF16)
                down = nn(cott[...], inner[...]).astype(BF16)
                for k, buffer in enumerate((reducer.given, reducer.kept)):
                    here = slice(k * (d // 2), (k + 1) * (d // 2))
                    buffer[0, 0] = both[here, :wide]
                    buffer[0, 1] = both[here, wide:]
                    buffer[0, 2] = down[here, :]
                    if k == 0:
                        reducer.begin(step - reducer.start)

        term[...] += nn(inner[...], cd[at])
        part[...] += nt(grads[...], c12[at])

    @pl.when(step == blocks - 1)
    def _():
        out_weight.start()
        for copy in tile(0):
            copy.start()

    @pl.when(step == blocks)
    def _():
        out_weight.wait()

    @pl.when(jnp.logical_and(step >= blocks, step < blocks + chunks))
    def _():
        i = step - blocks
        c, slot = chunks - 1 - i, lax.rem(i, 2)
        here = pl.ds(pl.multiple_of(c * CHUNK, CHUNK), CHUNK)
        for copy in tile(i):
            copy.wait()

        @pl.when(i < chunks - 1)
        def _():
            for copy in tile(i + 1):
                copy.start()

        @pl.when(i >= 2)
        def _():
            for copy in results(i - 2):
                copy.wait()

        cs, sn = layout.angles(c, fine, coarse)
        mid, sel, att, qpre = [tiles.at[slot, k] for k in range(4)]
        after_chunk(
            layout, c, heads, slopes, term[here, :], part[here, :], cot[here, :], mid, sel, att, xt[...], qpre, cs, sn,
            *[made.at[slot, k] for k in range(4)], ends.at[pl.ds(slot, 1)], state,
        )
        for copy in results(i):
            copy.start()

    @pl.when(step == blocks + chunks - 1)
    def _():
        e0[...] = state[...].astype(BF16)
        exchange.start()

    ride.after(step, had_b, pieces[15:], refs)
    for reducer in reducers:
        reducer.run(step, sums)

    @pl.when(step == reducers[-1].last)
    def _():
        saved.start()
        exchange.wait()
        arrived.start()
        for i in range(chunks - 2, chunks):
            for copy in results(i):
                copy.wait()
        arrived.wait()
        saved.wait()


def run_units(lengths, slopes, matrices, second, cot, second_t, cot_t, rows_in, angles, wo, pieces, ride, cut, depth, ident):
    n, d = second.shape
    chunks = n // CHUNK
    units = matrices[0].shape[1]
    blocks = units // HEAD
    rows = d // (4 * depth)
    turn = cut // HEAD
    reducers = [
        Reducer(0, turn, 3, depth, rows, (0, 2, 4, 6), 2, (4, 3, 2, 1), (1, 1, 1)),
        Reducer(turn, blocks - turn, 3, depth, rows, (0, 2, 4, 6), 2, (4, 3, 2, 1), (2, 2, 2), turn),
    ]
    geo = dict(blocks=blocks, cut=cut, d=d, units=units, chunks=chunks)
    turned = pltpu.VMEM((d, n), BF16)
    size = max(cut, units - cut)
    sums = (3, rows, units)
    return launch(
        functools.partial(units_kernel, geo, reducers, ride),
        "sglu_and_gradients",
        max(reducers[-1].last, blocks + chunks - 1) + 1,
        [lengths, slopes, *angles]
        + list(matrices)
        + [second, cot, second_t, cot_t, wo]
        + list(rows_in)
        + list(pieces)
        + ride.inputs,
        [smem(), smem()] + [once(a.shape) for a in angles] + [anywhere()] * (12 + len(pieces) + len(ride.inputs)),
        [struct((n, d))] * 4
        + [struct((chunks,) + state_shape(d)), struct(state_shape(d)), struct(sums, F32)]
        + ride.outs,
        [anywhere()] * (7 + len(ride.outs)),
        [
            pltpu.VMEM((n, d), F32),
            pltpu.VMEM((n, d), F32),
            pltpu.VMEM((n, d), BF16),
            pltpu.VMEM((n, d), BF16),
            turned,
            turned,
            pltpu.VMEM((d, size), BF16),
            pltpu.VMEM((d, size), BF16),
            pltpu.VMEM((size, d), BF16),
            pltpu.VMEM((2, d, 4 * HEAD), BF16),
            pltpu.VMEM((2, 2 * HEAD, d), BF16),
            pltpu.VMEM((n, 2 * HEAD), BF16),
            pltpu.VMEM((n, 4 * HEAD), BF16),
            pltpu.VMEM(state_shape(d), F32),
            pltpu.VMEM(state_shape(d), BF16),
            pltpu.VMEM(sums, F32),
            pltpu.VMEM(state_shape(d), BF16),
            pltpu.VMEM((2, 4, CHUNK, d), BF16),
            pltpu.VMEM((2, 4, CHUNK, d), BF16),
            pltpu.VMEM((2,) + state_shape(d), BF16),
            pltpu.SemaphoreType.DMA((2, 3, 8)),
            pltpu.SemaphoreType.DMA((11,)),
            pltpu.SemaphoreType.DMA((2, 3)),
            pltpu.SemaphoreType.DMA((2, 4)),
            pltpu.SemaphoreType.DMA((2, 5)),
        ]
        + [a for reducer in reducers for a in reducer.scratch]
        + ride.scratch,
        36 * n * d * units,
        partners=reducers[0].partners + ride.partners,
        ident=ident,
    )[:7]


def after_chunk(layout, c, heads, slopes, term, part, cot, mid, sel, att, wo, qpre, cs, sn, out_o, gmid_o, pair_o, gatt_o, et_o, state):
    middle = mid[...].astype(F32)
    out_o[...] = (middle + term).astype(BF16)
    grad_middle = cot.astype(F32) + norm_back(middle, scale_of(middle), part)
    branch = grad_middle.astype(BF16)
    gmid_o[...] = branch
    grad_mixed = nt(branch, wo)
    attended = att[...].astype(F32)
    scale = scale_of(attended)
    pair_o[...] = (grad_mixed * attended * scale).astype(BF16)
    grad_att = norm_back(attended, scale, grad_mixed * sel[...].astype(F32)) * layout.alive(c, 1)
    gatt_o[...] = grad_att.astype(BF16)
    keep = layout.keep(c)
    for h in range(heads):
        slope = slopes[h]
        query = featured(qpre[:, head_slice(h)].astype(F32), cs, sn)
        faded = (grad_att[:, head_slice(h)] * fade_from_start(slope, HEAD)).astype(BF16)
        old = state[h]
        et_o[0, h] = old.astype(BF16)
        state[h] = keep * (
            jnp.exp(jnp.full((1, 2 * HEAD), -slope * CHUNK, F32)) * old + nn(faded.T, query)
        )


def after_kernel(peers, count, lengths, slopes, term, part, cot, mid, sel, att, wo, qpre, fine, coarse, out_o, gmid_o, gsel_o, gatt_o, et_o, e0_o, state):
    step = pl.program_id(0)
    c = count // CHUNK - 1 - step
    layout = Layout(lengths, peers, count)

    @pl.when(step == 0)
    def _():
        state[...] = jnp.zeros_like(state)

    cs, sn = layout.angles(c, fine, coarse)
    after_chunk(
        layout, c, state.shape[0], slopes, term[...], part[...], cot[...], mid, sel, att, wo[...], qpre, cs, sn,
        out_o, gmid_o, gsel_o, gatt_o, et_o, state,
    )
    e0_o[...] = state[...].astype(BF16)


def run_after(peers, lengths, slopes, term, part, cot, mid, sel, att, wo, qpre, angles):
    n, d = cot.shape
    chunks = n // CHUNK
    back = lambda s: chunks - 1 - s
    tile = pl.BlockSpec((CHUNK, d), lambda s: (back(s), 0))
    return launch(
        functools.partial(after_kernel, peers, n),
        "output_and_row_gradients",
        chunks,
        [lengths, slopes, term, part, cot, mid, sel, att, wo, qpre, *angles],
        [smem(), smem()] + [tile] * 6 + [whole_block(wo.shape), tile] + [whole_block(a.shape) for a in angles],
        [struct((n, d))] * 4 + [struct((chunks,) + state_shape(d)), struct(state_shape(d))],
        [tile] * 4
        + [pl.BlockSpec((1,) + state_shape(d), lambda s: (back(s), 0, 0, 0)), whole_block(state_shape(d))],
        [pltpu.VMEM(state_shape(d), F32)],
        3 * n * d * d,
    )


def weights_kernel(items, peers, *refs):
    item = lax.div(pl.program_id(0), peers)
    lefts, right, out = refs[:-2], refs[-2], refs[-1]
    for i, left in enumerate(lefts):

        @pl.when(functools.reduce(jnp.logical_or, [item == t for t, w in enumerate(items) if w == i]))
        def _(left=left):
            block = left[...]
            block = block.reshape(-1, block.shape[-1])
            out[...] = nn(block, right[...]).astype(BF16)


def run_weights(lefts, items, rights, right_spec, peers, width):
    _, half, n = lefts[0].shape
    shape = (peers, len(items), 2 * half, width)
    which = lambda s: (lax.div(s, peers), lax.rem(s, peers))
    (out,) = launch(
        functools.partial(weights_kernel, items, peers),
        "weight_gradients",
        peers * len(items),
        list(lefts) + [rights],
        [whole_block(left.shape) for left in lefts] + [right_spec(which)],
        [struct(shape)],
        [pl.BlockSpec((None, None) + shape[2:], lambda s: (which(s)[1], which(s)[0], 0, 0))],
        [],
        4 * n * half * width * len(items) * peers,
    )
    return out


def head_back(slope, table, turned, qpre, kpre, value, grad, state, ending, cs, sn):
    qp, kp = qpre.astype(F32), kpre.astype(F32)
    qs, ks = sigmoid(qp), sigmoid(kp)
    qa, ka = qp * qs, kp * ks
    query = jnp.concatenate([qa * cs, qa * sn], axis=-1).astype(BF16)
    key = jnp.concatenate([ka * cs, ka * sn], axis=-1).astype(BF16)
    state, ending = state.astype(BF16), ending.astype(BF16)
    scores_t = (nt(key, query) * turned).astype(BF16)
    slope_s = (nt(grad, value) * table).astype(BF16)
    slope_t = (nt(value, grad) * turned).astype(BF16)
    start = fade_from_start(slope, HEAD)
    end = fade_to_end(slope, HEAD)
    grad_start = (grad.astype(F32) * start).astype(BF16)
    value_end = (value.astype(F32) * end).astype(BF16)
    dq = nn(slope_s, key) + nn(grad_start, state)
    dk = nn(slope_t, query) + nn(value_end, ending)
    dv = nn(scores_t, grad) + end * nt(key, ending)
    dq = dq[:, :HEAD] * cs + dq[:, HEAD:] * sn
    dk = dk[:, :HEAD] * cs + dk[:, HEAD:] * sn
    gq = (dq * (qs * (1.0 + qp * (1.0 - qs)))).astype(BF16)
    gk = (dk * (ks * (1.0 + kp * (1.0 - ks)))).astype(BF16)
    return gq, gk, dv.astype(BF16)


def attention_back_kernel(peers, count, lengths, slopes, qpre, kpre, values, gatt, st, came, et, left, fine, coarse, grads_o):
    chunks = count // CHUNK
    layout = Layout(lengths, peers, count)
    pair, c = lax.div(pl.program_id(0), chunks), lax.rem(pl.program_id(0), chunks)
    cs, sn = layout.angles(c, fine, coarse)
    before, after = layout.before(c), layout.after(c)
    span = (CHUNK * c).astype(F32)
    rest = (CHUNK * (chunks - 1 - c)).astype(F32)
    for h in range(2):
        slope = slopes[2 * pair + h]
        cols = head_slice(h)
        lane = jnp.zeros((1, 2 * HEAD), F32)
        state = st[0, h].astype(F32) + came[h].astype(F32) * (jnp.exp(lane - slope * span) * before)
        ending = et[0, h].astype(F32) + left[h].astype(F32) * (jnp.exp(lane - slope * rest) * after)
        table, turned = decay_table(slope, False), decay_table(slope, True)
        three = head_back(
            slope, table, turned, qpre[:, cols], kpre[:, cols], values[:, cols], gatt[:, cols], state, ending, cs, sn
        )
        for i in range(3):
            grads_o[i, :, cols] = three[i]


def run_attention_back(peers, lengths, slopes, qpre, kpre, values, gatt, st, came, et, left, angles):
    n, d = qpre.shape
    chunks = n // CHUNK
    pair = lambda s: lax.div(s, chunks)
    chunk = lambda s: lax.rem(s, chunks)
    tile = pl.BlockSpec((CHUNK, 2 * HEAD), lambda s: (chunk(s), pair(s)))
    states = pl.BlockSpec((1, 2, HEAD, 2 * HEAD), lambda s: (chunk(s), pair(s), 0, 0))
    ends = pl.BlockSpec((2, HEAD, 2 * HEAD), lambda s: (pair(s), 0, 0))
    return launch(
        functools.partial(attention_back_kernel, peers, n),
        "attention_backward",
        chunks * d // (2 * HEAD),
        [lengths, slopes, qpre, kpre, values, gatt, st, came, et, left, *angles],
        [smem(), smem(), tile, tile, tile, tile, states, ends, states, ends] + [whole_block(a.shape) for a in angles],
        [struct((3, n, d))],
        [pl.BlockSpec((3, CHUNK, 2 * HEAD), lambda s: (0, chunk(s), pair(s)))],
        [],
        18 * n * 256 * d,
    )


def projections_kernel(geo, outer, inner, lengths, slopes, *refs):
    chunks, blocks, d, n = geo["chunks"], geo["blocks"], geo["d"], geo["n"]
    refs = list(refs)
    take = lambda k: [refs.pop(0) for _ in range(k)]
    arrays_h = take(6)
    (came_h, left_h, fine, coarse, gsel_h, hid_h, gmid_h, mixt_h, normt_h) = take(9)
    weights_h = take(4)
    hidden_o, out, out2 = take(3)
    (qpre, kpre, val, gatt, st, et, came, gsel, gmid) = take(9)
    grads, block, decays, mixt, normt, left, sems, late_sems = take(8)
    places = Reducer.places(outer.depth)
    outer.bind(take(len(outer.scratch)), places)
    inner.bind(refs, places)
    step = pl.program_id(0)
    core = lax.rem(lax.axis_index("dp"), 2)
    me = lax.axis_index("mp")
    layout = Layout(lengths, 2, n)
    loads = [
        pltpu.make_async_copy(gmid_h, gmid, sems.at[4]),
        pltpu.make_async_copy(mixt_h.at[1 - core], mixt.at[pl.ds(0, d // 2), :], sems.at[0]),
        pltpu.make_async_copy(mixt_h.at[core], mixt.at[pl.ds(d // 2, d // 2), :], sems.at[1]),
        pltpu.make_async_copy(gsel_h, gsel, sems.at[5]),
        pltpu.make_async_copy(normt_h.at[1 - core], normt.at[pl.ds(0, d // 2), :], sems.at[2]),
        pltpu.make_async_copy(normt_h.at[core], normt.at[pl.ds(d // 2, d // 2), :], sems.at[3]),
    ]
    more = [
        pltpu.make_async_copy(src, dst, sems.at[6 + i])
        for i, (src, dst) in enumerate(zip(arrays_h + [came_h, left_h], (qpre, kpre, val, gatt, st, et, came, left)))
    ]
    select = pltpu.make_async_copy(weights_h[3], mixt, sems.at[14])

    def replaced(j):
        copies = []
        for side in range(2):
            cols = pl.ds(pl.multiple_of(((me if side == 0 else 1 - me) * blocks + j) * HEAD, HEAD), HEAD)
            for i, (src, dst) in enumerate(zip(weights_h[:3] + [hid_h], (qpre, kpre, gatt, val))):
                copies.append(pltpu.make_async_copy(src.at[:, cols], dst.at[:, cols], late_sems.at[j, side, i]))
        return copies

    @pl.when(step == 0)
    def _():
        for copy in loads:
            copy.start()
        for copy in loads[:3]:
            copy.wait()

    @pl.when(step < blocks)
    def _():
        slot = lax.rem(step, 2)
        mine = pl.ds(pl.multiple_of((me * blocks + step) * HEAD, HEAD), HEAD)
        theirs = pl.ds(pl.multiple_of(((1 - me) * blocks + step) * HEAD, HEAD), HEAD)
        gb = jnp.concatenate([gmid[:, mine], gmid[:, theirs]], axis=1)
        first = nn(mixt[...], gb).astype(BF16)

        @pl.when(step == 0)
        def _():
            for copy in loads[3:]:
                copy.wait()
            for copy in more:
                copy.start()

        gs = jnp.concatenate([gsel[:, mine], gsel[:, theirs]], axis=1)
        made = [first, nn(normt[...], gs).astype(BF16)]
        for k, buffer in enumerate((outer.given, outer.kept)):
            for i in range(2):
                buffer[slot, i] = made[i][k * (d // 2) : (k + 1) * (d // 2), :]
            if k == 0:
                outer.begin(step)

    @pl.when(jnp.logical_and(step >= blocks, step < 2 * blocks))
    def _():
        j = step - blocks
        for side in range(2):
            slope = slopes[(me if side == 0 else 1 - me) * blocks + j]
            for k in range(2):
                decays[side, k] = decay_table(slope, k == 1)

        def one(c, carry):
            here = pl.ds(pl.multiple_of(c * CHUNK, CHUNK), CHUNK)
            cs, sn = layout.angles(c, fine, coarse)
            before, after = layout.before(c), layout.after(c)
            span = (CHUNK * c).astype(F32)
            rest = (CHUNK * (chunks - 1 - c)).astype(F32)
            for side in range(2):
                h = (me if side == 0 else 1 - me) * blocks + j
                slope = slopes[h]
                cols = pl.ds(pl.multiple_of(h * HEAD, HEAD), HEAD)
                four = [ref[here, cols] for ref in (qpre, kpre, val, gatt)]
                lane = jnp.zeros((1, 2 * HEAD), F32)
                state = st[c, h].astype(F32) + came[h].astype(F32) * (jnp.exp(lane - slope * span) * before)
                ending = et[c, h].astype(F32) + left[h].astype(F32) * (jnp.exp(lane - slope * rest) * after)
                three = head_back(
                    slope, decays[side, 0], decays[side, 1], *four, state, ending, cs, sn
                )
                for i in range(3):
                    block[here, head_slice(2 * i + side)] = three[i]
                    grads[i, here, cols] = three[i]
            return carry

        lax.fori_loop(0, chunks, one, 0)
        slot = lax.rem(j, 2)
        made = nn(normt[...], block[...]).astype(BF16)
        for k, buffer in enumerate((inner.given, inner.kept)):
            for i in range(3):
                buffer[slot, i] = made[k * (d // 2) : (k + 1) * (d // 2), feature_slice(i)]
            if k == 0:
                inner.begin(j)
        for copy in replaced(j):
            copy.start()

    @pl.when(step == blocks - 1)
    def _():
        select.start()
        for copy in more:
            copy.wait()

    @pl.when(step == 2 * blocks)
    def _():
        select.wait()
        for j in range(blocks):
            for copy in replaced(j):
                copy.wait()

    @pl.when(jnp.logical_and(step >= 2 * blocks, step < 2 * blocks + chunks))
    def _():
        here = pl.ds(pl.multiple_of((step - 2 * blocks) * CHUNK, CHUNK), CHUNK)
        total = nt(gsel[here, :], mixt[...])
        for i, w in enumerate((qpre, kpre, gatt)):
            total = total + nt(grads[i, here, :], w[...])
        x = val[here, :].astype(F32)
        hidden_o[...] = (gmid[here, :].astype(F32) + norm_back(x, scale_of(x), total)).astype(BF16)

    outer.run(step, out)
    inner.run(step, out2)


def run_projections(lengths, slopes, qpre, kpre, values, gatt, st, et, came, left, angles, gsel, hidden, gmid, mixed_t, normed_t, weights, depth, ident):
    n, d = qpre.shape
    heads, chunks = d // HEAD, n // CHUNK
    blocks = heads // 2
    rows = d // (4 * depth)
    outer = Reducer(0, blocks, 2, depth, rows, (1, 4, 5, 6), 4, (1, 2, 3, 4), (2, 2))
    inner = Reducer(blocks, blocks, 3, depth, rows, (1, 2, 3, 4), 4, (1, 2, 3, 4), (2, 2, 2))
    steps = max(outer.last, inner.last, 2 * blocks + chunks - 1) + 1
    geo = dict(chunks=chunks, blocks=blocks, d=d, n=n)
    late = lambda s: jnp.clip(s - 2 * blocks, 0, chunks - 1)
    whole = pltpu.VMEM((n, d), BF16)
    states = pltpu.VMEM((chunks,) + state_shape(d), BF16)
    one = pltpu.VMEM(state_shape(d), BF16)
    turned = pltpu.VMEM((d, n), BF16)
    return launch(
        functools.partial(projections_kernel, geo, outer, inner),
        "attention_backward_and_gradients",
        steps,
        [lengths, slopes, qpre, kpre, values, gatt, st, et, came, left, *angles]
        + [gsel, hidden, gmid, mixed_t, normed_t]
        + list(weights),
        [smem(), smem()] + [anywhere()] * 8 + [once(a.shape) for a in angles] + [anywhere()] * 9,
        [struct((n, d)), struct((2, rows, d // 2), F32), struct((3, rows, d // 2), F32)],
        [
            pl.BlockSpec((CHUNK, d), lambda s: (late(s), 0)),
            whole_block((2, rows, d // 2)),
            whole_block((3, rows, d // 2)),
        ],
        [whole] * 4
        + [states, states, one, whole, whole]
        + [
            pltpu.VMEM((3, n, d), BF16),
            pltpu.VMEM((n, 6 * HEAD), BF16),
            pltpu.VMEM((2, 2, CHUNK, CHUNK), F32),
            turned,
            turned,
            one,
            pltpu.SemaphoreType.DMA((15,)),
            pltpu.SemaphoreType.DMA((blocks, 2, 4)),
        ]
        + outer.scratch
        + inner.scratch,
        30 * n * d * d,
        partners=outer.partners,
        ident=ident,
    )


def input_kernel(wq, wk, wv, ws, grads, gsel, hid, gmid, out):
    total = nt(grads[0], wq[...]) + nt(grads[1], wk[...]) + nt(grads[2], wv[...]) + nt(gsel[...], ws[...])
    x = hid[...].astype(F32)
    out[...] = (gmid[...].astype(F32) + norm_back(x, scale_of(x), total)).astype(BF16)


def run_input(weights, grads, gsel, hidden, gmid):
    n, d = hidden.shape
    tile = pl.BlockSpec((CHUNK, d), lambda c: (c, 0))
    return launch(
        input_kernel,
        "input_gradient",
        n // CHUNK,
        list(weights) + [grads, gsel, hidden, gmid],
        [whole_block(w.shape) for w in weights]
        + [
            pl.BlockSpec((3, CHUNK, d), lambda c: (0, c, 0)),
            tile,
            tile,
            tile,
        ],
        [struct((n, d))],
        [tile],
        [],
        8 * n * d * d,
    )


def reduced(lefts, items, rights, spec, peers, width):
    full = run_weights(lefts, items, rights, spec, peers, width)
    parts = lax.axis_size("dp")
    full = full.reshape(peers, len(items), 2, parts // 2, -1, width)
    full = jnp.swapaxes(full, 2, 3).reshape(peers, len(items), parts, -1, width)
    mine = lax.psum_scatter(full, "dp", scatter_dimension=2, tiled=False)
    return lax.psum_scatter(mine, "mp", scatter_dimension=0, tiled=False).astype(F32)


def per_device(
    hidden_in,
    query_weight,
    key_weight,
    value_weight,
    select_weight,
    out_weight,
    first_weight,
    second_weight,
    down_weight,
    decay_slope,
    doc_lengths,
    cotangent,
):
    count, d = hidden_in.shape
    heads, chunks = d // HEAD, count // CHUNK
    peers, parts = lax.axis_size("mp"), lax.axis_size("dp")
    me = lax.axis_index("mp")
    depth = parts // 4
    group = count * peers
    units = first_weight.shape[1]
    lengths = doc_lengths.astype(jnp.int32)
    angles = tables(group // 2)
    slopes = decay_slope
    matrices = (first_weight, second_weight, down_weight)
    riding = peers == 2

    if riding:
        cut = units // 256 * 128
        ranges = [(0, cut), (cut, units - cut)]
    else:
        ranges = [(0, units)]

    def like(arrays, count=None):
        return [struct(a.shape if count is None else (count,) + a.shape) for a in arrays]

    def over_mp(g):
        low, size = ranges[g]

        def source(w):
            def src(i, o):
                eighth = lax.rem(lax.axis_index("dp"), 8)
                if w < 2:
                    rows = d // 8
                    return i[w].at[pl.ds(pl.multiple_of(eighth * rows, 16), rows), pl.ds(low, size)]
                rows = size // 8
                return i[w].at[pl.ds(pl.multiple_of(low + eighth * rows, 16), rows), :]

            return src

        outs = [struct((d // 8, size)), struct((d // 8, size)), struct((size // 8, d))]
        return outs, [(source(w), lambda i, o, w=w: o[w], "mp", 1) for w in range(3)]

    def near(src, dst):
        return [
            (lambda i, o: src(i, o), lambda i, o: dst(i, o).at[0], "dp", 2),
            (lambda i, o: src(i, o), lambda i, o: dst(i, o).at[1], "dp", 4),
            (lambda i, o: src(i, o), lambda i, o: dst(i, o).at[2], "dp", 1),
        ]

    def far(src, dst, rows, balanced):
        top = -(-rows // 32) * 16 if balanced else 0
        upper, lower = pl.ds(0, top), pl.ds(top, rows - top)
        over_x = (lambda i, o: src(i, o).at[1, upper, :], lambda i, o: dst(i, o).at[0, upper, :], "dp", 2)
        return ([over_x] if balanced else []) + [
            (lambda i, o: src(i, o).at[0, lower, :], lambda i, o: dst(i, o).at[0, lower, :], "dp", 4),
            (lambda i, o: src(i, o).at[0], lambda i, o: dst(i, o).at[1], "dp", 1),
            (lambda i, o: src(i, o).at[1], lambda i, o: dst(i, o).at[2], "dp", 1),
        ]

    def onward(pieces, out, at, balanced):
        ref = lambda k: lambda i, o: o[k]
        one, two, three = [], [], []
        for w in range(3):
            one += near(pieces(w), ref(at + w))
            two += far(ref(at + w), ref(at + 3 + w), out[w].shape[0], balanced)
            three.append((lambda i, o, w=w: o[at + 3 + w].at[0], ref(at + 6 + w), "dp", 1))
        return like(out, 3) + like(out, 3) + like(out), [one, two, three]

    if riding:
        outs, copies = over_mp(0)
        more, phases = onward(lambda w: lambda i, o: o[w], outs, 3, True)
        outs_b, copies_b = over_mp(1)
        spans = [(0, chunks), (chunks + 1, 2 * chunks), (2 * chunks + 1, 3 * chunks - 2), (3 * chunks - 1,) * 2]
        guests = [
            Carry(matrices, outs + more, [span + (c,) for span, c in zip(spans, [copies] + phases)]),
            Carry(matrices, outs_b, [(chunks + 2, 3 * chunks - 1, copies_b)]),
        ]
        weights = [key_weight, value_weight, query_weight, select_weight, out_weight]
        kpre, values, st, qpre, sel, normed_t, attended, mixed_t, middle, second, second_t, cot_t, came, *got = run_forward(
            lengths, slopes, hidden_in, cotangent, weights, angles, parts, guests, ident=1
        )
    else:
        normed, normed_t, kpre, values, st, final = run_keys(
            peers, lengths, slopes, hidden_in, key_weight, value_weight, angles, parts
        )
        begin, start, last = jnp.int32(0), jnp.int32(0), (me + 1) * count - CHUNK
        for i in range(lengths.shape[1]):
            begin = jnp.where(last >= start, start, begin)
            start = start + lengths[0, i]
        passes = (begin < me * count).astype(F32)
        decay = jnp.exp(-slopes * count)
        finals = lax.all_gather(final, "mp")
        keeps = lax.all_gather(passes.reshape(1), "mp")[:, 0]

        def ahead(k, total):
            new = finals[k].astype(F32) + (keeps[k] * decay)[:, None, None] * total
            return jnp.where(k < me, new, total)

        came = lax.fori_loop(0, peers, ahead, jnp.zeros(final.shape, F32)).astype(BF16)
        qpre, sel, att = run_inside(
            peers, lengths, slopes, normed, query_weight, select_weight, kpre, values, st, angles
        )
        attended, mixed_t, middle, second, second_t, cot_t = run_mix(
            peers, lengths, slopes, att, qpre, came, sel, out_weight, hidden_in, cotangent, angles, parts
        )

    if riding:
        had_b = got[12:15]
        more, phases = onward(lambda w: lambda i, o: i[w], had_b, 0, True)
        ride = Carry(had_b, more, [(0, 1, phases[0]), (2, 3, phases[1]), (4, 4, phases[2])])
        output, grad_middle, grad_sel, grad_att, et, left, sglu = run_units(
            lengths, slopes, matrices, second, cotangent, second_t, cot_t, [middle, sel, attended, qpre],
            angles, out_weight, got[:12], ride, ranges[0][1], depth, ident=2,
        )
    else:
        sources = [lax.all_gather(w, "mp") for w in matrices]
        grads, term, part = run_sglu(second, cotangent, *sources)
        units_spec = lambda at: pl.BlockSpec((None, None, count, units), lambda s: at(s) + (0, 0))
        sglu = reduced([second_t, cot_t], (0, 0, 1), grads, units_spec, peers, units)
        output, grad_middle, grad_sel, grad_att, et, leaving = run_after(
            peers, lengths, slopes, term, part, cotangent, middle, sel, attended, out_weight, qpre, angles
        )
    inputs_weights = [query_weight, key_weight, value_weight, select_weight]
    if riding:
        grad_hidden, out_sel, inputs = run_projections(
            lengths, slopes, qpre, kpre, values, grad_att, st, et, came, left, angles, grad_sel,
            hidden_in, grad_middle, mixed_t, normed_t, inputs_weights, depth, ident=3,
        )
    else:
        leavings = lax.all_gather(leaving, "mp")

        def behind(step, total):
            k = peers - 1 - step
            new = leavings[k].astype(F32) + (keeps[k] * decay)[:, None, None] * total
            return jnp.where(k > me, new, total)

        left = lax.fori_loop(0, peers, behind, jnp.zeros(leaving.shape, F32)).astype(BF16)
        share = d // peers
        wide_spec = lambda at: pl.BlockSpec((None, count, share), lambda s: (at(s)[0], 0, at(s)[1]))
        pair = jnp.stack([grad_middle, grad_sel])
        out_sel = reduced([mixed_t, normed_t], (0, 1), pair, wide_spec, peers, share)
        (qkv,) = run_attention_back(
            peers, lengths, slopes, qpre, kpre, values, grad_att, st, came, et, left, angles
        )
        inputs = reduced([normed_t], (0, 0, 0), qkv, wide_spec, peers, share)
        (grad_hidden,) = run_input(inputs_weights, qkv, grad_sel, hidden_in, grad_middle)
    return (
        output,
        grad_hidden,
        inputs[0],
        inputs[1],
        inputs[2],
        out_sel[1],
        out_sel[0],
        sglu[0],
        sglu[1],
        jnp.transpose(sglu[2]),
    )


def solution(mesh):
    rows = P(("dp", "mp"), None)
    in_specs = (
        rows,
        P(),
        P(),
        P(),
        P(),
        P(),
        P(None, "mp"),
        P(None, "mp"),
        P("mp", None),
        P(),
        P("dp", None),
        rows,
    )
    out_specs = (rows, rows) + (P("dp", "mp"),) * 7 + (P("mp", "dp"),)
    return jax.shard_map(
        per_device, mesh=mesh, in_specs=in_specs, out_specs=out_specs, check_vma=False
    )
```
